32 devices in a mesh: seq: 16 (over z, x, core), req: 2 (over y).
Axes of the slice: x: 2, y: 2, z: 4, core: 2. Of those that a mesh axis runs over, the one named last changes fastest.
Arguments:
- tokens: bfloat16 [2048, 2048], P('seq'), may hold values from -6 to 6
- norm_gain: float32 [2048], replicated, may hold values from 0.5 to 1.5
- w_query: bfloat16 [2048, 1024], P(None, 'req'), as said below
- key_projection: bfloat16 [2048, 512], P(None, 'req')
- value_projection: bfloat16 [2048, 512], P(None, 'req'), may hold values from -0.125 to 0.125
- w_out: bfloat16 [1024, 2048], P('req'), may hold values from -0.1875 to 0.1875
- lengths: int32 [4], replicated, may hold values from 1 to 1365, 2048 in all
- block_split: int32 [16], replicated, may hold values from 0 to 15, each once
- page_slot: int32 [64], replicated, may hold values from 0 to 127, as said below
Outputs:
- hidden: bfloat16 [2048, 2048], P(('seq', 'req'))
- key_value_cache: bfloat16 [128, 2, 32, 512], P('seq', None, None, 'req')
The draws below stay inside these ranges and needn't reach their ends.
Inputs may be any that keep to these rules, and one draw needn't show every extreme that they name: block_split is a permutation; index i of seq holds block block_split[i] and its mirror. `page_slot`: distinct slots; slot s lies on index s // 8 of seq. `w_query`: a projection scaled like 2 / sqrt(2048).
All inputs are finite; a program needn't handle non-finite values.
Results may differ from the reference program's by a relative error of at most 0.014.
The reference program's roundings to bfloat16 on the way count: a program that leaves them out, or rounds other values in their place, can miss the bound.
Values may be sent and summed in bfloat16 or wider, within the bound.
No kernel may reach another device: no remote copies, remote signals or barrier semaphores. Data moves between devices by JAX's collectives and lax.ppermute only.
A program may use at most 128 MiB of HBM per device.

```python
import math
import jax
import jax.numpy as jnp
import numpy as np
from jax import lax

MODEL_WIDTH = 2048
QUERY_HEADS = 8
KEY_VALUE_HEADS = 4
HEAD_SIZE = 128
TOKENS_PER_SEQ = 128
REQS = 4
PAGE_TOKENS = 32
TOTAL_TOKENS = 2048
PAGES_PER_SEQ = 8
NPAGES = 64
N_SEQ = 16


def query_key_pair(key):
    base_key = jax.random.fold_in(key, 11)
    first_key, second_random_key = jax.random.split(base_key, 2)
    spread_values = 2.0 / math.sqrt(MODEL_WIDTH)
    query_matrix = jax.random.normal(first_key, (MODEL_WIDTH, QUERY_HEADS * HEAD_SIZE), jnp.float32) * spread_values
    noise_sample = jax.random.normal(second_random_key, (MODEL_WIDTH, KEY_VALUE_HEADS * HEAD_SIZE), jnp.float32) * spread_values
    key_weight = noise_sample
    return (query_matrix.astype(jnp.bfloat16), key_weight.astype(jnp.bfloat16))


def draw_w_query(key, part):
    return query_key_pair(key)[0]


def draw_key_projection(key, part):
    return query_key_pair(key)[1]


def draw_page_slot(key, part):
    base_key = jax.random.fold_in(key, 29)
    heat_key, noise_key, order_key, page_key = jax.random.split(base_key, 4)
    slot_total = N_SEQ * PAGES_PER_SEQ
    levels = jax.random.randint(heat_key, (N_SEQ,), 0, 4)
    heat = levels * levels * 400
    noise_sample = jax.random.randint(noise_key, (N_SEQ, PAGES_PER_SEQ), 0, 2000)
    scores = (heat[:, None] + noise_sample).reshape(slot_total)
    scores = scores.at[slot_total - 1].set(10000)
    ranks = scores * slot_total + jax.random.permutation(order_key, slot_total)
    chosen = jnp.argsort(-ranks, stable=True)[:NPAGES]
    shuffle = jax.random.permutation(page_key, NPAGES)
    return chosen[shuffle].astype(jnp.int32)


def level_of(stream_key, shape, pieces, least, largest):
    def one(dim, blocks):
        steps = jax.random.uniform(jax.random.fold_in(jax.random.fold_in(stream_key, 6), dim), (blocks,), jnp.float32, least / len(pieces), largest / len(pieces))
        return jnp.repeat(jnp.exp(steps), shape[dim] // blocks).reshape((-1,) + (1,) * (len(shape) - dim - 1))

    loudness = one(*pieces[0])
    for cut in pieces[1:]:
        loudness = loudness * one(*cut)
    return loudness


def profile(number_of, total, bound, lean):
    loads = [(1 << 20) // math.isqrt(standing ** lean) + 1 for standing in range(2, number_of + 1)]
    rest, given = total - bound - (number_of - 1), [1] * (number_of - 1)
    while rest > 0:
        movable = [i for i in range(number_of - 1) if given[i] < bound]
        whole, remaining = sum([loads[i] for i in movable]), rest
        for i in movable:
            addition = min(bound - given[i], max(1, remaining * loads[i] // whole), rest)
            given[i] = given[i] + addition
            rest = rest - addition
    return np.array([bound] + given)


def ragged(stream_key, number_of, total, most, skew):
    if number_of == 2:
        one = jax.random.randint(stream_key, (), max(1, total - most), min(most, total - 1) + 1)
        return jnp.stack([one, total - one])
    tallies = jnp.asarray(profile(number_of, total, most, skew), jnp.int32)
    twos = (number_of - 1) // 2
    source_of, receiver = tallies[1:1 + 2 * twos:2], tallies[2:2 + 2 * twos:2]
    margin = jnp.minimum(source_of - 1, most - receiver)
    passed = jax.random.randint(jax.random.fold_in(stream_key, 1), (twos,), 0, 1 << 20) % (margin + 1)
    tallies = tallies.at[1:1 + 2 * twos:2].set(source_of - passed).at[2:2 + 2 * twos:2].set(receiver + passed)
    return tallies[jax.random.permutation(jax.random.fold_in(stream_key, 2), number_of)]


def bell_draw(rng, dims, spread, most, shards=(), held_as=jnp.bfloat16):
    level = level_of(rng, dims, shards, -0.22, 0.18) if shards else 1.0
    values = jax.random.normal(rng, dims, jnp.float32) * spread * level
    return jnp.minimum(jnp.maximum(values, -most), most).astype(held_as)


def setup_inputs(seed: int = 0) -> dict:
    key_list = jax.random.split(jax.random.key(seed), 10)
    return {
        "tokens": bell_draw(key_list[0], (TOTAL_TOKENS, MODEL_WIDTH), 1.0, 6.0, ((0, 16),)),
        "norm_gain": jnp.clip(1.0 + 0.1 * jax.random.normal(key_list[1], (MODEL_WIDTH,), jnp.float32), 0.5, 1.5),
        "w_query": draw_w_query(jax.random.fold_in(key_list[9], 71), 0),
        "key_projection": draw_key_projection(jax.random.fold_in(key_list[9], 71), 0),
        "value_projection": bell_draw(key_list[4], (MODEL_WIDTH, KEY_VALUE_HEADS * HEAD_SIZE), MODEL_WIDTH ** -0.5, 0.125, ((1, 2),)),
        "w_out": bell_draw(key_list[5], (QUERY_HEADS * HEAD_SIZE, MODEL_WIDTH), (QUERY_HEADS * HEAD_SIZE) ** -0.5, 0.1875, ((0, 2),)),
        "lengths": ragged(key_list[6], REQS, TOTAL_TOKENS, 2 * TOTAL_TOKENS // 3, 2).astype(jnp.int32),
        "block_split": jax.random.permutation(key_list[7], N_SEQ).astype(jnp.int32),
        "page_slot": draw_page_slot(jax.random.fold_in(key_list[9], 71), 0),
    }


theta_base = 1000000.0
norm_eps = 1e-05
far_below = -1e+30

def rotary_rows(heads, offset_list):
    half_width = heads.shape[-1] // 2
    exponent = jnp.arange(half_width, dtype=jnp.float32) * (2.0 / heads.shape[-1])
    inv_freq = jnp.power(theta_base, -exponent)
    angle = offset_list.astype(jnp.float32)[:, None] * inv_freq[None, :]
    cosine = jnp.concatenate([jnp.cos(angle), jnp.cos(angle)], -1)[:, None, :]
    sine = jnp.concatenate([jnp.sin(angle), jnp.sin(angle)], -1)[:, None, :]
    rolled = jnp.concatenate([-heads[..., half_width:], heads[..., :half_width]], -1)
    return heads * cosine + rolled * sine

def slot_positions(block_split, lengths, total_rows, shard_rows):
    row_ids = jnp.arange(total_rows, dtype=jnp.int32)
    half_rows = shard_rows // 2
    cycle_size = block_split.shape[0]
    owner_dev = row_ids // shard_rows
    device_ids = jnp.arange(cycle_size, dtype=jnp.int32)
    first_block = lax.optimization_barrier(jnp.sum(jnp.where(owner_dev[:, None] == device_ids[None, :], block_split[None, :], 0), 1)).astype(jnp.int32)
    block_ids = jnp.where(row_ids % shard_rows < half_rows, first_block, 2 * cycle_size - 1 - first_block)
    position = (block_ids * half_rows + row_ids % half_rows).astype(jnp.int32)
    request_ends = jnp.cumsum(lengths).astype(jnp.int32)
    request_begins = (request_ends - lengths).astype(jnp.int32)
    request = lax.optimization_barrier(jnp.sum((position[:, None] >= request_ends[None, :]).astype(jnp.int32), 1)).astype(jnp.int32)
    prompt_ids = jnp.arange(lengths.shape[0], dtype=jnp.int32)
    begins = lax.optimization_barrier(jnp.sum(jnp.where(request[:, None] == prompt_ids[None, :], request_begins[None, :], 0), 1)).astype(jnp.int32)
    return (position, request, (position - begins).astype(jnp.int32))

def reference(tokens, norm_gain, w_query, key_projection, value_projection, w_out, lengths, block_split, page_slot):
    position, request, offset_list = slot_positions(block_split, lengths, TOTAL_TOKENS, TOKENS_PER_SEQ)
    widened = tokens.astype(jnp.float32)
    normalized_input = (widened * lax.rsqrt(lax.optimization_barrier(jnp.mean(widened * widened, -1, keepdims=True)) + norm_eps) * norm_gain).astype(jnp.bfloat16)
    query_rotated = rotary_rows(jnp.dot(normalized_input, w_query, preferred_element_type=jnp.float32).reshape(TOTAL_TOKENS, QUERY_HEADS, HEAD_SIZE), offset_list).astype(jnp.bfloat16)
    key_matrix_rows = rotary_rows(jnp.dot(normalized_input, key_projection, preferred_element_type=jnp.float32).reshape(TOTAL_TOKENS, KEY_VALUE_HEADS, HEAD_SIZE), offset_list).astype(jnp.bfloat16)
    value_matrix_rows = jnp.dot(normalized_input, value_projection, preferred_element_type=jnp.float32).astype(jnp.bfloat16)
    group_width = QUERY_HEADS // KEY_VALUE_HEADS
    scale_factor = 1.0 / math.sqrt(HEAD_SIZE)
    key_wide = key_matrix_rows.astype(jnp.float32)
    value_widened = value_matrix_rows.astype(jnp.float32).reshape(TOTAL_TOKENS, KEY_VALUE_HEADS, HEAD_SIZE)
    query_block_list = query_rotated.astype(jnp.float32).reshape(N_SEQ, TOKENS_PER_SEQ, KEY_VALUE_HEADS, group_width, HEAD_SIZE)
    block_pos = position.reshape(N_SEQ, TOKENS_PER_SEQ)
    block_req = request.reshape(N_SEQ, TOKENS_PER_SEQ)

    def attend_block(item):
        query_block, query_pos, query_req = item
        scores = jnp.einsum('qhgd,khd->hgqk', query_block, key_wide, precision=lax.Precision.HIGHEST) * scale_factor
        visible = (request[None, :] == query_req[:, None]) & (position[None, :] <= query_pos[:, None])
        scores = jnp.where(visible[None, None], scores, far_below)
        top_score = lax.optimization_barrier(jnp.max(scores, -1, keepdims=True))
        raised = jnp.where(visible[None, None], jnp.exp(scores - top_score), 0.0)
        denominator = lax.optimization_barrier(jnp.sum(raised, -1))
        rounded = lax.optimization_barrier(raised.astype(jnp.bfloat16)).astype(jnp.float32)
        result = jnp.einsum('hgqk,khd->hgqd', rounded, value_widened, precision=lax.Precision.HIGHEST)
        result = result / denominator[..., None]
        return jnp.transpose(result, (2, 0, 1, 3)).reshape(TOKENS_PER_SEQ, QUERY_HEADS * HEAD_SIZE)
    context = lax.map(attend_block, (query_block_list, block_pos, block_req)).reshape(TOTAL_TOKENS, QUERY_HEADS * HEAD_SIZE).astype(jnp.bfloat16)
    hidden = (tokens.astype(jnp.float32) + jnp.dot(context, w_out, preferred_element_type=jnp.float32)).astype(jnp.bfloat16)
    slot_ids = page_slot[position // PAGE_TOKENS]
    target_rows = slot_ids * PAGE_TOKENS + position % PAGE_TOKENS
    paired_rows = jnp.stack([key_matrix_rows.reshape(TOTAL_TOKENS, KEY_VALUE_HEADS * HEAD_SIZE), value_matrix_rows], 1)
    flattened = jnp.zeros((N_SEQ * PAGES_PER_SEQ * PAGE_TOKENS, 2, KEY_VALUE_HEADS * HEAD_SIZE), jnp.bfloat16).at[target_rows].set(paired_rows)
    key_value_cache = jnp.transpose(flattened.reshape(N_SEQ * PAGES_PER_SEQ, PAGE_TOKENS, 2, KEY_VALUE_HEADS * HEAD_SIZE), (0, 2, 1, 3))
    return (hidden, key_value_cache)
```

```python
import functools
import math

import jax
import jax.numpy as jnp
import numpy as np
from jax import lax
from jax.experimental import pallas as pl
from jax.experimental.pallas import tpu as pltpu
from jax.sharding import PartitionSpec as P

HEAD = 128
PAGE = 32
THETA = 1000000.0
EPS = 1e-05
MASKED = -1e30
FLOOR = -1e29
WEIGHT_STEPS = 4
VMEM_BYTES = 48 * 1024 * 1024

f32 = jnp.float32
bf16 = jnp.bfloat16


def whole_vmem():
    return pl.BlockSpec(memory_space=pltpu.VMEM)


def whole_smem():
    return pl.BlockSpec(memory_space=pltpu.SMEM)


def anywhere():
    return pl.BlockSpec(memory_space=pl.ANY)


def inverse_frequencies():
    exponent = np.arange(HEAD // 2, dtype=np.float64) * (2.0 / HEAD)
    freq = (THETA**-exponent).astype(np.float32)
    return jnp.asarray(np.concatenate([freq, freq])[None, :])


def first_block(block_ref, shard):
    blocks = block_ref.shape[0]
    first = block_ref[shard]
    return first, 2 * blocks - 1 - first


def prompt_begin(position, len_ref):
    begin = jnp.zeros_like(position)
    start = jnp.int32(0)
    for r in range(len_ref.shape[0] - 1):
        start = start + len_ref[r]
        begin = jnp.where(position >= start, start, begin)
    return begin


def rotary_tables(shard, block_ref, len_ref, freq, rows):
    half = rows // 2
    row = lax.broadcasted_iota(jnp.int32, (rows, HEAD), 0)
    lane = lax.broadcasted_iota(jnp.int32, (rows, HEAD), 1)
    first, second = first_block(block_ref, shard)
    position = jnp.where(row < half, first * half + row, second * half + row - half)
    rel = (position - prompt_begin(position, len_ref)).astype(f32)
    angle = rel * freq
    sine = jnp.sin(angle)
    return jnp.cos(angle), jnp.where(lane < HEAD // 2, -sine, sine)


def rotate(u, cosine, signed_sine):
    return u * cosine + pltpu.roll(u, HEAD // 2, 1) * signed_sine


def weight_copies(refs, scratch, sems):
    copies = []
    depth = scratch.shape[0] // WEIGHT_STEPS
    for step in range(WEIGHT_STEPS):
        group, column = [], 0
        for i, ref in enumerate(refs):
            rows, cols = pl.ds(step * depth, depth), pl.ds(column, ref.shape[1])
            group.append(
                pltpu.make_async_copy(ref.at[rows, :], scratch.at[rows, cols], sems.at[step, i])
            )
            column += ref.shape[1]
        copies.append(group)
    return copies


def stepped_dot(left, copies, scratch):
    depth = scratch.shape[0] // WEIGHT_STEPS
    total = None
    for step in range(WEIGHT_STEPS):
        for copy in copies[step]:
            copy.wait()
        rows = pl.ds(step * depth, depth)
        part = jnp.dot(left[:, step * depth : (step + 1) * depth], scratch[rows, :], preferred_element_type=f32)
        total = part if total is None else total + part
    return total


def key_value_kernel(
    block_ref, len_ref, freq_ref, tok_ref, gain_ref, wk_ref, wv_ref,
    normed_ref, kv_ref, cos_ref, sin_ref, weights, sems,
):
    copies = weight_copies((wk_ref, wv_ref), weights, sems)
    for group in copies:
        for copy in group:
            copy.start()
    rows = tok_ref.shape[0]
    cosine, sine = rotary_tables(lax.axis_index("seq"), block_ref, len_ref, freq_ref[...], rows)
    cos_ref[...] = cosine
    sin_ref[...] = sine
    wide = tok_ref[...].astype(f32)
    scale = lax.rsqrt(jnp.mean(wide * wide, -1, keepdims=True) + EPS)
    normed = (wide * scale * gain_ref[...]).astype(bf16)
    normed_ref[...] = normed
    product = stepped_dot(normed, copies, weights)
    key_width = wk_ref.shape[1]
    for h in range(key_width // HEAD):
        cols = slice(h * HEAD, (h + 1) * HEAD)
        kv_ref[:, cols] = rotate(product[:, cols], cosine, sine).astype(bf16)
    kv_ref[:, key_width:] = product[:, key_width:].astype(bf16)


def query_kernel(normed_ref, cos_ref, sin_ref, wq_ref, q_ref, weights, sems):
    copies = weight_copies((wq_ref,), weights, sems)
    for group in copies:
        for copy in group:
            copy.start()
    cosine, sine = cos_ref[...], sin_ref[...]
    product = stepped_dot(normed_ref[...], copies, weights)
    for h in range(wq_ref.shape[1] // HEAD):
        cols = slice(h * HEAD, (h + 1) * HEAD)
        q_ref[:, cols] = rotate(product[:, cols], cosine, sine).astype(bf16)


def attend_kernel(
    n, chunk, sources, block_ref, len_ref, slot_ref, q_ref, tok_ref, wo_ref, *rest,
):
    counts = [count for count, _ in sources]
    pieces, rest = rest[: len(counts)], rest[len(counts) :]
    send_ref, keep_ref, cache_ref, kv, wo, context, page_of, kv_sem, wo_sem = rest
    shard = lax.axis_index("seq")
    part = lax.axis_index("req")
    rows, q_width = q_ref.shape
    half = rows // 2
    key_width = kv.shape[1] // 2
    kv_heads = key_width // HEAD
    group = q_width // key_width

    for ref, (count, source_of) in zip(pieces, sources):
        for i in range(count):
            for block, at in zip(first_block(block_ref, source_of(shard, i)), (0, half)):
                pltpu.make_async_copy(
                    ref.at[pl.ds(i * rows + at, half), :],
                    kv.at[pl.ds(pl.multiple_of(block * half, half), half), :],
                    kv_sem,
                ).start()
    out_copy = pltpu.make_async_copy(wo_ref, wo, wo_sem)
    out_copy.start()

    slots = cache_ref.shape[0]
    for t in range(slots):
        page_of[t] = -1

    def note_page(p, carry):
        slot = slot_ref[p] - shard * slots

        @pl.when((slot >= 0) & (slot < slots))
        def _():
            page_of[slot] = p

        return carry

    lax.fori_loop(0, slot_ref.shape[0], note_page, 0)
    pltpu.make_async_copy(kv, kv, kv_sem).wait()

    for t in range(slots):
        page = page_of[t]

        @pl.when(page >= 0)
        def _():
            held = kv[pl.ds(pl.multiple_of(page * PAGE, PAGE), PAGE), :]
            cache_ref[t, 0] = held[:, :key_width]
            cache_ref[t, 1] = held[:, key_width:]

        @pl.when(page < 0)
        def _():
            cache_ref[t] = jnp.zeros(cache_ref.shape[1:], bf16)

    scale = math.log2(math.e) / math.sqrt(HEAD)
    for at, block in zip((0, half), first_block(block_ref, shard)):
        row_position = block * half + lax.broadcasted_iota(jnp.int32, (half, 1), 0)
        row_begin = prompt_begin(row_position, len_ref)
        lane = lax.broadcasted_iota(jnp.int32, (group * half, chunk), 1)
        ends = jnp.concatenate([row_position] * group, 0)
        begins = jnp.concatenate([row_begin] * group, 0)
        start = jnp.int32(0)
        lowest = jnp.int32(0)
        for r in range(len_ref.shape[0] - 1):
            start = start + len_ref[r]
            lowest = jnp.where(block * half >= start, start, lowest)
        queries = [
            jnp.concatenate(
                [
                    q_ref[at : at + half, (g * group + j) * HEAD : (g * group + j + 1) * HEAD]
                    for j in range(group)
                ],
                0,
            )
            for g in range(kv_heads)
        ]

        def absorb(c, state):
            offset = pl.multiple_of(c * chunk, chunk)
            visible = (lane >= begins - offset) & (lane <= ends - offset)
            out = []
            for g in range(kv_heads):
                top, total, acc = state[g]
                keys = kv[pl.ds(offset, chunk), g * HEAD : (g + 1) * HEAD]
                values = kv[pl.ds(offset, chunk), key_width + g * HEAD : key_width + (g + 1) * HEAD]
                scores = lax.dot_general(
                    queries[g], keys, (((1,), (1,)), ((), ())), preferred_element_type=f32
                )
                scores = jnp.where(visible, scores * scale, MASKED)
                new_top = jnp.maximum(top, jnp.max(scores, -1, keepdims=True))
                weights = jnp.exp2(scores - new_top)
                factor = jnp.exp2(top - new_top)
                total = total * factor + jnp.sum(weights, -1, keepdims=True)
                acc = acc * factor + jnp.dot(weights.astype(bf16), values, preferred_element_type=f32)
                out.append((new_top, total, acc))
            return tuple(out)

        zero = (
            jnp.full((group * half, 1), FLOOR, f32),
            jnp.zeros((group * half, 1), f32),
            jnp.zeros((group * half, HEAD), f32),
        )
        low = lowest // chunk
        high = (block * half + half + chunk - 1) // chunk
        state = lax.fori_loop(low, high, absorb, (zero,) * kv_heads)
        for g in range(kv_heads):
            _, total, acc = state[g]
            result = (acc / total).astype(bf16)
            for j in range(group):
                h = g * group + j
                context[at : at + half, h * HEAD : (h + 1) * HEAD] = result[j * half : (j + 1) * half]

    out_copy.wait()
    product = jnp.dot(context[...], wo[...], preferred_element_type=f32)
    near, far = product[:half], product[half:]
    tok = tok_ref[pl.ds(pl.multiple_of(part * half, half), half), :].astype(f32)
    mine = jnp.where(part == 0, near, far)
    theirs = jnp.where(part == 0, far, near)
    send_ref[...] = theirs.astype(bf16)
    keep_ref[...] = mine + tok


def gather_shards(kv, n):
    rows = kv.shape[0]
    if n % 4 or n > 16:
        everyone = lax.all_gather(kv, "seq", axis=0, tiled=True)
        return [everyone], [(n, lambda shard, i: i)]
    outer = n // 4

    def moved(shift, flip):
        def source_of(shard, i):
            plane, inner = shard // 4, shard % 4
            if flip & 2:
                inner = jnp.where(inner >= 2, inner - 2, inner + 2)
            if flip & 1:
                inner = inner + 1 - 2 * (inner % 2)
            plane = lax.rem(plane + outer - shift, outer)
            return plane * 4 + inner

        return source_of

    def swap(x, bit):
        return lax.ppermute(x, "seq", [(i, i ^ bit) for i in range(n)])

    arrays, sources = [kv], [(1, moved(0, 0))]
    for shift in range(1, outer):
        perm = [(i, (i + 4 * shift) % n) for i in range(n)]
        arrays.append(lax.ppermute(kv, "seq", perm))
        sources.append((1, moved(shift, 0)))
    for flip in (2, 1):
        held = list(zip(arrays, sources))
        for k, (x, _) in enumerate(held):
            arrays.append(swap(x, flip))
            if flip == 2:
                sources.append((1, moved(k, 2)))
            else:
                sources.append((1, moved(k % outer, 1 + 2 * (k // outer))))
    return arrays, sources


def on_device(
    n, parts, tokens, norm_gain, w_query, key_projection, value_projection, w_out, lengths, block_split, page_slot,
):
    rows, width = tokens.shape
    half = rows // 2
    q_width = w_query.shape[1]
    kv_width = key_projection.shape[1] + value_projection.shape[1]
    params = pltpu.CompilerParams(vmem_limit_bytes=VMEM_BYTES)
    struct = jax.ShapeDtypeStruct
    normed, kv, cosine, sine = pl.pallas_call(
        key_value_kernel,
        out_shape=(
            struct((rows, width), bf16),
            struct((rows, kv_width), bf16),
            struct((rows, HEAD), f32),
            struct((rows, HEAD), f32),
        ),
        in_specs=[whole_smem()] * 2 + [whole_vmem()] * 3 + [anywhere()] * 2,
        out_specs=(whole_vmem(),) * 4,
        scratch_shapes=[
            pltpu.VMEM((width, kv_width), bf16),
            pltpu.SemaphoreType.DMA((WEIGHT_STEPS, 2)),
        ],
        compiler_params=params,
        cost_estimate=pl.CostEstimate(
            flops=2 * rows * width * kv_width, bytes_accessed=2 * width * kv_width, transcendentals=0
        ),
        name="key_value",
    )(
        block_split, lengths, inverse_frequencies(), tokens, norm_gain.reshape(1, width),
        key_projection, value_projection,
    )
    queries = pl.pallas_call(
        query_kernel,
        out_shape=struct((rows, q_width), bf16),
        in_specs=[whole_vmem()] * 3 + [anywhere()],
        out_specs=whole_vmem(),
        scratch_shapes=[
            pltpu.VMEM((width, q_width), bf16),
            pltpu.SemaphoreType.DMA((WEIGHT_STEPS, 1)),
        ],
        compiler_params=params,
        cost_estimate=pl.CostEstimate(
            flops=2 * rows * width * q_width, bytes_accessed=2 * width * q_width, transcendentals=0
        ),
        name="query",
    )(normed, cosine, sine, w_query)
    arrays, sources = gather_shards(kv, n)
    total_rows = n * rows
    chunk = math.gcd(total_rows, 512)
    slots = 2 * rows // PAGE
    sent, kept, cache = pl.pallas_call(
        functools.partial(attend_kernel, n, chunk, sources),
        out_shape=(
            struct((half, width), bf16),
            struct((half, width), f32),
            struct((slots, 2, PAGE, kv_width // 2), bf16),
        ),
        in_specs=[whole_smem()] * 3 + [whole_vmem()] * 2 + [anywhere()] * (1 + len(arrays)),
        out_specs=(whole_vmem(),) * 3,
        scratch_shapes=[
            pltpu.VMEM((total_rows, kv_width), bf16),
            pltpu.VMEM(w_out.shape, bf16),
            pltpu.VMEM((rows, q_width), bf16),
            pltpu.SMEM((slots,), jnp.int32),
            pltpu.SemaphoreType.DMA,
            pltpu.SemaphoreType.DMA,
        ],
        compiler_params=params,
        cost_estimate=pl.CostEstimate(
            flops=4 * rows * total_rows * q_width, bytes_accessed=2 * total_rows * kv_width, transcendentals=0
        ),
        name="attend",
    )(block_split, lengths, page_slot, queries, tokens, w_out, *arrays)
    received = lax.ppermute(sent, "req", [(i, (i + 1) % parts) for i in range(parts)])
    hidden = (kept + received.astype(f32)).astype(bf16)
    return hidden, cache


def solution(mesh):
    in_specs = (
        P("seq", None),
        P(),
        P(None, "req"),
        P(None, "req"),
        P(None, "req"),
        P("req", None),
        P(),
        P(),
        P(),
    )
    out_specs = (P(("seq", "req"), None), P("seq", None, None, "req"))
    body = functools.partial(on_device, mesh.shape["seq"], mesh.shape["req"])
    return jax.shard_map(body, mesh=mesh, in_specs=in_specs, out_specs=out_specs, check_vma=False)
```

```python
import functools
import math

import jax
import jax.numpy as jnp
import numpy as np
from jax import lax
from jax.experimental import pallas as pl
from jax.experimental.pallas import tpu as pltpu
from jax.sharding import PartitionSpec as P

HEAD = 128
PAGE = 32
THETA = 1000000.0
EPS = 1e-05
MASKED = -1e30
FLOOR = -1e29
WEIGHT_STEPS = 4
MIB = 1024 * 1024
SCALE = math.log2(math.e) / math.sqrt(HEAD)

f32 = jnp.float32
bf16 = jnp.bfloat16
struct = jax.ShapeDtypeStruct


def in_vmem(count):
    return [pl.BlockSpec(memory_space=pltpu.VMEM)] * count


def in_smem(count):
    return [pl.BlockSpec(memory_space=pltpu.SMEM)] * count


def in_hbm(count):
    return [pl.BlockSpec(memory_space=pltpu.HBM)] * count


def kernel_params(mib):
    return pltpu.CompilerParams(vmem_limit_bytes=mib * MIB)


def cost(flops, moved):
    return pl.CostEstimate(flops=flops, bytes_accessed=moved, transcendentals=0)


def inverse_frequencies():
    exponent = np.arange(HEAD // 2, dtype=np.float64) * (2.0 / HEAD)
    freq = (THETA**-exponent).astype(np.float32)
    return jnp.asarray(np.concatenate([freq, freq])[None, :])


def blocks_of(block_ref, shard):
    first = block_ref[shard]
    return first, 2 * block_ref.shape[0] - 1 - first


def prompt_begin(position, len_ref):
    begin = jnp.zeros_like(position)
    start = jnp.int32(0)
    for r in range(len_ref.shape[0] - 1):
        start = start + len_ref[r]
        begin = jnp.where(position >= start, start, begin)
    return begin


def positions(block_ref, shards, rows, dim, shape):
    half = rows // 2
    index = lax.broadcasted_iota(jnp.int32, shape, dim)
    blocks = [block for shard in shards for block in blocks_of(block_ref, shard)]
    offset = blocks[0] * half
    for i, block in enumerate(blocks[1:], 1):
        offset = jnp.where(index >= i * half, (block - i) * half, offset)
    return index + offset


def rotate(u, cosine, signed_sine):
    return u * cosine + pltpu.roll(u, HEAD // 2, 1) * signed_sine


def weight_copies(refs, scratch, sems):
    copies = []
    depth = scratch.shape[0] // WEIGHT_STEPS
    for step in range(WEIGHT_STEPS):
        group, column = [], 0
        for i, ref in enumerate(refs):
            rows, cols = pl.ds(step * depth, depth), pl.ds(column, ref.shape[1])
            group.append(
                pltpu.make_async_copy(ref.at[rows, :], scratch.at[rows, cols], sems.at[step, i])
            )
            column += ref.shape[1]
        copies.append(group)
    return copies


def start_all(copies):
    for group in copies:
        for copy in group:
            copy.start()


def stepped_dot(left, copies, scratch):
    depth = scratch.shape[0] // WEIGHT_STEPS
    total = None
    for step in range(WEIGHT_STEPS):
        for copy in copies[step]:
            copy.wait()
        rows = slice(step * depth, (step + 1) * depth)
        part = jnp.dot(left[:, rows], scratch[rows, :], preferred_element_type=f32)
        total = part if total is None else total + part
    return total


def key_value_kernel(
    block_hbm, len_hbm, freq_hbm, tok_hbm, gain_hbm, wk_ref, wv_ref,
    normed_ref, kv_ref, cos_ref, sin_ref,
    block_ref, len_ref, freq_ref, tok_ref, gain_ref, weights, small_sems, sems,
):
    small = [
        pltpu.make_async_copy(source, target, small_sems.at[i])
        for i, (source, target) in enumerate(
            (
                (block_hbm, block_ref),
                (len_hbm, len_ref),
                (freq_hbm, freq_ref),
                (tok_hbm, tok_ref),
                (gain_hbm, gain_ref),
            )
        )
    ]
    copies = weight_copies((wk_ref, wv_ref), weights, sems)
    for copy in small:
        copy.start()
    start_all(copies)
    rows = tok_ref.shape[0]
    for copy in small[:3]:
        copy.wait()
    position = positions(block_ref, [lax.axis_index("seq")], rows, 0, (rows, HEAD))
    angle = (position - prompt_begin(position, len_ref)).astype(f32) * freq_ref[...]
    cosine, sine = jnp.cos(angle), jnp.sin(angle)
    lane = lax.broadcasted_iota(jnp.int32, (rows, HEAD), 1)
    sine = jnp.where(lane < HEAD // 2, -sine, sine)
    cos_ref[...] = cosine
    sin_ref[...] = sine
    for copy in small[3:]:
        copy.wait()
    wide = tok_ref[...].astype(f32)
    scale = lax.rsqrt(jnp.mean(wide * wide, -1, keepdims=True) + EPS)
    normed = (wide * scale * gain_ref[...]).astype(bf16)
    normed_ref[...] = normed
    product = stepped_dot(normed, copies, weights)
    key_width = wk_ref.shape[1]
    for h in range(key_width // HEAD):
        cols = slice(h * HEAD, (h + 1) * HEAD)
        kv_ref[:, cols] = rotate(product[:, cols], cosine, sine).astype(bf16)
    kv_ref[:, key_width:] = product[:, key_width:].astype(bf16)


def query_kernel(normed_ref, cos_ref, sin_ref, wq_ref, q_ref, weights, sems):
    copies = weight_copies((wq_ref,), weights, sems)
    start_all(copies)
    cosine, sine = cos_ref[...], sin_ref[...]
    product = stepped_dot(normed_ref[...], copies, weights)
    for h in range(wq_ref.shape[1] // HEAD):
        cols = slice(h * HEAD, (h + 1) * HEAD)
        q_ref[:, cols] = rotate(product[:, cols], cosine, sine).astype(bf16)


def attend_kernel(sources, first, last, block_ref, len_ref, q_ref, far_ref, *refs):
    pieces, refs = refs[: len(sources)], refs[len(sources) :]
    shard = lax.axis_index("seq")
    rows, q_width = q_ref.shape
    key_width = pieces[0].shape[1] // 2
    kv_heads = key_width // HEAD
    group = q_width // key_width
    both = 2 * rows
    q_pos = positions(block_ref, [shard, shard ^ 1], rows, 0, (both, 1))
    q_begin = prompt_begin(q_pos, len_ref)
    queries = [
        jnp.concatenate(
            [
                ref[:, h * HEAD : (h + 1) * HEAD]
                for h in range(g * group, (g + 1) * group)
                for ref in (q_ref, far_ref)
            ],
            0,
        )
        for g in range(kv_heads)
    ]

    def absorb(state, blocks, shards):
        width = rows * len(blocks)
        key_pos = positions(block_ref, shards, rows, 1, (1, width))
        bias = jnp.where((key_pos >= q_begin) & (key_pos <= q_pos), 0.0, MASKED)
        bias = jnp.concatenate([bias] * group, 0)
        out = []
        for g in range(kv_heads):
            top, total, acc = state[g]
            keys = jnp.concatenate([b[:, g * HEAD : (g + 1) * HEAD] for b in blocks], 0)
            values = jnp.concatenate(
                [b[:, key_width + g * HEAD : key_width + (g + 1) * HEAD] for b in blocks], 0
            )
            scores = lax.dot_general(
                queries[g], keys, (((1,), (1,)), ((), ())), preferred_element_type=f32
            )
            scores = scores * SCALE + bias
            new_top = jnp.maximum(top, jnp.max(scores, -1, keepdims=True))
            weights = jnp.exp2(scores - new_top)
            factor = jnp.exp2(top - new_top)
            total = total * factor + jnp.sum(weights, -1, keepdims=True)
            acc = acc * factor + jnp.dot(weights.astype(bf16), values, preferred_element_type=f32)
            out.append((new_top, total, acc))
        return tuple(out)

    if first:
        state = (
            (
                jnp.full((group * both, 1), FLOOR, f32),
                jnp.zeros((group * both, 1), f32),
                jnp.zeros((group * both, HEAD), f32),
            ),
        ) * kv_heads
    else:
        (top_ref, total_ref, acc_ref), refs = refs[:3], refs[3:]
        state = tuple(
            (top_ref[g][:, :1], total_ref[g][:, :1], acc_ref[g]) for g in range(kv_heads)
        )
    if all(count == 1 for count, _ in sources):
        for i in range(0, len(sources), 2):
            span = range(i, min(i + 2, len(sources)))
            state = absorb(
                state, [pieces[k][...] for k in span], [sources[k][1](shard, 0) for k in span]
            )
    else:
        for ref, (count, source_of) in zip(pieces, sources):

            def step(i, carried):
                at = pl.multiple_of(i * rows, rows)
                return absorb(carried, [ref[pl.ds(at, rows), :]], [source_of(shard, i)])

            state = lax.fori_loop(0, count, step, state)

    if not last:
        top_ref, total_ref, acc_ref = refs
        for g in range(kv_heads):
            top, total, acc = state[g]
            top_ref[g] = jnp.broadcast_to(top, acc.shape)
            total_ref[g] = jnp.broadcast_to(total, acc.shape)
            acc_ref[g] = acc
        return
    mine_ref, log_ref, packed_ref = refs
    lane = lax.broadcasted_iota(jnp.int32, (rows, HEAD), 1)
    logs = jnp.zeros((rows, HEAD), f32)
    parts = jnp.zeros((rows, HEAD), f32)
    for g in range(kv_heads):
        top, total, acc = state[g]
        some = total > 0.0
        safe = jnp.where(some, total, 1.0)
        result = acc / safe
        log_sum = jnp.where(some, top + jnp.log(safe) * math.log2(math.e), FLOOR)
        for j in range(group):
            h = g * group + j
            cols = slice(h * HEAD, (h + 1) * HEAD)
            near = slice(j * both, j * both + rows)
            far = slice(j * both + rows, (j + 1) * both)
            mine_ref[:, cols] = result[near]
            packed_ref[:, cols] = result[far].astype(bf16)
            logs = jnp.where(lane == h, log_sum[near], logs)
            left = log_sum[far]
            for t in range(3):
                part = left.astype(bf16).astype(f32)
                parts = jnp.where(lane == 3 * h + t, part, parts)
                left = left - part
    log_ref[...] = logs
    packed_ref[:, q_width:] = parts.astype(bf16)


def merge_kernel(mine_ref, log_ref, packed_ref, wo_ref, sent_ref, kept_ref):
    rows, q_width = mine_ref.shape
    half = rows // 2
    logs = log_ref[...]
    parts = packed_ref[:, q_width:].astype(f32)
    heads = []
    for h in range(q_width // HEAD):
        cols = slice(h * HEAD, (h + 1) * HEAD)
        near = logs[:, h : h + 1]
        far = parts[:, 3 * h : 3 * h + 1] + parts[:, 3 * h + 1 : 3 * h + 2] + parts[:, 3 * h + 2 : 3 * h + 3]
        top = jnp.maximum(near, far)
        near, far = jnp.exp2(near - top), jnp.exp2(far - top)
        joined = mine_ref[:, cols] * near + packed_ref[:, cols].astype(f32) * far
        heads.append((joined / (near + far)).astype(bf16))
    context = jnp.concatenate(heads, 1)
    upper = lax.axis_index("req") == 0
    kept_ref[...] = jnp.where(upper, context[:half], context[half:])
    leaving = jnp.where(upper, context[half:], context[:half])
    sent_ref[...] = jnp.dot(leaving, wo_ref[...], preferred_element_type=f32).astype(bf16)


def keep_kernel(context_ref, wo_ref, tok_ref, out_ref):
    half = context_ref.shape[0]
    first = pl.multiple_of(lax.axis_index("req") * half, half)
    residual = tok_ref[pl.ds(first, half), :].astype(f32)
    out_ref[...] = jnp.dot(context_ref[...], wo_ref[...], preferred_element_type=f32) + residual


def cache_kernel(sources, block_ref, slot_ref, *refs):
    pieces, (mine_ref, other_ref) = refs[: len(sources)], refs[len(sources) :]
    shard = lax.axis_index("seq")
    slots = mine_ref.shape[0]
    key_width = mine_ref.shape[3]
    rows = slots * PAGE // 2
    pages = rows // 2 // PAGE
    mine_ref[...] = jnp.zeros_like(mine_ref)
    other_ref[...] = jnp.zeros_like(other_ref)

    def place(ref, at, source):
        for k, block in enumerate(blocks_of(block_ref, source)):
            for j in range(pages):
                slot = slot_ref[block * pages + j]
                holder = slot // slots
                local = slot - holder * slots
                offset = at + (k * pages + j) * PAGE
                if not isinstance(offset, int):
                    offset = pl.multiple_of(offset, PAGE)
                for target, owner in ((mine_ref, shard), (other_ref, shard ^ 1)):

                    @pl.when(holder == owner)
                    def _():
                        target[local, 0] = ref[pl.ds(offset, PAGE), :key_width]
                        target[local, 1] = ref[pl.ds(offset, PAGE), key_width:]

    for ref, (count, source_of) in zip(pieces, sources):
        if count == 1:
            place(ref, 0, source_of(shard, 0))
        else:

            def step(i, carry):
                place(ref, i * rows, source_of(shard, i))
                return carry

            lax.fori_loop(0, count, step, 0)


def swap(x, n, bit):
    return lax.ppermute(x, "seq", [(i, i ^ bit) for i in range(n)])


def gather_shards(kv, n):
    if n % 4 or n > 16:
        same = [list(range(c, n, 2)) for c in range(2)]
        everyone = lax.all_gather(kv, "seq", axis=0, tiled=True, axis_index_groups=same)
        return [([everyone], [(n // 2, lambda shard, i: 2 * i + shard % 2)])]
    outer = n // 4

    def moved(shift, flip):
        def source_of(shard, i):
            plane = lax.rem(shard // 4 + outer - shift, outer)
            return plane * 4 + ((shard % 4) ^ flip)

        return 1, source_of

    early, late = [(kv, moved(0, 0)), (swap(kv, n, 2), moved(0, 2))], []
    for k, shift in enumerate(range(outer - 1, 0, -1)):
        turned = lax.ppermute(kv, "seq", [(i, (i + 4 * shift) % n) for i in range(n)])
        (early if k < 2 else late).append((turned, moved(shift, 0)))
        late.append((swap(turned, n, 2), moved(shift, 2)))
    return [tuple(zip(*group)) for group in (early, late) if group]


def on_device(
    n, parts, tokens, norm_gain, w_query, key_projection, value_projection, w_out, lengths, block_split, page_slot,
):
    rows, width = tokens.shape
    half = rows // 2
    q_width = w_query.shape[1]
    kv_width = key_projection.shape[1] + value_projection.shape[1]
    kv_heads = key_projection.shape[1] // HEAD
    stacked = 2 * rows * q_width // (kv_heads * HEAD)
    normed, kv, cosine, sine = pl.pallas_call(
        key_value_kernel,
        out_shape=(
            struct((rows, width), bf16),
            struct((rows, kv_width), bf16),
            struct((rows, HEAD), f32),
            struct((rows, HEAD), f32),
        ),
        in_specs=in_hbm(7),
        out_specs=tuple(in_vmem(4)),
        scratch_shapes=[
            pltpu.SMEM(block_split.shape, jnp.int32),
            pltpu.SMEM(lengths.shape, jnp.int32),
            pltpu.VMEM((1, HEAD), f32),
            pltpu.VMEM((rows, width), bf16),
            pltpu.VMEM((1, width), f32),
            pltpu.VMEM((width, kv_width), bf16),
            pltpu.SemaphoreType.DMA((5,)),
            pltpu.SemaphoreType.DMA((WEIGHT_STEPS, 2)),
        ],
        compiler_params=kernel_params(62),
        cost_estimate=cost(2 * rows * width * kv_width, 2 * width * kv_width),
        name="key_value",
    )(
        block_split, lengths, inverse_frequencies(), tokens, norm_gain.reshape(1, width),
        key_projection, value_projection,
    )
    queries = pl.pallas_call(
        query_kernel,
        out_shape=struct((rows, q_width), bf16),
        in_specs=in_vmem(3) + in_hbm(1),
        out_specs=in_vmem(1)[0],
        scratch_shapes=[
            pltpu.VMEM((width, q_width), bf16),
            pltpu.SemaphoreType.DMA((WEIGHT_STEPS, 1)),
        ],
        compiler_params=kernel_params(24),
        cost_estimate=cost(2 * rows * width * q_width, 2 * width * q_width),
        name="query",
    )(normed, cosine, sine, w_query)
    groups = gather_shards(kv, n)
    far_queries = swap(queries, n, 1)

    state = ()
    for i, (arrays, sources) in enumerate(groups):
        first, last = i == 0, i == len(groups) - 1
        if last:
            shapes = (
                struct((rows, q_width), f32),
                struct((rows, HEAD), f32),
                struct((rows, q_width + HEAD), bf16),
            )
        else:
            shapes = (struct((kv_heads, stacked, HEAD), f32),) * 3
        keys = sum(count for count, _ in sources) * rows
        state = pl.pallas_call(
            functools.partial(attend_kernel, sources, first, last),
            out_shape=shapes,
            in_specs=in_smem(2) + in_vmem(2 + len(arrays) + len(state)),
            out_specs=tuple(in_vmem(len(shapes))),
            compiler_params=kernel_params(32),
            cost_estimate=cost(8 * rows * keys * q_width, 2 * keys * kv_width),
            name="attend",
        )(block_split, lengths, queries, far_queries, *arrays, *state)
    mine, logs, packed = state
    packed = swap(packed, n, 1)
    sent, kept = pl.pallas_call(
        merge_kernel,
        out_shape=(struct((half, width), bf16), struct((half, q_width), bf16)),
        in_specs=in_vmem(4),
        out_specs=tuple(in_vmem(2)),
        compiler_params=kernel_params(24),
        cost_estimate=cost(rows * width * q_width, 2 * width * q_width),
        name="merge",
    )(mine, logs, packed, w_out)
    received = lax.ppermute(sent, "req", [(i, (i + 1) % parts) for i in range(parts)])
    kept = pl.pallas_call(
        keep_kernel,
        out_shape=struct((half, width), f32),
        in_specs=in_vmem(3),
        out_specs=in_vmem(1)[0],
        compiler_params=kernel_params(24),
        cost_estimate=cost(rows * width * q_width, 2 * width * q_width),
        name="keep",
    )(kept, w_out, tokens)

    arrays = [x for held, _ in groups for x in held]
    sources = [s for _, where in groups for s in where]
    arrays, _ = lax.optimization_barrier((arrays, sent))
    shape = (2 * rows // PAGE, 2, PAGE, kv_width // 2)
    cache, other = pl.pallas_call(
        functools.partial(cache_kernel, sources),
        out_shape=(struct(shape, bf16),) * 2,
        in_specs=in_smem(2) + in_vmem(len(arrays)),
        out_specs=tuple(in_vmem(2)),
        compiler_params=kernel_params(32),
        cost_estimate=cost(0, 4 * rows * kv_width),
        name="cache",
    )(block_split, page_slot, *arrays)
    cache = cache + swap(other, n, 1)
    hidden = (kept + received.astype(f32)).astype(bf16)
    return hidden, cache


def solution(mesh):
    in_specs = (
        P("seq", None),
        P(),
        P(None, "req"),
        P(None, "req"),
        P(None, "req"),
        P("req", None),
        P(),
        P(),
        P(),
    )
    out_specs = (P(("seq", "req"), None), P("seq", None, None, "req"))
    body = functools.partial(on_device, mesh.shape["seq"], mesh.shape["req"])
    return jax.shard_map(body, mesh=mesh, in_specs=in_specs, out_specs=out_specs, check_vma=False)
```

```python
import functools
import math

import jax
import jax.numpy as jnp
import numpy as np
from jax import lax
from jax.experimental import pallas as pl
from jax.experimental.pallas import tpu as pltpu
from jax.sharding import PartitionSpec as P

HEAD = 128
PAGE = 32
THETA = 1000000.0
EPS = 1e-05
MASKED = -1e30
FLOOR = -1e29
WEIGHT_STEPS = 4
MIB = 1024 * 1024
SCALE = math.log2(math.e) / math.sqrt(HEAD)

f32 = jnp.float32
bf16 = jnp.bfloat16
struct = jax.ShapeDtypeStruct


def in_vmem(count):
    return [pl.BlockSpec(memory_space=pltpu.VMEM)] * count


def in_smem(count):
    return [pl.BlockSpec(memory_space=pltpu.SMEM)] * count


def in_hbm(count):
    return [pl.BlockSpec(memory_space=pltpu.HBM)] * count


def kernel_params(mib):
    return pltpu.CompilerParams(vmem_limit_bytes=mib * MIB)


def cost(flops, moved):
    return pl.CostEstimate(flops=flops, bytes_accessed=moved, transcendentals=0)


def inverse_frequencies():
    exponent = np.arange(HEAD // 2, dtype=np.float64) * (2.0 / HEAD)
    freq = (THETA**-exponent).astype(np.float32)
    return jnp.asarray(np.concatenate([freq, freq])[None, :])


def blocks_of(block_ref, shard):
    first = block_ref[shard]
    return first, 2 * block_ref.shape[0] - 1 - first


def prompt_begin(position, len_ref):
    begin = jnp.zeros_like(position)
    start = jnp.int32(0)
    for r in range(len_ref.shape[0] - 1):
        start = start + len_ref[r]
        begin = jnp.where(position >= start, start, begin)
    return begin


def positions(block_ref, shards, rows, dim, shape):
    half = rows // 2
    index = lax.broadcasted_iota(jnp.int32, shape, dim)
    blocks = [block for shard in shards for block in blocks_of(block_ref, shard)]
    offset = blocks[0] * half
    for i, block in enumerate(blocks[1:], 1):
        offset = jnp.where(index >= i * half, (block - i) * half, offset)
    return index + offset


def rotate(u, cosine, signed_sine):
    return u * cosine + pltpu.roll(u, HEAD // 2, 1) * signed_sine


def weight_copies(refs, scratch, sems):
    copies = []
    depth = scratch.shape[0] // WEIGHT_STEPS
    for step in range(WEIGHT_STEPS):
        group, column = [], 0
        for i, ref in enumerate(refs):
            rows, cols = pl.ds(step * depth, depth), pl.ds(column, ref.shape[1])
            group.append(
                pltpu.make_async_copy(ref.at[rows, :], scratch.at[rows, cols], sems.at[step, i])
            )
            column += ref.shape[1]
        copies.append(group)
    return copies


def start_all(copies):
    for group in copies:
        for copy in group:
            copy.start()


def stepped_dot(left, copies, scratch):
    depth = scratch.shape[0] // WEIGHT_STEPS
    total = None
    for step in range(WEIGHT_STEPS):
        for copy in copies[step]:
            copy.wait()
        rows = slice(step * depth, (step + 1) * depth)
        part = jnp.dot(left[:, rows], scratch[rows, :], preferred_element_type=f32)
        total = part if total is None else total + part
    return total


def key_value_kernel(
    block_hbm, len_hbm, freq_hbm, tok_hbm, gain_hbm, wk_ref, wv_ref,
    normed_ref, kv_ref, cos_ref, sin_ref,
    block_ref, len_ref, freq_ref, tok_ref, gain_ref, weights, small_sems, sems,
):
    small = [
        pltpu.make_async_copy(source, target, small_sems.at[i])
        for i, (source, target) in enumerate(
            (
                (block_hbm, block_ref),
                (len_hbm, len_ref),
                (freq_hbm, freq_ref),
                (tok_hbm, tok_ref),
                (gain_hbm, gain_ref),
            )
        )
    ]
    copies = weight_copies((wk_ref, wv_ref), weights, sems)
    for copy in small:
        copy.start()
    start_all(copies)
    rows = tok_ref.shape[0]
    for copy in small[:3]:
        copy.wait()
    position = positions(block_ref, [lax.axis_index("seq")], rows, 0, (rows, HEAD))
    angle = (position - prompt_begin(position, len_ref)).astype(f32) * freq_ref[...]
    cosine, sine = jnp.cos(angle), jnp.sin(angle)
    lane = lax.broadcasted_iota(jnp.int32, (rows, HEAD), 1)
    sine = jnp.where(lane < HEAD // 2, -sine, sine)
    cos_ref[...] = cosine
    sin_ref[...] = sine
    for copy in small[3:]:
        copy.wait()
    wide = tok_ref[...].astype(f32)
    scale = lax.rsqrt(jnp.mean(wide * wide, -1, keepdims=True) + EPS)
    normed = (wide * scale * gain_ref[...]).astype(bf16)
    normed_ref[...] = normed
    product = stepped_dot(normed, copies, weights)
    key_width = wk_ref.shape[1]
    for h in range(key_width // HEAD):
        cols = slice(h * HEAD, (h + 1) * HEAD)
        kv_ref[:, cols] = rotate(product[:, cols], cosine, sine).astype(bf16)
    kv_ref[:, key_width:] = product[:, key_width:].astype(bf16)


def query_kernel(
    normed_hbm, cos_hbm, sin_hbm, wq_ref, q_ref, normed_ref, cos_ref, sin_ref, weights, small_sems, sems,
):
    small = [
        pltpu.make_async_copy(source, target, small_sems.at[i])
        for i, (source, target) in enumerate(
            ((normed_hbm, normed_ref), (cos_hbm, cos_ref), (sin_hbm, sin_ref))
        )
    ]
    copies = weight_copies((wq_ref,), weights, sems)
    for copy in small:
        copy.start()
    start_all(copies)
    for copy in small:
        copy.wait()
    cosine, sine = cos_ref[...], sin_ref[...]
    product = stepped_dot(normed_ref[...], copies, weights)
    for h in range(wq_ref.shape[1] // HEAD):
        cols = slice(h * HEAD, (h + 1) * HEAD)
        q_ref[:, cols] = rotate(product[:, cols], cosine, sine).astype(bf16)


def attend_kernel(sources, first, last, block_ref, len_ref, q_ref, far_ref, *refs):
    pieces, refs = refs[: len(sources)], refs[len(sources) :]
    shard = lax.axis_index("seq")
    rows, q_width = q_ref.shape
    key_width = pieces[0].shape[1] // 2
    kv_heads = key_width // HEAD
    group = q_width // key_width
    both = 2 * rows
    q_pos = positions(block_ref, [shard, shard ^ 1], rows, 0, (both, 1))
    q_begin = prompt_begin(q_pos, len_ref)
    queries = [
        jnp.concatenate(
            [
                ref[:, h * HEAD : (h + 1) * HEAD]
                for h in range(g * group, (g + 1) * group)
                for ref in (q_ref, far_ref)
            ],
            0,
        )
        for g in range(kv_heads)
    ]

    def absorb(state, blocks, shards):
        width = rows * len(blocks)
        key_pos = positions(block_ref, shards, rows, 1, (1, width))
        bias = jnp.where((key_pos >= q_begin) & (key_pos <= q_pos), 0.0, MASKED)
        bias = jnp.concatenate([bias] * group, 0)
        out = []
        for g in range(kv_heads):
            top, total, acc = state[g]
            keys = jnp.concatenate([b[:, g * HEAD : (g + 1) * HEAD] for b in blocks], 0)
            values = jnp.concatenate(
                [b[:, key_width + g * HEAD : key_width + (g + 1) * HEAD] for b in blocks], 0
            )
            scores = lax.dot_general(
                queries[g], keys, (((1,), (1,)), ((), ())), preferred_element_type=f32
            )
            scores = scores * SCALE + bias
            new_top = jnp.maximum(top, jnp.max(scores, -1, keepdims=True))
            weights = jnp.exp2(scores - new_top)
            factor = jnp.exp2(top - new_top)
            total = total * factor + jnp.sum(weights, -1, keepdims=True)
            acc = acc * factor + jnp.dot(weights.astype(bf16), values, preferred_element_type=f32)
            out.append((new_top, total, acc))
        return tuple(out)

    if first:
        state = (
            (
                jnp.full((group * both, 1), FLOOR, f32),
                jnp.zeros((group * both, 1), f32),
                jnp.zeros((group * both, HEAD), f32),
            ),
        ) * kv_heads
    else:
        (top_ref, total_ref, acc_ref), refs = refs[:3], refs[3:]
        state = tuple(
            (top_ref[g][:, :1], total_ref[g][:, :1], acc_ref[g]) for g in range(kv_heads)
        )
    if all(count == 1 for count, _ in sources):
        for i in range(0, len(sources), 2):
            span = range(i, min(i + 2, len(sources)))
            state = absorb(
                state, [pieces[k][...] for k in span], [sources[k][1](shard, 0) for k in span]
            )
    else:
        for ref, (count, source_of) in zip(pieces, sources):

            def step(i, carried):
                at = pl.multiple_of(i * rows, rows)
                return absorb(carried, [ref[pl.ds(at, rows), :]], [source_of(shard, i)])

            state = lax.fori_loop(0, count, step, state)

    if not last:
        top_ref, total_ref, acc_ref = refs
        for g in range(kv_heads):
            top, total, acc = state[g]
            top_ref[g] = jnp.broadcast_to(top, acc.shape)
            total_ref[g] = jnp.broadcast_to(total, acc.shape)
            acc_ref[g] = acc
        return
    mine_ref, stat_ref, packed_ref = refs
    heads = q_width // HEAD
    lane = lax.broadcasted_iota(jnp.int32, (rows, HEAD), 1)
    mine = jnp.zeros((rows, HEAD), f32)
    theirs = jnp.zeros((rows, HEAD), f32)
    for g in range(kv_heads):
        top, total, acc = state[g]
        for j in range(group):
            h = g * group + j
            cols = slice(h * HEAD, (h + 1) * HEAD)
            near = slice(j * both, j * both + rows)
            far = slice(j * both + rows, (j + 1) * both)
            mine_ref[:, cols] = acc[near]
            packed_ref[:, cols] = acc[far].astype(bf16)
            for value, at in ((top, h), (total, heads + h)):
                mine = jnp.where(lane == at, value[near], mine)
                theirs = jnp.where(lane % (2 * heads) == at, value[far], theirs)
    stat_ref[...] = mine
    high = theirs.astype(bf16).astype(f32)
    middle = (theirs - high).astype(bf16).astype(f32)
    low = theirs - high - middle
    third = lane // (2 * heads)
    parts = jnp.where(third == 0, high, jnp.where(third == 1, middle, low))
    packed_ref[:, q_width:] = parts.astype(bf16)


def merge_kernel(mine_ref, stat_ref, packed_ref, wo_ref, sent_ref, kept_ref):
    rows, q_width = mine_ref.shape
    heads = q_width // HEAD
    half = rows // 2
    near = stat_ref[...]
    parts = packed_ref[:, q_width:].astype(f32)
    far = parts
    for t in (1, 2):
        far = far + pltpu.roll(parts, HEAD - 2 * heads * t, 1)
    top = jnp.maximum(near, far)
    near_part, far_part = jnp.exp2(near - top), jnp.exp2(far - top)
    near_total, far_total = pltpu.roll(near, HEAD - heads, 1), pltpu.roll(far, HEAD - heads, 1)
    total = near_total * near_part + far_total * far_part
    near_part, far_part = near_part / total, far_part / total
    joined = []
    for h in range(heads):
        cols = slice(h * HEAD, (h + 1) * HEAD)
        ours = mine_ref[:, cols] * near_part[:, h : h + 1]
        theirs = packed_ref[:, cols].astype(f32) * far_part[:, h : h + 1]
        joined.append((ours + theirs).astype(bf16))
    context = jnp.concatenate(joined, 1)
    upper = lax.axis_index("req") == 0
    kept_ref[...] = jnp.where(upper, context[:half], context[half:])
    leaving = jnp.where(upper, context[half:], context[:half])
    sent_ref[...] = jnp.dot(leaving, wo_ref[...], preferred_element_type=f32).astype(bf16)


def keep_kernel(context_ref, wo_ref, tok_ref, out_ref):
    half = context_ref.shape[0]
    first = pl.multiple_of(lax.axis_index("req") * half, half)
    residual = tok_ref[pl.ds(first, half), :].astype(f32)
    out_ref[...] = jnp.dot(context_ref[...], wo_ref[...], preferred_element_type=f32) + residual


def cache_kernel(sources, block_ref, slot_ref, *refs):
    pieces, (mine_ref, other_ref) = refs[: len(sources)], refs[len(sources) :]
    shard = lax.axis_index("seq")
    slots = mine_ref.shape[0]
    key_width = mine_ref.shape[3]
    rows = slots * PAGE // 2
    pages = rows // 2 // PAGE
    mine_ref[...] = jnp.zeros_like(mine_ref)
    other_ref[...] = jnp.zeros_like(other_ref)

    def place(ref, at, source):
        for k, block in enumerate(blocks_of(block_ref, source)):
            for j in range(pages):
                slot = slot_ref[block * pages + j]
                holder = slot // slots
                local = slot - holder * slots
                offset = at + (k * pages + j) * PAGE
                if not isinstance(offset, int):
                    offset = pl.multiple_of(offset, PAGE)
                for target, owner in ((mine_ref, shard), (other_ref, shard ^ 1)):

                    @pl.when(holder == owner)
                    def _():
                        target[local, 0] = ref[pl.ds(offset, PAGE), :key_width]
                        target[local, 1] = ref[pl.ds(offset, PAGE), key_width:]

    for ref, (count, source_of) in zip(pieces, sources):
        if count == 1:
            place(ref, 0, source_of(shard, 0))
        else:

            def step(i, carry):
                place(ref, i * rows, source_of(shard, i))
                return carry

            lax.fori_loop(0, count, step, 0)


def swap(x, n, bit):
    return lax.ppermute(x, "seq", [(i, i ^ bit) for i in range(n)])


def gather_shards(kv, n):
    if n % 4 or n > 16:
        same = [list(range(c, n, 2)) for c in range(2)]
        everyone = lax.all_gather(kv, "seq", axis=0, tiled=True, axis_index_groups=same)
        return [([everyone], [(n // 2, lambda shard, i: 2 * i + shard % 2)])]
    outer = n // 4

    def moved(shift, flip):
        def source_of(shard, i):
            plane = lax.rem(shard // 4 + outer - shift, outer)
            return plane * 4 + ((shard % 4) ^ flip)

        return 1, source_of

    own, beside = (kv, moved(0, 0)), (swap(kv, n, 2), moved(0, 2))
    shifts = sorted(range(1, outer), key=lambda s: (min(s, outer - s), -s))
    along, across = [], []
    for shift in shifts:
        turned = lax.ppermute(kv, "seq", [(i, (i + 4 * shift) % n) for i in range(n)])
        along.append((turned, moved(shift, 0)))
        across.append((swap(turned, n, 2), moved(shift, 2)))
    groups = [[own, beside] + along[:2], along[2:] + across[:-2], across[-2:]]
    return [tuple(zip(*group)) for group in groups if group]


def on_device(
    n, parts, tokens, norm_gain, w_query, key_projection, value_projection, w_out, lengths, block_split, page_slot,
):
    rows, width = tokens.shape
    half = rows // 2
    q_width = w_query.shape[1]
    kv_width = key_projection.shape[1] + value_projection.shape[1]
    kv_heads = key_projection.shape[1] // HEAD
    stacked = 2 * rows * q_width // (kv_heads * HEAD)
    normed, kv, cosine, sine = pl.pallas_call(
        key_value_kernel,
        out_shape=(
            struct((rows, width), bf16),
            struct((rows, kv_width), bf16),
            struct((rows, HEAD), f32),
            struct((rows, HEAD), f32),
        ),
        in_specs=in_hbm(7),
        out_specs=tuple(in_vmem(4)),
        scratch_shapes=[
            pltpu.SMEM(block_split.shape, jnp.int32),
            pltpu.SMEM(lengths.shape, jnp.int32),
            pltpu.VMEM((1, HEAD), f32),
            pltpu.VMEM((rows, width), bf16),
            pltpu.VMEM((1, width), f32),
            pltpu.VMEM((width, kv_width), bf16),
            pltpu.SemaphoreType.DMA((5,)),
            pltpu.SemaphoreType.DMA((WEIGHT_STEPS, 2)),
        ],
        compiler_params=kernel_params(62),
        cost_estimate=cost(2 * rows * width * kv_width, 2 * width * kv_width),
        name="key_value",
    )(
        block_split, lengths, inverse_frequencies(), tokens, norm_gain.reshape(1, width),
        key_projection, value_projection,
    )
    groups = gather_shards(kv, n)
    if len(groups[0][0]) > 1:
        (own, beside, *others), sources = groups[0]
        normed, beside = lax.optimization_barrier((normed, beside))
        groups[0] = ((own, beside, *others), sources)
    queries = pl.pallas_call(
        query_kernel,
        out_shape=struct((rows, q_width), bf16),
        in_specs=in_hbm(4),
        out_specs=in_vmem(1)[0],
        scratch_shapes=[
            pltpu.VMEM((rows, width), bf16),
            pltpu.VMEM((rows, HEAD), f32),
            pltpu.VMEM((rows, HEAD), f32),
            pltpu.VMEM((width, q_width), bf16),
            pltpu.SemaphoreType.DMA((3,)),
            pltpu.SemaphoreType.DMA((WEIGHT_STEPS, 1)),
        ],
        compiler_params=kernel_params(62),
        cost_estimate=cost(2 * rows * width * q_width, 2 * width * q_width),
        name="query",
    )(normed, cosine, sine, w_query)
    far_queries = swap(queries, n, 1)

    state = ()
    for i, (arrays, sources) in enumerate(groups):
        first, last = i == 0, i == len(groups) - 1
        if last:
            shapes = (
                struct((rows, q_width), f32),
                struct((rows, HEAD), f32),
                struct((rows, q_width + HEAD), bf16),
            )
        else:
            shapes = (struct((kv_heads, stacked, HEAD), f32),) * 3
        keys = sum(count for count, _ in sources) * rows
        state = pl.pallas_call(
            functools.partial(attend_kernel, sources, first, last),
            out_shape=shapes,
            in_specs=in_smem(2) + in_vmem(2 + len(arrays) + len(state)),
            out_specs=tuple(in_vmem(len(shapes))),
            compiler_params=kernel_params(32),
            cost_estimate=cost(8 * rows * keys * q_width, 2 * keys * kv_width),
            name="attend",
        )(block_split, lengths, queries, far_queries, *arrays, *state)
    mine, stats, packed = state
    packed = swap(packed, n, 1)
    arrays = [x for held, _ in groups for x in held]
    sources = [s for _, where in groups for s in where]
    arrays, mine = lax.optimization_barrier((arrays, mine))
    shape = (2 * rows // PAGE, 2, PAGE, kv_width // 2)
    cache, other = pl.pallas_call(
        functools.partial(cache_kernel, sources),
        out_shape=(struct(shape, bf16),) * 2,
        in_specs=in_smem(2) + in_vmem(len(arrays)),
        out_specs=tuple(in_vmem(2)),
        compiler_params=kernel_params(32),
        cost_estimate=cost(0, 4 * rows * kv_width),
        name="cache",
    )(block_split, page_slot, *arrays)
    mine, cache, other = lax.optimization_barrier((mine, cache, other))
    sent, kept = pl.pallas_call(
        merge_kernel,
        out_shape=(struct((half, width), bf16), struct((half, q_width), bf16)),
        in_specs=in_vmem(4),
        out_specs=tuple(in_vmem(2)),
        compiler_params=kernel_params(24),
        cost_estimate=cost(rows * width * q_width, 2 * width * q_width),
        name="merge",
    )(mine, stats, packed, w_out)
    received = lax.ppermute(sent, "req", [(i, (i + 1) % parts) for i in range(parts)])
    kept = pl.pallas_call(
        keep_kernel,
        out_shape=struct((half, width), f32),
        in_specs=in_vmem(3),
        out_specs=in_vmem(1)[0],
        compiler_params=kernel_params(24),
        cost_estimate=cost(rows * width * q_width, 2 * width * q_width),
        name="keep",
    )(kept, w_out, tokens)

    cache = cache + swap(other, n, 1)
    hidden = (kept + received.astype(f32)).astype(bf16)
    return hidden, cache


def solution(mesh):
    in_specs = (
        P("seq", None),
        P(),
        P(None, "req"),
        P(None, "req"),
        P(None, "req"),
        P("req", None),
        P(),
        P(),
        P(),
    )
    out_specs = (P(("seq", "req"), None), P("seq", None, None, "req"))
    body = functools.partial(on_device, mesh.shape["seq"], mesh.shape["req"])
    return jax.shard_map(body, mesh=mesh, in_specs=in_specs, out_specs=out_specs, check_vma=False)
```

```python
import functools
import math

import jax
import jax.numpy as jnp
import numpy as np
from jax import lax
from jax.experimental import pallas as pl
from jax.experimental.pallas import tpu as pltpu
from jax.sharding import PartitionSpec as P

HEAD = 128
PAGE = 32
THETA = 1000000.0
EPS = 1e-05
MASKED = -1e30
FLOOR = -1e29
WEIGHT_STEPS = 4
MIB = 1024 * 1024
SCALE = math.log2(math.e) / math.sqrt(HEAD)

f32 = jnp.float32
bf16 = jnp.bfloat16
struct = jax.ShapeDtypeStruct


def in_vmem(count):
    return [pl.BlockSpec(memory_space=pltpu.VMEM)] * count


def in_smem(count):
    return [pl.BlockSpec(memory_space=pltpu.SMEM)] * count


def in_hbm(count):
    return [pl.BlockSpec(memory_space=pltpu.HBM)] * count


def kernel_params(mib):
    return pltpu.CompilerParams(vmem_limit_bytes=mib * MIB)


def cost(flops, moved):
    return pl.CostEstimate(flops=flops, bytes_accessed=moved, transcendentals=0)


def inverse_frequencies():
    exponent = np.arange(HEAD // 2, dtype=np.float64) * (2.0 / HEAD)
    freq = (THETA**-exponent).astype(np.float32)
    return jnp.asarray(np.concatenate([freq, freq])[None, :])


def blocks_of(block_ref, shard):
    first = block_ref[shard]
    return first, 2 * block_ref.shape[0] - 1 - first


def prompt_begin(position, len_ref):
    begin = jnp.zeros_like(position)
    start = jnp.int32(0)
    for r in range(len_ref.shape[0] - 1):
        start = start + len_ref[r]
        begin = jnp.where(position >= start, start, begin)
    return begin


def positions(block_ref, shards, rows, dim, shape):
    half = rows // 2
    index = lax.broadcasted_iota(jnp.int32, shape, dim)
    blocks = [block for shard in shards for block in blocks_of(block_ref, shard)]
    offset = blocks[0] * half
    for i, block in enumerate(blocks[1:], 1):
        offset = jnp.where(index >= i * half, (block - i) * half, offset)
    return index + offset


def rotate(u, cosine, signed_sine):
    return u * cosine + pltpu.roll(u, HEAD // 2, 1) * signed_sine


def weight_copies(refs, scratch, sems):
    copies = []
    depth = scratch.shape[0] // WEIGHT_STEPS
    for step in range(WEIGHT_STEPS):
        group, column = [], 0
        for i, ref in enumerate(refs):
            rows, cols = pl.ds(step * depth, depth), pl.ds(column, ref.shape[1])
            group.append(
                pltpu.make_async_copy(ref.at[rows, :], scratch.at[rows, cols], sems.at[step, i])
            )
            column += ref.shape[1]
        copies.append(group)
    return copies


def start_all(copies):
    for group in copies:
        for copy in group:
            copy.start()


def stepped_dot(left, copies, scratch):
    depth = scratch.shape[0] // WEIGHT_STEPS
    total = None
    for step in range(WEIGHT_STEPS):
        for copy in copies[step]:
            copy.wait()
        rows = slice(step * depth, (step + 1) * depth)
        part = jnp.dot(left[:, rows], scratch[rows, :], preferred_element_type=f32)
        total = part if total is None else total + part
    return total


def project_kernel(
    block_hbm, len_hbm, freq_hbm, tok_hbm, gain_hbm, wk_hbm, wv_hbm, wq_hbm,
    kv_ref, q_ref,
    block_ref, len_ref, freq_ref, tok_ref, gain_ref, kv_weights, q_weights, small_sems, kv_sems, q_sems,
):
    small = [
        pltpu.make_async_copy(source, target, small_sems.at[i])
        for i, (source, target) in enumerate(
            (
                (block_hbm, block_ref),
                (len_hbm, len_ref),
                (freq_hbm, freq_ref),
                (tok_hbm, tok_ref),
                (gain_hbm, gain_ref),
            )
        )
    ]
    kv_copies = weight_copies((wk_hbm, wv_hbm), kv_weights, kv_sems)
    q_copies = weight_copies((wq_hbm,), q_weights, q_sems)
    for copy in small:
        copy.start()
    start_all(kv_copies)
    start_all(q_copies)
    rows = tok_ref.shape[0]
    for copy in small[:3]:
        copy.wait()
    position = positions(block_ref, [lax.axis_index("seq")], rows, 0, (rows, HEAD))
    angle = (position - prompt_begin(position, len_ref)).astype(f32) * freq_ref[...]
    cosine, sine = jnp.cos(angle), jnp.sin(angle)
    lane = lax.broadcasted_iota(jnp.int32, (rows, HEAD), 1)
    sine = jnp.where(lane < HEAD // 2, -sine, sine)
    for copy in small[3:]:
        copy.wait()
    wide = tok_ref[...].astype(f32)
    scale = lax.rsqrt(jnp.mean(wide * wide, -1, keepdims=True) + EPS)
    normed = (wide * scale * gain_ref[...]).astype(bf16)
    product = stepped_dot(normed, kv_copies, kv_weights)
    key_width = wk_hbm.shape[1]
    for h in range(key_width // HEAD):
        cols = slice(h * HEAD, (h + 1) * HEAD)
        kv_ref[:, cols] = rotate(product[:, cols], cosine, sine).astype(bf16)
    kv_ref[:, key_width:] = product[:, key_width:].astype(bf16)
    product = stepped_dot(normed, q_copies, q_weights)
    for h in range(wq_hbm.shape[1] // HEAD):
        cols = slice(h * HEAD, (h + 1) * HEAD)
        q_ref[:, cols] = rotate(product[:, cols], cosine, sine).astype(bf16)


def attend_kernel(sources, block_ref, len_ref, q_ref, far_ref, *refs):
    pieces, refs = refs[: len(sources)], refs[len(sources) :]
    shard = lax.axis_index("seq")
    rows, q_width = q_ref.shape
    key_width = pieces[0].shape[1] // 2
    kv_heads = key_width // HEAD
    group = q_width // key_width
    both = 2 * rows
    q_pos = positions(block_ref, [shard, shard ^ 1], rows, 0, (both, 1))
    q_begin = prompt_begin(q_pos, len_ref)
    queries = [
        jnp.concatenate(
            [
                ref[:, h * HEAD : (h + 1) * HEAD]
                for h in range(g * group, (g + 1) * group)
                for ref in (q_ref, far_ref)
            ],
            0,
        )
        for g in range(kv_heads)
    ]

    def absorb(state, blocks, shards):
        width = rows * len(blocks)
        key_pos = positions(block_ref, shards, rows, 1, (1, width))
        bias = jnp.where((key_pos >= q_begin) & (key_pos <= q_pos), 0.0, MASKED)
        bias = jnp.concatenate([bias] * group, 0)
        out = []
        for g in range(kv_heads):
            top, total, acc = state[g]
            keys = jnp.concatenate([b[:, g * HEAD : (g + 1) * HEAD] for b in blocks], 0)
            values = jnp.concatenate(
                [b[:, key_width + g * HEAD : key_width + (g + 1) * HEAD] for b in blocks], 0
            )
            scores = lax.dot_general(
                queries[g], keys, (((1,), (1,)), ((), ())), preferred_element_type=f32
            )
            scores = scores * SCALE + bias
            new_top = jnp.maximum(top, jnp.max(scores, -1, keepdims=True))
            weights = jnp.exp2(scores - new_top)
            factor = jnp.exp2(top - new_top)
            total = total * factor + jnp.sum(weights, -1, keepdims=True)
            acc = acc * factor + jnp.dot(weights.astype(bf16), values, preferred_element_type=f32)
            out.append((new_top, total, acc))
        return tuple(out)

    state = (
        (
            jnp.full((group * both, 1), FLOOR, f32),
            jnp.zeros((group * both, 1), f32),
            jnp.zeros((group * both, HEAD), f32),
        ),
    ) * kv_heads
    if all(count == 1 for count, _ in sources):
        for i in range(0, len(sources), 2):
            span = range(i, min(i + 2, len(sources)))
            state = absorb(
                state, [pieces[k][...] for k in span], [sources[k][1](shard, 0) for k in span]
            )
    else:
        for ref, (count, source_of) in zip(pieces, sources):

            def step(i, carried):
                at = pl.multiple_of(i * rows, rows)
                return absorb(carried, [ref[pl.ds(at, rows), :]], [source_of(shard, i)])

            state = lax.fori_loop(0, count, step, state)

    mine_ref, stat_ref, packed_ref = refs
    heads = q_width // HEAD
    lane = lax.broadcasted_iota(jnp.int32, (rows, HEAD), 1)
    mine = jnp.zeros((rows, HEAD), f32)
    theirs = jnp.zeros((rows, HEAD), f32)
    for g in range(kv_heads):
        top, total, acc = state[g]
        for j in range(group):
            h = g * group + j
            cols = slice(h * HEAD, (h + 1) * HEAD)
            near = slice(j * both, j * both + rows)
            far = slice(j * both + rows, (j + 1) * both)
            mine_ref[:, cols] = acc[near]
            packed_ref[:, cols] = acc[far].astype(bf16)
            for value, at in ((top, h), (total, heads + h)):
                mine = jnp.where(lane == at, value[near], mine)
                theirs = jnp.where(lane % (2 * heads) == at, value[far], theirs)
    stat_ref[...] = mine
    high = theirs.astype(bf16).astype(f32)
    middle = (theirs - high).astype(bf16).astype(f32)
    low = theirs - high - middle
    third = lane // (2 * heads)
    parts = jnp.where(third == 0, high, jnp.where(third == 1, middle, low))
    packed_ref[:, q_width:] = parts.astype(bf16)


def merge_kernel(wo_ref, *refs):
    partials, (sent_ref, kept_ref) = refs[:-2], refs[-2:]
    rows, q_width = partials[0].shape
    heads = q_width // HEAD
    half = rows // 2
    held = []
    for mine_ref, stat_ref, packed_ref in zip(partials[::3], partials[1::3], partials[2::3]):
        parts = packed_ref[:, q_width:].astype(f32)
        stats = parts
        for t in (1, 2):
            stats = stats + pltpu.roll(parts, HEAD - 2 * heads * t, 1)
        held += [(mine_ref, stat_ref[...]), (packed_ref, stats)]
    top = functools.reduce(jnp.maximum, [stats for _, stats in held])
    shares = [jnp.exp2(stats - top) for _, stats in held]
    total = sum(
        share * pltpu.roll(stats, HEAD - heads, 1) for share, (_, stats) in zip(shares, held)
    )
    shares = [share / total for share in shares]
    joined = []
    for h in range(heads):
        cols = slice(h * HEAD, (h + 1) * HEAD)
        joined.append(
            sum(
                ref[:, cols].astype(f32) * share[:, h : h + 1]
                for (ref, _), share in zip(held, shares)
            ).astype(bf16)
        )
    context = jnp.concatenate(joined, 1)
    upper = lax.axis_index("req") == 0
    kept_ref[...] = jnp.where(upper, context[:half], context[half:])
    leaving = jnp.where(upper, context[half:], context[:half])
    sent_ref[...] = jnp.dot(leaving, wo_ref[...], preferred_element_type=f32).astype(bf16)


def keep_kernel(context_ref, wo_ref, tok_ref, out_ref):
    half = context_ref.shape[0]
    first = pl.multiple_of(lax.axis_index("req") * half, half)
    residual = tok_ref[pl.ds(first, half), :].astype(f32)
    out_ref[...] = jnp.dot(context_ref[...], wo_ref[...], preferred_element_type=f32) + residual


def cache_kernel(sources, block_ref, slot_ref, *refs):
    pieces, (mine_ref, other_ref) = refs[: len(sources)], refs[len(sources) :]
    shard = lax.axis_index("seq")
    slots = mine_ref.shape[0]
    key_width = mine_ref.shape[3]
    rows = slots * PAGE // 2
    pages = rows // 2 // PAGE
    mine_ref[...] = jnp.zeros_like(mine_ref)
    other_ref[...] = jnp.zeros_like(other_ref)

    def place(ref, at, source):
        for k, block in enumerate(blocks_of(block_ref, source)):
            for j in range(pages):
                slot = slot_ref[block * pages + j]
                holder = slot // slots
                local = slot - holder * slots
                offset = at + (k * pages + j) * PAGE
                if not isinstance(offset, int):
                    offset = pl.multiple_of(offset, PAGE)
                for target, owner in ((mine_ref, shard), (other_ref, shard ^ 1)):

                    @pl.when(holder == owner)
                    def _():
                        target[local, 0] = ref[pl.ds(offset, PAGE), :key_width]
                        target[local, 1] = ref[pl.ds(offset, PAGE), key_width:]

    for ref, (count, source_of) in zip(pieces, sources):
        if count == 1:
            place(ref, 0, source_of(shard, 0))
        else:

            def step(i, carry):
                place(ref, i * rows, source_of(shard, i))
                return carry

            lax.fori_loop(0, count, step, 0)


def swap(x, n, bit):
    return lax.ppermute(x, "seq", [(i, i ^ bit) for i in range(n)])


def gather_shards(kv, n):
    if n % 4 or n > 16:
        same = [list(range(c, n, 2)) for c in range(2)]
        everyone = lax.all_gather(kv, "seq", axis=0, tiled=True, axis_index_groups=same)
        return [([everyone], [(n // 2, lambda shard, i: 2 * i + shard % 2)])]
    outer = n // 4

    def moved(shift, flip):
        def source_of(shard, i):
            plane = lax.rem(shard // 4 + outer - shift, outer)
            return plane * 4 + ((shard % 4) ^ flip)

        return 1, source_of

    own, beside = (kv, moved(0, 0)), (swap(kv, n, 2), moved(0, 2))
    shifts = sorted(range(1, outer), key=lambda s: (min(s, outer - s), -s))
    along, across = [], []
    for shift in shifts:
        turned = lax.ppermute(kv, "seq", [(i, (i + 4 * shift) % n) for i in range(n)])
        along.append((turned, moved(shift, 0)))
        across.append((swap(turned, n, 2), moved(shift, 2)))
    groups = [[own, beside] + along[::2], along[1::2] + across[:1], across[1:]]
    return [tuple(zip(*group)) for group in groups if group]


def on_device(
    n, parts, tokens, norm_gain, w_query, key_projection, value_projection, w_out, lengths, block_split, page_slot,
):
    rows, width = tokens.shape
    half = rows // 2
    q_width = w_query.shape[1]
    kv_width = key_projection.shape[1] + value_projection.shape[1]
    kv, queries = pl.pallas_call(
        project_kernel,
        out_shape=(struct((rows, kv_width), bf16), struct((rows, q_width), bf16)),
        in_specs=in_hbm(8),
        out_specs=tuple(in_vmem(2)),
        scratch_shapes=[
            pltpu.SMEM(block_split.shape, jnp.int32),
            pltpu.SMEM(lengths.shape, jnp.int32),
            pltpu.VMEM((1, HEAD), f32),
            pltpu.VMEM((rows, width), bf16),
            pltpu.VMEM((1, width), f32),
            pltpu.VMEM((width, kv_width), bf16),
            pltpu.VMEM((width, q_width), bf16),
            pltpu.SemaphoreType.DMA((5,)),
            pltpu.SemaphoreType.DMA((WEIGHT_STEPS, 2)),
            pltpu.SemaphoreType.DMA((WEIGHT_STEPS, 1)),
        ],
        compiler_params=kernel_params(62),
        cost_estimate=cost(2 * rows * width * (kv_width + q_width), 2 * width * (kv_width + q_width)),
        name="project",
    )(
        block_split, lengths, inverse_frequencies(), tokens, norm_gain.reshape(1, width),
        key_projection, value_projection, w_query,
    )
    groups = gather_shards(kv, n)
    far_queries = swap(queries, n, 1)

    partials = []
    for arrays, sources in groups:
        keys = sum(count for count, _ in sources) * rows
        mine, stats, packed = pl.pallas_call(
            functools.partial(attend_kernel, sources),
            out_shape=(
                struct((rows, q_width), f32),
                struct((rows, HEAD), f32),
                struct((rows, q_width + HEAD), bf16),
            ),
            in_specs=in_smem(2) + in_vmem(2 + len(arrays)),
            out_specs=tuple(in_vmem(3)),
            compiler_params=kernel_params(32),
            cost_estimate=cost(8 * rows * keys * q_width, 2 * keys * kv_width),
            name="attend",
        )(block_split, lengths, queries, far_queries, *arrays)
        partials += [mine, stats, swap(packed, n, 1)]
        queries, partials[-2] = lax.optimization_barrier((queries, stats))
    arrays = [x for held, _ in groups for x in held]
    sources = [s for _, where in groups for s in where]
    arrays, mine = lax.optimization_barrier((arrays, mine))
    shape = (2 * rows // PAGE, 2, PAGE, kv_width // 2)
    cache, other = pl.pallas_call(
        functools.partial(cache_kernel, sources),
        out_shape=(struct(shape, bf16),) * 2,
        in_specs=in_smem(2) + in_vmem(len(arrays)),
        out_specs=tuple(in_vmem(2)),
        compiler_params=kernel_params(32),
        cost_estimate=cost(0, 4 * rows * kv_width),
        name="cache",
    )(block_split, page_slot, *arrays)
    partials[-3], cache, other = lax.optimization_barrier((mine, cache, other))
    sent, kept = pl.pallas_call(
        merge_kernel,
        out_shape=(struct((half, width), bf16), struct((half, q_width), bf16)),
        in_specs=in_vmem(1 + len(partials)),
        out_specs=tuple(in_vmem(2)),
        compiler_params=kernel_params(24),
        cost_estimate=cost(rows * width * q_width, 2 * width * q_width),
        name="merge",
    )(w_out, *partials)
    received = lax.ppermute(sent, "req", [(i, (i + 1) % parts) for i in range(parts)])
    kept = pl.pallas_call(
        keep_kernel,
        out_shape=struct((half, width), f32),
        in_specs=in_vmem(3),
        out_specs=in_vmem(1)[0],
        compiler_params=kernel_params(24),
        cost_estimate=cost(rows * width * q_width, 2 * width * q_width),
        name="keep",
    )(kept, w_out, tokens)

    cache = cache + swap(other, n, 1)
    hidden = (kept + received.astype(f32)).astype(bf16)
    return hidden, cache


def solution(mesh):
    in_specs = (
        P("seq", None),
        P(),
        P(None, "req"),
        P(None, "req"),
        P(None, "req"),
        P("req", None),
        P(),
        P(),
        P(),
    )
    out_specs = (P(("seq", "req"), None), P("seq", None, None, "req"))
    body = functools.partial(on_device, mesh.shape["seq"], mesh.shape["req"])
    return jax.shard_map(body, mesh=mesh, in_specs=in_specs, out_specs=out_specs, check_vma=False)
```

```python
import functools
import math

import jax
import jax.numpy as jnp
import numpy as np
from jax import lax
from jax.experimental import pallas as pl
from jax.experimental.pallas import tpu as pltpu
from jax.sharding import PartitionSpec as P

HEAD = 128
PAGE = 32
THETA = 1000000.0
EPS = 1e-05
MASKED = -1e30
FLOOR = -1e29
WEIGHT_STEPS = 4
MIB = 1024 * 1024
SCALE = math.log2(math.e) / math.sqrt(HEAD)

f32 = jnp.float32
bf16 = jnp.bfloat16
struct = jax.ShapeDtypeStruct


def in_vmem(count):
    return [pl.BlockSpec(memory_space=pltpu.VMEM)] * count


def in_smem(count):
    return [pl.BlockSpec(memory_space=pltpu.SMEM)] * count


def in_hbm(count):
    return [pl.BlockSpec(memory_space=pltpu.HBM)] * count


def kernel_params(mib):
    return pltpu.CompilerParams(vmem_limit_bytes=mib * MIB)


def cost(flops, moved):
    return pl.CostEstimate(flops=flops, bytes_accessed=moved, transcendentals=0)


def inverse_frequencies():
    exponent = np.arange(HEAD // 2, dtype=np.float64) * (2.0 / HEAD)
    freq = (THETA**-exponent).astype(np.float32)
    return jnp.asarray(np.concatenate([freq, freq])[None, :])


def blocks_of(block_ref, shard):
    first = block_ref[shard]
    return first, 2 * block_ref.shape[0] - 1 - first


def prompt_begin(position, len_ref):
    begin = jnp.zeros_like(position)
    start = jnp.int32(0)
    for r in range(len_ref.shape[0] - 1):
        start = start + len_ref[r]
        begin = jnp.where(position >= start, start, begin)
    return begin


def positions(block_ref, shards, rows, dim, shape):
    half = rows // 2
    index = lax.broadcasted_iota(jnp.int32, shape, dim)
    blocks = [block for shard in shards for block in blocks_of(block_ref, shard)]
    offset = blocks[0] * half
    for i, block in enumerate(blocks[1:], 1):
        offset = jnp.where(index >= i * half, (block - i) * half, offset)
    return index + offset


def rotate(u, cosine, signed_sine):
    return u * cosine + pltpu.roll(u, HEAD // 2, 1) * signed_sine


def weight_copies(refs, scratch, sems):
    copies = []
    depth = scratch.shape[0] // WEIGHT_STEPS
    for step in range(WEIGHT_STEPS):
        group, column = [], 0
        for i, ref in enumerate(refs):
            rows, cols = pl.ds(step * depth, depth), pl.ds(column, ref.shape[1])
            group.append(
                pltpu.make_async_copy(ref.at[rows, :], scratch.at[rows, cols], sems.at[step, i])
            )
            column += ref.shape[1]
        copies.append(group)
    return copies


def start_all(copies):
    for group in copies:
        for copy in group:
            copy.start()


def stepped_dot(left, copies, scratch):
    depth = scratch.shape[0] // WEIGHT_STEPS
    total = None
    for step in range(WEIGHT_STEPS):
        for copy in copies[step]:
            copy.wait()
        rows = slice(step * depth, (step + 1) * depth)
        part = jnp.dot(left[:, rows], scratch[rows, :], preferred_element_type=f32)
        total = part if total is None else total + part
    return total


def project_kernel(
    block_hbm, len_hbm, freq_hbm, tok_hbm, gain_hbm, wk_hbm, wv_hbm, wq_hbm,
    kv_ref, q_ref,
    block_ref, len_ref, freq_ref, tok_ref, gain_ref, kv_weights, q_weights, small_sems, kv_sems, q_sems,
):
    small = [
        pltpu.make_async_copy(source, target, small_sems.at[i])
        for i, (source, target) in enumerate(
            (
                (block_hbm, block_ref),
                (len_hbm, len_ref),
                (freq_hbm, freq_ref),
                (tok_hbm, tok_ref),
                (gain_hbm, gain_ref),
            )
        )
    ]
    kv_copies = weight_copies((wk_hbm, wv_hbm), kv_weights, kv_sems)
    q_copies = weight_copies((wq_hbm,), q_weights, q_sems)
    for copy in small:
        copy.start()
    start_all(kv_copies)
    start_all(q_copies)
    rows = tok_ref.shape[0]
    for copy in small[:3]:
        copy.wait()
    position = positions(block_ref, [lax.axis_index("seq")], rows, 0, (rows, HEAD))
    angle = (position - prompt_begin(position, len_ref)).astype(f32) * freq_ref[...]
    cosine, sine = jnp.cos(angle), jnp.sin(angle)
    lane = lax.broadcasted_iota(jnp.int32, (rows, HEAD), 1)
    sine = jnp.where(lane < HEAD // 2, -sine, sine)
    for copy in small[3:]:
        copy.wait()
    wide = tok_ref[...].astype(f32)
    scale = lax.rsqrt(jnp.mean(wide * wide, -1, keepdims=True) + EPS)
    normed = (wide * scale * gain_ref[...]).astype(bf16)
    product = stepped_dot(normed, kv_copies, kv_weights)
    key_width = wk_hbm.shape[1]
    for h in range(key_width // HEAD):
        cols = slice(h * HEAD, (h + 1) * HEAD)
        kv_ref[:, cols] = rotate(product[:, cols], cosine, sine).astype(bf16)
    kv_ref[:, key_width:] = product[:, key_width:].astype(bf16)
    product = stepped_dot(normed, q_copies, q_weights)
    for h in range(wq_hbm.shape[1] // HEAD):
        cols = slice(h * HEAD, (h + 1) * HEAD)
        q_ref[:, cols] = rotate(product[:, cols], cosine, sine).astype(bf16)


def attend_kernel(pieces, block_ref, len_ref, q_ref, far_ref, *refs):
    pieces, refs = with_refs(pieces, refs)
    shard = lax.axis_index("seq")
    rows, q_width = q_ref.shape
    key_width = pieces[0].arrays[0].shape[1] // 2
    kv_heads = key_width // HEAD
    group = q_width // key_width
    both = 2 * rows
    q_pos = positions(block_ref, [shard, shard ^ 1], rows, 0, (both, 1))
    q_begin = prompt_begin(q_pos, len_ref)
    queries = [
        jnp.concatenate(
            [
                ref[:, h * HEAD : (h + 1) * HEAD]
                for h in range(g * group, (g + 1) * group)
                for ref in (q_ref, far_ref)
            ],
            0,
        )
        for g in range(kv_heads)
    ]

    def absorb(state, blocks, shards):
        width = rows * len(blocks)
        key_pos = positions(block_ref, shards, rows, 1, (1, width))
        bias = jnp.where((key_pos >= q_begin) & (key_pos <= q_pos), 0.0, MASKED)
        bias = jnp.concatenate([bias] * group, 0)
        out = []
        for g in range(kv_heads):
            top, total, acc = state[g]
            keys = jnp.concatenate([b[:, g * HEAD : (g + 1) * HEAD] for b in blocks], 0)
            values = jnp.concatenate(
                [b[:, key_width + g * HEAD : key_width + (g + 1) * HEAD] for b in blocks], 0
            )
            scores = lax.dot_general(
                queries[g], keys, (((1,), (1,)), ((), ())), preferred_element_type=f32
            )
            scores = scores * SCALE + bias
            new_top = jnp.maximum(top, jnp.max(scores, -1, keepdims=True))
            weights = jnp.exp2(scores - new_top)
            factor = jnp.exp2(top - new_top)
            total = total * factor + jnp.sum(weights, -1, keepdims=True)
            acc = acc * factor + jnp.dot(weights.astype(bf16), values, preferred_element_type=f32)
            out.append((new_top, total, acc))
        return tuple(out)

    state = (
        (
            jnp.full((group * both, 1), FLOOR, f32),
            jnp.zeros((group * both, 1), f32),
            jnp.zeros((group * both, HEAD), f32),
        ),
    ) * kv_heads
    if all(piece.count == 1 for piece in pieces):
        for i in range(0, len(pieces), 2):
            pair = pieces[i : i + 2]
            state = absorb(
                state, [loaded(p, shard) for p in pair], [p.source_of(shard, 0) for p in pair]
            )
    else:
        for piece in pieces:

            def step(i, carried):
                at = pl.multiple_of(i * rows, rows)
                block = piece.arrays[0][pl.ds(at, rows), :]
                return absorb(carried, [block], [piece.source_of(shard, i)])

            state = lax.fori_loop(0, piece.count, step, state)

    mine_ref, stat_ref, packed_ref = refs
    heads = q_width // HEAD
    lane = lax.broadcasted_iota(jnp.int32, (rows, HEAD), 1)
    mine = jnp.zeros((rows, HEAD), f32)
    theirs = jnp.zeros((rows, HEAD), f32)
    for g in range(kv_heads):
        top, total, acc = state[g]
        for j in range(group):
            h = g * group + j
            cols = slice(h * HEAD, (h + 1) * HEAD)
            near = slice(j * both, j * both + rows)
            far = slice(j * both + rows, (j + 1) * both)
            mine_ref[:, cols] = acc[near]
            packed_ref[:, cols] = acc[far].astype(bf16)
            for value, at in ((top, h), (total, heads + h)):
                mine = jnp.where(lane == at, value[near], mine)
                theirs = jnp.where(lane % (2 * heads) == at, value[far], theirs)
    stat_ref[...] = mine
    high = theirs.astype(bf16).astype(f32)
    middle = (theirs - high).astype(bf16).astype(f32)
    low = theirs - high - middle
    third = lane // (2 * heads)
    parts = jnp.where(third == 0, high, jnp.where(third == 1, middle, low))
    packed_ref[:, q_width:] = parts.astype(bf16)


def merge_kernel(wo_ref, *refs):
    partials, (sent_ref, kept_ref) = refs[:-2], refs[-2:]
    rows, q_width = partials[0].shape
    heads = q_width // HEAD
    half = rows // 2
    held = []
    for mine_ref, stat_ref, packed_ref in zip(partials[::3], partials[1::3], partials[2::3]):
        parts = packed_ref[:, q_width:].astype(f32)
        stats = parts
        for t in (1, 2):
            stats = stats + pltpu.roll(parts, HEAD - 2 * heads * t, 1)
        held += [(mine_ref, stat_ref[...]), (packed_ref, stats)]
    top = functools.reduce(jnp.maximum, [stats for _, stats in held])
    shares = [jnp.exp2(stats - top) for _, stats in held]
    total = sum(
        share * pltpu.roll(stats, HEAD - heads, 1) for share, (_, stats) in zip(shares, held)
    )
    shares = [share / total for share in shares]
    joined = []
    for h in range(heads):
        cols = slice(h * HEAD, (h + 1) * HEAD)
        joined.append(
            sum(
                ref[:, cols].astype(f32) * share[:, h : h + 1]
                for (ref, _), share in zip(held, shares)
            ).astype(bf16)
        )
    context = jnp.concatenate(joined, 1)
    upper = lax.axis_index("req") == 0
    kept_ref[...] = jnp.where(upper, context[:half], context[half:])
    leaving = jnp.where(upper, context[half:], context[:half])
    sent_ref[...] = jnp.dot(leaving, wo_ref[...], preferred_element_type=f32).astype(bf16)


def keep_kernel(context_ref, wo_ref, tok_ref, out_ref):
    half = context_ref.shape[0]
    first = pl.multiple_of(lax.axis_index("req") * half, half)
    residual = tok_ref[pl.ds(first, half), :].astype(f32)
    out_ref[...] = jnp.dot(context_ref[...], wo_ref[...], preferred_element_type=f32) + residual


def cache_kernel(pieces, held, block_ref, slot_ref, *refs):
    pieces, refs = with_refs(pieces, refs)
    mine_ref, other_ref = refs[-2:]
    shard = lax.axis_index("seq")
    slots = mine_ref.shape[0]
    key_width = mine_ref.shape[3]
    rows = slots * PAGE // 2
    pages = rows // 2 // PAGE
    for i, target in enumerate((mine_ref, other_ref)):
        target[...] = refs[i][...] if held else jnp.zeros_like(target)

    def place(ref, at, source, wanted):
        for k, block in enumerate(blocks_of(block_ref, source)):
            for j in range(pages):
                slot = slot_ref[block * pages + j]
                holder = slot // slots
                local = slot - holder * slots
                offset = at + (k * pages + j) * PAGE
                if not isinstance(offset, int):
                    offset = pl.multiple_of(offset, PAGE)
                for target, owner in ((mine_ref, shard), (other_ref, shard ^ 1)):

                    @pl.when((holder == owner) & wanted)
                    def _():
                        target[local, 0] = ref[pl.ds(offset, PAGE), :key_width]
                        target[local, 1] = ref[pl.ds(offset, PAGE), key_width:]

    for piece in pieces:
        if piece.count == 1:
            source = piece.source_of(shard, 0)
            for i, ref in enumerate(piece.arrays):
                place(ref, 0, source, True if piece.pick is None else piece.pick(shard) == bool(i))
        else:

            def step(i, carry):
                place(piece.arrays[0], i * rows, piece.source_of(shard, i), True)
                return carry

            lax.fori_loop(0, piece.count, step, 0)


def swap(x, n, bit):
    return lax.ppermute(x, "seq", [(i, i ^ bit) for i in range(n)])


class Piece:
    def __init__(self, arrays, source_of, count=1, pick=None):
        self.arrays, self.source_of, self.count, self.pick = arrays, source_of, count, pick

    def moved(self, arrays):
        return Piece(arrays, self.source_of, self.count, self.pick)


def operands(pieces):
    return [x for piece in pieces for x in piece.arrays]


def with_refs(pieces, refs):
    out = []
    for piece in pieces:
        taken, refs = refs[: len(piece.arrays)], refs[len(piece.arrays) :]
        out.append(piece.moved(taken))
    return out, refs


def loaded(piece, shard):
    values = [ref[...] for ref in piece.arrays]
    return values[0] if piece.pick is None else jnp.where(piece.pick(shard), values[1], values[0])


def at_distance(bits):
    return lambda shard, i: shard ^ bits


def move(x, pairs):
    return lax.ppermute(x, "seq", pairs)


def outer_plane(i):
    return (i // 4 == 0) | (i // 4 == 3)


def on_device(
    n, parts, tokens, norm_gain, w_query, key_projection, value_projection, w_out, lengths, block_split, page_slot,
):
    rows, width = tokens.shape
    half = rows // 2
    q_width = w_query.shape[1]
    kv_width = key_projection.shape[1] + value_projection.shape[1]
    kv, queries = pl.pallas_call(
        project_kernel,
        out_shape=(struct((rows, kv_width), bf16), struct((rows, q_width), bf16)),
        in_specs=in_hbm(8),
        out_specs=tuple(in_vmem(2)),
        scratch_shapes=[
            pltpu.SMEM(block_split.shape, jnp.int32),
            pltpu.SMEM(lengths.shape, jnp.int32),
            pltpu.VMEM((1, HEAD), f32),
            pltpu.VMEM((rows, width), bf16),
            pltpu.VMEM((1, width), f32),
            pltpu.VMEM((width, kv_width), bf16),
            pltpu.VMEM((width, q_width), bf16),
            pltpu.SemaphoreType.DMA((5,)),
            pltpu.SemaphoreType.DMA((WEIGHT_STEPS, 2)),
            pltpu.SemaphoreType.DMA((WEIGHT_STEPS, 1)),
        ],
        compiler_params=kernel_params(62),
        cost_estimate=cost(2 * rows * width * (kv_width + q_width), 2 * width * (kv_width + q_width)),
        name="project",
    )(
        block_split, lengths, inverse_frequencies(), tokens, norm_gain.reshape(1, width),
        key_projection, value_projection, w_query,
    )
    far_queries = swap(queries, n, 1)

    def attend(pieces):
        keys = sum(piece.count for piece in pieces) * rows
        arrays = operands(pieces)
        mine, stats, packed = pl.pallas_call(
            functools.partial(attend_kernel, pieces),
            out_shape=(
                struct((rows, q_width), f32),
                struct((rows, HEAD), f32),
                struct((rows, q_width + HEAD), bf16),
            ),
            in_specs=in_smem(2) + in_vmem(2 + len(arrays)),
            out_specs=tuple(in_vmem(3)),
            compiler_params=kernel_params(32),
            cost_estimate=cost(8 * rows * keys * q_width, 2 * keys * kv_width),
            name="attend",
        )(block_split, lengths, queries, far_queries, *arrays)
        return [mine, stats, swap(packed, n, 1)]

    def place_pages(pieces, held=()):
        arrays = operands(pieces)
        shape = (2 * rows // PAGE, 2, PAGE, kv_width // 2)
        return pl.pallas_call(
            functools.partial(cache_kernel, pieces, bool(held)),
            out_shape=(struct(shape, bf16),) * 2,
            in_specs=in_smem(2) + in_vmem(len(arrays) + len(held)),
            out_specs=tuple(in_vmem(2)),
            input_output_aliases={2 + len(arrays) + i: i for i in range(len(held))},
            compiler_params=kernel_params(32),
            cost_estimate=cost(0, 4 * rows * kv_width),
            name="cache",
        )(block_split, page_slot, *arrays, *held)

    if n == 16:
        everyone = range(n)
        inner = [i for i in everyone if not outer_plane(i)]
        ends = [i for i in everyone if outer_plane(i)]
        second = move(kv, [(i, i ^ 8) for i in everyone])
        first = move(kv, [(i, i ^ 4) for i in everyone])
        beside = move(kv, [(i, i ^ 2) for i in everyone])
        middle = move(kv, [(i, i ^ 12) for i in inner])
        onward = move(second, [(i, i ^ 4) for i in inner])
        early = [
            Piece([kv], at_distance(0)),
            Piece([beside], at_distance(2)),
            Piece([first], at_distance(4)),
            Piece([second], at_distance(8)),
        ]
        partials = attend(early)
        held = place_pages(early)
        (middle, onward, *held), partials[1] = lax.optimization_barrier(
            ((middle, onward, *held), partials[1])
        )
        third = Piece([middle, onward], at_distance(12), pick=outer_plane)
        later = [
            Piece([move(first, [(i, i ^ 2) for i in everyone])], at_distance(6)),
            third,
            Piece([move(second, [(i, i ^ 2) for i in everyone])], at_distance(10)),
        ]
        last = third.moved(
            [move(middle, [(i, i ^ 2) for i in inner]), move(onward, [(i, i ^ 2) for i in ends])]
        )
        last.source_of = at_distance(14)
        queries, partials[1] = lax.optimization_barrier((queries, partials[1]))
        partials += attend(later)
        queries, partials[4] = lax.optimization_barrier((queries, partials[4]))
        partials += attend([last])
        remaining = later + [last]
    else:
        same = [list(range(c, n, 2)) for c in range(2)]
        gathered = lax.all_gather(kv, "seq", axis=0, tiled=True, axis_index_groups=same)
        remaining = [Piece([gathered], lambda shard, i: 2 * i + shard % 2, n // 2)]
        partials, held = attend(remaining), ()
    arrays, partials[-3] = lax.optimization_barrier((operands(remaining), partials[-3]))
    remaining, _ = with_refs(remaining, arrays)
    cache, other = place_pages(remaining, held)
    partials[-3], cache, other = lax.optimization_barrier((partials[-3], cache, other))
    sent, kept = pl.pallas_call(
        merge_kernel,
        out_shape=(struct((half, width), bf16), struct((half, q_width), bf16)),
        in_specs=in_vmem(1 + len(partials)),
        out_specs=tuple(in_vmem(2)),
        compiler_params=kernel_params(24),
        cost_estimate=cost(rows * width * q_width, 2 * width * q_width),
        name="merge",
    )(w_out, *partials)
    received = lax.ppermute(sent, "req", [(i, (i + 1) % parts) for i in range(parts)])
    kept = pl.pallas_call(
        keep_kernel,
        out_shape=struct((half, width), f32),
        in_specs=in_vmem(3),
        out_specs=in_vmem(1)[0],
        compiler_params=kernel_params(24),
        cost_estimate=cost(rows * width * q_width, 2 * width * q_width),
        name="keep",
    )(kept, w_out, tokens)

    cache = cache + swap(other, n, 1)
    hidden = (kept + received.astype(f32)).astype(bf16)
    return hidden, cache


def solution(mesh):
    in_specs = (
        P("seq", None),
        P(),
        P(None, "req"),
        P(None, "req"),
        P(None, "req"),
        P("req", None),
        P(),
        P(),
        P(),
    )
    out_specs = (P(("seq", "req"), None), P("seq", None, None, "req"))
    body = functools.partial(on_device, mesh.shape["seq"], mesh.shape["req"])
    return jax.shard_map(body, mesh=mesh, in_specs=in_specs, out_specs=out_specs, check_vma=False)
```

```python
import functools
import math

import jax
import jax.numpy as jnp
import numpy as np
from jax import lax
from jax.experimental import pallas as pl
from jax.experimental.pallas import tpu as pltpu
from jax.sharding import PartitionSpec as P

HEAD = 128
PAGE = 32
THETA = 1000000.0
EPS = 1e-05
MASKED = -1e30
FLOOR = -1e29
WEIGHT_STEPS = 4
MIB = 1024 * 1024
SCALE = math.log2(math.e) / math.sqrt(HEAD)

f32 = jnp.float32
bf16 = jnp.bfloat16
struct = jax.ShapeDtypeStruct


def in_vmem(count):
    return [pl.BlockSpec(memory_space=pltpu.VMEM)] * count


def in_smem(count):
    return [pl.BlockSpec(memory_space=pltpu.SMEM)] * count


def in_hbm(count):
    return [pl.BlockSpec(memory_space=pltpu.HBM)] * count


def kernel_params(mib):
    return pltpu.CompilerParams(vmem_limit_bytes=mib * MIB)


def cost(flops, moved):
    return pl.CostEstimate(flops=flops, bytes_accessed=moved, transcendentals=0)


def inverse_frequencies():
    exponent = np.arange(HEAD // 2, dtype=np.float64) * (2.0 / HEAD)
    freq = (THETA**-exponent).astype(np.float32)
    return jnp.asarray(np.concatenate([freq, freq])[None, :])


def blocks_of(block_ref, shard):
    first = block_ref[shard]
    return first, 2 * block_ref.shape[0] - 1 - first


def prompt_begin(position, len_ref):
    begin = jnp.zeros_like(position)
    start = jnp.int32(0)
    for r in range(len_ref.shape[0] - 1):
        start = start + len_ref[r]
        begin = jnp.where(position >= start, start, begin)
    return begin


def positions(block_ref, shards, rows, dim, shape):
    half = rows // 2
    index = lax.broadcasted_iota(jnp.int32, shape, dim)
    blocks = [block for shard in shards for block in blocks_of(block_ref, shard)]
    offset = blocks[0] * half
    for i, block in enumerate(blocks[1:], 1):
        offset = jnp.where(index >= i * half, (block - i) * half, offset)
    return index + offset


def rotate(u, cosine, signed_sine):
    return u * cosine + pltpu.roll(u, HEAD // 2, 1) * signed_sine


def weight_copies(refs, scratch, sems):
    copies = []
    depth = scratch.shape[0] // WEIGHT_STEPS
    for step in range(WEIGHT_STEPS):
        group, column = [], 0
        for i, ref in enumerate(refs):
            rows, cols = pl.ds(step * depth, depth), pl.ds(column, ref.shape[1])
            group.append(
                pltpu.make_async_copy(ref.at[rows, :], scratch.at[rows, cols], sems.at[step, i])
            )
            column += ref.shape[1]
        copies.append(group)
    return copies


def start_all(copies):
    for group in copies:
        for copy in group:
            copy.start()


def stepped_dot(left, copies, scratch):
    depth = scratch.shape[0] // WEIGHT_STEPS
    total = None
    for step in range(WEIGHT_STEPS):
        for copy in copies[step]:
            copy.wait()
        rows = slice(step * depth, (step + 1) * depth)
        part = jnp.dot(left[:, rows], scratch[rows, :], preferred_element_type=f32)
        total = part if total is None else total + part
    return total


def project_kernel(
    block_hbm, len_hbm, freq_hbm, tok_hbm, gain_hbm, wk_hbm, wv_hbm, wq_hbm,
    kv_ref, q_ref,
    block_ref, len_ref, freq_ref, tok_ref, gain_ref, kv_weights, q_weights, small_sems, kv_sems, q_sems,
):
    small = [
        pltpu.make_async_copy(source, target, small_sems.at[i])
        for i, (source, target) in enumerate(
            (
                (block_hbm, block_ref),
                (len_hbm, len_ref),
                (freq_hbm, freq_ref),
                (tok_hbm, tok_ref),
                (gain_hbm, gain_ref),
            )
        )
    ]
    kv_copies = weight_copies((wk_hbm, wv_hbm), kv_weights, kv_sems)
    q_copies = weight_copies((wq_hbm,), q_weights, q_sems)
    for copy in small:
        copy.start()
    start_all(kv_copies)
    start_all(q_copies)
    rows = tok_ref.shape[0]
    for copy in small[:3]:
        copy.wait()
    position = positions(block_ref, [lax.axis_index("seq")], rows, 0, (rows, HEAD))
    angle = (position - prompt_begin(position, len_ref)).astype(f32) * freq_ref[...]
    cosine, sine = jnp.cos(angle), jnp.sin(angle)
    lane = lax.broadcasted_iota(jnp.int32, (rows, HEAD), 1)
    sine = jnp.where(lane < HEAD // 2, -sine, sine)
    for copy in small[3:]:
        copy.wait()
    wide = tok_ref[...].astype(f32)
    scale = lax.rsqrt(jnp.mean(wide * wide, -1, keepdims=True) + EPS)
    normed = (wide * scale * gain_ref[...]).astype(bf16)
    product = stepped_dot(normed, kv_copies, kv_weights)
    key_width = wk_hbm.shape[1]
    for h in range(key_width // HEAD):
        cols = slice(h * HEAD, (h + 1) * HEAD)
        kv_ref[:, cols] = rotate(product[:, cols], cosine, sine).astype(bf16)
    kv_ref[:, key_width:] = product[:, key_width:].astype(bf16)
    product = stepped_dot(normed, q_copies, q_weights)
    for h in range(wq_hbm.shape[1] // HEAD):
        cols = slice(h * HEAD, (h + 1) * HEAD)
        q_ref[:, cols] = rotate(product[:, cols], cosine, sine).astype(bf16)


def attend_kernel(pieces, block_ref, len_ref, q_ref, far_ref, *refs):
    pieces, refs = with_refs(pieces, refs)
    shard = lax.axis_index("seq")
    rows, q_width = q_ref.shape
    key_width = pieces[0].arrays[0].shape[1] // 2
    kv_heads = key_width // HEAD
    group = q_width // key_width
    both = 2 * rows
    q_pos = positions(block_ref, [shard, shard ^ 1], rows, 0, (both, 1))
    q_begin = prompt_begin(q_pos, len_ref)
    queries = [
        jnp.concatenate(
            [
                ref[:, h * HEAD : (h + 1) * HEAD]
                for h in range(g * group, (g + 1) * group)
                for ref in (q_ref, far_ref)
            ],
            0,
        )
        for g in range(kv_heads)
    ]

    def absorb(state, blocks, shards):
        width = rows * len(blocks)
        key_pos = positions(block_ref, shards, rows, 1, (1, width))
        bias = jnp.where((key_pos >= q_begin) & (key_pos <= q_pos), 0.0, MASKED)
        bias = jnp.concatenate([bias] * group, 0)
        out = []
        for g in range(kv_heads):
            top, total, acc = state[g]
            keys = jnp.concatenate([b[:, g * HEAD : (g + 1) * HEAD] for b in blocks], 0)
            values = jnp.concatenate(
                [b[:, key_width + g * HEAD : key_width + (g + 1) * HEAD] for b in blocks], 0
            )
            scores = lax.dot_general(
                queries[g], keys, (((1,), (1,)), ((), ())), preferred_element_type=f32
            )
            scores = scores * SCALE + bias
            new_top = jnp.maximum(top, jnp.max(scores, -1, keepdims=True))
            weights = jnp.exp2(scores - new_top)
            factor = jnp.exp2(top - new_top)
            total = total * factor + jnp.sum(weights, -1, keepdims=True)
            acc = acc * factor + jnp.dot(weights.astype(bf16), values, preferred_element_type=f32)
            out.append((new_top, total, acc))
        return tuple(out)

    state = (
        (
            jnp.full((group * both, 1), FLOOR, f32),
            jnp.zeros((group * both, 1), f32),
            jnp.zeros((group * both, HEAD), f32),
        ),
    ) * kv_heads
    if all(piece.count == 1 for piece in pieces):
        for i in range(0, len(pieces), 2):
            pair = pieces[i : i + 2]
            state = absorb(
                state, [p.arrays[0][...] for p in pair], [p.source_of(shard, 0) for p in pair]
            )
    else:
        for piece in pieces:

            def step(i, carried):
                at = pl.multiple_of(i * rows, rows)
                block = piece.arrays[0][pl.ds(at, rows), :]
                return absorb(carried, [block], [piece.source_of(shard, i)])

            state = lax.fori_loop(0, piece.count, step, state)

    mine_ref, stat_ref, packed_ref = refs
    heads = q_width // HEAD
    lane = lax.broadcasted_iota(jnp.int32, (rows, HEAD), 1)
    mine = jnp.zeros((rows, HEAD), f32)
    theirs = jnp.zeros((rows, HEAD), f32)
    for g in range(kv_heads):
        top, total, acc = state[g]
        for j in range(group):
            h = g * group + j
            cols = slice(h * HEAD, (h + 1) * HEAD)
            near = slice(j * both, j * both + rows)
            far = slice(j * both + rows, (j + 1) * both)
            mine_ref[:, cols] = acc[near]
            packed_ref[:, cols] = acc[far].astype(bf16)
            for value, at in ((top, h), (total, heads + h)):
                mine = jnp.where(lane == at, value[near], mine)
                theirs = jnp.where(lane % (2 * heads) == at, value[far], theirs)
    stat_ref[...] = mine
    high = theirs.astype(bf16).astype(f32)
    middle = (theirs - high).astype(bf16).astype(f32)
    low = theirs - high - middle
    third = lane // (2 * heads)
    parts = jnp.where(third == 0, high, jnp.where(third == 1, middle, low))
    packed_ref[:, q_width:] = parts.astype(bf16)


def merge_kernel(wo_ref, *refs):
    partials, (sent_ref, kept_ref) = refs[:-2], refs[-2:]
    rows, q_width = partials[0].shape
    heads = q_width // HEAD
    half = rows // 2
    held = []
    for mine_ref, stat_ref, packed_ref in zip(partials[::3], partials[1::3], partials[2::3]):
        parts = packed_ref[:, q_width:].astype(f32)
        stats = parts
        for t in (1, 2):
            stats = stats + pltpu.roll(parts, HEAD - 2 * heads * t, 1)
        held += [(mine_ref, stat_ref[...]), (packed_ref, stats)]
    top = functools.reduce(jnp.maximum, [stats for _, stats in held])
    shares = [jnp.exp2(stats - top) for _, stats in held]
    total = sum(
        share * pltpu.roll(stats, HEAD - heads, 1) for share, (_, stats) in zip(shares, held)
    )
    shares = [share / total for share in shares]
    joined = []
    for h in range(heads):
        cols = slice(h * HEAD, (h + 1) * HEAD)
        joined.append(
            sum(
                ref[:, cols].astype(f32) * share[:, h : h + 1]
                for (ref, _), share in zip(held, shares)
            ).astype(bf16)
        )
    context = jnp.concatenate(joined, 1)
    upper = lax.axis_index("req") == 0
    kept_ref[...] = jnp.where(upper, context[:half], context[half:])
    leaving = jnp.where(upper, context[half:], context[:half])
    sent_ref[...] = jnp.dot(leaving, wo_ref[...], preferred_element_type=f32).astype(bf16)


def keep_kernel(context_ref, wo_ref, tok_ref, out_ref):
    half = context_ref.shape[0]
    first = pl.multiple_of(lax.axis_index("req") * half, half)
    residual = tok_ref[pl.ds(first, half), :].astype(f32)
    out_ref[...] = jnp.dot(context_ref[...], wo_ref[...], preferred_element_type=f32) + residual


def cache_kernel(pieces, held, block_ref, slot_ref, *refs):
    pieces, refs = with_refs(pieces, refs)
    mine_ref, other_ref = refs[-2:]
    shard = lax.axis_index("seq")
    slots = mine_ref.shape[0]
    key_width = mine_ref.shape[3]
    rows = slots * PAGE // 2
    pages = rows // 2 // PAGE
    for i, target in enumerate((mine_ref, other_ref)):
        target[...] = refs[i][...] if held else jnp.zeros_like(target)

    def place(ref, at, source):
        for k, block in enumerate(blocks_of(block_ref, source)):
            for j in range(pages):
                slot = slot_ref[block * pages + j]
                holder = slot // slots
                local = slot - holder * slots
                offset = at + (k * pages + j) * PAGE
                if not isinstance(offset, int):
                    offset = pl.multiple_of(offset, PAGE)
                for target, owner in ((mine_ref, shard), (other_ref, shard ^ 1)):

                    @pl.when(holder == owner)
                    def _():
                        target[local, 0] = ref[pl.ds(offset, PAGE), :key_width]
                        target[local, 1] = ref[pl.ds(offset, PAGE), key_width:]

    for piece in pieces:
        if piece.count == 1:
            place(piece.arrays[0], 0, piece.source_of(shard, 0))
        else:

            def step(i, carry):
                place(piece.arrays[0], i * rows, piece.source_of(shard, i))
                return carry

            lax.fori_loop(0, piece.count, step, 0)


def tied_all(pieces, other):
    arrays, other = lax.optimization_barrier((operands(pieces), other))
    return with_refs(pieces, arrays)[0], other


def tied(piece, other):
    (piece,), other = tied_all([piece], other)
    return piece, other


def swap(x, n, bit):
    return lax.ppermute(x, "seq", [(i, i ^ bit) for i in range(n)])


class Piece:
    def __init__(self, arrays, source_of, count=1):
        self.arrays, self.source_of, self.count = arrays, source_of, count

    def moved(self, arrays):
        return Piece(arrays, self.source_of, self.count)


def operands(pieces):
    return [x for piece in pieces for x in piece.arrays]


def with_refs(pieces, refs):
    out = []
    for piece in pieces:
        taken, refs = refs[: len(piece.arrays)], refs[len(piece.arrays) :]
        out.append(piece.moved(taken))
    return out, refs


def at_distance(bits):
    return lambda shard, i: shard ^ bits


def move(x, pairs):
    return lax.ppermute(x, "seq", pairs)


def on_device(
    n, parts, tokens, norm_gain, w_query, key_projection, value_projection, w_out, lengths, block_split, page_slot,
):
    rows, width = tokens.shape
    half = rows // 2
    q_width = w_query.shape[1]
    kv_width = key_projection.shape[1] + value_projection.shape[1]
    kv, queries = pl.pallas_call(
        project_kernel,
        out_shape=(struct((rows, kv_width), bf16), struct((rows, q_width), bf16)),
        in_specs=in_hbm(8),
        out_specs=tuple(in_vmem(2)),
        scratch_shapes=[
            pltpu.SMEM(block_split.shape, jnp.int32),
            pltpu.SMEM(lengths.shape, jnp.int32),
            pltpu.VMEM((1, HEAD), f32),
            pltpu.VMEM((rows, width), bf16),
            pltpu.VMEM((1, width), f32),
            pltpu.VMEM((width, kv_width), bf16),
            pltpu.VMEM((width, q_width), bf16),
            pltpu.SemaphoreType.DMA((5,)),
            pltpu.SemaphoreType.DMA((WEIGHT_STEPS, 2)),
            pltpu.SemaphoreType.DMA((WEIGHT_STEPS, 1)),
        ],
        compiler_params=kernel_params(62),
        cost_estimate=cost(2 * rows * width * (kv_width + q_width), 2 * width * (kv_width + q_width)),
        name="project",
    )(
        block_split, lengths, inverse_frequencies(), tokens, norm_gain.reshape(1, width),
        key_projection, value_projection, w_query,
    )
    far_queries = swap(queries, n, 1)

    def attend(pieces):
        keys = sum(piece.count for piece in pieces) * rows
        arrays = operands(pieces)
        mine, stats, packed = pl.pallas_call(
            functools.partial(attend_kernel, pieces),
            out_shape=(
                struct((rows, q_width), f32),
                struct((rows, HEAD), f32),
                struct((rows, q_width + HEAD), bf16),
            ),
            in_specs=in_smem(2) + in_vmem(2 + len(arrays)),
            out_specs=tuple(in_vmem(3)),
            compiler_params=kernel_params(32),
            cost_estimate=cost(8 * rows * keys * q_width, 2 * keys * kv_width),
            name="attend",
        )(block_split, lengths, queries, far_queries, *arrays)
        return [mine, stats, swap(packed, n, 1)]

    def place_pages(pieces, held=()):
        arrays = operands(pieces)
        shape = (2 * rows // PAGE, 2, PAGE, kv_width // 2)
        return pl.pallas_call(
            functools.partial(cache_kernel, pieces, bool(held)),
            out_shape=(struct(shape, bf16),) * 2,
            in_specs=in_smem(2) + in_vmem(len(arrays) + len(held)),
            out_specs=tuple(in_vmem(2)),
            input_output_aliases={2 + len(arrays) + i: i for i in range(len(held))},
            compiler_params=kernel_params(32),
            cost_estimate=cost(0, 4 * rows * kv_width),
            name="cache",
        )(block_split, page_slot, *arrays, *held)

    if n == 16:
        everyone = range(n)

        def along(shift, kv=kv):
            source = lambda shard, i: (shard + n - 4 * shift) % n
            return Piece([move(kv, [(i, (i + 4 * shift) % n) for i in everyone])], source)

        def across(piece):
            source = lambda shard, i: piece.source_of(shard ^ 2, i)
            return Piece([swap(piece.arrays[0], n, 2)], source)

        own = Piece([kv], at_distance(0))
        beside, first, second, third = across(own), along(3), along(1), along(2)
        first, later_kv = tied(first, kv)
        third = along(2, later_kv)
        early = [own, beside, first, second]
        first_across = across(first)
        partials = attend(early)
        third, partials[1] = tied(third, partials[1])
        later = [third, first_across]
        last = [across(second), across(third)]
        queries, partials[1] = lax.optimization_barrier((queries, partials[1]))
        partials += attend(later)
        placed, partials[4] = tied_all([own, beside, first, second], partials[4])
        held = place_pages(placed)
        queries, partials[4], held = lax.optimization_barrier((queries, partials[4], held))
        partials += attend(last)
        remaining = [third, first_across] + last
    else:
        same = [list(range(c, n, 2)) for c in range(2)]
        gathered = lax.all_gather(kv, "seq", axis=0, tiled=True, axis_index_groups=same)
        remaining = [Piece([gathered], lambda shard, i: 2 * i + shard % 2, n // 2)]
        partials, held = attend(remaining), ()
    arrays, partials[-3] = lax.optimization_barrier((operands(remaining), partials[-3]))
    remaining, _ = with_refs(remaining, arrays)
    cache, other = place_pages(remaining, held)
    partials[-3], cache, other = lax.optimization_barrier((partials[-3], cache, other))
    sent, kept = pl.pallas_call(
        merge_kernel,
        out_shape=(struct((half, width), bf16), struct((half, q_width), bf16)),
        in_specs=in_vmem(1 + len(partials)),
        out_specs=tuple(in_vmem(2)),
        compiler_params=kernel_params(24),
        cost_estimate=cost(rows * width * q_width, 2 * width * q_width),
        name="merge",
    )(w_out, *partials)
    received = lax.ppermute(sent, "req", [(i, (i + 1) % parts) for i in range(parts)])
    kept = pl.pallas_call(
        keep_kernel,
        out_shape=struct((half, width), f32),
        in_specs=in_vmem(3),
        out_specs=in_vmem(1)[0],
        compiler_params=kernel_params(24),
        cost_estimate=cost(rows * width * q_width, 2 * width * q_width),
        name="keep",
    )(kept, w_out, tokens)

    cache = cache + swap(other, n, 1)
    hidden = (kept + received.astype(f32)).astype(bf16)
    return hidden, cache


def solution(mesh):
    in_specs = (
        P("seq", None),
        P(),
        P(None, "req"),
        P(None, "req"),
        P(None, "req"),
        P("req", None),
        P(),
        P(),
        P(),
    )
    out_specs = (P(("seq", "req"), None), P("seq", None, None, "req"))
    body = functools.partial(on_device, mesh.shape["seq"], mesh.shape["req"])
    return jax.shard_map(body, mesh=mesh, in_specs=in_specs, out_specs=out_specs, check_vma=False)
```

```python
import functools
import math

import jax
import jax.numpy as jnp
import numpy as np
from jax import lax
from jax.experimental import pallas as pl
from jax.experimental.pallas import tpu as pltpu
from jax.sharding import PartitionSpec as P

HEAD = 128
PAGE = 32
THETA = 1000000.0
EPS = 1e-05
MASKED = -1e30
FLOOR = -1e29
WEIGHT_STEPS = 4
MIB = 1024 * 1024
SCALE = math.log2(math.e) / math.sqrt(HEAD)

f32 = jnp.float32
bf16 = jnp.bfloat16
struct = jax.ShapeDtypeStruct


def in_vmem(count):
    return [pl.BlockSpec(memory_space=pltpu.VMEM)] * count


def in_smem(count):
    return [pl.BlockSpec(memory_space=pltpu.SMEM)] * count


def in_hbm(count):
    return [pl.BlockSpec(memory_space=pltpu.HBM)] * count


def kernel_params(mib):
    return pltpu.CompilerParams(vmem_limit_bytes=mib * MIB)


def cost(flops, moved):
    return pl.CostEstimate(flops=flops, bytes_accessed=moved, transcendentals=0)


def inverse_frequencies():
    exponent = np.arange(HEAD // 2, dtype=np.float64) * (2.0 / HEAD)
    freq = (THETA**-exponent).astype(np.float32)
    return jnp.asarray(np.concatenate([freq, freq])[None, :])


def blocks_of(block_ref, shard):
    first = block_ref[shard]
    return first, 2 * block_ref.shape[0] - 1 - first


def prompt_begin(position, len_ref):
    begin = jnp.zeros_like(position)
    start = jnp.int32(0)
    for r in range(len_ref.shape[0] - 1):
        start = start + len_ref[r]
        begin = jnp.where(position >= start, start, begin)
    return begin


def positions(block_ref, shards, rows, dim, shape):
    half = rows // 2
    index = lax.broadcasted_iota(jnp.int32, shape, dim)
    blocks = [block for shard in shards for block in blocks_of(block_ref, shard)]
    offset = blocks[0] * half
    for i, block in enumerate(blocks[1:], 1):
        offset = jnp.where(index >= i * half, (block - i) * half, offset)
    return index + offset


def rotate(u, cosine, signed_sine):
    return u * cosine + pltpu.roll(u, HEAD // 2, 1) * signed_sine


def weight_copies(refs, scratch, sems):
    copies = []
    depth = scratch.shape[0] // WEIGHT_STEPS
    for step in range(WEIGHT_STEPS):
        group, column = [], 0
        for i, ref in enumerate(refs):
            rows, cols = pl.ds(step * depth, depth), pl.ds(column, ref.shape[1])
            group.append(
                pltpu.make_async_copy(ref.at[rows, :], scratch.at[rows, cols], sems.at[step, i])
            )
            column += ref.shape[1]
        copies.append(group)
    return copies


def start_all(copies):
    for group in copies:
        for copy in group:
            copy.start()


def stepped_dot(left, copies, scratch):
    depth = scratch.shape[0] // WEIGHT_STEPS
    total = None
    for step in range(WEIGHT_STEPS):
        for copy in copies[step]:
            copy.wait()
        rows = slice(step * depth, (step + 1) * depth)
        part = jnp.dot(left[:, rows], scratch[rows, :], preferred_element_type=f32)
        total = part if total is None else total + part
    return total


def project_kernel(
    block_hbm, len_hbm, freq_hbm, tok_hbm, gain_hbm, wk_hbm, wv_hbm, wq_hbm,
    kv_ref, q_ref,
    block_ref, len_ref, freq_ref, tok_ref, gain_ref, kv_weights, q_weights, small_sems, kv_sems, q_sems,
):
    small = [
        pltpu.make_async_copy(source, target, small_sems.at[i])
        for i, (source, target) in enumerate(
            (
                (block_hbm, block_ref),
                (len_hbm, len_ref),
                (freq_hbm, freq_ref),
                (tok_hbm, tok_ref),
                (gain_hbm, gain_ref),
            )
        )
    ]
    kv_copies = weight_copies((wk_hbm, wv_hbm), kv_weights, kv_sems)
    q_copies = weight_copies((wq_hbm,), q_weights, q_sems)
    for copy in small:
        copy.start()
    start_all(kv_copies)
    start_all(q_copies)
    rows = tok_ref.shape[0]
    for copy in small[:3]:
        copy.wait()
    position = positions(block_ref, [lax.axis_index("seq")], rows, 0, (rows, HEAD))
    angle = (position - prompt_begin(position, len_ref)).astype(f32) * freq_ref[...]
    cosine, sine = jnp.cos(angle), jnp.sin(angle)
    lane = lax.broadcasted_iota(jnp.int32, (rows, HEAD), 1)
    sine = jnp.where(lane < HEAD // 2, -sine, sine)
    for copy in small[3:]:
        copy.wait()
    wide = tok_ref[...].astype(f32)
    scale = lax.rsqrt(jnp.mean(wide * wide, -1, keepdims=True) + EPS)
    normed = (wide * scale * gain_ref[...]).astype(bf16)
    product = stepped_dot(normed, kv_copies, kv_weights)
    key_width = wk_hbm.shape[1]
    for h in range(key_width // HEAD):
        cols = slice(h * HEAD, (h + 1) * HEAD)
        kv_ref[:, cols] = rotate(product[:, cols], cosine, sine).astype(bf16)
    kv_ref[:, key_width:] = product[:, key_width:].astype(bf16)
    product = stepped_dot(normed, q_copies, q_weights)
    for h in range(wq_hbm.shape[1] // HEAD):
        cols = slice(h * HEAD, (h + 1) * HEAD)
        q_ref[:, cols] = rotate(product[:, cols], cosine, sine).astype(bf16)


def attend_kernel(pieces, block_ref, len_ref, q_ref, far_ref, *refs):
    pieces, refs = with_refs(pieces, refs)
    shard = lax.axis_index("seq")
    rows, q_width = q_ref.shape
    key_width = pieces[0].arrays[0].shape[1] // 2
    kv_heads = key_width // HEAD
    group = q_width // key_width
    both = 2 * rows
    q_pos = positions(block_ref, [shard, shard ^ 1], rows, 0, (both, 1))
    q_begin = prompt_begin(q_pos, len_ref)
    queries = [
        jnp.concatenate(
            [
                ref[:, h * HEAD : (h + 1) * HEAD]
                for h in range(g * group, (g + 1) * group)
                for ref in (q_ref, far_ref)
            ],
            0,
        )
        for g in range(kv_heads)
    ]

    def absorb(state, blocks, shards):
        width = rows * len(blocks)
        key_pos = positions(block_ref, shards, rows, 1, (1, width))
        bias = jnp.where((key_pos >= q_begin) & (key_pos <= q_pos), 0.0, MASKED)
        bias = jnp.concatenate([bias] * group, 0)
        out = []
        for g in range(kv_heads):
            top, total, acc = state[g]
            keys = jnp.concatenate([b[:, g * HEAD : (g + 1) * HEAD] for b in blocks], 0)
            values = jnp.concatenate(
                [b[:, key_width + g * HEAD : key_width + (g + 1) * HEAD] for b in blocks], 0
            )
            scores = lax.dot_general(
                queries[g], keys, (((1,), (1,)), ((), ())), preferred_element_type=f32
            )
            scores = scores * SCALE + bias
            new_top = jnp.maximum(top, jnp.max(scores, -1, keepdims=True))
            weights = jnp.exp2(scores - new_top)
            factor = jnp.exp2(top - new_top)
            total = total * factor + jnp.sum(weights, -1, keepdims=True)
            acc = acc * factor + jnp.dot(weights.astype(bf16), values, preferred_element_type=f32)
            out.append((new_top, total, acc))
        return tuple(out)

    state = (
        (
            jnp.full((group * both, 1), FLOOR, f32),
            jnp.zeros((group * both, 1), f32),
            jnp.zeros((group * both, HEAD), f32),
        ),
    ) * kv_heads
    if all(piece.count == 1 for piece in pieces):
        for i in range(0, len(pieces), 2):
            pair = pieces[i : i + 2]
            state = absorb(
                state, [p.arrays[0][...] for p in pair], [p.source_of(shard, 0) for p in pair]
            )
    else:
        for piece in pieces:

            def step(i, carried):
                at = pl.multiple_of(i * rows, rows)
                block = piece.arrays[0][pl.ds(at, rows), :]
                return absorb(carried, [block], [piece.source_of(shard, i)])

            state = lax.fori_loop(0, piece.count, step, state)

    mine_ref, stat_ref, packed_ref = refs
    heads = q_width // HEAD
    lane = lax.broadcasted_iota(jnp.int32, (rows, HEAD), 1)
    mine = jnp.zeros((rows, HEAD), f32)
    theirs = jnp.zeros((rows, HEAD), f32)
    for g in range(kv_heads):
        top, total, acc = state[g]
        for j in range(group):
            h = g * group + j
            cols = slice(h * HEAD, (h + 1) * HEAD)
            near = slice(j * both, j * both + rows)
            far = slice(j * both + rows, (j + 1) * both)
            mine_ref[:, cols] = acc[near]
            packed_ref[:, cols] = acc[far].astype(bf16)
            for value, at in ((top, h), (total, heads + h)):
                mine = jnp.where(lane == at, value[near], mine)
                theirs = jnp.where(lane % (2 * heads) == at, value[far], theirs)
    stat_ref[...] = mine
    high = theirs.astype(bf16).astype(f32)
    middle = (theirs - high).astype(bf16).astype(f32)
    low = theirs - high - middle
    third = lane // (2 * heads)
    parts = jnp.where(third == 0, high, jnp.where(third == 1, middle, low))
    packed_ref[:, q_width:] = parts.astype(bf16)


def stage_kernel(q_ref, kv_ref, q_out, kv_out):
    q_out[...] = q_ref[...]
    kv_out[...] = kv_ref[...]


def joined_rows(partials, first, half):
    q_width = partials[0].shape[1]
    heads = q_width // HEAD
    span = pl.ds(pl.multiple_of(first, half), half)
    held = []
    for mine_ref, stat_ref, packed_ref in zip(partials[::3], partials[1::3], partials[2::3]):
        parts = packed_ref[span, q_width:].astype(f32)
        stats = parts
        for t in (1, 2):
            stats = stats + pltpu.roll(parts, HEAD - 2 * heads * t, 1)
        held += [(mine_ref, stat_ref[span, :]), (packed_ref, stats)]
    top = functools.reduce(jnp.maximum, [stats for _, stats in held])
    shares = [jnp.exp2(stats - top) for _, stats in held]
    total = sum(
        share * pltpu.roll(stats, HEAD - heads, 1) for share, (_, stats) in zip(shares, held)
    )
    shares = [share / total for share in shares]
    context = []
    for h in range(heads):
        cols = slice(h * HEAD, (h + 1) * HEAD)
        context.append(
            sum(
                ref[span, cols].astype(f32) * share[:, h : h + 1]
                for (ref, _), share in zip(held, shares)
            ).astype(bf16)
        )
    return jnp.concatenate(context, 1)


def leave_kernel(wo_ref, *refs):
    partials, sent_ref = refs[:-1], refs[-1]
    half = sent_ref.shape[0]
    context = joined_rows(partials, (1 - lax.axis_index("req")) * half, half)
    sent_ref[...] = jnp.dot(context, wo_ref[...], preferred_element_type=f32).astype(bf16)


def keep_kernel(wo_ref, tok_ref, *refs):
    partials, out_ref = refs[:-1], refs[-1]
    half = out_ref.shape[0]
    first = lax.axis_index("req") * half
    context = joined_rows(partials, first, half)
    residual = tok_ref[pl.ds(pl.multiple_of(first, half), half), :].astype(f32)
    out_ref[...] = jnp.dot(context, wo_ref[...], preferred_element_type=f32) + residual


def cache_kernel(pieces, held, block_ref, slot_ref, *refs):
    pieces, refs = with_refs(pieces, refs)
    mine_ref, other_ref = refs[-2:]
    shard = lax.axis_index("seq")
    slots = mine_ref.shape[0]
    key_width = mine_ref.shape[3]
    rows = slots * PAGE // 2
    pages = rows // 2 // PAGE
    for i, target in enumerate((mine_ref, other_ref)):
        target[...] = refs[i][...] if held else jnp.zeros_like(target)

    def place(ref, at, source):
        for k, block in enumerate(blocks_of(block_ref, source)):
            for j in range(pages):
                slot = slot_ref[block * pages + j]
                holder = slot // slots
                local = slot - holder * slots
                offset = at + (k * pages + j) * PAGE
                if not isinstance(offset, int):
                    offset = pl.multiple_of(offset, PAGE)
                for target, owner in ((mine_ref, shard), (other_ref, shard ^ 1)):

                    @pl.when(holder == owner)
                    def _():
                        target[local, 0] = ref[pl.ds(offset, PAGE), :key_width]
                        target[local, 1] = ref[pl.ds(offset, PAGE), key_width:]

    for piece in pieces:
        if piece.count == 1:
            place(piece.arrays[0], 0, piece.source_of(shard, 0))
        else:

            def step(i, carry):
                place(piece.arrays[0], i * rows, piece.source_of(shard, i))
                return carry

            lax.fori_loop(0, piece.count, step, 0)


def tied_all(pieces, other):
    arrays, other = lax.optimization_barrier((operands(pieces), other))
    return with_refs(pieces, arrays)[0], other


def tied(piece, other):
    (piece,), other = tied_all([piece], other)
    return piece, other


def swap(x, n, bit):
    return lax.ppermute(x, "seq", [(i, i ^ bit) for i in range(n)])


class Piece:
    def __init__(self, arrays, source_of, count=1):
        self.arrays, self.source_of, self.count = arrays, source_of, count

    def moved(self, arrays):
        return Piece(arrays, self.source_of, self.count)


def operands(pieces):
    return [x for piece in pieces for x in piece.arrays]


def with_refs(pieces, refs):
    out = []
    for piece in pieces:
        taken, refs = refs[: len(piece.arrays)], refs[len(piece.arrays) :]
        out.append(piece.moved(taken))
    return out, refs


def at_distance(bits):
    return lambda shard, i: shard ^ bits


def move(x, pairs):
    return lax.ppermute(x, "seq", pairs)


def on_device(
    n, parts, tokens, norm_gain, w_query, key_projection, value_projection, w_out, lengths, block_split, page_slot,
):
    rows, width = tokens.shape
    half = rows // 2
    q_width = w_query.shape[1]
    kv_width = key_projection.shape[1] + value_projection.shape[1]
    kv, queries = pl.pallas_call(
        project_kernel,
        out_shape=(struct((rows, kv_width), bf16), struct((rows, q_width), bf16)),
        in_specs=in_hbm(8),
        out_specs=tuple(in_vmem(2)),
        scratch_shapes=[
            pltpu.SMEM(block_split.shape, jnp.int32),
            pltpu.SMEM(lengths.shape, jnp.int32),
            pltpu.VMEM((1, HEAD), f32),
            pltpu.VMEM((rows, width), bf16),
            pltpu.VMEM((1, width), f32),
            pltpu.VMEM((width, kv_width), bf16),
            pltpu.VMEM((width, q_width), bf16),
            pltpu.SemaphoreType.DMA((5,)),
            pltpu.SemaphoreType.DMA((WEIGHT_STEPS, 2)),
            pltpu.SemaphoreType.DMA((WEIGHT_STEPS, 1)),
        ],
        compiler_params=kernel_params(62),
        cost_estimate=cost(2 * rows * width * (kv_width + q_width), 2 * width * (kv_width + q_width)),
        name="project",
    )(
        block_split, lengths, inverse_frequencies(), tokens, norm_gain.reshape(1, width),
        key_projection, value_projection, w_query,
    )
    far_queries = swap(queries, n, 1)

    def attend(pieces):
        keys = sum(piece.count for piece in pieces) * rows
        arrays = operands(pieces)
        mine, stats, packed = pl.pallas_call(
            functools.partial(attend_kernel, pieces),
            out_shape=(
                struct((rows, q_width), f32),
                struct((rows, HEAD), f32),
                struct((rows, q_width + HEAD), bf16),
            ),
            in_specs=in_smem(2) + in_vmem(2 + len(arrays)),
            out_specs=tuple(in_vmem(3)),
            compiler_params=kernel_params(32),
            cost_estimate=cost(8 * rows * keys * q_width, 2 * keys * kv_width),
            name="attend",
        )(block_split, lengths, queries, far_queries, *arrays)
        return [mine, stats, swap(packed, n, 1)]

    def place_pages(pieces, held=()):
        arrays = operands(pieces)
        shape = (2 * rows // PAGE, 2, PAGE, kv_width // 2)
        return pl.pallas_call(
            functools.partial(cache_kernel, pieces, bool(held)),
            out_shape=(struct(shape, bf16),) * 2,
            in_specs=in_smem(2) + in_vmem(len(arrays) + len(held)),
            out_specs=tuple(in_vmem(2)),
            input_output_aliases={2 + len(arrays) + i: i for i in range(len(held))},
            compiler_params=kernel_params(32),
            cost_estimate=cost(0, 4 * rows * kv_width),
            name="cache",
        )(block_split, page_slot, *arrays, *held)

    if n == 16:

        def swapped(piece, bits):
            source = lambda shard, i: piece.source_of(shard ^ bits, i)
            return Piece([swap(piece.arrays[0], n, bits)], source)

        own = Piece([kv], at_distance(0))
        second, first, beside = swapped(own, 8), swapped(own, 4), swapped(own, 2)
        queries, kv = pl.pallas_call(
            stage_kernel,
            out_shape=(struct(queries.shape, bf16), struct(kv.shape, bf16)),
            in_specs=in_vmem(2),
            out_specs=tuple(in_vmem(2)),
            compiler_params=kernel_params(24),
            cost_estimate=cost(0, 8 * rows * kv_width),
            name="stage",
        )(queries, kv)
        (second, beside), kv = tied_all([second, beside], kv)
        own = own.moved([kv])
        third = swapped(second, 4)
        early = [own, beside, first, second, third]
        late = [swapped(second, 2), swapped(first, 2), swapped(third, 2)]
        partials = attend(early)
        placed, partials[1] = tied_all(early, partials[1])
        held = place_pages(placed)
        queries, partials[1], held = lax.optimization_barrier((queries, partials[1], held))
        partials += attend(late)
        remaining = late
    else:
        same = [list(range(c, n, 2)) for c in range(2)]
        gathered = lax.all_gather(kv, "seq", axis=0, tiled=True, axis_index_groups=same)
        remaining = [Piece([gathered], lambda shard, i: 2 * i + shard % 2, n // 2)]
        partials, held = attend(remaining), ()
    arrays, partials[-3] = lax.optimization_barrier((operands(remaining), partials[-3]))
    remaining, _ = with_refs(remaining, arrays)
    cache, other = place_pages(remaining, held)
    partials[-3], cache, other = lax.optimization_barrier((partials[-3], cache, other))
    sent = pl.pallas_call(
        leave_kernel,
        out_shape=struct((half, width), bf16),
        in_specs=in_vmem(1 + len(partials)),
        out_specs=in_vmem(1)[0],
        compiler_params=kernel_params(24),
        cost_estimate=cost(rows * width * q_width, 2 * width * q_width),
        name="leave",
    )(w_out, *partials)
    received = lax.ppermute(sent, "req", [(i, (i + 1) % parts) for i in range(parts)])
    kept = pl.pallas_call(
        keep_kernel,
        out_shape=struct((half, width), f32),
        in_specs=in_vmem(2 + len(partials)),
        out_specs=in_vmem(1)[0],
        compiler_params=kernel_params(24),
        cost_estimate=cost(rows * width * q_width, 2 * width * q_width),
        name="keep",
    )(w_out, tokens, *partials)
    cache = cache + swap(other, n, 1)
    hidden = (kept + received.astype(f32)).astype(bf16)
    return hidden, cache


def solution(mesh):
    in_specs = (
        P("seq", None),
        P(),
        P(None, "req"),
        P(None, "req"),
        P(None, "req"),
        P("req", None),
        P(),
        P(),
        P(),
    )
    out_specs = (P(("seq", "req"), None), P("seq", None, None, "req"))
    body = functools.partial(on_device, mesh.shape["seq"], mesh.shape["req"])
    return jax.shard_map(body, mesh=mesh, in_specs=in_specs, out_specs=out_specs, check_vma=False)
```

```python
import functools
import math

import jax
import jax.numpy as jnp
import numpy as np
from jax import lax
from jax.experimental import pallas as pl
from jax.experimental.pallas import tpu as pltpu
from jax.sharding import PartitionSpec as P

HEAD = 128
PAGE = 32
THETA = 1000000.0
EPS = 1e-05
MASKED = -1e30
FLOOR = -1e29
WEIGHT_STEPS = 4
MIB = 1024 * 1024
SCALE = math.log2(math.e) / math.sqrt(HEAD)

f32 = jnp.float32
bf16 = jnp.bfloat16
struct = jax.ShapeDtypeStruct


def in_vmem(count):
    return [pl.BlockSpec(memory_space=pltpu.VMEM)] * count


def in_smem(count):
    return [pl.BlockSpec(memory_space=pltpu.SMEM)] * count


def in_hbm(count):
    return [pl.BlockSpec(memory_space=pltpu.HBM)] * count


def kernel_params(mib):
    return pltpu.CompilerParams(vmem_limit_bytes=mib * MIB)


def cost(flops, moved):
    return pl.CostEstimate(flops=flops, bytes_accessed=moved, transcendentals=0)


def inverse_frequencies():
    exponent = np.arange(HEAD // 2, dtype=np.float64) * (2.0 / HEAD)
    freq = (THETA**-exponent).astype(np.float32)
    return jnp.asarray(np.concatenate([freq, freq])[None, :])


def blocks_of(block_ref, shard):
    first = block_ref[shard]
    return first, 2 * block_ref.shape[0] - 1 - first


def prompt_begin(position, len_ref):
    begin = jnp.zeros_like(position)
    start = jnp.int32(0)
    for r in range(len_ref.shape[0] - 1):
        start = start + len_ref[r]
        begin = jnp.where(position >= start, start, begin)
    return begin


def positions(block_ref, shards, rows, dim, shape):
    half = rows // 2
    index = lax.broadcasted_iota(jnp.int32, shape, dim)
    blocks = [block for shard in shards for block in blocks_of(block_ref, shard)]
    offset = blocks[0] * half
    for i, block in enumerate(blocks[1:], 1):
        offset = jnp.where(index >= i * half, (block - i) * half, offset)
    return index + offset


def rotate(u, cosine, signed_sine):
    return u * cosine + pltpu.roll(u, HEAD // 2, 1) * signed_sine


def weight_copies(refs, scratch, sems):
    copies = []
    depth = scratch.shape[0] // WEIGHT_STEPS
    for step in range(WEIGHT_STEPS):
        group, column = [], 0
        for i, ref in enumerate(refs):
            rows, cols = pl.ds(step * depth, depth), pl.ds(column, ref.shape[1])
            group.append(
                pltpu.make_async_copy(ref.at[rows, :], scratch.at[rows, cols], sems.at[step, i])
            )
            column += ref.shape[1]
        copies.append(group)
    return copies


def start_all(copies):
    for group in copies:
        for copy in group:
            copy.start()


def stepped_dot(left, copies, scratch):
    depth = scratch.shape[0] // WEIGHT_STEPS
    total = None
    for step in range(WEIGHT_STEPS):
        for copy in copies[step]:
            copy.wait()
        rows = slice(step * depth, (step + 1) * depth)
        part = jnp.dot(left[:, rows], scratch[rows, :], preferred_element_type=f32)
        total = part if total is None else total + part
    return total


def project_kernel(
    block_hbm, len_hbm, freq_hbm, tok_hbm, gain_hbm, wk_hbm, wv_hbm, wq_hbm,
    kv_ref, q_ref,
    block_ref, len_ref, freq_ref, tok_ref, gain_ref, kv_weights, q_weights, small_sems, kv_sems, q_sems,
):
    small = [
        pltpu.make_async_copy(source, target, small_sems.at[i])
        for i, (source, target) in enumerate(
            (
                (block_hbm, block_ref),
                (len_hbm, len_ref),
                (freq_hbm, freq_ref),
                (tok_hbm, tok_ref),
                (gain_hbm, gain_ref),
            )
        )
    ]
    kv_copies = weight_copies((wk_hbm, wv_hbm), kv_weights, kv_sems)
    q_copies = weight_copies((wq_hbm,), q_weights, q_sems)
    for copy in small:
        copy.start()
    start_all(kv_copies)
    start_all(q_copies)
    rows = tok_ref.shape[0]
    for copy in small[:3]:
        copy.wait()
    position = positions(block_ref, [lax.axis_index("seq")], rows, 0, (rows, HEAD))
    angle = (position - prompt_begin(position, len_ref)).astype(f32) * freq_ref[...]
    cosine, sine = jnp.cos(angle), jnp.sin(angle)
    lane = lax.broadcasted_iota(jnp.int32, (rows, HEAD), 1)
    sine = jnp.where(lane < HEAD // 2, -sine, sine)
    for copy in small[3:]:
        copy.wait()
    wide = tok_ref[...].astype(f32)
    scale = lax.rsqrt(jnp.mean(wide * wide, -1, keepdims=True) + EPS)
    normed = (wide * scale * gain_ref[...]).astype(bf16)
    product = stepped_dot(normed, kv_copies, kv_weights)
    key_width = wk_hbm.shape[1]
    for h in range(key_width // HEAD):
        cols = slice(h * HEAD, (h + 1) * HEAD)
        kv_ref[:, cols] = rotate(product[:, cols], cosine, sine).astype(bf16)
    kv_ref[:, key_width:] = product[:, key_width:].astype(bf16)
    product = stepped_dot(normed, q_copies, q_weights)
    for h in range(wq_hbm.shape[1] // HEAD):
        cols = slice(h * HEAD, (h + 1) * HEAD)
        q_ref[:, cols] = rotate(product[:, cols], cosine, sine).astype(bf16)


def attend_kernel(pieces, block_ref, len_ref, q_ref, far_ref, *refs):
    pieces, refs = with_refs(pieces, refs)
    shard = lax.axis_index("seq")
    rows, q_width = q_ref.shape
    key_width = pieces[0].arrays[0].shape[1] // 2
    kv_heads = key_width // HEAD
    group = q_width // key_width
    both = 2 * rows
    q_pos = positions(block_ref, [shard, shard ^ 1], rows, 0, (both, 1))
    q_begin = prompt_begin(q_pos, len_ref)
    queries = [
        jnp.concatenate(
            [
                ref[:, h * HEAD : (h + 1) * HEAD]
                for h in range(g * group, (g + 1) * group)
                for ref in (q_ref, far_ref)
            ],
            0,
        )
        for g in range(kv_heads)
    ]

    def absorb(state, blocks, shards):
        width = rows * len(blocks)
        key_pos = positions(block_ref, shards, rows, 1, (1, width))
        bias = jnp.where((key_pos >= q_begin) & (key_pos <= q_pos), 0.0, MASKED)
        bias = jnp.concatenate([bias] * group, 0)
        out = []
        for g in range(kv_heads):
            top, total, acc = state[g]
            keys = jnp.concatenate([b[:, g * HEAD : (g + 1) * HEAD] for b in blocks], 0)
            values = jnp.concatenate(
                [b[:, key_width + g * HEAD : key_width + (g + 1) * HEAD] for b in blocks], 0
            )
            scores = lax.dot_general(
                queries[g], keys, (((1,), (1,)), ((), ())), preferred_element_type=f32
            )
            scores = scores * SCALE + bias
            new_top = jnp.maximum(top, jnp.max(scores, -1, keepdims=True))
            weights = jnp.exp2(scores - new_top)
            factor = jnp.exp2(top - new_top)
            total = total * factor + jnp.sum(weights, -1, keepdims=True)
            acc = acc * factor + jnp.dot(weights.astype(bf16), values, preferred_element_type=f32)
            out.append((new_top, total, acc))
        return tuple(out)

    state = (
        (
            jnp.full((group * both, 1), FLOOR, f32),
            jnp.zeros((group * both, 1), f32),
            jnp.zeros((group * both, HEAD), f32),
        ),
    ) * kv_heads
    if all(piece.count == 1 for piece in pieces):
        for i in range(0, len(pieces), 2):
            pair = pieces[i : i + 2]
            state = absorb(
                state, [p.arrays[0][...] for p in pair], [p.source_of(shard, 0) for p in pair]
            )
    else:
        for piece in pieces:

            def step(i, carried):
                at = pl.multiple_of(i * rows, rows)
                block = piece.arrays[0][pl.ds(at, rows), :]
                return absorb(carried, [block], [piece.source_of(shard, i)])

            state = lax.fori_loop(0, piece.count, step, state)

    mine_ref, stat_ref, packed_ref = refs
    heads = q_width // HEAD
    lane = lax.broadcasted_iota(jnp.int32, (rows, HEAD), 1)
    mine = jnp.zeros((rows, HEAD), f32)
    theirs = jnp.zeros((rows, HEAD), f32)
    for g in range(kv_heads):
        top, total, acc = state[g]
        for j in range(group):
            h = g * group + j
            cols = slice(h * HEAD, (h + 1) * HEAD)
            near = slice(j * both, j * both + rows)
            far = slice(j * both + rows, (j + 1) * both)
            mine_ref[:, cols] = acc[near]
            packed_ref[:, cols] = acc[far].astype(bf16)
            for value, at in ((top, h), (total, heads + h)):
                mine = jnp.where(lane == at, value[near], mine)
                theirs = jnp.where(lane % (2 * heads) == at, value[far], theirs)
    stat_ref[...] = mine
    high = theirs.astype(bf16).astype(f32)
    middle = (theirs - high).astype(bf16).astype(f32)
    low = theirs - high - middle
    third = lane // (2 * heads)
    parts = jnp.where(third == 0, high, jnp.where(third == 1, middle, low))
    packed_ref[:, q_width:] = parts.astype(bf16)


def stage_kernel(q_ref, kv_ref, q_out, kv_out):
    q_out[...] = q_ref[...]
    kv_out[...] = kv_ref[...]


def joined_rows(partials, first, half):
    q_width = partials[0].shape[1]
    heads = q_width // HEAD
    span = pl.ds(pl.multiple_of(first, half), half)
    held = []
    for mine_ref, stat_ref, packed_ref in zip(partials[::3], partials[1::3], partials[2::3]):
        parts = packed_ref[span, q_width:].astype(f32)
        stats = parts
        for t in (1, 2):
            stats = stats + pltpu.roll(parts, HEAD - 2 * heads * t, 1)
        held += [(mine_ref, stat_ref[span, :]), (packed_ref, stats)]
    top = functools.reduce(jnp.maximum, [stats for _, stats in held])
    shares = [jnp.exp2(stats - top) for _, stats in held]
    total = sum(
        share * pltpu.roll(stats, HEAD - heads, 1) for share, (_, stats) in zip(shares, held)
    )
    shares = [share / total for share in shares]
    context = []
    for h in range(heads):
        cols = slice(h * HEAD, (h + 1) * HEAD)
        context.append(
            sum(
                ref[span, cols].astype(f32) * share[:, h : h + 1]
                for (ref, _), share in zip(held, shares)
            ).astype(bf16)
        )
    return jnp.concatenate(context, 1)


def leave_kernel(wo_ref, *refs):
    partials, sent_ref = refs[:-1], refs[-1]
    half = sent_ref.shape[0]
    context = joined_rows(partials, (1 - lax.axis_index("req")) * half, half)
    sent_ref[...] = jnp.dot(context, wo_ref[...], preferred_element_type=f32).astype(bf16)


def keep_kernel(wo_ref, tok_ref, *refs):
    partials, out_ref = refs[:-1], refs[-1]
    half = out_ref.shape[0]
    first = lax.axis_index("req") * half
    context = joined_rows(partials, first, half)
    residual = tok_ref[pl.ds(pl.multiple_of(first, half), half), :].astype(f32)
    out_ref[...] = jnp.dot(context, wo_ref[...], preferred_element_type=f32) + residual


def cache_kernel(pieces, held, block_ref, slot_ref, *refs):
    pieces, refs = with_refs(pieces, refs)
    mine_ref, other_ref = refs[-2:]
    shard = lax.axis_index("seq")
    slots = mine_ref.shape[0]
    key_width = mine_ref.shape[3]
    rows = slots * PAGE // 2
    pages = rows // 2 // PAGE
    for i, target in enumerate((mine_ref, other_ref)):
        target[...] = refs[i][...] if held else jnp.zeros_like(target)

    def place(ref, at, source):
        for k, block in enumerate(blocks_of(block_ref, source)):
            for j in range(pages):
                slot = slot_ref[block * pages + j]
                holder = slot // slots
                local = slot - holder * slots
                offset = at + (k * pages + j) * PAGE
                if not isinstance(offset, int):
                    offset = pl.multiple_of(offset, PAGE)
                for target, owner in ((mine_ref, shard), (other_ref, shard ^ 1)):

                    @pl.when(holder == owner)
                    def _():
                        target[local, 0] = ref[pl.ds(offset, PAGE), :key_width]
                        target[local, 1] = ref[pl.ds(offset, PAGE), key_width:]

    for piece in pieces:
        if piece.count == 1:
            place(piece.arrays[0], 0, piece.source_of(shard, 0))
        else:

            def step(i, carry):
                place(piece.arrays[0], i * rows, piece.source_of(shard, i))
                return carry

            lax.fori_loop(0, piece.count, step, 0)


def tied_all(pieces, other):
    arrays, other = lax.optimization_barrier((operands(pieces), other))
    return with_refs(pieces, arrays)[0], other


def tied(piece, other):
    (piece,), other = tied_all([piece], other)
    return piece, other


def swap(x, n, bit):
    return lax.ppermute(x, "seq", [(i, i ^ bit) for i in range(n)])


class Piece:
    def __init__(self, arrays, source_of, count=1):
        self.arrays, self.source_of, self.count = arrays, source_of, count

    def moved(self, arrays):
        return Piece(arrays, self.source_of, self.count)


def operands(pieces):
    return [x for piece in pieces for x in piece.arrays]


def with_refs(pieces, refs):
    out = []
    for piece in pieces:
        taken, refs = refs[: len(piece.arrays)], refs[len(piece.arrays) :]
        out.append(piece.moved(taken))
    return out, refs


def at_distance(bits):
    return lambda shard, i: shard ^ bits


def move(x, pairs):
    return lax.ppermute(x, "seq", pairs)


def on_device(
    n, parts, tokens, norm_gain, w_query, key_projection, value_projection, w_out, lengths, block_split, page_slot,
):
    rows, width = tokens.shape
    half = rows // 2
    q_width = w_query.shape[1]
    kv_width = key_projection.shape[1] + value_projection.shape[1]
    kv, queries = pl.pallas_call(
        project_kernel,
        out_shape=(struct((rows, kv_width), bf16), struct((rows, q_width), bf16)),
        in_specs=in_hbm(8),
        out_specs=tuple(in_vmem(2)),
        scratch_shapes=[
            pltpu.SMEM(block_split.shape, jnp.int32),
            pltpu.SMEM(lengths.shape, jnp.int32),
            pltpu.VMEM((1, HEAD), f32),
            pltpu.VMEM((rows, width), bf16),
            pltpu.VMEM((1, width), f32),
            pltpu.VMEM((width, kv_width), bf16),
            pltpu.VMEM((width, q_width), bf16),
            pltpu.SemaphoreType.DMA((5,)),
            pltpu.SemaphoreType.DMA((WEIGHT_STEPS, 2)),
            pltpu.SemaphoreType.DMA((WEIGHT_STEPS, 1)),
        ],
        compiler_params=kernel_params(62),
        cost_estimate=cost(2 * rows * width * (kv_width + q_width), 2 * width * (kv_width + q_width)),
        name="project",
    )(
        block_split, lengths, inverse_frequencies(), tokens, norm_gain.reshape(1, width),
        key_projection, value_projection, w_query,
    )
    far_queries = swap(queries, n, 1)

    def attend(pieces):
        keys = sum(piece.count for piece in pieces) * rows
        arrays = operands(pieces)
        mine, stats, packed = pl.pallas_call(
            functools.partial(attend_kernel, pieces),
            out_shape=(
                struct((rows, q_width), f32),
                struct((rows, HEAD), f32),
                struct((rows, q_width + HEAD), bf16),
            ),
            in_specs=in_smem(2) + in_vmem(2 + len(arrays)),
            out_specs=tuple(in_vmem(3)),
            compiler_params=kernel_params(32),
            cost_estimate=cost(8 * rows * keys * q_width, 2 * keys * kv_width),
            name="attend",
        )(block_split, lengths, queries, far_queries, *arrays)
        return [mine, stats, swap(packed, n, 1)]

    def place_pages(pieces, held=()):
        arrays = operands(pieces)
        shape = (2 * rows // PAGE, 2, PAGE, kv_width // 2)
        return pl.pallas_call(
            functools.partial(cache_kernel, pieces, bool(held)),
            out_shape=(struct(shape, bf16),) * 2,
            in_specs=in_smem(2) + in_vmem(len(arrays) + len(held)),
            out_specs=tuple(in_vmem(2)),
            input_output_aliases={2 + len(arrays) + i: i for i in range(len(held))},
            compiler_params=kernel_params(32),
            cost_estimate=cost(0, 4 * rows * kv_width),
            name="cache",
        )(block_split, page_slot, *arrays, *held)

    if n == 16:

        def swapped(piece, bits):
            source = lambda shard, i: piece.source_of(shard ^ bits, i)
            return Piece([swap(piece.arrays[0], n, bits)], source)

        own = Piece([kv], at_distance(0))
        second, first, beside = swapped(own, 8), swapped(own, 4), swapped(own, 2)
        queries, kv = pl.pallas_call(
            stage_kernel,
            out_shape=(struct(queries.shape, bf16), struct(kv.shape, bf16)),
            in_specs=in_vmem(2),
            out_specs=tuple(in_vmem(2)),
            compiler_params=kernel_params(24),
            cost_estimate=cost(0, 8 * rows * kv_width),
            name="stage",
        )(queries, kv)
        first_across = swapped(first, 2)
        (second, beside, first_across), kv = tied_all([second, beside, first_across], kv)
        own = own.moved([kv])
        third = swapped(second, 4)
        early = [own, beside, first, second, first_across]
        late = [third, swapped(second, 2), swapped(third, 2)]
        partials = attend(early)
        placed, partials[1] = tied_all(early, partials[1])
        held = place_pages(placed)
        queries, partials[1], held = lax.optimization_barrier((queries, partials[1], held))
        partials += attend(late)
        remaining = late
    else:
        same = [list(range(c, n, 2)) for c in range(2)]
        gathered = lax.all_gather(kv, "seq", axis=0, tiled=True, axis_index_groups=same)
        remaining = [Piece([gathered], lambda shard, i: 2 * i + shard % 2, n // 2)]
        partials, held = attend(remaining), ()
    arrays, partials[-3] = lax.optimization_barrier((operands(remaining), partials[-3]))
    remaining, _ = with_refs(remaining, arrays)
    cache, other = place_pages(remaining, held)
    partials[-3], cache, other = lax.optimization_barrier((partials[-3], cache, other))
    sent = pl.pallas_call(
        leave_kernel,
        out_shape=struct((half, width), bf16),
        in_specs=in_vmem(1 + len(partials)),
        out_specs=in_vmem(1)[0],
        compiler_params=kernel_params(24),
        cost_estimate=cost(rows * width * q_width, 2 * width * q_width),
        name="leave",
    )(w_out, *partials)
    received = lax.ppermute(sent, "req", [(i, (i + 1) % parts) for i in range(parts)])
    kept = pl.pallas_call(
        keep_kernel,
        out_shape=struct((half, width), f32),
        in_specs=in_vmem(2 + len(partials)),
        out_specs=in_vmem(1)[0],
        compiler_params=kernel_params(24),
        cost_estimate=cost(rows * width * q_width, 2 * width * q_width),
        name="keep",
    )(w_out, tokens, *partials)
    cache = cache + swap(other, n, 1)
    hidden = (kept + received.astype(f32)).astype(bf16)
    return hidden, cache


def solution(mesh):
    in_specs = (
        P("seq", None),
        P(),
        P(None, "req"),
        P(None, "req"),
        P(None, "req"),
        P("req", None),
        P(),
        P(),
        P(),
    )
    out_specs = (P(("seq", "req"), None), P("seq", None, None, "req"))
    body = functools.partial(on_device, mesh.shape["seq"], mesh.shape["req"])
    return jax.shard_map(body, mesh=mesh, in_specs=in_specs, out_specs=out_specs, check_vma=False)
```

```python
import functools
import math

import jax
import jax.numpy as jnp
import numpy as np
from jax import lax
from jax.experimental import pallas as pl
from jax.experimental.pallas import tpu as pltpu
from jax.sharding import PartitionSpec as P

HEAD = 128
PAGE = 32
THETA = 1000000.0
EPS = 1e-05
MASKED = -1e30
FLOOR = -1e29
WEIGHT_STEPS = 4
MIB = 1024 * 1024
SCALE = math.log2(math.e) / math.sqrt(HEAD)

f32 = jnp.float32
bf16 = jnp.bfloat16
struct = jax.ShapeDtypeStruct


def in_vmem(count):
    return [pl.BlockSpec(memory_space=pltpu.VMEM)] * count


def in_smem(count):
    return [pl.BlockSpec(memory_space=pltpu.SMEM)] * count


def in_hbm(count):
    return [pl.BlockSpec(memory_space=pltpu.HBM)] * count


def kernel_params(mib):
    return pltpu.CompilerParams(vmem_limit_bytes=mib * MIB)


def cost(flops, moved):
    return pl.CostEstimate(flops=flops, bytes_accessed=moved, transcendentals=0)


def inverse_frequencies():
    exponent = np.arange(HEAD // 2, dtype=np.float64) * (2.0 / HEAD)
    freq = (THETA**-exponent).astype(np.float32)
    return jnp.asarray(np.concatenate([freq, freq])[None, :])


def blocks_of(block_ref, shard):
    first = block_ref[shard]
    return first, 2 * block_ref.shape[0] - 1 - first


def prompt_begin(position, len_ref):
    begin = jnp.zeros_like(position)
    start = jnp.int32(0)
    for r in range(len_ref.shape[0] - 1):
        start = start + len_ref[r]
        begin = jnp.where(position >= start, start, begin)
    return begin


def positions(blocks, half, dim, shape):
    index = lax.broadcasted_iota(jnp.int32, shape, dim)
    offset = blocks[0] * half
    for i, block in enumerate(blocks[1:], 1):
        offset = jnp.where(index >= i * half, (block - i) * half, offset)
    return index + offset


def rotate(u, cosine, signed_sine):
    return u * cosine + pltpu.roll(u, HEAD // 2, 1) * signed_sine


def weight_copies(refs, scratch, sems):
    copies = []
    depth = scratch.shape[0] // WEIGHT_STEPS
    for step in range(WEIGHT_STEPS):
        group, column = [], 0
        for i, ref in enumerate(refs):
            rows, cols = pl.ds(step * depth, depth), pl.ds(column, ref.shape[1])
            group.append(
                pltpu.make_async_copy(ref.at[rows, :], scratch.at[rows, cols], sems.at[step, i])
            )
            column += ref.shape[1]
        copies.append(group)
    return copies


def start_all(copies):
    for group in copies:
        for copy in group:
            copy.start()


def stepped_dot(left, copies, scratch):
    depth = scratch.shape[0] // WEIGHT_STEPS
    total = None
    for step in range(WEIGHT_STEPS):
        for copy in copies[step]:
            copy.wait()
        rows = slice(step * depth, (step + 1) * depth)
        part = jnp.dot(left[:, rows], scratch[rows, :], preferred_element_type=f32)
        total = part if total is None else total + part
    return total


def project_kernel(
    block_hbm, len_hbm, freq_hbm, tok_hbm, gain_hbm, wk_hbm, wv_hbm, wq_hbm,
    kv_ref, q_ref,
    block_ref, len_ref, freq_ref, tok_ref, gain_ref, kv_weights, q_weights, small_sems, kv_sems, q_sems,
):
    small = [
        pltpu.make_async_copy(source, target, small_sems.at[i])
        for i, (source, target) in enumerate(
            (
                (block_hbm, block_ref),
                (len_hbm, len_ref),
                (freq_hbm, freq_ref),
                (tok_hbm, tok_ref),
                (gain_hbm, gain_ref),
            )
        )
    ]
    kv_copies = weight_copies((wk_hbm, wv_hbm), kv_weights, kv_sems)
    q_copies = weight_copies((wq_hbm,), q_weights, q_sems)
    for copy in small:
        copy.start()
    start_all(kv_copies)
    start_all(q_copies)
    rows = tok_ref.shape[0]
    for copy in small[:3]:
        copy.wait()
    position = positions(blocks_of(block_ref, lax.axis_index("seq")), rows // 2, 0, (rows, HEAD))
    angle = (position - prompt_begin(position, len_ref)).astype(f32) * freq_ref[...]
    cosine, sine = jnp.cos(angle), jnp.sin(angle)
    lane = lax.broadcasted_iota(jnp.int32, (rows, HEAD), 1)
    sine = jnp.where(lane < HEAD // 2, -sine, sine)
    for copy in small[3:]:
        copy.wait()
    wide = tok_ref[...].astype(f32)
    scale = lax.rsqrt(jnp.mean(wide * wide, -1, keepdims=True) + EPS)
    normed = (wide * scale * gain_ref[...]).astype(bf16)
    product = stepped_dot(normed, kv_copies, kv_weights)
    key_width = wk_hbm.shape[1]
    for h in range(key_width // HEAD):
        cols = slice(h * HEAD, (h + 1) * HEAD)
        kv_ref[:, cols] = rotate(product[:, cols], cosine, sine).astype(bf16)
    kv_ref[:, key_width:] = product[:, key_width:].astype(bf16)
    product = stepped_dot(normed, q_copies, q_weights)
    for h in range(wq_hbm.shape[1] // HEAD):
        cols = slice(h * HEAD, (h + 1) * HEAD)
        q_ref[:, cols] = rotate(product[:, cols], cosine, sine).astype(bf16)


def attend_kernel(pieces, side, block_ref, len_ref, q_ref, far_ref, *refs):
    pieces, refs = with_refs(pieces, refs)
    shard = lax.axis_index("seq")
    rows, q_width = q_ref.shape
    key_width = pieces[0].arrays[0].shape[1] // 2
    kv_heads = key_width // HEAD
    group = q_width // key_width
    shards = [shard, shard ^ 1]
    if side is None:
        taken, span = rows, slice(None)
        blocks = [block for s in shards for block in blocks_of(block_ref, s)]
    else:
        part = lax.axis_index("req")
        part = 1 - part if side else part
        taken = rows // 2
        span = pl.ds(pl.multiple_of(part * taken, taken), taken)
        blocks = [jnp.where(part == 0, *blocks_of(block_ref, s)) for s in shards]
    both = 2 * taken
    q_pos = positions(blocks, rows // 2, 0, (both, 1))
    q_begin = prompt_begin(q_pos, len_ref)
    queries = [
        jnp.concatenate(
            [
                ref[span, h * HEAD : (h + 1) * HEAD]
                for h in range(g * group, (g + 1) * group)
                for ref in (q_ref, far_ref)
            ],
            0,
        )
        for g in range(kv_heads)
    ]

    def absorb(state, blocks, sources):
        width = rows * len(blocks)
        held = [block for s in sources for block in blocks_of(block_ref, s)]
        key_pos = positions(held, rows // 2, 1, (1, width))
        bias = jnp.where((key_pos >= q_begin) & (key_pos <= q_pos), 0.0, MASKED)
        bias = jnp.concatenate([bias] * group, 0)
        out = []
        for g in range(kv_heads):
            top, total, acc = state[g]
            keys = jnp.concatenate([b[:, g * HEAD : (g + 1) * HEAD] for b in blocks], 0)
            values = jnp.concatenate(
                [b[:, key_width + g * HEAD : key_width + (g + 1) * HEAD] for b in blocks], 0
            )
            scores = lax.dot_general(
                queries[g], keys, (((1,), (1,)), ((), ())), preferred_element_type=f32
            )
            scores = scores * SCALE + bias
            new_top = jnp.maximum(top, jnp.max(scores, -1, keepdims=True))
            weights = jnp.exp2(scores - new_top)
            factor = jnp.exp2(top - new_top)
            total = total * factor + jnp.sum(weights, -1, keepdims=True)
            acc = acc * factor + jnp.dot(weights.astype(bf16), values, preferred_element_type=f32)
            out.append((new_top, total, acc))
        return tuple(out)

    state = (
        (
            jnp.full((group * both, 1), FLOOR, f32),
            jnp.zeros((group * both, 1), f32),
            jnp.zeros((group * both, HEAD), f32),
        ),
    ) * kv_heads
    if all(piece.count == 1 for piece in pieces):
        for i in range(0, len(pieces), 2):
            pair = pieces[i : i + 2]
            state = absorb(
                state, [p.arrays[0][...] for p in pair], [p.source_of(shard, 0) for p in pair]
            )
    else:
        for piece in pieces:

            def step(i, carried):
                at = pl.multiple_of(i * rows, rows)
                block = piece.arrays[0][pl.ds(at, rows), :]
                return absorb(carried, [block], [piece.source_of(shard, i)])

            state = lax.fori_loop(0, piece.count, step, state)

    mine_ref, stat_ref, packed_ref = refs
    heads = q_width // HEAD
    lane = lax.broadcasted_iota(jnp.int32, (taken, HEAD), 1)
    mine = jnp.zeros((taken, HEAD), f32)
    theirs = jnp.zeros((taken, HEAD), f32)
    for g in range(kv_heads):
        top, total, acc = state[g]
        for j in range(group):
            h = g * group + j
            cols = slice(h * HEAD, (h + 1) * HEAD)
            near = slice(j * both, j * both + taken)
            far = slice(j * both + taken, (j + 1) * both)
            mine_ref[:, cols] = acc[near]
            packed_ref[:, cols] = acc[far].astype(bf16)
            for value, at in ((top, h), (total, heads + h)):
                mine = jnp.where(lane == at, value[near], mine)
                theirs = jnp.where(lane % (2 * heads) == at, value[far], theirs)
    stat_ref[...] = mine
    high = theirs.astype(bf16).astype(f32)
    middle = (theirs - high).astype(bf16).astype(f32)
    low = theirs - high - middle
    third = lane // (2 * heads)
    parts = jnp.where(third == 0, high, jnp.where(third == 1, middle, low))
    packed_ref[:, q_width:] = parts.astype(bf16)


def stage_kernel(q_ref, kv_ref, q_out, kv_out):
    q_out[...] = q_ref[...]
    kv_out[...] = kv_ref[...]


def joined_rows(partials, first, half):
    q_width = partials[0].shape[1]
    heads = q_width // HEAD
    part = pl.ds(pl.multiple_of(first, half), half)
    held = []
    for mine_ref, stat_ref, packed_ref in zip(partials[::3], partials[1::3], partials[2::3]):
        span = slice(None) if mine_ref.shape[0] == half else part
        parts = packed_ref[span, q_width:].astype(f32)
        stats = parts
        for t in (1, 2):
            stats = stats + pltpu.roll(parts, HEAD - 2 * heads * t, 1)
        held += [(mine_ref, span, stat_ref[span, :]), (packed_ref, span, stats)]
    top = functools.reduce(jnp.maximum, [stats for _, _, stats in held])
    shares = [jnp.exp2(stats - top) for _, _, stats in held]
    total = sum(
        share * pltpu.roll(stats, HEAD - heads, 1) for share, (_, _, stats) in zip(shares, held)
    )
    shares = [share / total for share in shares]
    context = []
    for h in range(heads):
        cols = slice(h * HEAD, (h + 1) * HEAD)
        context.append(
            sum(
                ref[span, cols].astype(f32) * share[:, h : h + 1]
                for (ref, span, _), share in zip(held, shares)
            ).astype(bf16)
        )
    return jnp.concatenate(context, 1)


def leave_kernel(wo_ref, *refs):
    partials, sent_ref = refs[:-1], refs[-1]
    half = sent_ref.shape[0]
    context = joined_rows(partials, (1 - lax.axis_index("req")) * half, half)
    sent_ref[...] = jnp.dot(context, wo_ref[...], preferred_element_type=f32).astype(bf16)


def keep_kernel(wo_ref, tok_ref, *refs):
    partials, out_ref = refs[:-1], refs[-1]
    half = out_ref.shape[0]
    first = lax.axis_index("req") * half
    context = joined_rows(partials, first, half)
    residual = tok_ref[pl.ds(pl.multiple_of(first, half), half), :].astype(f32)
    out_ref[...] = jnp.dot(context, wo_ref[...], preferred_element_type=f32) + residual


def finish_kernel(kept_ref, received_ref, mine_ref, other_ref, hidden_ref, cache_ref):
    hidden_ref[...] = (kept_ref[...] + received_ref[...].astype(f32)).astype(bf16)
    cache_ref[...] = mine_ref[...] + other_ref[...]


def cache_kernel(pieces, held, block_ref, slot_ref, *refs):
    pieces, refs = with_refs(pieces, refs)
    mine_ref, other_ref = refs[-2:]
    shard = lax.axis_index("seq")
    slots = mine_ref.shape[0]
    key_width = mine_ref.shape[3]
    rows = slots * PAGE // 2
    pages = rows // 2 // PAGE
    for i, target in enumerate((mine_ref, other_ref)):
        target[...] = refs[i][...] if held else jnp.zeros_like(target)

    def place(ref, at, source):
        for k, block in enumerate(blocks_of(block_ref, source)):
            for j in range(pages):
                slot = slot_ref[block * pages + j]
                holder = slot // slots
                local = slot - holder * slots
                offset = at + (k * pages + j) * PAGE
                if not isinstance(offset, int):
                    offset = pl.multiple_of(offset, PAGE)
                for target, owner in ((mine_ref, shard), (other_ref, shard ^ 1)):

                    @pl.when(holder == owner)
                    def _():
                        target[local, 0] = ref[pl.ds(offset, PAGE), :key_width]
                        target[local, 1] = ref[pl.ds(offset, PAGE), key_width:]

    for piece in pieces:
        if piece.count == 1:
            place(piece.arrays[0], 0, piece.source_of(shard, 0))
        else:

            def step(i, carry):
                place(piece.arrays[0], i * rows, piece.source_of(shard, i))
                return carry

            lax.fori_loop(0, piece.count, step, 0)


def tied_all(pieces, other):
    arrays, other = lax.optimization_barrier((operands(pieces), other))
    return with_refs(pieces, arrays)[0], other


def tied(piece, other):
    (piece,), other = tied_all([piece], other)
    return piece, other


def swap(x, n, bit):
    return lax.ppermute(x, "seq", [(i, i ^ bit) for i in range(n)])


class Piece:
    def __init__(self, arrays, source_of, count=1):
        self.arrays, self.source_of, self.count = arrays, source_of, count

    def moved(self, arrays):
        return Piece(arrays, self.source_of, self.count)


def operands(pieces):
    return [x for piece in pieces for x in piece.arrays]


def with_refs(pieces, refs):
    out = []
    for piece in pieces:
        taken, refs = refs[: len(piece.arrays)], refs[len(piece.arrays) :]
        out.append(piece.moved(taken))
    return out, refs


def at_distance(bits):
    return lambda shard, i: shard ^ bits


def move(x, pairs):
    return lax.ppermute(x, "seq", pairs)


def on_device(
    n, parts, tokens, norm_gain, w_query, key_projection, value_projection, w_out, lengths, block_split, page_slot,
):
    rows, width = tokens.shape
    half = rows // 2
    q_width = w_query.shape[1]
    kv_width = key_projection.shape[1] + value_projection.shape[1]
    kv, queries = pl.pallas_call(
        project_kernel,
        out_shape=(struct((rows, kv_width), bf16), struct((rows, q_width), bf16)),
        in_specs=in_hbm(8),
        out_specs=tuple(in_vmem(2)),
        scratch_shapes=[
            pltpu.SMEM(block_split.shape, jnp.int32),
            pltpu.SMEM(lengths.shape, jnp.int32),
            pltpu.VMEM((1, HEAD), f32),
            pltpu.VMEM((rows, width), bf16),
            pltpu.VMEM((1, width), f32),
            pltpu.VMEM((width, kv_width), bf16),
            pltpu.VMEM((width, q_width), bf16),
            pltpu.SemaphoreType.DMA((5,)),
            pltpu.SemaphoreType.DMA((WEIGHT_STEPS, 2)),
            pltpu.SemaphoreType.DMA((WEIGHT_STEPS, 1)),
        ],
        compiler_params=kernel_params(62),
        cost_estimate=cost(2 * rows * width * (kv_width + q_width), 2 * width * (kv_width + q_width)),
        name="project",
    )(
        block_split, lengths, inverse_frequencies(), tokens, norm_gain.reshape(1, width),
        key_projection, value_projection, w_query,
    )
    far_queries = swap(queries, n, 1)

    def attend(pieces, side=None):
        arrays = operands(pieces)
        taken = rows if side is None else half
        mine, stats, packed = pl.pallas_call(
            functools.partial(attend_kernel, pieces, side),
            out_shape=(
                struct((taken, q_width), f32),
                struct((taken, HEAD), f32),
                struct((taken, q_width + HEAD), bf16),
            ),
            in_specs=in_smem(2) + in_vmem(2 + len(arrays)),
            out_specs=tuple(in_vmem(3)),
            compiler_params=kernel_params(32),
            cost_estimate=cost(0, 0),
            name="attend",
        )(block_split, lengths, queries, far_queries, *arrays)
        return [mine, stats, swap(packed, n, 1)]

    def place_pages(pieces, held=()):
        arrays = operands(pieces)
        shape = (2 * rows // PAGE, 2, PAGE, kv_width // 2)
        return pl.pallas_call(
            functools.partial(cache_kernel, pieces, bool(held)),
            out_shape=(struct(shape, bf16),) * 2,
            in_specs=in_smem(2) + in_vmem(len(arrays) + len(held)),
            out_specs=tuple(in_vmem(2)),
            input_output_aliases={2 + len(arrays) + i: i for i in range(len(held))},
            compiler_params=kernel_params(32),
            cost_estimate=cost(0, 0),
            name="cache",
        )(block_split, page_slot, *arrays, *held)

    if n == 16:

        def swapped(piece, bits):
            source = lambda shard, i: piece.source_of(shard ^ bits, i)
            return Piece([swap(piece.arrays[0], n, bits)], source)

        own = Piece([kv], at_distance(0))
        second, first, beside = swapped(own, 8), swapped(own, 4), swapped(own, 2)
        queries, kv = pl.pallas_call(
            stage_kernel,
            out_shape=(struct(queries.shape, bf16), struct(kv.shape, bf16)),
            in_specs=in_vmem(2),
            out_specs=tuple(in_vmem(2)),
            compiler_params=kernel_params(24),
            cost_estimate=cost(0, 8 * rows * kv_width),
            name="stage",
        )(queries, kv)
        first_across = swapped(first, 2)
        (second, beside, first_across), kv = tied_all([second, beside, first_across], kv)
        own = own.moved([kv])
        third = swapped(second, 4)
        early = [own, beside, first, second, first_across, third]
        late = [swapped(second, 2), swapped(third, 2)]
        partials = attend(early)
        placed, partials[1] = tied_all(early, partials[1])
        held = place_pages(placed)
        queries, partials[1], held = lax.optimization_barrier((queries, partials[1], held))
        remaining = late
    else:
        same = [list(range(c, n, 2)) for c in range(2)]
        gathered = lax.all_gather(kv, "seq", axis=0, tiled=True, axis_index_groups=same)
        remaining = [Piece([gathered], lambda shard, i: 2 * i + shard % 2, n // 2)]
        partials, held = [], ()
    leaving = attend(remaining, 1)
    queries, leaving[1] = lax.optimization_barrier((queries, leaving[1]))
    staying = attend(remaining, 0)
    leaving[0], staying[1] = lax.optimization_barrier((leaving[0], staying[1]))
    sent = pl.pallas_call(
        leave_kernel,
        out_shape=struct((half, width), bf16),
        in_specs=in_vmem(4 + len(partials)),
        out_specs=in_vmem(1)[0],
        compiler_params=kernel_params(24),
        cost_estimate=cost(0, 0),
        name="leave",
    )(w_out, *partials, *leaving)
    received = lax.ppermute(sent, "req", [(i, (i + 1) % parts) for i in range(parts)])
    remaining, sent = tied_all(remaining, sent)
    cache, other = place_pages(remaining, held)
    kept = pl.pallas_call(
        keep_kernel,
        out_shape=struct((half, width), f32),
        in_specs=in_vmem(5 + len(partials)),
        out_specs=in_vmem(1)[0],
        compiler_params=kernel_params(24),
        cost_estimate=cost(0, 0),
        name="keep",
    )(w_out, tokens, *partials, *staying)
    return pl.pallas_call(
        finish_kernel,
        out_shape=(struct((half, width), bf16), struct(cache.shape, bf16)),
        in_specs=in_vmem(4),
        out_specs=tuple(in_vmem(2)),
        compiler_params=kernel_params(24),
        cost_estimate=cost(0, 0),
        name="finish",
    )(kept, received, cache, swap(other, n, 1))


def solution(mesh):
    in_specs = (
        P("seq", None),
        P(),
        P(None, "req"),
        P(None, "req"),
        P(None, "req"),
        P("req", None),
        P(),
        P(),
        P(),
    )
    out_specs = (P(("seq", "req"), None), P("seq", None, None, "req"))
    body = functools.partial(on_device, mesh.shape["seq"], mesh.shape["req"])
    return jax.shard_map(body, mesh=mesh, in_specs=in_specs, out_specs=out_specs, check_vma=False)
```

```python
import functools
import math

import jax
import jax.numpy as jnp
import numpy as np
from jax import lax
from jax.experimental import pallas as pl
from jax.experimental.pallas import tpu as pltpu
from jax.sharding import PartitionSpec as P

HEAD = 128
PAGE = 32
THETA = 1000000.0
EPS = 1e-05
MASKED = -1e30
FLOOR = -1e29
WEIGHT_STEPS = 4
MIB = 1024 * 1024
SCALE = math.log2(math.e) / math.sqrt(HEAD)

f32 = jnp.float32
bf16 = jnp.bfloat16
struct = jax.ShapeDtypeStruct


def in_vmem(count):
    return [pl.BlockSpec(memory_space=pltpu.VMEM)] * count


def in_smem(count):
    return [pl.BlockSpec(memory_space=pltpu.SMEM)] * count


def in_hbm(count):
    return [pl.BlockSpec(memory_space=pltpu.HBM)] * count


def kernel_params(mib):
    return pltpu.CompilerParams(vmem_limit_bytes=mib * MIB)


def cost(flops, moved):
    return pl.CostEstimate(flops=flops, bytes_accessed=moved, transcendentals=0)


def inverse_frequencies():
    exponent = np.arange(HEAD // 2, dtype=np.float64) * (2.0 / HEAD)
    freq = (THETA**-exponent).astype(np.float32)
    return jnp.asarray(np.concatenate([freq, freq])[None, :])


def blocks_of(block_ref, shard):
    first = block_ref[shard]
    return first, 2 * block_ref.shape[0] - 1 - first


def prompt_begin(position, len_ref):
    begin = jnp.zeros_like(position)
    start = jnp.int32(0)
    for r in range(len_ref.shape[0] - 1):
        start = start + len_ref[r]
        begin = jnp.where(position >= start, start, begin)
    return begin


def positions(blocks, half, dim, shape):
    index = lax.broadcasted_iota(jnp.int32, shape, dim)
    offset = blocks[0] * half
    for i, block in enumerate(blocks[1:], 1):
        offset = jnp.where(index >= i * half, (block - i) * half, offset)
    return index + offset


def rotate(u, cosine, signed_sine):
    return u * cosine + pltpu.roll(u, HEAD // 2, 1) * signed_sine


def weight_copies(refs, scratch, sems):
    copies = []
    depth = scratch.shape[0] // WEIGHT_STEPS
    for step in range(WEIGHT_STEPS):
        group, column = [], 0
        for i, ref in enumerate(refs):
            rows, cols = pl.ds(step * depth, depth), pl.ds(column, ref.shape[1])
            group.append(
                pltpu.make_async_copy(ref.at[rows, :], scratch.at[rows, cols], sems.at[step, i])
            )
            column += ref.shape[1]
        copies.append(group)
    return copies


def start_all(copies):
    for group in copies:
        for copy in group:
            copy.start()


def stepped_dot(left, copies, scratch):
    depth = scratch.shape[0] // WEIGHT_STEPS
    total = None
    for step in range(WEIGHT_STEPS):
        for copy in copies[step]:
            copy.wait()
        rows = slice(step * depth, (step + 1) * depth)
        part = jnp.dot(left[:, rows], scratch[rows, :], preferred_element_type=f32)
        total = part if total is None else total + part
    return total


def project_kernel(
    block_hbm, len_hbm, freq_hbm, tok_hbm, gain_hbm, wk_hbm, wv_hbm, wq_hbm,
    kv_ref, both_ref,
    block_ref, len_ref, freq_ref, tok_ref, gain_ref, kv_weights, q_weights, small_sems, kv_sems, q_sems,
):
    small = [
        pltpu.make_async_copy(source, target, small_sems.at[i])
        for i, (source, target) in enumerate(
            (
                (block_hbm, block_ref),
                (len_hbm, len_ref),
                (freq_hbm, freq_ref),
                (tok_hbm, tok_ref),
                (gain_hbm, gain_ref),
            )
        )
    ]
    kv_copies = weight_copies((wk_hbm, wv_hbm), kv_weights, kv_sems)
    q_copies = weight_copies((wq_hbm,), q_weights, q_sems)
    for copy in small:
        copy.start()
    start_all(kv_copies)
    start_all(q_copies)
    rows = tok_ref.shape[0]
    for copy in small[:3]:
        copy.wait()
    position = positions(blocks_of(block_ref, lax.axis_index("seq")), rows // 2, 0, (rows, HEAD))
    angle = (position - prompt_begin(position, len_ref)).astype(f32) * freq_ref[...]
    cosine, sine = jnp.cos(angle), jnp.sin(angle)
    lane = lax.broadcasted_iota(jnp.int32, (rows, HEAD), 1)
    sine = jnp.where(lane < HEAD // 2, -sine, sine)
    for copy in small[3:]:
        copy.wait()
    wide = tok_ref[...].astype(f32)
    scale = lax.rsqrt(jnp.mean(wide * wide, -1, keepdims=True) + EPS)
    normed = (wide * scale * gain_ref[...]).astype(bf16)
    product = stepped_dot(normed, kv_copies, kv_weights)
    key_width = wk_hbm.shape[1]
    for h in range(key_width // HEAD):
        cols = slice(h * HEAD, (h + 1) * HEAD)
        kv_ref[:, cols] = rotate(product[:, cols], cosine, sine).astype(bf16)
    kv_ref[:, key_width:] = product[:, key_width:].astype(bf16)
    both_ref[:, : kv_ref.shape[1]] = kv_ref[...]
    product = stepped_dot(normed, q_copies, q_weights)
    for h in range(wq_hbm.shape[1] // HEAD):
        cols = slice(h * HEAD, (h + 1) * HEAD)
        turned = rotate(product[:, cols], cosine, sine).astype(bf16)
        both_ref[:, pl.ds(kv_ref.shape[1] + h * HEAD, HEAD)] = turned


def attend_kernel(pieces, side, block_ref, len_ref, q_ref, far_ref, *refs):
    pieces, refs = with_refs(pieces, refs)
    shard = lax.axis_index("seq")
    rows, q_width = q_ref.shape
    key_width = pieces[0].arrays[0].shape[1] // 2
    kv_heads = key_width // HEAD
    group = q_width // key_width
    shards = [shard, shard ^ 1]
    if side is None:
        taken, span = rows, slice(None)
        blocks = [block for s in shards for block in blocks_of(block_ref, s)]
    else:
        part = lax.axis_index("req")
        part = 1 - part if side else part
        taken = rows // 2
        span = pl.ds(pl.multiple_of(part * taken, taken), taken)
        blocks = [jnp.where(part == 0, *blocks_of(block_ref, s)) for s in shards]
    both = 2 * taken
    q_pos = positions(blocks, rows // 2, 0, (both, 1))
    q_begin = prompt_begin(q_pos, len_ref)
    queries = [
        jnp.concatenate(
            [
                ref[span, h * HEAD : (h + 1) * HEAD]
                for h in range(g * group, (g + 1) * group)
                for ref in (q_ref, far_ref)
            ],
            0,
        )
        for g in range(kv_heads)
    ]

    def absorb(state, blocks, sources):
        width = rows * len(blocks)
        held = [block for s in sources for block in blocks_of(block_ref, s)]
        key_pos = positions(held, rows // 2, 1, (1, width))
        bias = jnp.where((key_pos >= q_begin) & (key_pos <= q_pos), 0.0, MASKED)
        bias = jnp.concatenate([bias] * group, 0)
        out = []
        for g in range(kv_heads):
            top, total, acc = state[g]
            keys = jnp.concatenate([b[:, g * HEAD : (g + 1) * HEAD] for b in blocks], 0)
            values = jnp.concatenate(
                [b[:, key_width + g * HEAD : key_width + (g + 1) * HEAD] for b in blocks], 0
            )
            scores = lax.dot_general(
                queries[g], keys, (((1,), (1,)), ((), ())), preferred_element_type=f32
            )
            scores = scores * SCALE + bias
            new_top = jnp.maximum(top, jnp.max(scores, -1, keepdims=True))
            weights = jnp.exp2(scores - new_top)
            factor = jnp.exp2(top - new_top)
            total = total * factor + jnp.sum(weights, -1, keepdims=True)
            acc = acc * factor + jnp.dot(weights.astype(bf16), values, preferred_element_type=f32)
            out.append((new_top, total, acc))
        return tuple(out)

    state = (
        (
            jnp.full((group * both, 1), FLOOR, f32),
            jnp.zeros((group * both, 1), f32),
            jnp.zeros((group * both, HEAD), f32),
        ),
    ) * kv_heads
    if all(piece.count == 1 for piece in pieces):
        for i in range(0, len(pieces), 2):
            pair = pieces[i : i + 2]
            state = absorb(
                state, [p.arrays[0][...] for p in pair], [p.source_of(shard, 0) for p in pair]
            )
    else:
        for piece in pieces:

            def step(i, carried):
                at = pl.multiple_of(i * rows, rows)
                block = piece.arrays[0][pl.ds(at, rows), :]
                return absorb(carried, [block], [piece.source_of(shard, i)])

            state = lax.fori_loop(0, piece.count, step, state)

    mine_ref, stat_ref, packed_ref = refs
    heads = q_width // HEAD
    lane = lax.broadcasted_iota(jnp.int32, (taken, HEAD), 1)
    mine = jnp.zeros((taken, HEAD), f32)
    theirs = jnp.zeros((taken, HEAD), f32)
    for g in range(kv_heads):
        top, total, acc = state[g]
        for j in range(group):
            h = g * group + j
            cols = slice(h * HEAD, (h + 1) * HEAD)
            near = slice(j * both, j * both + taken)
            far = slice(j * both + taken, (j + 1) * both)
            mine_ref[:, cols] = acc[near]
            packed_ref[:, cols] = acc[far].astype(bf16)
            for value, at in ((top, h), (total, heads + h)):
                mine = jnp.where(lane == at, value[near], mine)
                theirs = jnp.where(lane % (2 * heads) == at, value[far], theirs)
    stat_ref[...] = mine
    high = theirs.astype(bf16).astype(f32)
    middle = (theirs - high).astype(bf16).astype(f32)
    low = theirs - high - middle
    third = lane // (2 * heads)
    parts = jnp.where(third == 0, high, jnp.where(third == 1, middle, low))
    packed_ref[:, q_width:] = parts.astype(bf16)


def stage_kernel(both_ref, kv_out, q_out):
    kv_out[...] = both_ref[:, : kv_out.shape[1]]
    q_out[...] = both_ref[:, kv_out.shape[1] :]


def joined_rows(partials, first, half):
    q_width = partials[0].shape[1]
    heads = q_width // HEAD
    part = pl.ds(pl.multiple_of(first, half), half)
    held = []
    for mine_ref, stat_ref, packed_ref in zip(partials[::3], partials[1::3], partials[2::3]):
        span = slice(None) if mine_ref.shape[0] == half else part
        parts = packed_ref[span, q_width:].astype(f32)
        stats = parts
        for t in (1, 2):
            stats = stats + pltpu.roll(parts, HEAD - 2 * heads * t, 1)
        held += [(mine_ref, span, stat_ref[span, :]), (packed_ref, span, stats)]
    top = functools.reduce(jnp.maximum, [stats for _, _, stats in held])
    shares = [jnp.exp2(stats - top) for _, _, stats in held]
    total = sum(
        share * pltpu.roll(stats, HEAD - heads, 1) for share, (_, _, stats) in zip(shares, held)
    )
    shares = [share / total for share in shares]
    context = []
    for h in range(heads):
        cols = slice(h * HEAD, (h + 1) * HEAD)
        context.append(
            sum(
                ref[span, cols].astype(f32) * share[:, h : h + 1]
                for (ref, span, _), share in zip(held, shares)
            ).astype(bf16)
        )
    return jnp.concatenate(context, 1)


def leave_kernel(wo_ref, *refs):
    partials, sent_ref = refs[:-1], refs[-1]
    half = sent_ref.shape[0]
    context = joined_rows(partials, (1 - lax.axis_index("req")) * half, half)
    sent_ref[...] = jnp.dot(context, wo_ref[...], preferred_element_type=f32).astype(bf16)


def keep_kernel(wo_ref, tok_ref, *refs):
    partials, out_ref = refs[:-1], refs[-1]
    half = out_ref.shape[0]
    first = lax.axis_index("req") * half
    context = joined_rows(partials, first, half)
    residual = tok_ref[pl.ds(pl.multiple_of(first, half), half), :].astype(f32)
    out_ref[...] = jnp.dot(context, wo_ref[...], preferred_element_type=f32) + residual


def finish_kernel(kept_ref, received_ref, mine_ref, other_ref, hidden_ref, cache_ref):
    hidden_ref[...] = (kept_ref[...] + received_ref[...].astype(f32)).astype(bf16)
    cache_ref[...] = mine_ref[...] + other_ref[...]


def cache_kernel(pieces, block_ref, slot_ref, *refs):
    pieces, (mine_ref, other_ref) = with_refs(pieces, refs)
    shard = lax.axis_index("seq")
    slots = mine_ref.shape[0]
    key_width = mine_ref.shape[3]
    rows = slots * PAGE // 2
    pages = rows // 2 // PAGE
    for target in (mine_ref, other_ref):
        target[...] = jnp.zeros_like(target)

    def place(ref, at, source):
        for k, block in enumerate(blocks_of(block_ref, source)):
            for j in range(pages):
                slot = slot_ref[block * pages + j]
                holder = slot // slots
                local = slot - holder * slots
                offset = at + (k * pages + j) * PAGE
                if not isinstance(offset, int):
                    offset = pl.multiple_of(offset, PAGE)
                for target, owner in ((mine_ref, shard), (other_ref, shard ^ 1)):

                    @pl.when(holder == owner)
                    def _():
                        target[local, 0] = ref[pl.ds(offset, PAGE), :key_width]
                        target[local, 1] = ref[pl.ds(offset, PAGE), key_width:]

    for piece in pieces:
        if piece.count == 1:
            place(piece.arrays[0], 0, piece.source_of(shard, 0))
        else:

            def step(i, carry):
                place(piece.arrays[0], i * rows, piece.source_of(shard, i))
                return carry

            lax.fori_loop(0, piece.count, step, 0)


def tied_all(pieces, other):
    arrays, other = lax.optimization_barrier((operands(pieces), other))
    return with_refs(pieces, arrays)[0], other


def tied(piece, other):
    (piece,), other = tied_all([piece], other)
    return piece, other


def swap(x, n, bit):
    return lax.ppermute(x, "seq", [(i, i ^ bit) for i in range(n)])


class Piece:
    def __init__(self, arrays, source_of, count=1):
        self.arrays, self.source_of, self.count = arrays, source_of, count

    def moved(self, arrays):
        return Piece(arrays, self.source_of, self.count)


def operands(pieces):
    return [x for piece in pieces for x in piece.arrays]


def with_refs(pieces, refs):
    out = []
    for piece in pieces:
        taken, refs = refs[: len(piece.arrays)], refs[len(piece.arrays) :]
        out.append(piece.moved(taken))
    return out, refs


def at_distance(bits):
    return lambda shard, i: shard ^ bits


def move(x, pairs):
    return lax.ppermute(x, "seq", pairs)


def on_device(
    n, parts, tokens, norm_gain, w_query, key_projection, value_projection, w_out, lengths, block_split, page_slot,
):
    rows, width = tokens.shape
    half = rows // 2
    q_width = w_query.shape[1]
    kv_width = key_projection.shape[1] + value_projection.shape[1]
    kv, both = pl.pallas_call(
        project_kernel,
        out_shape=(struct((rows, kv_width), bf16), struct((rows, kv_width + q_width), bf16)),
        in_specs=in_hbm(8),
        out_specs=tuple(in_vmem(2)),
        scratch_shapes=[
            pltpu.SMEM(block_split.shape, jnp.int32),
            pltpu.SMEM(lengths.shape, jnp.int32),
            pltpu.VMEM((1, HEAD), f32),
            pltpu.VMEM((rows, width), bf16),
            pltpu.VMEM((1, width), f32),
            pltpu.VMEM((width, kv_width), bf16),
            pltpu.VMEM((width, q_width), bf16),
            pltpu.SemaphoreType.DMA((5,)),
            pltpu.SemaphoreType.DMA((WEIGHT_STEPS, 2)),
            pltpu.SemaphoreType.DMA((WEIGHT_STEPS, 1)),
        ],
        compiler_params=kernel_params(62),
        cost_estimate=cost(2 * rows * width * (kv_width + q_width), 2 * width * (kv_width + q_width)),
        name="project",
    )(
        block_split, lengths, inverse_frequencies(), tokens, norm_gain.reshape(1, width),
        key_projection, value_projection, w_query,
    )
    staged, queries = pl.pallas_call(
        stage_kernel,
        out_shape=(struct((rows, kv_width), bf16), struct((rows, q_width), bf16)),
        in_specs=in_vmem(1),
        out_specs=tuple(in_vmem(2)),
        compiler_params=kernel_params(24),
        cost_estimate=cost(0, 0),
        name="stage",
    )(both)
    far_queries = swap(queries, n, 1)

    def attend(pieces, side=None):
        arrays = operands(pieces)
        taken = rows if side is None else half
        mine, stats, packed = pl.pallas_call(
            functools.partial(attend_kernel, pieces, side),
            out_shape=(
                struct((taken, q_width), f32),
                struct((taken, HEAD), f32),
                struct((taken, q_width + HEAD), bf16),
            ),
            in_specs=in_smem(2) + in_vmem(2 + len(arrays)),
            out_specs=tuple(in_vmem(3)),
            compiler_params=kernel_params(32),
            cost_estimate=cost(0, 0),
            name="attend",
        )(block_split, lengths, queries, far_queries, *arrays)
        return [mine, stats, swap(packed, n, 1)]

    def place_pages(pieces):
        arrays = operands(pieces)
        shape = (2 * rows // PAGE, 2, PAGE, kv_width // 2)
        return pl.pallas_call(
            functools.partial(cache_kernel, pieces),
            out_shape=(struct(shape, bf16),) * 2,
            in_specs=in_smem(2) + in_vmem(len(arrays)),
            out_specs=tuple(in_vmem(2)),
            compiler_params=kernel_params(32),
            cost_estimate=cost(0, 0),
            name="cache",
        )(block_split, page_slot, *arrays)

    if n == 16:

        def swapped(piece, bits):
            source = lambda shard, i: piece.source_of(shard ^ bits, i)
            return Piece([swap(piece.arrays[0], n, bits)], source)

        own = Piece([kv], at_distance(0))
        second, first, beside = swapped(own, 8), swapped(own, 4), swapped(own, 2)
        first_across = swapped(first, 2)
        second, staged = tied(second, staged)
        own = own.moved([staged])
        third = swapped(second, 4)
        (second, first_across, beside), _ = tied_all([second, first_across, beside], ())
        partials = attend([own, beside, first, second, first_across, third])
        queries, partials[1] = lax.optimization_barrier((queries, partials[1]))
        remaining = [swapped(second, 2), swapped(third, 2)]
        placed = [own, beside, first, second, first_across, third] + remaining
    else:
        same = [list(range(c, n, 2)) for c in range(2)]
        gathered = lax.all_gather(kv, "seq", axis=0, tiled=True, axis_index_groups=same)
        remaining = [Piece([gathered], lambda shard, i: 2 * i + shard % 2, n // 2)]
        partials, placed = [], remaining
    leaving = attend(remaining, 1)
    queries, leaving[1] = lax.optimization_barrier((queries, leaving[1]))
    staying = attend(remaining, 0)
    leaving[0], staying[1] = lax.optimization_barrier((leaving[0], staying[1]))
    sent = pl.pallas_call(
        leave_kernel,
        out_shape=struct((half, width), bf16),
        in_specs=in_vmem(4 + len(partials)),
        out_specs=in_vmem(1)[0],
        compiler_params=kernel_params(24),
        cost_estimate=cost(0, 0),
        name="leave",
    )(w_out, *partials, *leaving)
    received = lax.ppermute(sent, "req", [(i, (i + 1) % parts) for i in range(parts)])
    placed, (staging, sent) = tied_all(placed, (staying[2], sent))
    staying[2] = staging
    cache, other = place_pages(placed)
    kept = pl.pallas_call(
        keep_kernel,
        out_shape=struct((half, width), f32),
        in_specs=in_vmem(5 + len(partials)),
        out_specs=in_vmem(1)[0],
        compiler_params=kernel_params(24),
        cost_estimate=cost(0, 0),
        name="keep",
    )(w_out, tokens, *partials, *staying)
    return pl.pallas_call(
        finish_kernel,
        out_shape=(struct((half, width), bf16), struct(cache.shape, bf16)),
        in_specs=in_vmem(4),
        out_specs=tuple(in_vmem(2)),
        compiler_params=kernel_params(24),
        cost_estimate=cost(0, 0),
        name="finish",
    )(kept, received, cache, swap(other, n, 1))


def solution(mesh):
    in_specs = (
        P("seq", None),
        P(),
        P(None, "req"),
        P(None, "req"),
        P(None, "req"),
        P("req", None),
        P(),
        P(),
        P(),
    )
    out_specs = (P(("seq", "req"), None), P("seq", None, None, "req"))
    body = functools.partial(on_device, mesh.shape["seq"], mesh.shape["req"])
    return jax.shard_map(body, mesh=mesh, in_specs=in_specs, out_specs=out_specs, check_vma=False)
```

```python
import functools
import math

import jax
import jax.numpy as jnp
import numpy as np
from jax import lax
from jax.experimental import pallas as pl
from jax.experimental.pallas import tpu as pltpu
from jax.sharding import PartitionSpec as P

HEAD = 128
PAGE = 32
THETA = 1000000.0
EPS = 1e-05
MASKED = -1e30
FLOOR = -1e29
WEIGHT_STEPS = 2
MIB = 1024 * 1024
SCALE = math.log2(math.e) / math.sqrt(HEAD)

f32 = jnp.float32
bf16 = jnp.bfloat16
struct = jax.ShapeDtypeStruct


def in_vmem(count):
    return [pl.BlockSpec(memory_space=pltpu.VMEM)] * count


def in_smem(count):
    return [pl.BlockSpec(memory_space=pltpu.SMEM)] * count


def in_hbm(count):
    return [pl.BlockSpec(memory_space=pltpu.HBM)] * count


def kernel_params(mib):
    return pltpu.CompilerParams(vmem_limit_bytes=mib * MIB)


def cost(flops, moved):
    return pl.CostEstimate(flops=flops, bytes_accessed=moved, transcendentals=0)


def inverse_frequencies():
    exponent = np.arange(HEAD // 2, dtype=np.float64) * (2.0 / HEAD)
    freq = (THETA**-exponent).astype(np.float32)
    return jnp.asarray(np.concatenate([freq, freq])[None, :])


def blocks_of(block_ref, shard):
    first = block_ref[shard]
    return first, 2 * block_ref.shape[0] - 1 - first


def prompt_begin(position, len_ref):
    begin = jnp.zeros_like(position)
    start = jnp.int32(0)
    for r in range(len_ref.shape[0] - 1):
        start = start + len_ref[r]
        begin = jnp.where(position >= start, start, begin)
    return begin


def positions(blocks, half, dim, shape):
    index = lax.broadcasted_iota(jnp.int32, shape, dim)
    offset = blocks[0] * half
    for i, block in enumerate(blocks[1:], 1):
        offset = jnp.where(index >= i * half, (block - i) * half, offset)
    return index + offset


def rotate(u, cosine, signed_sine):
    return u * cosine + pltpu.roll(u, HEAD // 2, 1) * signed_sine


def weight_copies(source, scratch, sems):
    depth = scratch.shape[0] // WEIGHT_STEPS
    return [
        pltpu.make_async_copy(
            source.at[pl.ds(step * depth, depth), :], scratch.at[pl.ds(step * depth, depth), :], sems.at[step]
        )
        for step in range(WEIGHT_STEPS)
    ]


def stepped_dot(left, copies, scratch):
    depth = scratch.shape[0] // WEIGHT_STEPS
    total = None
    for step, copy in enumerate(copies):
        copy.wait()
        rows = slice(step * depth, (step + 1) * depth)
        part = jnp.dot(left[:, rows], scratch[rows, :], preferred_element_type=f32)
        total = part if total is None else total + part
    return total


def project_kernel(
    block_hbm, len_hbm, freq_hbm, tok_hbm, gain_hbm, wk_hbm, wv_hbm, wq_hbm,
    kv_hbm, both_hbm,
    block_ref, len_ref, freq_ref, tok_ref, gain_ref, k_weights, v_weights, q_weights, both_ref,
    small_sems, k_sems, v_sems, q_sems, out_sems,
):
    small = [
        pltpu.make_async_copy(source, target, small_sems.at[i])
        for i, (source, target) in enumerate(
            (
                (tok_hbm, tok_ref),
                (block_hbm, block_ref),
                (len_hbm, len_ref),
                (freq_hbm, freq_ref),
                (gain_hbm, gain_ref),
            )
        )
    ]
    k_copies = weight_copies(wk_hbm, k_weights, k_sems)
    v_copies = weight_copies(wv_hbm, v_weights, v_sems)
    q_copies = weight_copies(wq_hbm, q_weights, q_sems)
    for copy in small + k_copies + v_copies + q_copies:
        copy.start()
    rows = tok_ref.shape[0]
    key_width = wk_hbm.shape[1]
    kv_width = kv_hbm.shape[1]
    for copy in small[1:4]:
        copy.wait()
    position = positions(blocks_of(block_ref, lax.axis_index("seq")), rows // 2, 0, (rows, HEAD))
    angle = (position - prompt_begin(position, len_ref)).astype(f32) * freq_ref[...]
    cosine, sine = jnp.cos(angle), jnp.sin(angle)
    lane = lax.broadcasted_iota(jnp.int32, (rows, HEAD), 1)
    sine = jnp.where(lane < HEAD // 2, -sine, sine)
    for copy in small[:1] + small[4:]:
        copy.wait()
    wide = tok_ref[...].astype(f32)
    scale = lax.rsqrt(jnp.mean(wide * wide, -1, keepdims=True) + EPS)
    normed = (wide * scale * gain_ref[...]).astype(bf16)
    product = stepped_dot(normed, k_copies, k_weights)
    for h in range(key_width // HEAD):
        cols = slice(h * HEAD, (h + 1) * HEAD)
        both_ref[:, cols] = rotate(product[:, cols], cosine, sine).astype(bf16)
    both_ref[:, key_width:kv_width] = stepped_dot(normed, v_copies, v_weights).astype(bf16)
    kv_part = both_ref.at[:, pl.ds(0, kv_width)]
    q_part = pl.ds(kv_width, wq_hbm.shape[1])
    writes = [
        pltpu.make_async_copy(kv_part, kv_hbm, out_sems.at[0]),
        pltpu.make_async_copy(kv_part, both_hbm.at[:, pl.ds(0, kv_width)], out_sems.at[1]),
    ]
    for copy in writes:
        copy.start()
    product = stepped_dot(normed, q_copies, q_weights)
    for h in range(wq_hbm.shape[1] // HEAD):
        cols = slice(h * HEAD, (h + 1) * HEAD)
        turned = rotate(product[:, cols], cosine, sine).astype(bf16)
        both_ref[:, kv_width + h * HEAD : kv_width + (h + 1) * HEAD] = turned
    writes.append(pltpu.make_async_copy(both_ref.at[:, q_part], both_hbm.at[:, q_part], out_sems.at[2]))
    writes[2].start()
    for copy in writes:
        copy.wait()


def attend_kernel(pieces, side, key_pos_ref, q_pos_ref, q_begin_ref, q_ref, far_ref, *refs):
    pieces, refs = with_refs(pieces, refs)
    shard = lax.axis_index("seq")
    rows, q_width = q_ref.shape
    key_width = pieces[0].arrays[0].shape[1] // 2
    kv_heads = key_width // HEAD
    group = q_width // key_width
    if side is None:
        taken, first = rows, 0
        span = slice(None)
    else:
        part = lax.axis_index("req")
        taken = rows // 2
        first = pl.multiple_of((1 - part if side else part) * taken, taken)
        span = pl.ds(first, taken)
    both = 2 * taken

    def of_both_cores(ref):
        return jnp.concatenate(
            [ref[pl.ds(pl.multiple_of(core * rows + first, taken), taken), :] for core in (0, 1)], 0
        )

    q_pos, q_begin = of_both_cores(q_pos_ref), of_both_cores(q_begin_ref)
    queries = [
        jnp.concatenate(
            [
                ref[span, h * HEAD : (h + 1) * HEAD]
                for h in range(g * group, (g + 1) * group)
                for ref in (q_ref, far_ref)
            ],
            0,
        )
        for g in range(kv_heads)
    ]

    def absorb(state, blocks, sources):
        bias = []
        for source in sources:
            key_pos = key_pos_ref[pl.ds(source, 1), :]
            bias.append(jnp.where((key_pos >= q_begin) & (key_pos <= q_pos), 0.0, MASKED))
        bias = jnp.concatenate(bias, 1)
        bias = jnp.concatenate([bias] * group, 0)
        out = []
        for g in range(kv_heads):
            top, total, acc = state[g]
            keys = jnp.concatenate([b[:, g * HEAD : (g + 1) * HEAD] for b in blocks], 0)
            values = jnp.concatenate(
                [b[:, key_width + g * HEAD : key_width + (g + 1) * HEAD] for b in blocks], 0
            )
            scores = lax.dot_general(
                queries[g], keys, (((1,), (1,)), ((), ())), preferred_element_type=f32
            )
            scores = scores * SCALE + bias
            new_top = jnp.maximum(top, jnp.max(scores, -1, keepdims=True))
            weights = jnp.exp2(scores - new_top)
            factor = jnp.exp2(top - new_top)
            total = total * factor + jnp.sum(weights, -1, keepdims=True)
            acc = acc * factor + jnp.dot(weights.astype(bf16), values, preferred_element_type=f32)
            out.append((new_top, total, acc))
        return tuple(out)

    state = (
        (
            jnp.full((group * both, 1), FLOOR, f32),
            jnp.zeros((group * both, 1), f32),
            jnp.zeros((group * both, HEAD), f32),
        ),
    ) * kv_heads
    if all(piece.count == 1 for piece in pieces):
        for i in range(0, len(pieces), 2):
            pair = pieces[i : i + 2]
            state = absorb(
                state, [p.arrays[0][...] for p in pair], [p.source_of(shard, 0) for p in pair]
            )
    else:
        for piece in pieces:

            def step(i, carried):
                at = pl.multiple_of(i * rows, rows)
                block = piece.arrays[0][pl.ds(at, rows), :]
                return absorb(carried, [block], [piece.source_of(shard, i)])

            state = lax.fori_loop(0, piece.count, step, state)

    mine_ref, stat_ref, packed_ref = refs
    heads = q_width // HEAD
    lane = lax.broadcasted_iota(jnp.int32, (taken, HEAD), 1)
    mine = jnp.zeros((taken, HEAD), f32)
    theirs = jnp.zeros((taken, HEAD), f32)
    for g in range(kv_heads):
        top, total, acc = state[g]
        for j in range(group):
            h = g * group + j
            cols = slice(h * HEAD, (h + 1) * HEAD)
            near = slice(j * both, j * both + taken)
            far = slice(j * both + taken, (j + 1) * both)
            mine_ref[:, cols] = acc[near]
            packed_ref[:, cols] = acc[far].astype(bf16)
            for value, at in ((top, h), (total, heads + h)):
                mine = jnp.where(lane == at, value[near], mine)
                theirs = jnp.where(lane % (2 * heads) == at, value[far], theirs)
    stat_ref[...] = mine
    high = theirs.astype(bf16).astype(f32)
    middle = (theirs - high).astype(bf16).astype(f32)
    low = theirs - high - middle
    third = lane // (2 * heads)
    parts = jnp.where(third == 0, high, jnp.where(third == 1, middle, low))
    packed_ref[:, q_width:] = parts.astype(bf16)


def stage_kernel(block_ref, len_ref, both_ref, kv_out, q_out, key_pos_ref, q_pos_ref, q_begin_ref):
    kv_out[...] = both_ref[:, : kv_out.shape[1]]
    q_out[...] = both_ref[:, kv_out.shape[1] :]
    shards, rows = key_pos_ref.shape
    shard = lax.axis_index("seq")

    def lay(s, carry):
        key_pos_ref[pl.ds(s, 1), :] = positions(blocks_of(block_ref, s), rows // 2, 1, (1, rows))
        return carry

    lax.fori_loop(0, shards, lay, 0, unroll=shards <= 16)
    blocks = [block for s in (shard, shard ^ 1) for block in blocks_of(block_ref, s)]
    q_pos = positions(blocks, rows // 2, 0, q_pos_ref.shape)
    q_pos_ref[...] = q_pos
    q_begin_ref[...] = prompt_begin(q_pos, len_ref)


def joined_rows(partials, first, half):
    q_width = partials[0].shape[1]
    heads = q_width // HEAD
    part = pl.ds(pl.multiple_of(first, half), half)
    held = []
    for mine_ref, stat_ref, packed_ref in zip(partials[::3], partials[1::3], partials[2::3]):
        span = slice(None) if mine_ref.shape[0] == half else part
        parts = packed_ref[span, q_width:].astype(f32)
        stats = parts
        for t in (1, 2):
            stats = stats + pltpu.roll(parts, HEAD - 2 * heads * t, 1)
        held += [(mine_ref, span, stat_ref[span, :]), (packed_ref, span, stats)]
    top = functools.reduce(jnp.maximum, [stats for _, _, stats in held])
    shares = [jnp.exp2(stats - top) for _, _, stats in held]
    total = sum(
        share * pltpu.roll(stats, HEAD - heads, 1) for share, (_, _, stats) in zip(shares, held)
    )
    shares = [share / total for share in shares]
    context = []
    for h in range(heads):
        cols = slice(h * HEAD, (h + 1) * HEAD)
        context.append(
            sum(
                ref[span, cols].astype(f32) * share[:, h : h + 1]
                for (ref, span, _), share in zip(held, shares)
            ).astype(bf16)
        )
    return jnp.concatenate(context, 1)


def leave_kernel(wo_ref, *refs):
    partials, sent_ref = refs[:-1], refs[-1]
    half = sent_ref.shape[0]
    context = joined_rows(partials, (1 - lax.axis_index("req")) * half, half)
    sent_ref[...] = jnp.dot(context, wo_ref[...], preferred_element_type=f32).astype(bf16)


def keep_kernel(wo_ref, tok_ref, *refs):
    partials, out_ref = refs[:-1], refs[-1]
    half = out_ref.shape[0]
    first = lax.axis_index("req") * half
    context = joined_rows(partials, first, half)
    residual = tok_ref[pl.ds(pl.multiple_of(first, half), half), :].astype(f32)
    out_ref[...] = jnp.dot(context, wo_ref[...], preferred_element_type=f32) + residual


def finish_kernel(kept_ref, received_ref, mine_ref, other_ref, hidden_ref, cache_ref):
    hidden_ref[...] = (kept_ref[...] + received_ref[...].astype(f32)).astype(bf16)
    cache_ref[...] = mine_ref[...] + other_ref[...]


def cache_kernel(pieces, block_ref, slot_ref, *refs):
    pieces, (mine_ref, other_ref) = with_refs(pieces, refs)
    shard = lax.axis_index("seq")
    slots = mine_ref.shape[0]
    key_width = mine_ref.shape[3]
    rows = slots * PAGE // 2
    pages = rows // 2 // PAGE
    for target in (mine_ref, other_ref):
        target[...] = jnp.zeros_like(target)

    def place(ref, at, source):
        for k, block in enumerate(blocks_of(block_ref, source)):
            for j in range(pages):
                slot = slot_ref[block * pages + j]
                holder = slot // slots
                local = slot - holder * slots
                offset = at + (k * pages + j) * PAGE
                if not isinstance(offset, int):
                    offset = pl.multiple_of(offset, PAGE)
                for target, owner in ((mine_ref, shard), (other_ref, shard ^ 1)):

                    @pl.when(holder == owner)
                    def _():
                        target[local, 0] = ref[pl.ds(offset, PAGE), :key_width]
                        target[local, 1] = ref[pl.ds(offset, PAGE), key_width:]

    for piece in pieces:
        if piece.count == 1:
            place(piece.arrays[0], 0, piece.source_of(shard, 0))
        else:

            def step(i, carry):
                place(piece.arrays[0], i * rows, piece.source_of(shard, i))
                return carry

            lax.fori_loop(0, piece.count, step, 0)


def tied_all(pieces, other):
    arrays, other = lax.optimization_barrier((operands(pieces), other))
    return with_refs(pieces, arrays)[0], other


def tied(piece, other):
    (piece,), other = tied_all([piece], other)
    return piece, other


def swap(x, n, bit):
    return lax.ppermute(x, "seq", [(i, i ^ bit) for i in range(n)])


class Piece:
    def __init__(self, arrays, source_of, count=1):
        self.arrays, self.source_of, self.count = arrays, source_of, count

    def moved(self, arrays):
        return Piece(arrays, self.source_of, self.count)


def operands(pieces):
    return [x for piece in pieces for x in piece.arrays]


def with_refs(pieces, refs):
    out = []
    for piece in pieces:
        taken, refs = refs[: len(piece.arrays)], refs[len(piece.arrays) :]
        out.append(piece.moved(taken))
    return out, refs


def at_distance(bits):
    return lambda shard, i: shard ^ bits


def move(x, pairs):
    return lax.ppermute(x, "seq", pairs)


def on_device(
    n, parts, tokens, norm_gain, w_query, key_projection, value_projection, w_out, lengths, block_split, page_slot,
):
    rows, width = tokens.shape
    half = rows // 2
    q_width = w_query.shape[1]
    kv_width = key_projection.shape[1] + value_projection.shape[1]
    kv, both = pl.pallas_call(
        project_kernel,
        out_shape=(struct((rows, kv_width), bf16), struct((rows, kv_width + q_width), bf16)),
        in_specs=in_hbm(8),
        out_specs=tuple(in_hbm(2)),
        scratch_shapes=[
            pltpu.SMEM(block_split.shape, jnp.int32),
            pltpu.SMEM(lengths.shape, jnp.int32),
            pltpu.VMEM((1, HEAD), f32),
            pltpu.VMEM((rows, width), bf16),
            pltpu.VMEM((1, width), f32),
            pltpu.VMEM(key_projection.shape, bf16),
            pltpu.VMEM(value_projection.shape, bf16),
            pltpu.VMEM((width, q_width), bf16),
            pltpu.VMEM((rows, kv_width + q_width), bf16),
            pltpu.SemaphoreType.DMA((5,)),
            pltpu.SemaphoreType.DMA((WEIGHT_STEPS,)),
            pltpu.SemaphoreType.DMA((WEIGHT_STEPS,)),
            pltpu.SemaphoreType.DMA((WEIGHT_STEPS,)),
            pltpu.SemaphoreType.DMA((3,)),
        ],
        compiler_params=kernel_params(62),
        cost_estimate=cost(2 * rows * width * (kv_width + q_width), 2 * width * (kv_width + q_width)),
        name="project",
    )(
        block_split, lengths, inverse_frequencies(), tokens, norm_gain.reshape(1, width),
        key_projection, value_projection, w_query,
    )
    staged, queries, *places = pl.pallas_call(
        stage_kernel,
        out_shape=(
            struct((rows, kv_width), bf16),
            struct((rows, q_width), bf16),
            struct((n, rows), jnp.int32),
            struct((2 * rows, HEAD), jnp.int32),
            struct((2 * rows, HEAD), jnp.int32),
        ),
        in_specs=in_smem(2) + in_vmem(1),
        out_specs=tuple(in_vmem(5)),
        compiler_params=kernel_params(24),
        cost_estimate=cost(0, 0),
        name="stage",
    )(block_split, lengths, both)
    far_queries = swap(queries, n, 1)

    def attend(pieces, side=None):
        arrays = operands(pieces)
        taken = rows if side is None else half
        mine, stats, packed = pl.pallas_call(
            functools.partial(attend_kernel, pieces, side),
            out_shape=(
                struct((taken, q_width), f32),
                struct((taken, HEAD), f32),
                struct((taken, q_width + HEAD), bf16),
            ),
            in_specs=in_vmem(5 + len(arrays)),
            out_specs=tuple(in_vmem(3)),
            compiler_params=kernel_params(32),
            cost_estimate=cost(0, 0),
            name="attend",
        )(*places, queries, far_queries, *arrays)
        return [mine, stats, packed]

    def place_pages(pieces):
        arrays = operands(pieces)
        shape = (2 * rows // PAGE, 2, PAGE, kv_width // 2)
        return pl.pallas_call(
            functools.partial(cache_kernel, pieces),
            out_shape=(struct(shape, bf16),) * 2,
            in_specs=in_smem(2) + in_vmem(len(arrays)),
            out_specs=tuple(in_vmem(2)),
            compiler_params=kernel_params(32),
            cost_estimate=cost(0, 0),
            name="cache",
        )(block_split, page_slot, *arrays)

    if n == 16:

        def swapped(piece, bits):
            source = lambda shard, i: piece.source_of(shard ^ bits, i)
            return Piece([swap(piece.arrays[0], n, bits)], source)

        own = Piece([kv], at_distance(0))
        second, first, beside = swapped(own, 8), swapped(own, 4), swapped(own, 2)
        first_across = swapped(first, 2)
        second, staged = tied(second, staged)
        own = own.moved([staged])
        third = swapped(second, 4)
        (second, first_across, beside), _ = tied_all([second, first_across, beside], ())
        partials = attend([own, beside, first, second, first_across, third])
        partials[2] = swap(partials[2], n, 1)
        queries, partials[1] = lax.optimization_barrier((queries, partials[1]))
        remaining = [swapped(second, 2), swapped(third, 2)]
        placed = [own, beside, first, second, first_across, third] + remaining
    else:
        same = [list(range(c, n, 2)) for c in range(2)]
        gathered = lax.all_gather(kv, "seq", axis=0, tiled=True, axis_index_groups=same)
        remaining = [Piece([gathered], lambda shard, i: 2 * i + shard % 2, n // 2)]
        partials, placed = [], remaining
    leaving = attend(remaining, 1)
    queries, leaving[1] = lax.optimization_barrier((queries, leaving[1]))
    leaving[2] = swap(leaving[2], n, 1)
    staying = attend(remaining, 0)
    leaving[0], staying[1] = lax.optimization_barrier((leaving[0], staying[1]))
    sent = pl.pallas_call(
        leave_kernel,
        out_shape=struct((half, width), bf16),
        in_specs=in_vmem(4 + len(partials)),
        out_specs=in_vmem(1)[0],
        compiler_params=kernel_params(24),
        cost_estimate=cost(0, 0),
        name="leave",
    )(w_out, *partials, *leaving)
    received = lax.ppermute(sent, "req", [(i, (i + 1) % parts) for i in range(parts)])
    staying[2] = swap(staying[2], n, 1)
    placed, (staying[2], sent) = tied_all(placed, (staying[2], sent))
    cache, other = place_pages(placed)
    kept = pl.pallas_call(
        keep_kernel,
        out_shape=struct((half, width), f32),
        in_specs=in_vmem(5 + len(partials)),
        out_specs=in_vmem(1)[0],
        compiler_params=kernel_params(24),
        cost_estimate=cost(0, 0),
        name="keep",
    )(w_out, tokens, *partials, *staying)
    return pl.pallas_call(
        finish_kernel,
        out_shape=(struct((half, width), bf16), struct(cache.shape, bf16)),
        in_specs=in_vmem(4),
        out_specs=tuple(in_vmem(2)),
        compiler_params=kernel_params(24),
        cost_estimate=cost(0, 0),
        name="finish",
    )(kept, received, cache, swap(other, n, 1))


def solution(mesh):
    in_specs = (
        P("seq", None),
        P(),
        P(None, "req"),
        P(None, "req"),
        P(None, "req"),
        P("req", None),
        P(),
        P(),
        P(),
    )
    out_specs = (P(("seq", "req"), None), P("seq", None, None, "req"))
    body = functools.partial(on_device, mesh.shape["seq"], mesh.shape["req"])
    return jax.shard_map(body, mesh=mesh, in_specs=in_specs, out_specs=out_specs, check_vma=False)
```

```python
import functools
import math

import jax
import jax.numpy as jnp
import numpy as np
from jax import lax
from jax.experimental import pallas as pl
from jax.experimental.pallas import tpu as pltpu
from jax.sharding import PartitionSpec as P

HEAD = 128
PAGE = 32
THETA = 1000000.0
EPS = 1e-05
MASKED = -1e30
FLOOR = -1e29
WEIGHT_STEPS = 2
MIB = 1024 * 1024
SCALE = math.log2(math.e) / math.sqrt(HEAD)

f32 = jnp.float32
bf16 = jnp.bfloat16
struct = jax.ShapeDtypeStruct


def in_vmem(count):
    return [pl.BlockSpec(memory_space=pltpu.VMEM)] * count


def in_smem(count):
    return [pl.BlockSpec(memory_space=pltpu.SMEM)] * count


def in_hbm(count):
    return [pl.BlockSpec(memory_space=pltpu.HBM)] * count


def kernel_params(mib):
    return pltpu.CompilerParams(vmem_limit_bytes=mib * MIB)


def cost(flops, moved):
    return pl.CostEstimate(flops=flops, bytes_accessed=moved, transcendentals=0)


def rotary_constants(half):
    exponent = np.arange(HEAD // 2, dtype=np.float64) * (2.0 / HEAD)
    freq = np.tile(THETA**-exponent, 2)[None, :]
    angle = np.arange(half, dtype=np.float64)[:, None] * freq
    rows = [np.cos(angle), np.sin(angle), np.broadcast_to(freq, (8, HEAD))]
    return jnp.asarray(np.concatenate(rows).astype(np.float32))


def blocks_of(block_ref, shard):
    first = block_ref[shard]
    return first, 2 * block_ref.shape[0] - 1 - first


def prompt_begin(position, len_ref):
    begin = jnp.zeros_like(position)
    start = jnp.int32(0)
    for r in range(len_ref.shape[0] - 1):
        start = start + len_ref[r]
        begin = jnp.where(position >= start, start, begin)
    return begin


def positions(blocks, half, dim, shape):
    index = lax.broadcasted_iota(jnp.int32, shape, dim)
    offset = blocks[0] * half
    for i, block in enumerate(blocks[1:], 1):
        offset = jnp.where(index >= i * half, (block - i) * half, offset)
    return index + offset


def rotate(u, cosine, signed_sine):
    return u * cosine + pltpu.roll(u, HEAD // 2, 1) * signed_sine


def weight_copies(source, scratch, sems):
    depth = scratch.shape[0] // WEIGHT_STEPS
    return [
        pltpu.make_async_copy(
            source.at[pl.ds(step * depth, depth), :], scratch.at[pl.ds(step * depth, depth), :], sems.at[step]
        )
        for step in range(WEIGHT_STEPS)
    ]


def stepped_dot(left, copies, scratch):
    depth = scratch.shape[0] // WEIGHT_STEPS
    total = None
    for step, copy in enumerate(copies):
        copy.wait()
        rows = slice(step * depth, (step + 1) * depth)
        part = jnp.dot(left[:, rows], scratch[rows, :], preferred_element_type=f32)
        total = part if total is None else total + part
    return total


def rotary_tables(block_ref, len_ref, turn_ref, half):
    prompts = len_ref.shape[0]
    blocks = blocks_of(block_ref, lax.axis_index("seq"))
    starts = [jnp.int32(0)]
    for r in range(prompts - 1):
        starts.append(starts[-1] + len_ref[r])
    count = 2 * prompts
    index = lax.broadcasted_iota(jnp.int32, (count, HEAD), 0)
    base = jnp.zeros((count, HEAD), jnp.int32)
    for k, block in enumerate(blocks):
        for p, start in enumerate(starts):
            base = jnp.where(index == k * prompts + p, block * half - start, base)
    angle = base.astype(f32) * turn_ref[2 * half : 2 * half + 1, :]
    base_cos, base_sin = jnp.cos(angle), jnp.sin(angle)
    row_cos, row_sin = turn_ref[:half, :], turn_ref[half : 2 * half, :]
    row = lax.broadcasted_iota(jnp.int32, (half, HEAD), 0)
    lane = lax.broadcasted_iota(jnp.int32, (half, HEAD), 1)
    cosines, sines = [], []
    for k, block in enumerate(blocks):
        at = k * prompts
        cos, sin = base_cos[at : at + 1], base_sin[at : at + 1]
        for p in range(1, prompts):
            inside = row >= starts[p] - block * half
            cos = jnp.where(inside, base_cos[at + p : at + p + 1], cos)
            sin = jnp.where(inside, base_sin[at + p : at + p + 1], sin)
        cosines.append(row_cos * cos - row_sin * sin)
        sine = row_sin * cos + row_cos * sin
        sines.append(jnp.where(lane < HEAD // 2, -sine, sine))
    return jnp.concatenate(cosines, 0), jnp.concatenate(sines, 0)


def project_kernel(
    block_hbm, len_hbm, turn_hbm, tok_hbm, gain_hbm, wk_hbm, wv_hbm, wq_hbm,
    kv_hbm, both_hbm,
    block_ref, len_ref, turn_ref, tok_ref, gain_ref, k_weights, v_weights, q_weights, both_ref,
    small_sems, k_sems, v_sems, q_sems, out_sems,
):
    small = [
        pltpu.make_async_copy(source, target, small_sems.at[i])
        for i, (source, target) in enumerate(
            (
                (tok_hbm, tok_ref),
                (block_hbm, block_ref),
                (len_hbm, len_ref),
                (turn_hbm, turn_ref),
                (gain_hbm, gain_ref),
            )
        )
    ]
    k_copies = weight_copies(wk_hbm, k_weights, k_sems)
    v_copies = weight_copies(wv_hbm, v_weights, v_sems)
    q_copies = weight_copies(wq_hbm, q_weights, q_sems)
    for copy in small + k_copies + v_copies + q_copies:
        copy.start()
    rows = tok_ref.shape[0]
    key_width = wk_hbm.shape[1]
    kv_width = kv_hbm.shape[1]
    for copy in small:
        copy.wait()
    wide = tok_ref[...].astype(f32)
    scale = lax.rsqrt(jnp.mean(wide * wide, -1, keepdims=True) + EPS)
    normed = (wide * scale * gain_ref[...]).astype(bf16)
    cosine, sine = rotary_tables(block_ref, len_ref, turn_ref, rows // 2)
    product = stepped_dot(normed, k_copies, k_weights)
    for h in range(key_width // HEAD):
        cols = slice(h * HEAD, (h + 1) * HEAD)
        both_ref[:, cols] = rotate(product[:, cols], cosine, sine).astype(bf16)
    both_ref[:, key_width:kv_width] = stepped_dot(normed, v_copies, v_weights).astype(bf16)
    kv_part = both_ref.at[:, pl.ds(0, kv_width)]
    q_part = pl.ds(kv_width, wq_hbm.shape[1])
    writes = [
        pltpu.make_async_copy(kv_part, kv_hbm, out_sems.at[0]),
        pltpu.make_async_copy(kv_part, both_hbm.at[:, pl.ds(0, kv_width)], out_sems.at[1]),
    ]
    for copy in writes:
        copy.start()
    product = stepped_dot(normed, q_copies, q_weights)
    for h in range(wq_hbm.shape[1] // HEAD):
        cols = slice(h * HEAD, (h + 1) * HEAD)
        turned = rotate(product[:, cols], cosine, sine).astype(bf16)
        both_ref[:, kv_width + h * HEAD : kv_width + (h + 1) * HEAD] = turned
    writes.append(pltpu.make_async_copy(both_ref.at[:, q_part], both_hbm.at[:, q_part], out_sems.at[2]))
    writes[2].start()
    for copy in writes:
        copy.wait()


def attend_kernel(pieces, side, key_pos_ref, q_pos_ref, q_begin_ref, q_ref, far_ref, *refs):
    pieces, refs = with_refs(pieces, refs)
    shard = lax.axis_index("seq")
    rows, q_width = q_ref.shape
    key_width = pieces[0].arrays[0].shape[1] // 2
    kv_heads = key_width // HEAD
    group = q_width // key_width
    if side is None:
        taken, first = rows, 0
        span = slice(None)
    else:
        part = lax.axis_index("req")
        taken = rows // 2
        first = pl.multiple_of((1 - part if side else part) * taken, taken)
        span = pl.ds(first, taken)
    both = 2 * taken

    def of_both_cores(ref):
        return jnp.concatenate(
            [ref[pl.ds(pl.multiple_of(core * rows + first, taken), taken), :] for core in (0, 1)], 0
        )

    q_pos, q_begin = of_both_cores(q_pos_ref), of_both_cores(q_begin_ref)
    queries = [
        jnp.concatenate(
            [
                ref[span, h * HEAD : (h + 1) * HEAD]
                for h in range(g * group, (g + 1) * group)
                for ref in (q_ref, far_ref)
            ],
            0,
        )
        for g in range(kv_heads)
    ]

    def absorb(state, blocks, sources):
        bias = []
        for source in sources:
            key_pos = key_pos_ref[pl.ds(source, 1), :]
            bias.append(jnp.where((key_pos >= q_begin) & (key_pos <= q_pos), 0.0, MASKED))
        bias = jnp.concatenate(bias, 1)
        bias = jnp.concatenate([bias] * group, 0)
        out = []
        for g in range(kv_heads):
            top, total, acc = state[g]
            keys = jnp.concatenate([b[:, g * HEAD : (g + 1) * HEAD] for b in blocks], 0)
            values = jnp.concatenate(
                [b[:, key_width + g * HEAD : key_width + (g + 1) * HEAD] for b in blocks], 0
            )
            scores = lax.dot_general(
                queries[g], keys, (((1,), (1,)), ((), ())), preferred_element_type=f32
            )
            scores = scores * SCALE + bias
            new_top = jnp.maximum(top, jnp.max(scores, -1, keepdims=True))
            weights = jnp.exp2(scores - new_top)
            factor = jnp.exp2(top - new_top)
            total = total * factor + jnp.sum(weights, -1, keepdims=True)
            acc = acc * factor + jnp.dot(weights.astype(bf16), values, preferred_element_type=f32)
            out.append((new_top, total, acc))
        return tuple(out)

    state = (
        (
            jnp.full((group * both, 1), FLOOR, f32),
            jnp.zeros((group * both, 1), f32),
            jnp.zeros((group * both, HEAD), f32),
        ),
    ) * kv_heads
    if all(piece.count == 1 for piece in pieces):
        for i in range(0, len(pieces), 2):
            pair = pieces[i : i + 2]
            state = absorb(
                state, [p.arrays[0][...] for p in pair], [p.source_of(shard, 0) for p in pair]
            )
    else:
        for piece in pieces:

            def step(i, carried):
                at = pl.multiple_of(i * rows, rows)
                block = piece.arrays[0][pl.ds(at, rows), :]
                return absorb(carried, [block], [piece.source_of(shard, i)])

            state = lax.fori_loop(0, piece.count, step, state)

    mine_ref, stat_ref, packed_ref = refs
    heads = q_width // HEAD
    lane = lax.broadcasted_iota(jnp.int32, (taken, HEAD), 1)
    mine = jnp.zeros((taken, HEAD), f32)
    theirs = jnp.zeros((taken, HEAD), f32)
    for g in range(kv_heads):
        top, total, acc = state[g]
        for j in range(group):
            h = g * group + j
            cols = slice(h * HEAD, (h + 1) * HEAD)
            near = slice(j * both, j * both + taken)
            far = slice(j * both + taken, (j + 1) * both)
            mine_ref[:, cols] = acc[near]
            packed_ref[:, cols] = acc[far].astype(bf16)
            for value, at in ((top, h), (total, heads + h)):
                mine = jnp.where(lane == at, value[near], mine)
                theirs = jnp.where(lane % (2 * heads) == at, value[far], theirs)
    stat_ref[...] = mine
    high = theirs.astype(bf16).astype(f32)
    middle = (theirs - high).astype(bf16).astype(f32)
    low = theirs - high - middle
    third = lane // (2 * heads)
    parts = jnp.where(third == 0, high, jnp.where(third == 1, middle, low))
    packed_ref[:, q_width:] = parts.astype(bf16)


def stage_kernel(block_ref, len_ref, both_ref, kv_out, q_out, key_pos_ref, q_pos_ref, q_begin_ref):
    kv_out[...] = both_ref[:, : kv_out.shape[1]]
    q_out[...] = both_ref[:, kv_out.shape[1] :]
    shards, rows = key_pos_ref.shape
    shard = lax.axis_index("seq")

    def lay(s, carry):
        key_pos_ref[pl.ds(s, 1), :] = positions(blocks_of(block_ref, s), rows // 2, 1, (1, rows))
        return carry

    lax.fori_loop(0, shards, lay, 0, unroll=shards <= 16)
    blocks = [block for s in (shard, shard ^ 1) for block in blocks_of(block_ref, s)]
    q_pos = positions(blocks, rows // 2, 0, q_pos_ref.shape)
    q_pos_ref[...] = q_pos
    q_begin_ref[...] = prompt_begin(q_pos, len_ref)


def joined_rows(partials, first, half):
    q_width = partials[0].shape[1]
    heads = q_width // HEAD
    part = pl.ds(pl.multiple_of(first, half), half)
    held = []
    for mine_ref, stat_ref, packed_ref in zip(partials[::3], partials[1::3], partials[2::3]):
        span = slice(None) if mine_ref.shape[0] == half else part
        parts = packed_ref[span, q_width:].astype(f32)
        stats = parts
        for t in (1, 2):
            stats = stats + pltpu.roll(parts, HEAD - 2 * heads * t, 1)
        held += [(mine_ref, span, stat_ref[span, :]), (packed_ref, span, stats)]
    top = functools.reduce(jnp.maximum, [stats for _, _, stats in held])
    shares = [jnp.exp2(stats - top) for _, _, stats in held]
    total = sum(
        share * pltpu.roll(stats, HEAD - heads, 1) for share, (_, _, stats) in zip(shares, held)
    )
    shares = [share / total for share in shares]
    context = []
    for h in range(heads):
        cols = slice(h * HEAD, (h + 1) * HEAD)
        context.append(
            sum(
                ref[span, cols].astype(f32) * share[:, h : h + 1]
                for (ref, span, _), share in zip(held, shares)
            ).astype(bf16)
        )
    return jnp.concatenate(context, 1)


def leave_kernel(wo_ref, *refs):
    partials, sent_ref = refs[:-1], refs[-1]
    half = sent_ref.shape[0]
    context = joined_rows(partials, (1 - lax.axis_index("req")) * half, half)
    sent_ref[...] = jnp.dot(context, wo_ref[...], preferred_element_type=f32).astype(bf16)


def keep_kernel(wo_ref, tok_ref, mine_ref, *refs):
    others, partials, (out_ref, cache_ref) = refs[:2], refs[2:-2], refs[-2:]
    share = mine_ref.shape[0] // 2
    for i, other_ref in enumerate(others):
        part = slice(i * share, (i + 1) * share)
        cache_ref[part] = mine_ref[part] + other_ref[...]
    half = out_ref.shape[0]
    first = lax.axis_index("req") * half
    context = joined_rows(partials, first, half)
    residual = tok_ref[pl.ds(pl.multiple_of(first, half), half), :].astype(f32)
    out_ref[...] = jnp.dot(context, wo_ref[...], preferred_element_type=f32) + residual


def finish_kernel(kept_ref, received_ref, hidden_ref):
    hidden_ref[...] = (kept_ref[...] + received_ref[...].astype(f32)).astype(bf16)


def cache_kernel(pieces, block_ref, slot_ref, *refs):
    pieces, (mine_ref, *other_refs) = with_refs(pieces, refs)
    shard = lax.axis_index("seq")
    slots = mine_ref.shape[0]
    key_width = mine_ref.shape[3]
    rows = slots * PAGE // 2
    pages = rows // 2 // PAGE
    for target in (mine_ref, *other_refs):
        target[...] = jnp.zeros_like(target)
    share = slots // len(other_refs)

    def place(ref, at, source):
        for k, block in enumerate(blocks_of(block_ref, source)):
            for j in range(pages):
                slot = slot_ref[block * pages + j]
                holder = slot // slots
                local = slot - holder * slots
                offset = at + (k * pages + j) * PAGE
                if not isinstance(offset, int):
                    offset = pl.multiple_of(offset, PAGE)

                def write(target, at_slot):
                    target[at_slot, 0] = ref[pl.ds(offset, PAGE), :key_width]
                    target[at_slot, 1] = ref[pl.ds(offset, PAGE), key_width:]

                @pl.when(holder == shard)
                def _():
                    write(mine_ref, local)

                for i, target in enumerate(other_refs):

                    @pl.when((holder == shard ^ 1) & (local // share == i))
                    def _():
                        write(target, local - i * share)

    for piece in pieces:
        if piece.count == 1:
            place(piece.arrays[0], 0, piece.source_of(shard, 0))
        else:

            def step(i, carry):
                place(piece.arrays[0], i * rows, piece.source_of(shard, i))
                return carry

            lax.fori_loop(0, piece.count, step, 0)


def tied_all(pieces, other):
    arrays, other = lax.optimization_barrier((operands(pieces), other))
    return with_refs(pieces, arrays)[0], other


def tied(piece, other):
    (piece,), other = tied_all([piece], other)
    return piece, other


def swap(x, n, bit):
    return lax.ppermute(x, "seq", [(i, i ^ bit) for i in range(n)])


class Piece:
    def __init__(self, arrays, source_of, count=1):
        self.arrays, self.source_of, self.count = arrays, source_of, count

    def moved(self, arrays):
        return Piece(arrays, self.source_of, self.count)


def operands(pieces):
    return [x for piece in pieces for x in piece.arrays]


def with_refs(pieces, refs):
    out = []
    for piece in pieces:
        taken, refs = refs[: len(piece.arrays)], refs[len(piece.arrays) :]
        out.append(piece.moved(taken))
    return out, refs


def at_distance(bits):
    return lambda shard, i: shard ^ bits


def move(x, pairs):
    return lax.ppermute(x, "seq", pairs)


def on_device(
    n, parts, tokens, norm_gain, w_query, key_projection, value_projection, w_out, lengths, block_split, page_slot,
):
    rows, width = tokens.shape
    half = rows // 2
    q_width = w_query.shape[1]
    kv_width = key_projection.shape[1] + value_projection.shape[1]
    kv, both = pl.pallas_call(
        project_kernel,
        out_shape=(struct((rows, kv_width), bf16), struct((rows, kv_width + q_width), bf16)),
        in_specs=in_hbm(8),
        out_specs=tuple(in_hbm(2)),
        scratch_shapes=[
            pltpu.SMEM(block_split.shape, jnp.int32),
            pltpu.SMEM(lengths.shape, jnp.int32),
            pltpu.VMEM((2 * half + 8, HEAD), f32),
            pltpu.VMEM((rows, width), bf16),
            pltpu.VMEM((1, width), f32),
            pltpu.VMEM(key_projection.shape, bf16),
            pltpu.VMEM(value_projection.shape, bf16),
            pltpu.VMEM((width, q_width), bf16),
            pltpu.VMEM((rows, kv_width + q_width), bf16),
            pltpu.SemaphoreType.DMA((5,)),
            pltpu.SemaphoreType.DMA((WEIGHT_STEPS,)),
            pltpu.SemaphoreType.DMA((WEIGHT_STEPS,)),
            pltpu.SemaphoreType.DMA((WEIGHT_STEPS,)),
            pltpu.SemaphoreType.DMA((3,)),
        ],
        compiler_params=kernel_params(62),
        cost_estimate=cost(2 * rows * width * (kv_width + q_width), 2 * width * (kv_width + q_width)),
        name="project",
    )(
        block_split, lengths, rotary_constants(half), tokens, norm_gain.reshape(1, width),
        key_projection, value_projection, w_query,
    )
    staged, queries, *places = pl.pallas_call(
        stage_kernel,
        out_shape=(
            struct((rows, kv_width), bf16),
            struct((rows, q_width), bf16),
            struct((n, rows), jnp.int32),
            struct((2 * rows, HEAD), jnp.int32),
            struct((2 * rows, HEAD), jnp.int32),
        ),
        in_specs=in_smem(2) + in_vmem(1),
        out_specs=tuple(in_vmem(5)),
        compiler_params=kernel_params(24),
        cost_estimate=cost(0, 0),
        name="stage",
    )(block_split, lengths, both)
    far_queries = swap(queries, n, 1)

    def attend(pieces, side=None):
        arrays = operands(pieces)
        taken = rows if side is None else half
        mine, stats, packed = pl.pallas_call(
            functools.partial(attend_kernel, pieces, side),
            out_shape=(
                struct((taken, q_width), f32),
                struct((taken, HEAD), f32),
                struct((taken, q_width + HEAD), bf16),
            ),
            in_specs=in_vmem(5 + len(arrays)),
            out_specs=tuple(in_vmem(3)),
            compiler_params=kernel_params(32),
            cost_estimate=cost(0, 0),
            name="attend",
        )(*places, queries, far_queries, *arrays)
        return [mine, stats, packed]

    def place_pages(pieces):
        arrays = operands(pieces)
        shape = (2 * rows // PAGE, 2, PAGE, kv_width // 2)
        return pl.pallas_call(
            functools.partial(cache_kernel, pieces),
            out_shape=(struct(shape, bf16),) + (struct((shape[0] // 2,) + shape[1:], bf16),) * 2,
            in_specs=in_smem(2) + in_vmem(len(arrays)),
            out_specs=tuple(in_vmem(1 + 2)),
            compiler_params=kernel_params(32),
            cost_estimate=cost(0, 0),
            name="cache",
        )(block_split, page_slot, *arrays)

    if n == 16:

        def swapped(piece, bits):
            source = lambda shard, i: piece.source_of(shard ^ bits, i)
            return Piece([swap(piece.arrays[0], n, bits)], source)

        own = Piece([kv], at_distance(0))
        second, first, beside = swapped(own, 8), swapped(own, 4), swapped(own, 2)
        first_across = swapped(first, 2)
        second, staged = tied(second, staged)
        own = own.moved([staged])
        third = swapped(second, 4)
        (second, first_across, beside), _ = tied_all([second, first_across, beside], ())
        partials = attend([own, beside, first, second, first_across, third])
        partials[2] = swap(partials[2], n, 1)
        queries, partials[1] = lax.optimization_barrier((queries, partials[1]))
        remaining = [swapped(second, 2), swapped(third, 2)]
        placed = [own, beside, first, second, first_across, third] + remaining
    else:
        same = [list(range(c, n, 2)) for c in range(2)]
        gathered = lax.all_gather(kv, "seq", axis=0, tiled=True, axis_index_groups=same)
        remaining = [Piece([gathered], lambda shard, i: 2 * i + shard % 2, n // 2)]
        partials, placed = [], remaining
    leaving = attend(remaining, 1)
    queries, leaving[1] = lax.optimization_barrier((queries, leaving[1]))
    leaving[2] = swap(leaving[2], n, 1)
    staying = attend(remaining, 0)
    leaving[0], staying[1] = lax.optimization_barrier((leaving[0], staying[1]))
    sent = pl.pallas_call(
        leave_kernel,
        out_shape=struct((half, width), bf16),
        in_specs=in_vmem(4 + len(partials)),
        out_specs=in_vmem(1)[0],
        compiler_params=kernel_params(24),
        cost_estimate=cost(0, 0),
        name="leave",
    )(w_out, *partials, *leaving)
    received = lax.ppermute(sent, "req", [(i, (i + 1) % parts) for i in range(parts)])
    staying[2] = swap(staying[2], n, 1)
    placed, (staying[2], sent) = tied_all(placed, (staying[2], sent))
    cache, *other = place_pages(placed)
    kept, cache = pl.pallas_call(
        keep_kernel,
        out_shape=(struct((half, width), f32), struct(cache.shape, bf16)),
        in_specs=in_vmem(6 + 2 + len(partials)),
        out_specs=tuple(in_vmem(2)),
        compiler_params=kernel_params(24),
        cost_estimate=cost(0, 0),
        name="keep",
    )(w_out, tokens, cache, *[swap(x, n, 1) for x in other], *partials, *staying)
    hidden = pl.pallas_call(
        finish_kernel,
        out_shape=struct((half, width), bf16),
        in_specs=in_vmem(2),
        out_specs=in_vmem(1)[0],
        compiler_params=kernel_params(24),
        cost_estimate=cost(0, 0),
        name="finish",
    )(kept, received)
    return hidden, cache


def solution(mesh):
    in_specs = (
        P("seq", None),
        P(),
        P(None, "req"),
        P(None, "req"),
        P(None, "req"),
        P("req", None),
        P(),
        P(),
        P(),
    )
    out_specs = (P(("seq", "req"), None), P("seq", None, None, "req"))
    body = functools.partial(on_device, mesh.shape["seq"], mesh.shape["req"])
    return jax.shard_map(body, mesh=mesh, in_specs=in_specs, out_specs=out_specs, check_vma=False)
```

```python
import functools
import math

import jax
import jax.numpy as jnp
import numpy as np
from jax import lax
from jax.experimental import pallas as pl
from jax.experimental.pallas import tpu as pltpu
from jax.sharding import PartitionSpec as P

HEAD = 128
PAGE = 32
THETA = 1000000.0
EPS = 1e-05
MASKED = -1e30
FLOOR = -1e29
WEIGHT_STEPS = 2
MIB = 1024 * 1024
SCALE = math.log2(math.e) / math.sqrt(HEAD)

f32 = jnp.float32
bf16 = jnp.bfloat16
struct = jax.ShapeDtypeStruct


def in_vmem(count):
    return [pl.BlockSpec(memory_space=pltpu.VMEM)] * count


def in_smem(count):
    return [pl.BlockSpec(memory_space=pltpu.SMEM)] * count


def in_hbm(count):
    return [pl.BlockSpec(memory_space=pltpu.HBM)] * count


def kernel_params(mib):
    return pltpu.CompilerParams(vmem_limit_bytes=mib * MIB)


def cost(flops, moved):
    return pl.CostEstimate(flops=flops, bytes_accessed=moved, transcendentals=0)


def rotary_constants(half):
    exponent = np.arange(HEAD // 2, dtype=np.float64) * (2.0 / HEAD)
    freq = np.tile(THETA**-exponent, 2)[None, :]
    angle = np.arange(half, dtype=np.float64)[:, None] * freq
    rows = [np.cos(angle), np.sin(angle), np.broadcast_to(freq, (8, HEAD))]
    return jnp.asarray(np.concatenate(rows).astype(np.float32))


def blocks_of(block_ref, shard):
    first = block_ref[shard]
    return first, 2 * block_ref.shape[0] - 1 - first


def prompt_begin(position, len_ref):
    begin = jnp.zeros_like(position)
    start = jnp.int32(0)
    for r in range(len_ref.shape[0] - 1):
        start = start + len_ref[r]
        begin = jnp.where(position >= start, start, begin)
    return begin


def positions(blocks, half, dim, shape):
    index = lax.broadcasted_iota(jnp.int32, shape, dim)
    offset = blocks[0] * half
    for i, block in enumerate(blocks[1:], 1):
        offset = jnp.where(index >= i * half, (block - i) * half, offset)
    return index + offset


def rotate(u, cosine, signed_sine):
    return u * cosine + pltpu.roll(u, HEAD // 2, 1) * signed_sine


def weight_copies(source, scratch, sems):
    depth = scratch.shape[0] // WEIGHT_STEPS
    return [
        pltpu.make_async_copy(
            source.at[pl.ds(step * depth, depth), :], scratch.at[pl.ds(step * depth, depth), :], sems.at[step]
        )
        for step in range(WEIGHT_STEPS)
    ]


def stepped_dot(left, copies, scratch):
    depth = scratch.shape[0] // WEIGHT_STEPS
    total = None
    for step, copy in enumerate(copies):
        copy.wait()
        rows = slice(step * depth, (step + 1) * depth)
        part = jnp.dot(left[:, rows], scratch[rows, :], preferred_element_type=f32)
        total = part if total is None else total + part
    return total


def rotary_tables(block_ref, len_ref, turn_ref, half):
    prompts = len_ref.shape[0]
    blocks = blocks_of(block_ref, lax.axis_index("seq"))
    starts = [jnp.int32(0)]
    for r in range(prompts - 1):
        starts.append(starts[-1] + len_ref[r])
    count = 2 * prompts
    index = lax.broadcasted_iota(jnp.int32, (count, HEAD), 0)
    base = jnp.zeros((count, HEAD), jnp.int32)
    for k, block in enumerate(blocks):
        for p, start in enumerate(starts):
            base = jnp.where(index == k * prompts + p, block * half - start, base)
    angle = base.astype(f32) * turn_ref[2 * half : 2 * half + 1, :]
    base_cos, base_sin = jnp.cos(angle), jnp.sin(angle)
    row_cos, row_sin = turn_ref[:half, :], turn_ref[half : 2 * half, :]
    row = lax.broadcasted_iota(jnp.int32, (half, HEAD), 0)
    lane = lax.broadcasted_iota(jnp.int32, (half, HEAD), 1)
    cosines, sines = [], []
    for k, block in enumerate(blocks):
        at = k * prompts
        cos, sin = base_cos[at : at + 1], base_sin[at : at + 1]
        for p in range(1, prompts):
            inside = row >= starts[p] - block * half
            cos = jnp.where(inside, base_cos[at + p : at + p + 1], cos)
            sin = jnp.where(inside, base_sin[at + p : at + p + 1], sin)
        cosines.append(row_cos * cos - row_sin * sin)
        sine = row_sin * cos + row_cos * sin
        sines.append(jnp.where(lane < HEAD // 2, -sine, sine))
    return jnp.concatenate(cosines, 0), jnp.concatenate(sines, 0)


def project_kernel(
    block_hbm, len_hbm, turn_hbm, tok_hbm, gain_hbm, wk_hbm, wv_hbm, wq_hbm,
    kv_hbm, both_hbm,
    block_ref, len_ref, turn_ref, tok_ref, gain_ref, k_weights, v_weights, q_weights, both_ref,
    small_sems, k_sems, v_sems, q_sems, out_sems,
):
    small = [
        pltpu.make_async_copy(source, target, small_sems.at[i])
        for i, (source, target) in enumerate(
            (
                (tok_hbm, tok_ref),
                (block_hbm, block_ref),
                (len_hbm, len_ref),
                (turn_hbm, turn_ref),
                (gain_hbm, gain_ref),
            )
        )
    ]
    k_copies = weight_copies(wk_hbm, k_weights, k_sems)
    v_copies = weight_copies(wv_hbm, v_weights, v_sems)
    q_copies = weight_copies(wq_hbm, q_weights, q_sems)
    for copy in small:
        copy.start()
    for i, copy in enumerate(k_copies + v_copies + q_copies):
        copy.start(priority=1 - i % 2)
    rows = tok_ref.shape[0]
    key_width = wk_hbm.shape[1]
    kv_width = kv_hbm.shape[1]
    for copy in small:
        copy.wait()
    wide = tok_ref[...].astype(f32)
    scale = lax.rsqrt(jnp.mean(wide * wide, -1, keepdims=True) + EPS)
    normed = (wide * scale * gain_ref[...]).astype(bf16)
    cosine, sine = rotary_tables(block_ref, len_ref, turn_ref, rows // 2)
    product = stepped_dot(normed, k_copies, k_weights)
    for h in range(key_width // HEAD):
        cols = slice(h * HEAD, (h + 1) * HEAD)
        both_ref[:, cols] = rotate(product[:, cols], cosine, sine).astype(bf16)
    both_ref[:, key_width:kv_width] = stepped_dot(normed, v_copies, v_weights).astype(bf16)
    kv_part = both_ref.at[:, pl.ds(0, kv_width)]
    q_part = pl.ds(kv_width, wq_hbm.shape[1])
    writes = [
        pltpu.make_async_copy(kv_part, kv_hbm, out_sems.at[0]),
        pltpu.make_async_copy(kv_part, both_hbm.at[:, pl.ds(0, kv_width)], out_sems.at[1]),
    ]
    for copy in writes:
        copy.start()
    product = stepped_dot(normed, q_copies, q_weights)
    for h in range(wq_hbm.shape[1] // HEAD):
        cols = slice(h * HEAD, (h + 1) * HEAD)
        turned = rotate(product[:, cols], cosine, sine).astype(bf16)
        both_ref[:, kv_width + h * HEAD : kv_width + (h + 1) * HEAD] = turned
    writes.append(pltpu.make_async_copy(both_ref.at[:, q_part], both_hbm.at[:, q_part], out_sems.at[2]))
    writes[2].start()
    for copy in writes:
        copy.wait()


def attend_kernel(pieces, side, key_pos_ref, q_pos_ref, q_begin_ref, q_ref, far_ref, *refs):
    pieces, refs = with_refs(pieces, refs)
    shard = lax.axis_index("seq")
    rows, q_width = q_ref.shape
    key_width = pieces[0].arrays[0].shape[1] // 2
    kv_heads = key_width // HEAD
    group = q_width // key_width
    if side is None:
        taken, first = rows, 0
        span = slice(None)
    else:
        part = lax.axis_index("req")
        taken = rows // 2
        first = pl.multiple_of((1 - part if side else part) * taken, taken)
        span = pl.ds(first, taken)
    both = 2 * taken

    def of_both_cores(ref):
        return jnp.concatenate(
            [ref[pl.ds(pl.multiple_of(core * rows + first, taken), taken), :] for core in (0, 1)], 0
        )

    q_pos, q_begin = of_both_cores(q_pos_ref), of_both_cores(q_begin_ref)
    queries = [
        jnp.concatenate(
            [
                ref[span, h * HEAD : (h + 1) * HEAD]
                for h in range(g * group, (g + 1) * group)
                for ref in (q_ref, far_ref)
            ],
            0,
        )
        for g in range(kv_heads)
    ]

    def absorb(state, blocks, sources):
        bias = []
        for source in sources:
            key_pos = key_pos_ref[pl.ds(source, 1), :]
            bias.append(jnp.where((key_pos >= q_begin) & (key_pos <= q_pos), 0.0, MASKED))
        bias = jnp.concatenate(bias, 1)
        bias = jnp.concatenate([bias] * group, 0)
        out = []
        for g in range(kv_heads):
            top, total, acc = state[g]
            keys = jnp.concatenate([b[:, g * HEAD : (g + 1) * HEAD] for b in blocks], 0)
            values = jnp.concatenate(
                [b[:, key_width + g * HEAD : key_width + (g + 1) * HEAD] for b in blocks], 0
            )
            scores = lax.dot_general(
                queries[g], keys, (((1,), (1,)), ((), ())), preferred_element_type=f32
            )
            scores = scores * SCALE + bias
            new_top = jnp.maximum(top, jnp.max(scores, -1, keepdims=True))
            weights = jnp.exp2(scores - new_top)
            factor = jnp.exp2(top - new_top)
            total = total * factor + jnp.sum(weights, -1, keepdims=True)
            acc = acc * factor + jnp.dot(weights.astype(bf16), values, preferred_element_type=f32)
            out.append((new_top, total, acc))
        return tuple(out)

    state = (
        (
            jnp.full((group * both, 1), FLOOR, f32),
            jnp.zeros((group * both, 1), f32),
            jnp.zeros((group * both, HEAD), f32),
        ),
    ) * kv_heads
    if all(piece.count == 1 for piece in pieces):
        for i in range(0, len(pieces), 2):
            pair = pieces[i : i + 2]
            state = absorb(
                state, [p.arrays[0][...] for p in pair], [p.source_of(shard, 0) for p in pair]
            )
    else:
        for piece in pieces:

            def step(i, carried):
                at = pl.multiple_of(i * rows, rows)
                block = piece.arrays[0][pl.ds(at, rows), :]
                return absorb(carried, [block], [piece.source_of(shard, i)])

            state = lax.fori_loop(0, piece.count, step, state)

    mine_ref, stat_ref, packed_ref = refs
    heads = q_width // HEAD
    lane = lax.broadcasted_iota(jnp.int32, (taken, HEAD), 1)
    mine = jnp.zeros((taken, HEAD), f32)
    theirs = jnp.zeros((taken, HEAD), f32)
    for g in range(kv_heads):
        top, total, acc = state[g]
        for j in range(group):
            h = g * group + j
            cols = slice(h * HEAD, (h + 1) * HEAD)
            near = slice(j * both, j * both + taken)
            far = slice(j * both + taken, (j + 1) * both)
            mine_ref[:, cols] = acc[near]
            packed_ref[:, cols] = acc[far].astype(bf16)
            for value, at in ((top, h), (total, heads + h)):
                mine = jnp.where(lane == at, value[near], mine)
                theirs = jnp.where(lane % (2 * heads) == at, value[far], theirs)
    stat_ref[...] = mine
    high = theirs.astype(bf16).astype(f32)
    middle = (theirs - high).astype(bf16).astype(f32)
    low = theirs - high - middle
    third = lane // (2 * heads)
    parts = jnp.where(third == 0, high, jnp.where(third == 1, middle, low))
    packed_ref[:, q_width:] = parts.astype(bf16)


def stage_kernel(block_ref, len_ref, both_ref, kv_out, q_out, key_pos_ref, q_pos_ref, q_begin_ref):
    kv_out[...] = both_ref[:, : kv_out.shape[1]]
    q_out[...] = both_ref[:, kv_out.shape[1] :]
    shards, rows = key_pos_ref.shape
    shard = lax.axis_index("seq")

    def lay(s, carry):
        key_pos_ref[pl.ds(s, 1), :] = positions(blocks_of(block_ref, s), rows // 2, 1, (1, rows))
        return carry

    lax.fori_loop(0, shards, lay, 0, unroll=shards <= 16)
    blocks = [block for s in (shard, shard ^ 1) for block in blocks_of(block_ref, s)]
    q_pos = positions(blocks, rows // 2, 0, q_pos_ref.shape)
    q_pos_ref[...] = q_pos
    q_begin_ref[...] = prompt_begin(q_pos, len_ref)


def joined_rows(partials, first, half):
    q_width = partials[0].shape[1]
    heads = q_width // HEAD
    part = pl.ds(pl.multiple_of(first, half), half)
    held = []
    for mine_ref, stat_ref, packed_ref in zip(partials[::3], partials[1::3], partials[2::3]):
        span = slice(None) if mine_ref.shape[0] == half else part
        parts = packed_ref[span, q_width:].astype(f32)
        stats = parts
        for t in (1, 2):
            stats = stats + pltpu.roll(parts, HEAD - 2 * heads * t, 1)
        held += [(mine_ref, span, stat_ref[span, :]), (packed_ref, span, stats)]
    top = functools.reduce(jnp.maximum, [stats for _, _, stats in held])
    shares = [jnp.exp2(stats - top) for _, _, stats in held]
    total = sum(
        share * pltpu.roll(stats, HEAD - heads, 1) for share, (_, _, stats) in zip(shares, held)
    )
    shares = [share / total for share in shares]
    context = []
    for h in range(heads):
        cols = slice(h * HEAD, (h + 1) * HEAD)
        context.append(
            sum(
                ref[span, cols].astype(f32) * share[:, h : h + 1]
                for (ref, span, _), share in zip(held, shares)
            ).astype(bf16)
        )
    return jnp.concatenate(context, 1)


def leave_kernel(wo_ref, *refs):
    partials, sent_ref = refs[:-1], refs[-1]
    half = sent_ref.shape[0]
    context = joined_rows(partials, (1 - lax.axis_index("req")) * half, half)
    sent_ref[...] = jnp.dot(context, wo_ref[...], preferred_element_type=f32).astype(bf16)


def keep_kernel(wo_ref, tok_ref, mine_ref, *refs):
    others, partials, (out_ref, cache_ref) = refs[:2], refs[2:-2], refs[-2:]
    share = mine_ref.shape[0] // 2
    for i, other_ref in enumerate(others):
        part = slice(i * share, (i + 1) * share)
        cache_ref[part] = mine_ref[part] + other_ref[...]
    half = out_ref.shape[0]
    first = lax.axis_index("req") * half
    context = joined_rows(partials, first, half)
    residual = tok_ref[pl.ds(pl.multiple_of(first, half), half), :].astype(f32)
    out_ref[...] = jnp.dot(context, wo_ref[...], preferred_element_type=f32) + residual


def finish_kernel(kept_ref, received_ref, hidden_ref):
    hidden_ref[...] = (kept_ref[...] + received_ref[...].astype(f32)).astype(bf16)


def cache_kernel(pieces, block_ref, slot_ref, *refs):
    pieces, (mine_ref, *other_refs) = with_refs(pieces, refs)
    shard = lax.axis_index("seq")
    slots = mine_ref.shape[0]
    key_width = mine_ref.shape[3]
    rows = slots * PAGE // 2
    pages = rows // 2 // PAGE
    for target in (mine_ref, *other_refs):
        target[...] = jnp.zeros_like(target)
    share = slots // len(other_refs)

    def place(ref, at, source):
        for k, block in enumerate(blocks_of(block_ref, source)):
            for j in range(pages):
                slot = slot_ref[block * pages + j]
                holder = slot // slots
                local = slot - holder * slots
                offset = at + (k * pages + j) * PAGE
                if not isinstance(offset, int):
                    offset = pl.multiple_of(offset, PAGE)

                def write(target, at_slot):
                    target[at_slot, 0] = ref[pl.ds(offset, PAGE), :key_width]
                    target[at_slot, 1] = ref[pl.ds(offset, PAGE), key_width:]

                @pl.when(holder == shard)
                def _():
                    write(mine_ref, local)

                for i, target in enumerate(other_refs):

                    @pl.when((holder == shard ^ 1) & (local // share == i))
                    def _():
                        write(target, local - i * share)

    for piece in pieces:
        if piece.count == 1:
            place(piece.arrays[0], 0, piece.source_of(shard, 0))
        else:

            def step(i, carry):
                place(piece.arrays[0], i * rows, piece.source_of(shard, i))
                return carry

            lax.fori_loop(0, piece.count, step, 0)


def tied_all(pieces, other):
    arrays, other = lax.optimization_barrier((operands(pieces), other))
    return with_refs(pieces, arrays)[0], other


def tied(piece, other):
    (piece,), other = tied_all([piece], other)
    return piece, other


def swap(x, n, bit):
    return lax.ppermute(x, "seq", [(i, i ^ bit) for i in range(n)])


class Piece:
    def __init__(self, arrays, source_of, count=1):
        self.arrays, self.source_of, self.count = arrays, source_of, count

    def moved(self, arrays):
        return Piece(arrays, self.source_of, self.count)


def operands(pieces):
    return [x for piece in pieces for x in piece.arrays]


def with_refs(pieces, refs):
    out = []
    for piece in pieces:
        taken, refs = refs[: len(piece.arrays)], refs[len(piece.arrays) :]
        out.append(piece.moved(taken))
    return out, refs


def at_distance(bits):
    return lambda shard, i: shard ^ bits


def move(x, pairs):
    return lax.ppermute(x, "seq", pairs)


def on_device(
    n, parts, tokens, norm_gain, w_query, key_projection, value_projection, w_out, lengths, block_split, page_slot,
):
    rows, width = tokens.shape
    half = rows // 2
    q_width = w_query.shape[1]
    kv_width = key_projection.shape[1] + value_projection.shape[1]
    kv, both = pl.pallas_call(
        project_kernel,
        out_shape=(struct((rows, kv_width), bf16), struct((rows, kv_width + q_width), bf16)),
        in_specs=in_hbm(8),
        out_specs=tuple(in_hbm(2)),
        scratch_shapes=[
            pltpu.SMEM(block_split.shape, jnp.int32),
            pltpu.SMEM(lengths.shape, jnp.int32),
            pltpu.VMEM((2 * half + 8, HEAD), f32),
            pltpu.VMEM((rows, width), bf16),
            pltpu.VMEM((1, width), f32),
            pltpu.VMEM(key_projection.shape, bf16),
            pltpu.VMEM(value_projection.shape, bf16),
            pltpu.VMEM((width, q_width), bf16),
            pltpu.VMEM((rows, kv_width + q_width), bf16),
            pltpu.SemaphoreType.DMA((5,)),
            pltpu.SemaphoreType.DMA((WEIGHT_STEPS,)),
            pltpu.SemaphoreType.DMA((WEIGHT_STEPS,)),
            pltpu.SemaphoreType.DMA((WEIGHT_STEPS,)),
            pltpu.SemaphoreType.DMA((3,)),
        ],
        compiler_params=kernel_params(62),
        cost_estimate=cost(2 * rows * width * (kv_width + q_width), 2 * width * (kv_width + q_width)),
        name="project",
    )(
        block_split, lengths, rotary_constants(half), tokens, norm_gain.reshape(1, width),
        key_projection, value_projection, w_query,
    )
    staged, queries, *places = pl.pallas_call(
        stage_kernel,
        out_shape=(
            struct((rows, kv_width), bf16),
            struct((rows, q_width), bf16),
            struct((n, rows), jnp.int32),
            struct((2 * rows, HEAD), jnp.int32),
            struct((2 * rows, HEAD), jnp.int32),
        ),
        in_specs=in_smem(2) + in_vmem(1),
        out_specs=tuple(in_vmem(5)),
        compiler_params=kernel_params(24),
        cost_estimate=cost(0, 0),
        name="stage",
    )(block_split, lengths, both)
    far_queries = swap(queries, n, 1)

    def attend(pieces, side=None):
        arrays = operands(pieces)
        taken = rows if side is None else half
        mine, stats, packed = pl.pallas_call(
            functools.partial(attend_kernel, pieces, side),
            out_shape=(
                struct((taken, q_width), f32),
                struct((taken, HEAD), f32),
                struct((taken, q_width + HEAD), bf16),
            ),
            in_specs=in_vmem(5 + len(arrays)),
            out_specs=tuple(in_vmem(3)),
            compiler_params=kernel_params(32),
            cost_estimate=cost(0, 0),
            name="attend",
        )(*places, queries, far_queries, *arrays)
        return [mine, stats, packed]

    def place_pages(pieces):
        arrays = operands(pieces)
        shape = (2 * rows // PAGE, 2, PAGE, kv_width // 2)
        return pl.pallas_call(
            functools.partial(cache_kernel, pieces),
            out_shape=(struct(shape, bf16),) + (struct((shape[0] // 2,) + shape[1:], bf16),) * 2,
            in_specs=in_smem(2) + in_vmem(len(arrays)),
            out_specs=tuple(in_vmem(1 + 2)),
            compiler_params=kernel_params(32),
            cost_estimate=cost(0, 0),
            name="cache",
        )(block_split, page_slot, *arrays)

    if n == 16:

        def swapped(piece, bits):
            source = lambda shard, i: piece.source_of(shard ^ bits, i)
            return Piece([swap(piece.arrays[0], n, bits)], source)

        own = Piece([kv], at_distance(0))
        second, first, beside = swapped(own, 8), swapped(own, 4), swapped(own, 2)
        first_across = swapped(first, 2)
        second, staged = tied(second, staged)
        own = own.moved([staged])
        third = swapped(second, 4)
        (second, first_across, beside), _ = tied_all([second, first_across, beside], ())
        partials = attend([own, beside, first, second, first_across, third])
        partials[2] = swap(partials[2], n, 1)
        queries, partials[1] = lax.optimization_barrier((queries, partials[1]))
        remaining = [swapped(second, 2), swapped(third, 2)]
        placed = [own, beside, first, second, first_across, third] + remaining
    else:
        same = [list(range(c, n, 2)) for c in range(2)]
        gathered = lax.all_gather(kv, "seq", axis=0, tiled=True, axis_index_groups=same)
        remaining = [Piece([gathered], lambda shard, i: 2 * i + shard % 2, n // 2)]
        partials, placed = [], remaining
    leaving = attend(remaining, 1)
    queries, leaving[1] = lax.optimization_barrier((queries, leaving[1]))
    leaving[2] = swap(leaving[2], n, 1)
    staying = attend(remaining, 0)
    leaving[0], staying[1] = lax.optimization_barrier((leaving[0], staying[1]))
    sent = pl.pallas_call(
        leave_kernel,
        out_shape=struct((half, width), bf16),
        in_specs=in_vmem(4 + len(partials)),
        out_specs=in_vmem(1)[0],
        compiler_params=kernel_params(24),
        cost_estimate=cost(0, 0),
        name="leave",
    )(w_out, *partials, *leaving)
    received = lax.ppermute(sent, "req", [(i, (i + 1) % parts) for i in range(parts)])
    staying[2] = swap(staying[2], n, 1)
    placed, (staying[2], sent) = tied_all(placed, (staying[2], sent))
    cache, *other = place_pages(placed)
    kept, cache = pl.pallas_call(
        keep_kernel,
        out_shape=(struct((half, width), f32), struct(cache.shape, bf16)),
        in_specs=in_vmem(6 + 2 + len(partials)),
        out_specs=tuple(in_vmem(2)),
        compiler_params=kernel_params(24),
        cost_estimate=cost(0, 0),
        name="keep",
    )(w_out, tokens, cache, *[swap(x, n, 1) for x in other], *partials, *staying)
    hidden = pl.pallas_call(
        finish_kernel,
        out_shape=struct((half, width), bf16),
        in_specs=in_vmem(2),
        out_specs=in_vmem(1)[0],
        compiler_params=kernel_params(24),
        cost_estimate=cost(0, 0),
        name="finish",
    )(kept, received)
    return hidden, cache


def solution(mesh):
    in_specs = (
        P("seq", None),
        P(),
        P(None, "req"),
        P(None, "req"),
        P(None, "req"),
        P("req", None),
        P(),
        P(),
        P(),
    )
    out_specs = (P(("seq", "req"), None), P("seq", None, None, "req"))
    body = functools.partial(on_device, mesh.shape["seq"], mesh.shape["req"])
    return jax.shard_map(body, mesh=mesh, in_specs=in_specs, out_specs=out_specs, check_vma=False)
```

```python
import functools
import math

import jax
import jax.numpy as jnp
import numpy as np
from jax import lax
from jax.experimental import pallas as pl
from jax.experimental.pallas import tpu as pltpu
from jax.sharding import PartitionSpec as P

HEAD = 128
PAGE = 32
THETA = 1000000.0
EPS = 1e-05
MASKED = -1e30
FLOOR = -1e29
WEIGHT_STEPS = 2
MIB = 1024 * 1024
SCALE = math.log2(math.e) / math.sqrt(HEAD)

f32 = jnp.float32
bf16 = jnp.bfloat16
struct = jax.ShapeDtypeStruct


def in_vmem(count):
    return [pl.BlockSpec(memory_space=pltpu.VMEM)] * count


def in_smem(count):
    return [pl.BlockSpec(memory_space=pltpu.SMEM)] * count


def in_hbm(count):
    return [pl.BlockSpec(memory_space=pltpu.HBM)] * count


def kernel_params(mib):
    return pltpu.CompilerParams(vmem_limit_bytes=mib * MIB)


def cost(flops, moved):
    return pl.CostEstimate(flops=flops, bytes_accessed=moved, transcendentals=0)


def rotary_constants(half):
    exponent = np.arange(HEAD // 2, dtype=np.float64) * (2.0 / HEAD)
    freq = np.tile(THETA**-exponent, 2)[None, :]
    angle = np.arange(half, dtype=np.float64)[:, None] * freq
    rows = [np.cos(angle), np.sin(angle), np.broadcast_to(freq, (8, HEAD))]
    return jnp.asarray(np.concatenate(rows).astype(np.float32))


def blocks_of(block_ref, shard):
    first = block_ref[shard]
    return first, 2 * block_ref.shape[0] - 1 - first


def positions(blocks, half, dim, shape):
    index = lax.broadcasted_iota(jnp.int32, shape, dim)
    offset = blocks[0] * half
    for i, block in enumerate(blocks[1:], 1):
        offset = jnp.where(index >= i * half, (block - i) * half, offset)
    return index + offset


def rotate(u, cosine, signed_sine):
    return u * cosine + pltpu.roll(u, HEAD // 2, 1) * signed_sine


def weight_copies(source, scratch, sems):
    depth = scratch.shape[0] // WEIGHT_STEPS
    return [
        pltpu.make_async_copy(
            source.at[pl.ds(step * depth, depth), :], scratch.at[pl.ds(step * depth, depth), :], sems.at[step]
        )
        for step in range(WEIGHT_STEPS)
    ]


def stepped_dot(left, copies, scratch):
    depth = scratch.shape[0] // WEIGHT_STEPS
    total = None
    for step, copy in enumerate(copies):
        copy.wait()
        rows = slice(step * depth, (step + 1) * depth)
        part = jnp.dot(left[:, rows], scratch[rows, :], preferred_element_type=f32)
        total = part if total is None else total + part
    return total


def rotary_tables(block_ref, len_ref, turn_ref, half):
    prompts = len_ref.shape[0]
    blocks = blocks_of(block_ref, lax.axis_index("seq"))
    starts = [jnp.int32(0)]
    for r in range(prompts - 1):
        starts.append(starts[-1] + len_ref[r])
    count = 2 * prompts
    index = lax.broadcasted_iota(jnp.int32, (count, HEAD), 0)
    base = jnp.zeros((count, HEAD), jnp.int32)
    for k, block in enumerate(blocks):
        for p, start in enumerate(starts):
            base = jnp.where(index == k * prompts + p, block * half - start, base)
    angle = base.astype(f32) * turn_ref[2 * half : 2 * half + 1, :]
    base_cos, base_sin = jnp.cos(angle), jnp.sin(angle)
    row_cos, row_sin = turn_ref[:half, :], turn_ref[half : 2 * half, :]
    row = lax.broadcasted_iota(jnp.int32, (half, HEAD), 0)
    lane = lax.broadcasted_iota(jnp.int32, (half, HEAD), 1)
    cosines, sines = [], []
    for k, block in enumerate(blocks):
        at = k * prompts
        cos, sin = base_cos[at : at + 1], base_sin[at : at + 1]
        for p in range(1, prompts):
            inside = row >= starts[p] - block * half
            cos = jnp.where(inside, base_cos[at + p : at + p + 1], cos)
            sin = jnp.where(inside, base_sin[at + p : at + p + 1], sin)
        cosines.append(row_cos * cos - row_sin * sin)
        sine = row_sin * cos + row_cos * sin
        sines.append(jnp.where(lane < HEAD // 2, -sine, sine))
    return jnp.concatenate(cosines, 0), jnp.concatenate(sines, 0)


def project_kernel(
    block_hbm, len_hbm, turn_hbm, tok_hbm, gain_hbm, wk_hbm, wv_hbm, wq_hbm,
    kv_hbm, both_hbm,
    block_ref, len_ref, turn_ref, tok_ref, gain_ref, k_weights, v_weights, q_weights, both_ref,
    small_sems, k_sems, v_sems, q_sems, out_sems,
):
    small = [
        pltpu.make_async_copy(source, target, small_sems.at[i])
        for i, (source, target) in enumerate(
            (
                (tok_hbm, tok_ref),
                (block_hbm, block_ref),
                (len_hbm, len_ref),
                (turn_hbm, turn_ref),
                (gain_hbm, gain_ref),
            )
        )
    ]
    k_copies = weight_copies(wk_hbm, k_weights, k_sems)
    v_copies = weight_copies(wv_hbm, v_weights, v_sems)
    q_copies = weight_copies(wq_hbm, q_weights, q_sems)
    for copy in small:
        copy.start()
    for i, copy in enumerate(k_copies + v_copies + q_copies):
        copy.start(priority=1 - i % 2)
    rows = tok_ref.shape[0]
    key_width = wk_hbm.shape[1]
    kv_width = kv_hbm.shape[1]
    for copy in small:
        copy.wait()
    wide = tok_ref[...].astype(f32)
    scale = lax.rsqrt(jnp.mean(wide * wide, -1, keepdims=True) + EPS)
    normed = (wide * scale * gain_ref[...]).astype(bf16)
    cosine, sine = rotary_tables(block_ref, len_ref, turn_ref, rows // 2)
    product = stepped_dot(normed, k_copies, k_weights)
    for h in range(key_width // HEAD):
        cols = slice(h * HEAD, (h + 1) * HEAD)
        both_ref[:, cols] = rotate(product[:, cols], cosine, sine).astype(bf16)
    both_ref[:, key_width:kv_width] = stepped_dot(normed, v_copies, v_weights).astype(bf16)
    kv_part = both_ref.at[:, pl.ds(0, kv_width)]
    q_part = pl.ds(kv_width, wq_hbm.shape[1])
    writes = [
        pltpu.make_async_copy(kv_part, kv_hbm, out_sems.at[0]),
        pltpu.make_async_copy(kv_part, both_hbm.at[:, pl.ds(0, kv_width)], out_sems.at[1]),
    ]
    for copy in writes:
        copy.start()
    product = stepped_dot(normed, q_copies, q_weights)
    for h in range(wq_hbm.shape[1] // HEAD):
        cols = slice(h * HEAD, (h + 1) * HEAD)
        turned = rotate(product[:, cols], cosine, sine).astype(bf16)
        both_ref[:, kv_width + h * HEAD : kv_width + (h + 1) * HEAD] = turned
    writes.append(pltpu.make_async_copy(both_ref.at[:, q_part], both_hbm.at[:, q_part], out_sems.at[2]))
    writes[2].start()
    for copy in writes:
        copy.wait()


def attend_kernel(pieces, side, key_pos_ref, q_pos_ref, q_begin_ref, q_ref, far_ref, *refs):
    pieces, refs = with_refs(pieces, refs)
    shard = lax.axis_index("seq")
    rows, q_width = q_ref.shape
    key_width = pieces[0].arrays[0].shape[1] // 2
    kv_heads = key_width // HEAD
    group = q_width // key_width
    if side is None:
        taken, first = rows, 0
        span = slice(None)
    else:
        part = lax.axis_index("req")
        taken = rows // 2
        first = pl.multiple_of((1 - part if side else part) * taken, taken)
        span = pl.ds(first, taken)
    both = 2 * taken

    def of_both_cores(ref):
        return jnp.concatenate(
            [ref[pl.ds(pl.multiple_of(core * rows + first, taken), taken), :] for core in (0, 1)], 0
        )

    q_pos, q_begin = of_both_cores(q_pos_ref), of_both_cores(q_begin_ref)
    queries = [
        jnp.concatenate(
            [
                ref[span, h * HEAD : (h + 1) * HEAD]
                for h in range(g * group, (g + 1) * group)
                for ref in (q_ref, far_ref)
            ],
            0,
        )
        for g in range(kv_heads)
    ]

    def absorb(state, blocks, sources):
        bias = []
        for source in sources:
            key_pos = key_pos_ref[pl.ds(source, 1), :]
            bias.append(jnp.where((key_pos >= q_begin) & (key_pos <= q_pos), 0.0, MASKED))
        bias = jnp.concatenate(bias, 1)
        bias = jnp.concatenate([bias] * group, 0)
        out = []
        for g in range(kv_heads):
            top, total, acc = state[g]
            keys = jnp.concatenate([b[:, g * HEAD : (g + 1) * HEAD] for b in blocks], 0)
            values = jnp.concatenate(
                [b[:, key_width + g * HEAD : key_width + (g + 1) * HEAD] for b in blocks], 0
            )
            scores = lax.dot_general(
                queries[g], keys, (((1,), (1,)), ((), ())), preferred_element_type=f32
            )
            scores = scores * SCALE + bias
            new_top = jnp.maximum(top, jnp.max(scores, -1, keepdims=True))
            weights = jnp.exp2(scores - new_top)
            factor = jnp.exp2(top - new_top)
            total = total * factor + jnp.sum(weights, -1, keepdims=True)
            acc = acc * factor + jnp.dot(weights.astype(bf16), values, preferred_element_type=f32)
            out.append((new_top, total, acc))
        return tuple(out)

    state = (
        (
            jnp.full((group * both, 1), FLOOR, f32),
            jnp.zeros((group * both, 1), f32),
            jnp.zeros((group * both, HEAD), f32),
        ),
    ) * kv_heads
    if all(piece.count == 1 for piece in pieces):
        for i in range(0, len(pieces), 2):
            pair = pieces[i : i + 2]
            state = absorb(
                state, [p.arrays[0][...] for p in pair], [p.source_of(shard, 0) for p in pair]
            )
    else:
        for piece in pieces:

            def step(i, carried):
                at = pl.multiple_of(i * rows, rows)
                block = piece.arrays[0][pl.ds(at, rows), :]
                return absorb(carried, [block], [piece.source_of(shard, i)])

            state = lax.fori_loop(0, piece.count, step, state)

    mine_ref, stat_ref, packed_ref = refs
    heads = q_width // HEAD
    lane = lax.broadcasted_iota(jnp.int32, (taken, HEAD), 1)
    mine = jnp.zeros((taken, HEAD), f32)
    theirs = jnp.zeros((taken, HEAD), f32)
    for g in range(kv_heads):
        top, total, acc = state[g]
        for j in range(group):
            h = g * group + j
            cols = slice(h * HEAD, (h + 1) * HEAD)
            near = slice(j * both, j * both + taken)
            far = slice(j * both + taken, (j + 1) * both)
            mine_ref[:, cols] = acc[near]
            packed_ref[:, cols] = acc[far].astype(bf16)
            for value, at in ((top, h), (total, heads + h)):
                mine = jnp.where(lane == at, value[near], mine)
                theirs = jnp.where(lane % (2 * heads) == at, value[far], theirs)
    stat_ref[...] = mine
    high = theirs.astype(bf16).astype(f32)
    middle = (theirs - high).astype(bf16).astype(f32)
    low = theirs - high - middle
    third = lane // (2 * heads)
    parts = jnp.where(third == 0, high, jnp.where(third == 1, middle, low))
    packed_ref[:, q_width:] = parts.astype(bf16)


def stage_kernel(block_ref, len_ref, both_ref, kv_out, q_out, key_pos_ref, q_pos_ref, q_begin_ref):
    kv_out[...] = both_ref[:, : kv_out.shape[1]]
    q_out[...] = both_ref[:, kv_out.shape[1] :]
    shards, rows = key_pos_ref.shape
    half = rows // 2
    shard = lax.axis_index("seq")

    def picked(values, mask):
        return jnp.sum(jnp.where(mask, values, 0.0), -1, keepdims=True).astype(jnp.int32)

    def lanes(shape):
        return lax.broadcasted_iota(jnp.int32, shape, 1)

    blocks = block_ref[...].astype(f32)
    square = (shards, shards)
    first = picked(blocks, lanes(square) == lax.broadcasted_iota(jnp.int32, square, 0))
    index = lanes((shards, rows))
    key_pos_ref[...] = index + jnp.where(index < half, first, 2 * shards - 2 - first) * half

    held = []
    for s in (shard, shard ^ 1):
        first = picked(blocks, lanes(block_ref.shape) == s)
        held += [first, 2 * shards - 1 - first]
    q_pos = positions(held, half, 0, q_pos_ref.shape)
    q_pos_ref[...] = q_pos
    lengths = len_ref[...].astype(f32)
    begin = jnp.zeros_like(q_pos)
    for r in range(1, len_ref.shape[1]):
        start = picked(lengths, lanes(len_ref.shape) < r)
        begin = jnp.where(q_pos >= start, start, begin)
    q_begin_ref[...] = begin


def joined_rows(partials, first, half):
    q_width = partials[0].shape[1]
    heads = q_width // HEAD
    part = pl.ds(pl.multiple_of(first, half), half)
    held = []
    for mine_ref, stat_ref, packed_ref in zip(partials[::3], partials[1::3], partials[2::3]):
        span = slice(None) if mine_ref.shape[0] == half else part
        parts = packed_ref[span, q_width:].astype(f32)
        stats = parts
        for t in (1, 2):
            stats = stats + pltpu.roll(parts, HEAD - 2 * heads * t, 1)
        held += [(mine_ref, span, stat_ref[span, :]), (packed_ref, span, stats)]
    top = functools.reduce(jnp.maximum, [stats for _, _, stats in held])
    shares = [jnp.exp2(stats - top) for _, _, stats in held]
    total = sum(
        share * pltpu.roll(stats, HEAD - heads, 1) for share, (_, _, stats) in zip(shares, held)
    )
    shares = [share / total for share in shares]
    context = []
    for h in range(heads):
        cols = slice(h * HEAD, (h + 1) * HEAD)
        context.append(
            sum(
                ref[span, cols].astype(f32) * share[:, h : h + 1]
                for (ref, span, _), share in zip(held, shares)
            ).astype(bf16)
        )
    return jnp.concatenate(context, 1)


def leave_kernel(wo_ref, *refs):
    partials, sent_ref = refs[:-1], refs[-1]
    half = sent_ref.shape[0]
    context = joined_rows(partials, (1 - lax.axis_index("req")) * half, half)
    sent_ref[...] = jnp.dot(context, wo_ref[...], preferred_element_type=f32).astype(bf16)


def keep_kernel(wo_ref, tok_ref, mine_ref, *refs):
    others, partials, (out_ref, cache_ref) = refs[:2], refs[2:-2], refs[-2:]
    share = mine_ref.shape[0] // 2
    for i, other_ref in enumerate(others):
        part = slice(i * share, (i + 1) * share)
        cache_ref[part] = mine_ref[part] + other_ref[...]
    half = out_ref.shape[0]
    first = lax.axis_index("req") * half
    context = joined_rows(partials, first, half)
    residual = tok_ref[pl.ds(pl.multiple_of(first, half), half), :].astype(f32)
    out_ref[...] = jnp.dot(context, wo_ref[...], preferred_element_type=f32) + residual


def finish_kernel(kept_ref, received_ref, hidden_ref):
    hidden_ref[...] = (kept_ref[...] + received_ref[...].astype(f32)).astype(bf16)


def cache_kernel(pieces, block_ref, slot_ref, *refs):
    pieces, (mine_ref, *other_refs) = with_refs(pieces, refs)
    shard = lax.axis_index("seq")
    slots = mine_ref.shape[0]
    key_width = mine_ref.shape[3]
    rows = slots * PAGE // 2
    pages = rows // 2 // PAGE
    for target in (mine_ref, *other_refs):
        target[...] = jnp.zeros_like(target)
    share = slots // len(other_refs)

    def place(ref, at, source):
        for k, block in enumerate(blocks_of(block_ref, source)):
            for j in range(pages):
                slot = slot_ref[block * pages + j]
                holder = slot // slots
                local = slot - holder * slots
                offset = at + (k * pages + j) * PAGE
                if not isinstance(offset, int):
                    offset = pl.multiple_of(offset, PAGE)

                def write(target, at_slot):
                    target[at_slot, 0] = ref[pl.ds(offset, PAGE), :key_width]
                    target[at_slot, 1] = ref[pl.ds(offset, PAGE), key_width:]

                @pl.when(holder == shard)
                def _():
                    write(mine_ref, local)

                for i, target in enumerate(other_refs):

                    @pl.when((holder == shard ^ 1) & (local // share == i))
                    def _():
                        write(target, local - i * share)

    for piece in pieces:
        if piece.count == 1:
            place(piece.arrays[0], 0, piece.source_of(shard, 0))
        else:

            def step(i, carry):
                place(piece.arrays[0], i * rows, piece.source_of(shard, i))
                return carry

            lax.fori_loop(0, piece.count, step, 0)


def tied_all(pieces, other):
    arrays, other = lax.optimization_barrier((operands(pieces), other))
    return with_refs(pieces, arrays)[0], other


def tied(piece, other):
    (piece,), other = tied_all([piece], other)
    return piece, other


def swap(x, n, bit):
    return lax.ppermute(x, "seq", [(i, i ^ bit) for i in range(n)])


class Piece:
    def __init__(self, arrays, source_of, count=1):
        self.arrays, self.source_of, self.count = arrays, source_of, count

    def moved(self, arrays):
        return Piece(arrays, self.source_of, self.count)


def operands(pieces):
    return [x for piece in pieces for x in piece.arrays]


def with_refs(pieces, refs):
    out = []
    for piece in pieces:
        taken, refs = refs[: len(piece.arrays)], refs[len(piece.arrays) :]
        out.append(piece.moved(taken))
    return out, refs


def at_distance(bits):
    return lambda shard, i: shard ^ bits


def move(x, pairs):
    return lax.ppermute(x, "seq", pairs)


def on_device(
    n, parts, tokens, norm_gain, w_query, key_projection, value_projection, w_out, lengths, block_split, page_slot,
):
    rows, width = tokens.shape
    half = rows // 2
    q_width = w_query.shape[1]
    kv_width = key_projection.shape[1] + value_projection.shape[1]
    kv, both = pl.pallas_call(
        project_kernel,
        out_shape=(struct((rows, kv_width), bf16), struct((rows, kv_width + q_width), bf16)),
        in_specs=in_hbm(8),
        out_specs=tuple(in_hbm(2)),
        scratch_shapes=[
            pltpu.SMEM(block_split.shape, jnp.int32),
            pltpu.SMEM(lengths.shape, jnp.int32),
            pltpu.VMEM((2 * half + 8, HEAD), f32),
            pltpu.VMEM((rows, width), bf16),
            pltpu.VMEM((1, width), f32),
            pltpu.VMEM(key_projection.shape, bf16),
            pltpu.VMEM(value_projection.shape, bf16),
            pltpu.VMEM((width, q_width), bf16),
            pltpu.VMEM((rows, kv_width + q_width), bf16),
            pltpu.SemaphoreType.DMA((5,)),
            pltpu.SemaphoreType.DMA((WEIGHT_STEPS,)),
            pltpu.SemaphoreType.DMA((WEIGHT_STEPS,)),
            pltpu.SemaphoreType.DMA((WEIGHT_STEPS,)),
            pltpu.SemaphoreType.DMA((3,)),
        ],
        compiler_params=kernel_params(62),
        cost_estimate=cost(2 * rows * width * (kv_width + q_width), 2 * width * (kv_width + q_width)),
        name="project",
    )(
        block_split, lengths, rotary_constants(half), tokens, norm_gain.reshape(1, width),
        key_projection, value_projection, w_query,
    )
    staged, queries, *places = pl.pallas_call(
        stage_kernel,
        out_shape=(
            struct((rows, kv_width), bf16),
            struct((rows, q_width), bf16),
            struct((n, rows), jnp.int32),
            struct((2 * rows, HEAD), jnp.int32),
            struct((2 * rows, HEAD), jnp.int32),
        ),
        in_specs=in_vmem(3),
        out_specs=tuple(in_vmem(5)),
        compiler_params=kernel_params(24),
        cost_estimate=cost(0, 0),
        name="stage",
    )(block_split.reshape(1, n), lengths.reshape(1, -1), both)
    far_queries = swap(queries, n, 1)

    def attend(pieces, side=None):
        arrays = operands(pieces)
        taken = rows if side is None else half
        mine, stats, packed = pl.pallas_call(
            functools.partial(attend_kernel, pieces, side),
            out_shape=(
                struct((taken, q_width), f32),
                struct((taken, HEAD), f32),
                struct((taken, q_width + HEAD), bf16),
            ),
            in_specs=in_vmem(5 + len(arrays)),
            out_specs=tuple(in_vmem(3)),
            compiler_params=kernel_params(32),
            cost_estimate=cost(0, 0),
            name="attend",
        )(*places, queries, far_queries, *arrays)
        return [mine, stats, packed]

    def place_pages(pieces):
        arrays = operands(pieces)
        shape = (2 * rows // PAGE, 2, PAGE, kv_width // 2)
        return pl.pallas_call(
            functools.partial(cache_kernel, pieces),
            out_shape=(struct(shape, bf16),) + (struct((shape[0] // 2,) + shape[1:], bf16),) * 2,
            in_specs=in_smem(2) + in_vmem(len(arrays)),
            out_specs=tuple(in_vmem(1 + 2)),
            compiler_params=kernel_params(32),
            cost_estimate=cost(0, 0),
            name="cache",
        )(block_split, page_slot, *arrays)

    if n == 16:

        def swapped(piece, bits):
            source = lambda shard, i: piece.source_of(shard ^ bits, i)
            return Piece([swap(piece.arrays[0], n, bits)], source)

        own = Piece([kv], at_distance(0))
        second, first, beside = swapped(own, 8), swapped(own, 4), swapped(own, 2)
        first_across = swapped(first, 2)
        second, staged = tied(second, staged)
        own = own.moved([staged])
        third = swapped(second, 4)
        (second, first_across, beside), _ = tied_all([second, first_across, beside], ())
        second_across = swapped(second, 2)
        partials = attend([own, beside, first, second, first_across, third, second_across])
        partials[2] = swap(partials[2], n, 1)
        queries, partials[1] = lax.optimization_barrier((queries, partials[1]))
        remaining = [swapped(third, 2)]
        placed = [own, beside, first, second, first_across, third, second_across] + remaining
    else:
        same = [list(range(c, n, 2)) for c in range(2)]
        gathered = lax.all_gather(kv, "seq", axis=0, tiled=True, axis_index_groups=same)
        remaining = [Piece([gathered], lambda shard, i: 2 * i + shard % 2, n // 2)]
        partials, placed = [], remaining
    leaving = attend(remaining, 1)
    queries, leaving[1] = lax.optimization_barrier((queries, leaving[1]))
    leaving[2] = swap(leaving[2], n, 1)
    staying = attend(remaining, 0)
    leaving[0], staying[1] = lax.optimization_barrier((leaving[0], staying[1]))
    sent = pl.pallas_call(
        leave_kernel,
        out_shape=struct((half, width), bf16),
        in_specs=in_vmem(4 + len(partials)),
        out_specs=in_vmem(1)[0],
        compiler_params=kernel_params(24),
        cost_estimate=cost(0, 0),
        name="leave",
    )(w_out, *partials, *leaving)
    received = lax.ppermute(sent, "req", [(i, (i + 1) % parts) for i in range(parts)])
    staying[2] = swap(staying[2], n, 1)
    placed, (staying[2], sent) = tied_all(placed, (staying[2], sent))
    cache, *other = place_pages(placed)
    kept, cache = pl.pallas_call(
        keep_kernel,
        out_shape=(struct((half, width), f32), struct(cache.shape, bf16)),
        in_specs=in_vmem(6 + 2 + len(partials)),
        out_specs=tuple(in_vmem(2)),
        compiler_params=kernel_params(24),
        cost_estimate=cost(0, 0),
        name="keep",
    )(w_out, tokens, cache, *[swap(x, n, 1) for x in other], *partials, *staying)
    hidden = pl.pallas_call(
        finish_kernel,
        out_shape=struct((half, width), bf16),
        in_specs=in_vmem(2),
        out_specs=in_vmem(1)[0],
        compiler_params=kernel_params(24),
        cost_estimate=cost(0, 0),
        name="finish",
    )(kept, received)
    return hidden, cache


def solution(mesh):
    in_specs = (
        P("seq", None),
        P(),
        P(None, "req"),
        P(None, "req"),
        P(None, "req"),
        P("req", None),
        P(),
        P(),
        P(),
    )
    out_specs = (P(("seq", "req"), None), P("seq", None, None, "req"))
    body = functools.partial(on_device, mesh.shape["seq"], mesh.shape["req"])
    return jax.shard_map(body, mesh=mesh, in_specs=in_specs, out_specs=out_specs, check_vma=False)
```

```python
import functools
import math

import jax
import jax.numpy as jnp
import numpy as np
from jax import lax
from jax.experimental import pallas as pl
from jax.experimental.pallas import tpu as pltpu
from jax.sharding import PartitionSpec as P

HEAD = 128
PAGE = 32
THETA = 1000000.0
EPS = 1e-05
MASKED = -1e30
FLOOR = -1e29
WEIGHT_STEPS = 2
MIB = 1024 * 1024
SCALE = math.log2(math.e) / math.sqrt(HEAD)

f32 = jnp.float32
bf16 = jnp.bfloat16
struct = jax.ShapeDtypeStruct


def in_vmem(count):
    return [pl.BlockSpec(memory_space=pltpu.VMEM)] * count


def in_smem(count):
    return [pl.BlockSpec(memory_space=pltpu.SMEM)] * count


def in_hbm(count):
    return [pl.BlockSpec(memory_space=pltpu.HBM)] * count


def kernel_params(mib):
    return pltpu.CompilerParams(vmem_limit_bytes=mib * MIB)


def cost(flops, moved):
    return pl.CostEstimate(flops=flops, bytes_accessed=moved, transcendentals=0)


def rotary_constants(half):
    exponent = np.arange(HEAD // 2, dtype=np.float64) * (2.0 / HEAD)
    freq = np.tile(THETA**-exponent, 2)[None, :]
    angle = np.arange(half, dtype=np.float64)[:, None] * freq
    rows = [np.cos(angle), np.sin(angle), np.broadcast_to(freq, (8, HEAD))]
    return jnp.asarray(np.concatenate(rows).astype(np.float32))


def blocks_of(block_ref, shard):
    first = block_ref[shard]
    return first, 2 * block_ref.shape[0] - 1 - first


def positions(blocks, half, dim, shape):
    index = lax.broadcasted_iota(jnp.int32, shape, dim)
    offset = blocks[0] * half
    for i, block in enumerate(blocks[1:], 1):
        offset = jnp.where(index >= i * half, (block - i) * half, offset)
    return index + offset


def rotate(u, cosine, signed_sine):
    return u * cosine + pltpu.roll(u, HEAD // 2, 1) * signed_sine


def weight_copies(source, scratch, sems):
    depth = scratch.shape[0] // WEIGHT_STEPS
    return [
        pltpu.make_async_copy(
            source.at[pl.ds(step * depth, depth), :], scratch.at[pl.ds(step * depth, depth), :], sems.at[step]
        )
        for step in range(WEIGHT_STEPS)
    ]


def stepped_dot(left, copies, scratch):
    depth = scratch.shape[0] // WEIGHT_STEPS
    total = None
    for step, copy in enumerate(copies):
        copy.wait()
        rows = slice(step * depth, (step + 1) * depth)
        part = jnp.dot(left[:, rows], scratch[rows, :], preferred_element_type=f32)
        total = part if total is None else total + part
    return total


def rotary_tables(block_ref, len_ref, turn_ref, half):
    prompts = len_ref.shape[0]
    blocks = blocks_of(block_ref, lax.axis_index("seq"))
    starts = [jnp.int32(0)]
    for r in range(prompts - 1):
        starts.append(starts[-1] + len_ref[r])
    count = 2 * prompts
    index = lax.broadcasted_iota(jnp.int32, (count, HEAD), 0)
    base = jnp.zeros((count, HEAD), jnp.int32)
    for k, block in enumerate(blocks):
        for p, start in enumerate(starts):
            base = jnp.where(index == k * prompts + p, block * half - start, base)
    angle = base.astype(f32) * turn_ref[2 * half : 2 * half + 1, :]
    base_cos, base_sin = jnp.cos(angle), jnp.sin(angle)
    row_cos, row_sin = turn_ref[:half, :], turn_ref[half : 2 * half, :]
    row = lax.broadcasted_iota(jnp.int32, (half, HEAD), 0)
    lane = lax.broadcasted_iota(jnp.int32, (half, HEAD), 1)
    cosines, sines = [], []
    for k, block in enumerate(blocks):
        at = k * prompts
        cos, sin = base_cos[at : at + 1], base_sin[at : at + 1]
        for p in range(1, prompts):
            inside = row >= starts[p] - block * half
            cos = jnp.where(inside, base_cos[at + p : at + p + 1], cos)
            sin = jnp.where(inside, base_sin[at + p : at + p + 1], sin)
        cosines.append(row_cos * cos - row_sin * sin)
        sine = row_sin * cos + row_cos * sin
        sines.append(jnp.where(lane < HEAD // 2, -sine, sine))
    return jnp.concatenate(cosines, 0), jnp.concatenate(sines, 0)


def project_kernel(
    block_hbm, len_hbm, turn_hbm, tok_hbm, gain_hbm, wk_hbm, wv_hbm,
    kv_hbm, normed_hbm, turned_hbm,
    block_ref, len_ref, turn_ref, tok_ref, gain_ref, k_weights, v_weights, kv_ref, normed_ref, turned_ref,
    small_sems, k_sems, v_sems, out_sems,
):
    small = [
        pltpu.make_async_copy(source, target, small_sems.at[i])
        for i, (source, target) in enumerate(
            (
                (tok_hbm, tok_ref),
                (block_hbm, block_ref),
                (len_hbm, len_ref),
                (turn_hbm, turn_ref),
                (gain_hbm, gain_ref),
            )
        )
    ]
    k_copies = weight_copies(wk_hbm, k_weights, k_sems)
    v_copies = weight_copies(wv_hbm, v_weights, v_sems)
    for copy in small + k_copies + v_copies:
        copy.start()
    rows = tok_ref.shape[0]
    key_width = wk_hbm.shape[1]
    for copy in small:
        copy.wait()
    wide = tok_ref[...].astype(f32)
    scale = lax.rsqrt(jnp.mean(wide * wide, -1, keepdims=True) + EPS)
    normed = (wide * scale * gain_ref[...]).astype(bf16)
    normed_ref[...] = normed
    writes = [
        pltpu.make_async_copy(source, target, out_sems.at[i])
        for i, (source, target) in enumerate(
            ((normed_ref, normed_hbm), (turned_ref, turned_hbm), (kv_ref, kv_hbm))
        )
    ]
    writes[0].start()
    cosine, sine = rotary_tables(block_ref, len_ref, turn_ref, rows // 2)
    turned_ref[:, :HEAD] = cosine
    turned_ref[:, HEAD:] = sine
    writes[1].start()
    product = stepped_dot(normed, k_copies, k_weights)
    for h in range(key_width // HEAD):
        cols = slice(h * HEAD, (h + 1) * HEAD)
        kv_ref[:, cols] = rotate(product[:, cols], cosine, sine).astype(bf16)
    kv_ref[:, key_width:] = stepped_dot(normed, v_copies, v_weights).astype(bf16)
    writes[2].start()
    for copy in writes:
        copy.wait()


def query_kernel(normed_ref, turned_ref, wq_ref, q_ref):
    product = jnp.dot(normed_ref[...], wq_ref[...], preferred_element_type=f32)
    cosine, sine = turned_ref[:, :HEAD], turned_ref[:, HEAD:]
    for h in range(q_ref.shape[1] // HEAD):
        cols = slice(h * HEAD, (h + 1) * HEAD)
        q_ref[:, cols] = rotate(product[:, cols], cosine, sine).astype(bf16)


def attend_kernel(pieces, side, key_pos_ref, q_pos_ref, q_begin_ref, q_ref, far_ref, *refs):
    pieces, refs = with_refs(pieces, refs)
    shard = lax.axis_index("seq")
    rows, q_width = q_ref.shape
    key_width = pieces[0].arrays[0].shape[1] // 2
    kv_heads = key_width // HEAD
    group = q_width // key_width
    if side is None:
        taken, first = rows, 0
        span = slice(None)
    else:
        part = lax.axis_index("req")
        taken = rows // 2
        first = pl.multiple_of((1 - part if side else part) * taken, taken)
        span = pl.ds(first, taken)
    both = 2 * taken

    def of_both_cores(ref):
        return jnp.concatenate(
            [ref[pl.ds(pl.multiple_of(core * rows + first, taken), taken), :] for core in (0, 1)], 0
        )

    q_pos, q_begin = of_both_cores(q_pos_ref), of_both_cores(q_begin_ref)
    queries = [
        jnp.concatenate(
            [
                ref[span, h * HEAD : (h + 1) * HEAD]
                for h in range(g * group, (g + 1) * group)
                for ref in (q_ref, far_ref)
            ],
            0,
        )
        for g in range(kv_heads)
    ]

    def absorb(state, blocks, sources):
        bias = []
        for source in sources:
            key_pos = key_pos_ref[pl.ds(source, 1), :]
            bias.append(jnp.where((key_pos >= q_begin) & (key_pos <= q_pos), 0.0, MASKED))
        bias = jnp.concatenate(bias, 1)
        bias = jnp.concatenate([bias] * group, 0)
        out = []
        for g in range(kv_heads):
            top, total, acc = state[g]
            keys = jnp.concatenate([b[:, g * HEAD : (g + 1) * HEAD] for b in blocks], 0)
            values = jnp.concatenate(
                [b[:, key_width + g * HEAD : key_width + (g + 1) * HEAD] for b in blocks], 0
            )
            scores = lax.dot_general(
                queries[g], keys, (((1,), (1,)), ((), ())), preferred_element_type=f32
            )
            scores = scores * SCALE + bias
            new_top = jnp.maximum(top, jnp.max(scores, -1, keepdims=True))
            weights = jnp.exp2(scores - new_top)
            factor = jnp.exp2(top - new_top)
            total = total * factor + jnp.sum(weights, -1, keepdims=True)
            acc = acc * factor + jnp.dot(weights.astype(bf16), values, preferred_element_type=f32)
            out.append((new_top, total, acc))
        return tuple(out)

    state = (
        (
            jnp.full((group * both, 1), FLOOR, f32),
            jnp.zeros((group * both, 1), f32),
            jnp.zeros((group * both, HEAD), f32),
        ),
    ) * kv_heads
    if all(piece.count == 1 for piece in pieces):
        for i in range(0, len(pieces), 2):
            pair = pieces[i : i + 2]
            state = absorb(
                state, [p.arrays[0][...] for p in pair], [p.source_of(shard, 0) for p in pair]
            )
    else:
        for piece in pieces:

            def step(i, carried):
                at = pl.multiple_of(i * rows, rows)
                block = piece.arrays[0][pl.ds(at, rows), :]
                return absorb(carried, [block], [piece.source_of(shard, i)])

            state = lax.fori_loop(0, piece.count, step, state)

    mine_ref, stat_ref, packed_ref = refs
    heads = q_width // HEAD
    lane = lax.broadcasted_iota(jnp.int32, (taken, HEAD), 1)
    mine = jnp.zeros((taken, HEAD), f32)
    theirs = jnp.zeros((taken, HEAD), f32)
    for g in range(kv_heads):
        top, total, acc = state[g]
        for j in range(group):
            h = g * group + j
            cols = slice(h * HEAD, (h + 1) * HEAD)
            near = slice(j * both, j * both + taken)
            far = slice(j * both + taken, (j + 1) * both)
            mine_ref[:, cols] = acc[near]
            packed_ref[:, cols] = acc[far].astype(bf16)
            for value, at in ((top, h), (total, heads + h)):
                mine = jnp.where(lane == at, value[near], mine)
                theirs = jnp.where(lane % (2 * heads) == at, value[far], theirs)
    stat_ref[...] = mine
    high = theirs.astype(bf16).astype(f32)
    middle = (theirs - high).astype(bf16).astype(f32)
    low = theirs - high - middle
    third = lane // (2 * heads)
    parts = jnp.where(third == 0, high, jnp.where(third == 1, middle, low))
    packed_ref[:, q_width:] = parts.astype(bf16)


def stage_kernel(block_ref, len_ref, kv_ref, kv_out, key_pos_ref, q_pos_ref, q_begin_ref):
    kv_out[...] = kv_ref[...]
    shards, rows = key_pos_ref.shape
    half = rows // 2
    shard = lax.axis_index("seq")

    def picked(values, mask):
        return jnp.sum(jnp.where(mask, values, 0.0), -1, keepdims=True).astype(jnp.int32)

    def lanes(shape):
        return lax.broadcasted_iota(jnp.int32, shape, 1)

    blocks = block_ref[...].astype(f32)
    square = (shards, shards)
    first = picked(blocks, lanes(square) == lax.broadcasted_iota(jnp.int32, square, 0))
    index = lanes((shards, rows))
    key_pos_ref[...] = index + jnp.where(index < half, first, 2 * shards - 2 - first) * half

    held = []
    for s in (shard, shard ^ 1):
        first = picked(blocks, lanes(block_ref.shape) == s)
        held += [first, 2 * shards - 1 - first]
    q_pos = positions(held, half, 0, q_pos_ref.shape)
    q_pos_ref[...] = q_pos
    lengths = len_ref[...].astype(f32)
    begin = jnp.zeros_like(q_pos)
    for r in range(1, len_ref.shape[1]):
        start = picked(lengths, lanes(len_ref.shape) < r)
        begin = jnp.where(q_pos >= start, start, begin)
    q_begin_ref[...] = begin


def joined_rows(partials, first, half):
    q_width = partials[0].shape[1]
    heads = q_width // HEAD
    part = pl.ds(pl.multiple_of(first, half), half)
    held = []
    for mine_ref, stat_ref, packed_ref in zip(partials[::3], partials[1::3], partials[2::3]):
        span = slice(None) if mine_ref.shape[0] == half else part
        parts = packed_ref[span, q_width:].astype(f32)
        stats = parts
        for t in (1, 2):
            stats = stats + pltpu.roll(parts, HEAD - 2 * heads * t, 1)
        held += [(mine_ref, span, stat_ref[span, :]), (packed_ref, span, stats)]
    top = functools.reduce(jnp.maximum, [stats for _, _, stats in held])
    shares = [jnp.exp2(stats - top) for _, _, stats in held]
    total = sum(
        share * pltpu.roll(stats, HEAD - heads, 1) for share, (_, _, stats) in zip(shares, held)
    )
    shares = [share / total for share in shares]
    context = []
    for h in range(heads):
        cols = slice(h * HEAD, (h + 1) * HEAD)
        context.append(
            sum(
                ref[span, cols].astype(f32) * share[:, h : h + 1]
                for (ref, span, _), share in zip(held, shares)
            ).astype(bf16)
        )
    return jnp.concatenate(context, 1)


def leave_kernel(wo_ref, *refs):
    partials, sent_ref = refs[:-1], refs[-1]
    half = sent_ref.shape[0]
    context = joined_rows(partials, (1 - lax.axis_index("req")) * half, half)
    sent_ref[...] = jnp.dot(context, wo_ref[...], preferred_element_type=f32).astype(bf16)


def keep_kernel(wo_ref, tok_ref, mine_ref, *refs):
    others, partials, (out_ref, cache_ref) = refs[:2], refs[2:-2], refs[-2:]
    share = mine_ref.shape[0] // 2
    for i, other_ref in enumerate(others):
        part = slice(i * share, (i + 1) * share)
        cache_ref[part] = mine_ref[part] + other_ref[...]
    half = out_ref.shape[0]
    first = lax.axis_index("req") * half
    context = joined_rows(partials, first, half)
    residual = tok_ref[pl.ds(pl.multiple_of(first, half), half), :].astype(f32)
    out_ref[...] = jnp.dot(context, wo_ref[...], preferred_element_type=f32) + residual


def finish_kernel(kept_ref, received_ref, hidden_ref):
    hidden_ref[...] = (kept_ref[...] + received_ref[...].astype(f32)).astype(bf16)


def cache_kernel(pieces, block_ref, slot_ref, *refs):
    pieces, (mine_ref, *other_refs) = with_refs(pieces, refs)
    shard = lax.axis_index("seq")
    slots = mine_ref.shape[0]
    key_width = mine_ref.shape[3]
    rows = slots * PAGE // 2
    pages = rows // 2 // PAGE
    for target in (mine_ref, *other_refs):
        target[...] = jnp.zeros_like(target)
    share = slots // len(other_refs)

    def place(ref, at, source):
        for k, block in enumerate(blocks_of(block_ref, source)):
            for j in range(pages):
                slot = slot_ref[block * pages + j]
                holder = slot // slots
                local = slot - holder * slots
                offset = at + (k * pages + j) * PAGE
                if not isinstance(offset, int):
                    offset = pl.multiple_of(offset, PAGE)

                def write(target, at_slot):
                    target[at_slot, 0] = ref[pl.ds(offset, PAGE), :key_width]
                    target[at_slot, 1] = ref[pl.ds(offset, PAGE), key_width:]

                @pl.when(holder == shard)
                def _():
                    write(mine_ref, local)

                for i, target in enumerate(other_refs):

                    @pl.when((holder == shard ^ 1) & (local // share == i))
                    def _():
                        write(target, local - i * share)

    for piece in pieces:
        if piece.count == 1:
            place(piece.arrays[0], 0, piece.source_of(shard, 0))
        else:

            def step(i, carry):
                place(piece.arrays[0], i * rows, piece.source_of(shard, i))
                return carry

            lax.fori_loop(0, piece.count, step, 0)


def tied_all(pieces, other):
    arrays, other = lax.optimization_barrier((operands(pieces), other))
    return with_refs(pieces, arrays)[0], other


def tied(piece, other):
    (piece,), other = tied_all([piece], other)
    return piece, other


def swap(x, n, bit):
    return lax.ppermute(x, "seq", [(i, i ^ bit) for i in range(n)])


class Piece:
    def __init__(self, arrays, source_of, count=1):
        self.arrays, self.source_of, self.count = arrays, source_of, count

    def moved(self, arrays):
        return Piece(arrays, self.source_of, self.count)


def operands(pieces):
    return [x for piece in pieces for x in piece.arrays]


def with_refs(pieces, refs):
    out = []
    for piece in pieces:
        taken, refs = refs[: len(piece.arrays)], refs[len(piece.arrays) :]
        out.append(piece.moved(taken))
    return out, refs


def at_distance(bits):
    return lambda shard, i: shard ^ bits


def move(x, pairs):
    return lax.ppermute(x, "seq", pairs)


def on_device(
    n, parts, tokens, norm_gain, w_query, key_projection, value_projection, w_out, lengths, block_split, page_slot,
):
    rows, width = tokens.shape
    half = rows // 2
    q_width = w_query.shape[1]
    kv_width = key_projection.shape[1] + value_projection.shape[1]
    kv, normed, turned = pl.pallas_call(
        project_kernel,
        out_shape=(
            struct((rows, kv_width), bf16),
            struct((rows, width), bf16),
            struct((rows, 2 * HEAD), f32),
        ),
        in_specs=in_hbm(7),
        out_specs=tuple(in_hbm(3)),
        scratch_shapes=[
            pltpu.SMEM(block_split.shape, jnp.int32),
            pltpu.SMEM(lengths.shape, jnp.int32),
            pltpu.VMEM((2 * half + 8, HEAD), f32),
            pltpu.VMEM((rows, width), bf16),
            pltpu.VMEM((1, width), f32),
            pltpu.VMEM(key_projection.shape, bf16),
            pltpu.VMEM(value_projection.shape, bf16),
            pltpu.VMEM((rows, kv_width), bf16),
            pltpu.VMEM((rows, width), bf16),
            pltpu.VMEM((rows, 2 * HEAD), f32),
            pltpu.SemaphoreType.DMA((5,)),
            pltpu.SemaphoreType.DMA((WEIGHT_STEPS,)),
            pltpu.SemaphoreType.DMA((WEIGHT_STEPS,)),
            pltpu.SemaphoreType.DMA((3,)),
        ],
        compiler_params=kernel_params(62),
        cost_estimate=cost(0, 0),
        name="project",
    )(
        block_split, lengths, rotary_constants(half), tokens, norm_gain.reshape(1, width),
        key_projection, value_projection,
    )
    staged, *places = pl.pallas_call(
        stage_kernel,
        out_shape=(
            struct((rows, kv_width), bf16),
            struct((n, rows), jnp.int32),
            struct((2 * rows, HEAD), jnp.int32),
            struct((2 * rows, HEAD), jnp.int32),
        ),
        in_specs=in_vmem(3),
        out_specs=tuple(in_vmem(4)),
        compiler_params=kernel_params(24),
        cost_estimate=cost(10**9, 10**7),
        name="stage",
    )(block_split.reshape(1, n), lengths.reshape(1, -1), kv)

    def project_queries(normed):
        queries = pl.pallas_call(
            query_kernel,
            out_shape=struct((rows, q_width), bf16),
            in_specs=in_vmem(3),
            out_specs=in_vmem(1)[0],
            compiler_params=kernel_params(24),
            cost_estimate=cost(0, 0),
            name="query",
        )(normed, turned, w_query)
        return queries, swap(queries, n, 1)

    def attend(queries, far_queries, pieces, side=None):
        arrays = operands(pieces)
        taken = rows if side is None else half
        mine, stats, packed = pl.pallas_call(
            functools.partial(attend_kernel, pieces, side),
            out_shape=(
                struct((taken, q_width), f32),
                struct((taken, HEAD), f32),
                struct((taken, q_width + HEAD), bf16),
            ),
            in_specs=in_vmem(5 + len(arrays)),
            out_specs=tuple(in_vmem(3)),
            compiler_params=kernel_params(32),
            cost_estimate=cost(0, 0),
            name="attend",
        )(*places, queries, far_queries, *arrays)
        return [mine, stats, packed]

    def place_pages(pieces):
        arrays = operands(pieces)
        shape = (2 * rows // PAGE, 2, PAGE, kv_width // 2)
        return pl.pallas_call(
            functools.partial(cache_kernel, pieces),
            out_shape=(struct(shape, bf16),) + (struct((shape[0] // 2,) + shape[1:], bf16),) * 2,
            in_specs=in_smem(2) + in_vmem(len(arrays)),
            out_specs=tuple(in_vmem(1 + 2)),
            compiler_params=kernel_params(32),
            cost_estimate=cost(0, 0),
            name="cache",
        )(block_split, page_slot, *arrays)

    if n == 16:

        def swapped(piece, bits):
            source = lambda shard, i: piece.source_of(shard ^ bits, i)
            return Piece([swap(piece.arrays[0], n, bits)], source)

        own = Piece([kv], at_distance(0))
        second, first, beside = swapped(own, 8), swapped(own, 4), swapped(own, 2)
        first_across = swapped(first, 2)
        second, staged = tied(second, staged)
        own = own.moved([staged])
        third = swapped(second, 4)
        second, normed = tied(second, normed)
        (second, first_across, beside), _ = tied_all([second, first_across, beside], ())
        queries, far_queries = project_queries(normed)
        third, queries = tied(third, queries)
        early = [own, beside, first, second, first_across, third]
        partials = attend(queries, far_queries, early)
        partials[2] = swap(partials[2], n, 1)
        queries, partials[1] = lax.optimization_barrier((queries, partials[1]))
        remaining = [swapped(second, 2), swapped(third, 2)]
        placed = early + remaining
    else:
        same = [list(range(c, n, 2)) for c in range(2)]
        gathered = lax.all_gather(kv, "seq", axis=0, tiled=True, axis_index_groups=same)
        remaining = [Piece([gathered], lambda shard, i: 2 * i + shard % 2, n // 2)]
        partials, placed = [], remaining
        queries, far_queries = project_queries(normed)
    leaving = attend(queries, far_queries, remaining, 1)
    queries, leaving[1] = lax.optimization_barrier((queries, leaving[1]))
    leaving[2] = swap(leaving[2], n, 1)
    staying = attend(queries, far_queries, remaining, 0)
    leaving[0], staying[1] = lax.optimization_barrier((leaving[0], staying[1]))
    sent = pl.pallas_call(
        leave_kernel,
        out_shape=struct((half, width), bf16),
        in_specs=in_vmem(4 + len(partials)),
        out_specs=in_vmem(1)[0],
        compiler_params=kernel_params(24),
        cost_estimate=cost(0, 0),
        name="leave",
    )(w_out, *partials, *leaving)
    received = lax.ppermute(sent, "req", [(i, (i + 1) % parts) for i in range(parts)])
    staying[2] = swap(staying[2], n, 1)
    placed, (staying[2], sent) = tied_all(placed, (staying[2], sent))
    cache, *other = place_pages(placed)
    kept, cache = pl.pallas_call(
        keep_kernel,
        out_shape=(struct((half, width), f32), struct(cache.shape, bf16)),
        in_specs=in_vmem(6 + 2 + len(partials)),
        out_specs=tuple(in_vmem(2)),
        compiler_params=kernel_params(24),
        cost_estimate=cost(0, 0),
        name="keep",
    )(w_out, tokens, cache, *[swap(x, n, 1) for x in other], *partials, *staying)
    hidden = pl.pallas_call(
        finish_kernel,
        out_shape=struct((half, width), bf16),
        in_specs=in_vmem(2),
        out_specs=in_vmem(1)[0],
        compiler_params=kernel_params(24),
        cost_estimate=cost(0, 0),
        name="finish",
    )(kept, received)
    return hidden, cache


def solution(mesh):
    in_specs = (
        P("seq", None),
        P(),
        P(None, "req"),
        P(None, "req"),
        P(None, "req"),
        P("req", None),
        P(),
        P(),
        P(),
    )
    out_specs = (P(("seq", "req"), None), P("seq", None, None, "req"))
    body = functools.partial(on_device, mesh.shape["seq"], mesh.shape["req"])
    return jax.shard_map(body, mesh=mesh, in_specs=in_specs, out_specs=out_specs, check_vma=False)
```

```python
import functools
import math

import jax
import jax.numpy as jnp
import numpy as np
from jax import lax
from jax.experimental import pallas as pl
from jax.experimental.pallas import tpu as pltpu
from jax.sharding import PartitionSpec as P

HEAD = 128
PAGE = 32
THETA = 1000000.0
EPS = 1e-05
MASKED = -1e30
FLOOR = -1e29
WEIGHT_STEPS = 2
MIB = 1024 * 1024
SCALE = math.log2(math.e) / math.sqrt(HEAD)

f32 = jnp.float32
bf16 = jnp.bfloat16
struct = jax.ShapeDtypeStruct


def in_vmem(count):
    return [pl.BlockSpec(memory_space=pltpu.VMEM)] * count


def in_smem(count):
    return [pl.BlockSpec(memory_space=pltpu.SMEM)] * count


def in_hbm(count):
    return [pl.BlockSpec(memory_space=pltpu.HBM)] * count


def kernel_params(mib):
    return pltpu.CompilerParams(vmem_limit_bytes=mib * MIB)


def cost(flops, moved):
    return pl.CostEstimate(flops=flops, bytes_accessed=moved, transcendentals=0)


def rotary_constants(half):
    exponent = np.arange(HEAD // 2, dtype=np.float64) * (2.0 / HEAD)
    freq = np.tile(THETA**-exponent, 2)[None, :]
    angle = np.arange(half, dtype=np.float64)[:, None] * freq
    rows = [np.cos(angle), np.sin(angle), np.broadcast_to(freq, (8, HEAD))]
    return jnp.asarray(np.concatenate(rows).astype(np.float32))


def blocks_of(block_ref, shard):
    first = block_ref[shard]
    return first, 2 * block_ref.shape[0] - 1 - first


def positions(blocks, half, dim, shape):
    index = lax.broadcasted_iota(jnp.int32, shape, dim)
    offset = blocks[0] * half
    for i, block in enumerate(blocks[1:], 1):
        offset = jnp.where(index >= i * half, (block - i) * half, offset)
    return index + offset


def rotate(u, cosine, signed_sine):
    return u * cosine + pltpu.roll(u, HEAD // 2, 1) * signed_sine


def weight_copies(source, scratch, sems):
    depth = scratch.shape[0] // WEIGHT_STEPS
    return [
        pltpu.make_async_copy(
            source.at[pl.ds(step * depth, depth), :], scratch.at[pl.ds(step * depth, depth), :], sems.at[step]
        )
        for step in range(WEIGHT_STEPS)
    ]


def stepped_dot(left, copies, scratch):
    depth = scratch.shape[0] // WEIGHT_STEPS
    total = None
    for step, copy in enumerate(copies):
        copy.wait()
        rows = slice(step * depth, (step + 1) * depth)
        part = jnp.dot(left[:, rows], scratch[rows, :], preferred_element_type=f32)
        total = part if total is None else total + part
    return total


def rotary_tables(block_ref, len_ref, turn_ref, half):
    prompts = len_ref.shape[0]
    blocks = blocks_of(block_ref, lax.axis_index("seq"))
    starts = [jnp.int32(0)]
    for r in range(prompts - 1):
        starts.append(starts[-1] + len_ref[r])
    count = 2 * prompts
    index = lax.broadcasted_iota(jnp.int32, (count, HEAD), 0)
    base = jnp.zeros((count, HEAD), jnp.int32)
    for k, block in enumerate(blocks):
        for p, start in enumerate(starts):
            base = jnp.where(index == k * prompts + p, block * half - start, base)
    angle = base.astype(f32) * turn_ref[2 * half : 2 * half + 1, :]
    base_cos, base_sin = jnp.cos(angle), jnp.sin(angle)
    row_cos, row_sin = turn_ref[:half, :], turn_ref[half : 2 * half, :]
    row = lax.broadcasted_iota(jnp.int32, (half, HEAD), 0)
    lane = lax.broadcasted_iota(jnp.int32, (half, HEAD), 1)
    cosines, sines = [], []
    for k, block in enumerate(blocks):
        at = k * prompts
        cos, sin = base_cos[at : at + 1], base_sin[at : at + 1]
        for p in range(1, prompts):
            inside = row >= starts[p] - block * half
            cos = jnp.where(inside, base_cos[at + p : at + p + 1], cos)
            sin = jnp.where(inside, base_sin[at + p : at + p + 1], sin)
        cosines.append(row_cos * cos - row_sin * sin)
        sine = row_sin * cos + row_cos * sin
        sines.append(jnp.where(lane < HEAD // 2, -sine, sine))
    return jnp.concatenate(cosines, 0), jnp.concatenate(sines, 0)


def project_kernel(
    block_hbm, len_hbm, turn_hbm, tok_hbm, gain_hbm, wk_hbm, wv_hbm,
    kv_hbm, normed_hbm, turned_hbm,
    block_ref, len_ref, turn_ref, tok_ref, gain_ref, k_weights, v_weights, kv_ref, normed_ref, turned_ref,
    small_sems, k_sems, v_sems, out_sems,
):
    small = [
        pltpu.make_async_copy(source, target, small_sems.at[i])
        for i, (source, target) in enumerate(
            (
                (tok_hbm, tok_ref),
                (block_hbm, block_ref),
                (len_hbm, len_ref),
                (turn_hbm, turn_ref),
                (gain_hbm, gain_ref),
            )
        )
    ]
    k_copies = weight_copies(wk_hbm, k_weights, k_sems)
    v_copies = weight_copies(wv_hbm, v_weights, v_sems)
    for copy in small + k_copies + v_copies:
        copy.start()
    rows = tok_ref.shape[0]
    key_width = wk_hbm.shape[1]
    for copy in small:
        copy.wait()
    wide = tok_ref[...].astype(f32)
    scale = lax.rsqrt(jnp.mean(wide * wide, -1, keepdims=True) + EPS)
    normed = (wide * scale * gain_ref[...]).astype(bf16)
    normed_ref[...] = normed
    writes = [
        pltpu.make_async_copy(source, target, out_sems.at[i])
        for i, (source, target) in enumerate(
            ((normed_ref, normed_hbm), (turned_ref, turned_hbm), (kv_ref, kv_hbm))
        )
    ]
    writes[0].start()
    cosine, sine = rotary_tables(block_ref, len_ref, turn_ref, rows // 2)
    turned_ref[:, :HEAD] = cosine
    turned_ref[:, HEAD:] = sine
    writes[1].start()
    product = stepped_dot(normed, k_copies, k_weights)
    for h in range(key_width // HEAD):
        cols = slice(h * HEAD, (h + 1) * HEAD)
        kv_ref[:, cols] = rotate(product[:, cols], cosine, sine).astype(bf16)
    kv_ref[:, key_width:] = stepped_dot(normed, v_copies, v_weights).astype(bf16)
    writes[2].start()
    for copy in writes:
        copy.wait()


def query_kernel(normed_ref, turned_ref, wq_ref, q_ref):
    product = jnp.dot(normed_ref[...], wq_ref[...], preferred_element_type=f32)
    cosine, sine = turned_ref[:, :HEAD], turned_ref[:, HEAD:]
    for h in range(q_ref.shape[1] // HEAD):
        cols = slice(h * HEAD, (h + 1) * HEAD)
        q_ref[:, cols] = rotate(product[:, cols], cosine, sine).astype(bf16)


def attend_kernel(pieces, side, key_pos_ref, q_pos_ref, q_begin_ref, q_ref, far_ref, *refs):
    pieces, refs = with_refs(pieces, refs)
    shard = lax.axis_index("seq")
    rows, q_width = q_ref.shape
    key_width = pieces[0].arrays[0].shape[1] // 2
    kv_heads = key_width // HEAD
    group = q_width // key_width
    if side is None:
        taken, first = rows, 0
        span = slice(None)
    else:
        part = lax.axis_index("req")
        taken = rows // 2
        first = pl.multiple_of((1 - part if side else part) * taken, taken)
        span = pl.ds(first, taken)
    both = 2 * taken

    def of_both_cores(ref):
        return jnp.concatenate(
            [ref[pl.ds(pl.multiple_of(core * rows + first, taken), taken), :] for core in (0, 1)], 0
        )

    q_pos, q_begin = of_both_cores(q_pos_ref), of_both_cores(q_begin_ref)
    queries = [
        jnp.concatenate(
            [
                ref[span, h * HEAD : (h + 1) * HEAD]
                for h in range(g * group, (g + 1) * group)
                for ref in (q_ref, far_ref)
            ],
            0,
        )
        for g in range(kv_heads)
    ]

    def absorb(state, blocks, sources):
        bias = []
        for source in sources:
            key_pos = key_pos_ref[pl.ds(source, 1), :]
            bias.append(jnp.where((key_pos >= q_begin) & (key_pos <= q_pos), 0.0, MASKED))
        bias = jnp.concatenate(bias, 1)
        bias = jnp.concatenate([bias] * group, 0)
        out = []
        for g in range(kv_heads):
            top, total, acc = state[g]
            keys = jnp.concatenate([b[:, g * HEAD : (g + 1) * HEAD] for b in blocks], 0)
            values = jnp.concatenate(
                [b[:, key_width + g * HEAD : key_width + (g + 1) * HEAD] for b in blocks], 0
            )
            scores = lax.dot_general(
                queries[g], keys, (((1,), (1,)), ((), ())), preferred_element_type=f32
            )
            scores = scores * SCALE + bias
            new_top = jnp.maximum(top, jnp.max(scores, -1, keepdims=True))
            weights = jnp.exp2(scores - new_top)
            factor = jnp.exp2(top - new_top)
            total = total * factor + jnp.sum(weights, -1, keepdims=True)
            acc = acc * factor + jnp.dot(weights.astype(bf16), values, preferred_element_type=f32)
            out.append((new_top, total, acc))
        return tuple(out)

    state = (
        (
            jnp.full((group * both, 1), FLOOR, f32),
            jnp.zeros((group * both, 1), f32),
            jnp.zeros((group * both, HEAD), f32),
        ),
    ) * kv_heads
    if all(piece.count == 1 for piece in pieces):
        for i in range(0, len(pieces), 2):
            pair = pieces[i : i + 2]
            state = absorb(
                state, [p.arrays[0][...] for p in pair], [p.source_of(shard, 0) for p in pair]
            )
    else:
        for piece in pieces:

            def step(i, carried):
                at = pl.multiple_of(i * rows, rows)
                block = piece.arrays[0][pl.ds(at, rows), :]
                return absorb(carried, [block], [piece.source_of(shard, i)])

            state = lax.fori_loop(0, piece.count, step, state)

    mine_ref, stat_ref, packed_ref = refs
    heads = q_width // HEAD
    lane = lax.broadcasted_iota(jnp.int32, (taken, HEAD), 1)
    mine = jnp.zeros((taken, HEAD), f32)
    theirs = jnp.zeros((taken, HEAD), f32)
    for g in range(kv_heads):
        top, total, acc = state[g]
        for j in range(group):
            h = g * group + j
            cols = slice(h * HEAD, (h + 1) * HEAD)
            near = slice(j * both, j * both + taken)
            far = slice(j * both + taken, (j + 1) * both)
            mine_ref[:, cols] = acc[near]
            packed_ref[:, cols] = acc[far].astype(bf16)
            for value, at in ((top, h), (total, heads + h)):
                mine = jnp.where(lane == at, value[near], mine)
                theirs = jnp.where(lane % (2 * heads) == at, value[far], theirs)
    stat_ref[...] = mine
    high = theirs.astype(bf16).astype(f32)
    middle = (theirs - high).astype(bf16).astype(f32)
    low = theirs - high - middle
    third = lane // (2 * heads)
    parts = jnp.where(third == 0, high, jnp.where(third == 1, middle, low))
    packed_ref[:, q_width:] = parts.astype(bf16)


def stage_kernel(block_ref, len_ref, kv_ref, kv_out, key_pos_ref, q_pos_ref, q_begin_ref):
    kv_out[...] = kv_ref[...]
    shards, rows = key_pos_ref.shape
    half = rows // 2
    shard = lax.axis_index("seq")

    def picked(values, mask):
        return jnp.sum(jnp.where(mask, values, 0.0), -1, keepdims=True).astype(jnp.int32)

    def lanes(shape):
        return lax.broadcasted_iota(jnp.int32, shape, 1)

    blocks = block_ref[...].astype(f32)
    square = (shards, shards)
    first = picked(blocks, lanes(square) == lax.broadcasted_iota(jnp.int32, square, 0))
    index = lanes((shards, rows))
    key_pos_ref[...] = index + jnp.where(index < half, first, 2 * shards - 2 - first) * half

    held = []
    for s in (shard, shard ^ 1):
        first = picked(blocks, lanes(block_ref.shape) == s)
        held += [first, 2 * shards - 1 - first]
    q_pos = positions(held, half, 0, q_pos_ref.shape)
    q_pos_ref[...] = q_pos
    lengths = len_ref[...].astype(f32)
    begin = jnp.zeros_like(q_pos)
    for r in range(1, len_ref.shape[1]):
        start = picked(lengths, lanes(len_ref.shape) < r)
        begin = jnp.where(q_pos >= start, start, begin)
    q_begin_ref[...] = begin


def joined_rows(partials, first, half):
    q_width = partials[0].shape[1]
    heads = q_width // HEAD
    part = pl.ds(pl.multiple_of(first, half), half)
    held = []
    for mine_ref, stat_ref, packed_ref in zip(partials[::3], partials[1::3], partials[2::3]):
        span = slice(None) if mine_ref.shape[0] == half else part
        parts = packed_ref[span, q_width:].astype(f32)
        stats = parts
        for t in (1, 2):
            stats = stats + pltpu.roll(parts, HEAD - 2 * heads * t, 1)
        held += [(mine_ref, span, stat_ref[span, :]), (packed_ref, span, stats)]
    top = functools.reduce(jnp.maximum, [stats for _, _, stats in held])
    shares = [jnp.exp2(stats - top) for _, _, stats in held]
    total = sum(
        share * pltpu.roll(stats, HEAD - heads, 1) for share, (_, _, stats) in zip(shares, held)
    )
    shares = [share / total for share in shares]
    context = []
    for h in range(heads):
        cols = slice(h * HEAD, (h + 1) * HEAD)
        context.append(
            sum(
                ref[span, cols].astype(f32) * share[:, h : h + 1]
                for (ref, span, _), share in zip(held, shares)
            ).astype(bf16)
        )
    return jnp.concatenate(context, 1)


def leave_kernel(wo_ref, *refs):
    partials, sent_ref = refs[:-1], refs[-1]
    half = sent_ref.shape[0]
    context = joined_rows(partials, (1 - lax.axis_index("req")) * half, half)
    sent_ref[...] = jnp.dot(context, wo_ref[...], preferred_element_type=f32).astype(bf16)


def keep_kernel(wo_ref, tok_ref, mine_ref, *refs):
    others, partials, (out_ref, cache_ref) = refs[:2], refs[2:-2], refs[-2:]
    share = mine_ref.shape[0] // 2
    for i, other_ref in enumerate(others):
        part = slice(i * share, (i + 1) * share)
        cache_ref[part] = mine_ref[part] + other_ref[...]
    half = out_ref.shape[0]
    first = lax.axis_index("req") * half
    context = joined_rows(partials, first, half)
    residual = tok_ref[pl.ds(pl.multiple_of(first, half), half), :].astype(f32)
    out_ref[...] = jnp.dot(context, wo_ref[...], preferred_element_type=f32) + residual


def finish_kernel(kept_ref, received_ref, hidden_ref):
    hidden_ref[...] = (kept_ref[...] + received_ref[...].astype(f32)).astype(bf16)


def cache_kernel(pieces, block_ref, slot_ref, *refs):
    pieces, (mine_ref, *other_refs) = with_refs(pieces, refs)
    shard = lax.axis_index("seq")
    slots = mine_ref.shape[0]
    key_width = mine_ref.shape[3]
    rows = slots * PAGE // 2
    pages = rows // 2 // PAGE
    for target in (mine_ref, *other_refs):
        target[...] = jnp.zeros_like(target)
    share = slots // len(other_refs)

    def place(ref, at, source):
        for k, block in enumerate(blocks_of(block_ref, source)):
            for j in range(pages):
                slot = slot_ref[block * pages + j]
                holder = slot // slots
                local = slot - holder * slots
                offset = at + (k * pages + j) * PAGE
                if not isinstance(offset, int):
                    offset = pl.multiple_of(offset, PAGE)

                def write(target, at_slot):
                    target[at_slot, 0] = ref[pl.ds(offset, PAGE), :key_width]
                    target[at_slot, 1] = ref[pl.ds(offset, PAGE), key_width:]

                @pl.when(holder == shard)
                def _():
                    write(mine_ref, local)

                for i, target in enumerate(other_refs):

                    @pl.when((holder == shard ^ 1) & (local // share == i))
                    def _():
                        write(target, local - i * share)

    for piece in pieces:
        if piece.count == 1:
            place(piece.arrays[0], 0, piece.source_of(shard, 0))
        else:

            def step(i, carry):
                place(piece.arrays[0], i * rows, piece.source_of(shard, i))
                return carry

            lax.fori_loop(0, piece.count, step, 0)


def tied_all(pieces, other):
    arrays, other = lax.optimization_barrier((operands(pieces), other))
    return with_refs(pieces, arrays)[0], other


def tied(piece, other):
    (piece,), other = tied_all([piece], other)
    return piece, other


def swap(x, n, bit):
    return lax.ppermute(x, "seq", [(i, i ^ bit) for i in range(n)])


class Piece:
    def __init__(self, arrays, source_of, count=1):
        self.arrays, self.source_of, self.count = arrays, source_of, count

    def moved(self, arrays):
        return Piece(arrays, self.source_of, self.count)


def operands(pieces):
    return [x for piece in pieces for x in piece.arrays]


def with_refs(pieces, refs):
    out = []
    for piece in pieces:
        taken, refs = refs[: len(piece.arrays)], refs[len(piece.arrays) :]
        out.append(piece.moved(taken))
    return out, refs


def at_distance(bits):
    return lambda shard, i: shard ^ bits


def move(x, pairs):
    return lax.ppermute(x, "seq", pairs)


def on_device(
    n, parts, tokens, norm_gain, w_query, key_projection, value_projection, w_out, lengths, block_split, page_slot,
):
    rows, width = tokens.shape
    half = rows // 2
    q_width = w_query.shape[1]
    kv_width = key_projection.shape[1] + value_projection.shape[1]
    kv, normed, turned = pl.pallas_call(
        project_kernel,
        out_shape=(
            struct((rows, kv_width), bf16),
            struct((rows, width), bf16),
            struct((rows, 2 * HEAD), f32),
        ),
        in_specs=in_hbm(7),
        out_specs=tuple(in_hbm(3)),
        scratch_shapes=[
            pltpu.SMEM(block_split.shape, jnp.int32),
            pltpu.SMEM(lengths.shape, jnp.int32),
            pltpu.VMEM((2 * half + 8, HEAD), f32),
            pltpu.VMEM((rows, width), bf16),
            pltpu.VMEM((1, width), f32),
            pltpu.VMEM(key_projection.shape, bf16),
            pltpu.VMEM(value_projection.shape, bf16),
            pltpu.VMEM((rows, kv_width), bf16),
            pltpu.VMEM((rows, width), bf16),
            pltpu.VMEM((rows, 2 * HEAD), f32),
            pltpu.SemaphoreType.DMA((5,)),
            pltpu.SemaphoreType.DMA((WEIGHT_STEPS,)),
            pltpu.SemaphoreType.DMA((WEIGHT_STEPS,)),
            pltpu.SemaphoreType.DMA((3,)),
        ],
        compiler_params=kernel_params(62),
        cost_estimate=cost(0, 0),
        name="project",
    )(
        block_split, lengths, rotary_constants(half), tokens, norm_gain.reshape(1, width),
        key_projection, value_projection,
    )
    staged, *places = pl.pallas_call(
        stage_kernel,
        out_shape=(
            struct((rows, kv_width), bf16),
            struct((n, rows), jnp.int32),
            struct((2 * rows, HEAD), jnp.int32),
            struct((2 * rows, HEAD), jnp.int32),
        ),
        in_specs=in_vmem(3),
        out_specs=tuple(in_vmem(4)),
        compiler_params=kernel_params(24),
        cost_estimate=cost(10**9, 10**7),
        name="stage",
    )(block_split.reshape(1, n), lengths.reshape(1, -1), kv)

    def project_queries(normed):
        queries = pl.pallas_call(
            query_kernel,
            out_shape=struct((rows, q_width), bf16),
            in_specs=in_vmem(3),
            out_specs=in_vmem(1)[0],
            compiler_params=kernel_params(24),
            cost_estimate=cost(0, 0),
            name="query",
        )(normed, turned, w_query)
        return queries, swap(queries, n, 1)

    def attend(queries, far_queries, pieces, side=None):
        arrays = operands(pieces)
        taken = rows if side is None else half
        mine, stats, packed = pl.pallas_call(
            functools.partial(attend_kernel, pieces, side),
            out_shape=(
                struct((taken, q_width), f32),
                struct((taken, HEAD), f32),
                struct((taken, q_width + HEAD), bf16),
            ),
            in_specs=in_vmem(5 + len(arrays)),
            out_specs=tuple(in_vmem(3)),
            compiler_params=kernel_params(32),
            cost_estimate=cost(0, 0),
            name="attend",
        )(*places, queries, far_queries, *arrays)
        return [mine, stats, packed]

    def place_pages(pieces):
        arrays = operands(pieces)
        shape = (2 * rows // PAGE, 2, PAGE, kv_width // 2)
        return pl.pallas_call(
            functools.partial(cache_kernel, pieces),
            out_shape=(struct(shape, bf16),) + (struct((shape[0] // 2,) + shape[1:], bf16),) * 2,
            in_specs=in_smem(2) + in_vmem(len(arrays)),
            out_specs=tuple(in_vmem(1 + 2)),
            compiler_params=kernel_params(32),
            cost_estimate=cost(0, 0),
            name="cache",
        )(block_split, page_slot, *arrays)

    if n == 16:

        def swapped(piece, bits):
            source = lambda shard, i: piece.source_of(shard ^ bits, i)
            return Piece([swap(piece.arrays[0], n, bits)], source)

        own = Piece([kv], at_distance(0))
        second, first, beside = swapped(own, 8), swapped(own, 4), swapped(own, 2)
        first_across = swapped(first, 2)
        second, staged = tied(second, staged)
        own = own.moved([staged])
        third = swapped(second, 4)
        last = swapped(second, 6)
        second, normed = tied(second, normed)
        (second, first_across, beside), _ = tied_all([second, first_across, beside], ())
        queries, far_queries = project_queries(normed)
        early = [own, beside, first, second, first_across, last]
        partials = attend(queries, far_queries, early)
        partials[2] = swap(partials[2], n, 1)
        queries, partials[1] = lax.optimization_barrier((queries, partials[1]))
        remaining = [third, swapped(second, 2)]
        placed = early + remaining
    else:
        same = [list(range(c, n, 2)) for c in range(2)]
        gathered = lax.all_gather(kv, "seq", axis=0, tiled=True, axis_index_groups=same)
        remaining = [Piece([gathered], lambda shard, i: 2 * i + shard % 2, n // 2)]
        partials, placed = [], remaining
        queries, far_queries = project_queries(normed)
    leaving = attend(queries, far_queries, remaining, 1)
    queries, leaving[1] = lax.optimization_barrier((queries, leaving[1]))
    leaving[2] = swap(leaving[2], n, 1)
    staying = attend(queries, far_queries, remaining, 0)
    leaving[0], staying[1] = lax.optimization_barrier((leaving[0], staying[1]))
    sent = pl.pallas_call(
        leave_kernel,
        out_shape=struct((half, width), bf16),
        in_specs=in_vmem(4 + len(partials)),
        out_specs=in_vmem(1)[0],
        compiler_params=kernel_params(24),
        cost_estimate=cost(0, 0),
        name="leave",
    )(w_out, *partials, *leaving)
    received = lax.ppermute(sent, "req", [(i, (i + 1) % parts) for i in range(parts)])
    staying[2] = swap(staying[2], n, 1)
    placed, (staying[2], sent) = tied_all(placed, (staying[2], sent))
    cache, *other = place_pages(placed)
    kept, cache = pl.pallas_call(
        keep_kernel,
        out_shape=(struct((half, width), f32), struct(cache.shape, bf16)),
        in_specs=in_vmem(6 + 2 + len(partials)),
        out_specs=tuple(in_vmem(2)),
        compiler_params=kernel_params(24),
        cost_estimate=cost(0, 0),
        name="keep",
    )(w_out, tokens, cache, *[swap(x, n, 1) for x in other], *partials, *staying)
    hidden = pl.pallas_call(
        finish_kernel,
        out_shape=struct((half, width), bf16),
        in_specs=in_vmem(2),
        out_specs=in_vmem(1)[0],
        compiler_params=kernel_params(24),
        cost_estimate=cost(0, 0),
        name="finish",
    )(kept, received)
    return hidden, cache


def solution(mesh):
    in_specs = (
        P("seq", None),
        P(),
        P(None, "req"),
        P(None, "req"),
        P(None, "req"),
        P("req", None),
        P(),
        P(),
        P(),
    )
    out_specs = (P(("seq", "req"), None), P("seq", None, None, "req"))
    body = functools.partial(on_device, mesh.shape["seq"], mesh.shape["req"])
    return jax.shard_map(body, mesh=mesh, in_specs=in_specs, out_specs=out_specs, check_vma=False)
```

```python
import functools
import math

import jax
import jax.numpy as jnp
import numpy as np
from jax import lax
from jax.experimental import pallas as pl
from jax.experimental.pallas import tpu as pltpu
from jax.sharding import PartitionSpec as P

HEAD = 128
PAGE = 32
THETA = 1000000.0
EPS = 1e-05
MASKED = -1e30
FLOOR = -1e29
WEIGHT_STEPS = 2
MIB = 1024 * 1024
SCALE = math.log2(math.e) / math.sqrt(HEAD)

f32 = jnp.float32
bf16 = jnp.bfloat16
struct = jax.ShapeDtypeStruct


def in_vmem(count):
    return [pl.BlockSpec(memory_space=pltpu.VMEM)] * count


def in_smem(count):
    return [pl.BlockSpec(memory_space=pltpu.SMEM)] * count


def in_hbm(count):
    return [pl.BlockSpec(memory_space=pltpu.HBM)] * count


def kernel_params(mib):
    return pltpu.CompilerParams(vmem_limit_bytes=mib * MIB)


def cost(flops, moved):
    return pl.CostEstimate(flops=flops, bytes_accessed=moved, transcendentals=0)


def rotary_constants(half):
    exponent = np.arange(HEAD // 2, dtype=np.float64) * (2.0 / HEAD)
    freq = np.tile(THETA**-exponent, 2)[None, :]
    angle = np.arange(half, dtype=np.float64)[:, None] * freq
    rows = [np.cos(angle), np.sin(angle), np.broadcast_to(freq, (8, HEAD))]
    return jnp.asarray(np.concatenate(rows).astype(np.float32))


def blocks_of(block_ref, shard):
    first = block_ref[shard]
    return first, 2 * block_ref.shape[0] - 1 - first


def positions(blocks, half, dim, shape):
    index = lax.broadcasted_iota(jnp.int32, shape, dim)
    offset = blocks[0] * half
    for i, block in enumerate(blocks[1:], 1):
        offset = jnp.where(index >= i * half, (block - i) * half, offset)
    return index + offset


def rotate(u, cosine, signed_sine):
    return u * cosine + pltpu.roll(u, HEAD // 2, 1) * signed_sine


def weight_copies(source, scratch, sems):
    depth = scratch.shape[0] // WEIGHT_STEPS
    return [
        pltpu.make_async_copy(
            source.at[pl.ds(step * depth, depth), :], scratch.at[pl.ds(step * depth, depth), :], sems.at[step]
        )
        for step in range(WEIGHT_STEPS)
    ]


def stepped_dot(left, copies, scratch):
    depth = scratch.shape[0] // WEIGHT_STEPS
    total = None
    for step, copy in enumerate(copies):
        copy.wait()
        rows = slice(step * depth, (step + 1) * depth)
        part = jnp.dot(left[:, rows], scratch[rows, :], preferred_element_type=f32)
        total = part if total is None else total + part
    return total


def rotary_tables(block_ref, len_ref, turn_ref, half):
    prompts = len_ref.shape[0]
    blocks = blocks_of(block_ref, lax.axis_index("seq"))
    starts = [jnp.int32(0)]
    for r in range(prompts - 1):
        starts.append(starts[-1] + len_ref[r])
    count = 2 * prompts
    index = lax.broadcasted_iota(jnp.int32, (count, HEAD), 0)
    base = jnp.zeros((count, HEAD), jnp.int32)
    for k, block in enumerate(blocks):
        for p, start in enumerate(starts):
            base = jnp.where(index == k * prompts + p, block * half - start, base)
    angle = base.astype(f32) * turn_ref[2 * half : 2 * half + 1, :]
    base_cos, base_sin = jnp.cos(angle), jnp.sin(angle)
    row_cos, row_sin = turn_ref[:half, :], turn_ref[half : 2 * half, :]
    row = lax.broadcasted_iota(jnp.int32, (half, HEAD), 0)
    lane = lax.broadcasted_iota(jnp.int32, (half, HEAD), 1)
    cosines, sines = [], []
    for k, block in enumerate(blocks):
        at = k * prompts
        cos, sin = base_cos[at : at + 1], base_sin[at : at + 1]
        for p in range(1, prompts):
            inside = row >= starts[p] - block * half
            cos = jnp.where(inside, base_cos[at + p : at + p + 1], cos)
            sin = jnp.where(inside, base_sin[at + p : at + p + 1], sin)
        cosines.append(row_cos * cos - row_sin * sin)
        sine = row_sin * cos + row_cos * sin
        sines.append(jnp.where(lane < HEAD // 2, -sine, sine))
    return jnp.concatenate(cosines, 0), jnp.concatenate(sines, 0)


def project_kernel(
    block_hbm, len_hbm, turn_hbm, tok_hbm, gain_hbm, wk_hbm, wv_hbm,
    kv_hbm, normed_hbm, turned_hbm,
    block_ref, len_ref, turn_ref, tok_ref, gain_ref, k_weights, v_weights, kv_ref, normed_ref, turned_ref,
    small_sems, k_sems, v_sems, out_sems,
):
    small = [
        pltpu.make_async_copy(source, target, small_sems.at[i])
        for i, (source, target) in enumerate(
            (
                (tok_hbm, tok_ref),
                (block_hbm, block_ref),
                (len_hbm, len_ref),
                (turn_hbm, turn_ref),
                (gain_hbm, gain_ref),
            )
        )
    ]
    k_copies = weight_copies(wk_hbm, k_weights, k_sems)
    v_copies = weight_copies(wv_hbm, v_weights, v_sems)
    for copy in small + k_copies + v_copies:
        copy.start()
    rows = tok_ref.shape[0]
    key_width = wk_hbm.shape[1]
    for copy in small:
        copy.wait()
    wide = tok_ref[...].astype(f32)
    scale = lax.rsqrt(jnp.mean(wide * wide, -1, keepdims=True) + EPS)
    normed = (wide * scale * gain_ref[...]).astype(bf16)
    normed_ref[...] = normed
    writes = [
        pltpu.make_async_copy(source, target, out_sems.at[i])
        for i, (source, target) in enumerate(
            ((normed_ref, normed_hbm), (turned_ref, turned_hbm), (kv_ref, kv_hbm))
        )
    ]
    writes[0].start()
    cosine, sine = rotary_tables(block_ref, len_ref, turn_ref, rows // 2)
    turned_ref[:, :HEAD] = cosine
    turned_ref[:, HEAD:] = sine
    writes[1].start()
    product = stepped_dot(normed, k_copies, k_weights)
    for h in range(key_width // HEAD):
        cols = slice(h * HEAD, (h + 1) * HEAD)
        kv_ref[:, cols] = rotate(product[:, cols], cosine, sine).astype(bf16)
    kv_ref[:, key_width:] = stepped_dot(normed, v_copies, v_weights).astype(bf16)
    writes[2].start()
    for copy in writes:
        copy.wait()


def query_kernel(normed_ref, turned_ref, wq_ref, q_ref):
    product = jnp.dot(normed_ref[...], wq_ref[...], preferred_element_type=f32)
    cosine, sine = turned_ref[:, :HEAD], turned_ref[:, HEAD:]
    for h in range(q_ref.shape[1] // HEAD):
        cols = slice(h * HEAD, (h + 1) * HEAD)
        q_ref[:, cols] = rotate(product[:, cols], cosine, sine).astype(bf16)


def attend_kernel(pieces, side, key_pos_ref, q_pos_ref, q_begin_ref, q_ref, far_ref, *refs):
    pieces, refs = with_refs(pieces, refs)
    shard = lax.axis_index("seq")
    rows, q_width = q_ref.shape
    key_width = pieces[0].arrays[0].shape[1] // 2
    kv_heads = key_width // HEAD
    group = q_width // key_width
    if side is None:
        taken, first = rows, 0
        span = slice(None)
    else:
        part = lax.axis_index("req")
        taken = rows // 2
        first = pl.multiple_of((1 - part if side else part) * taken, taken)
        span = pl.ds(first, taken)
    both = 2 * taken

    def of_both_cores(ref):
        return jnp.concatenate(
            [ref[pl.ds(pl.multiple_of(core * rows + first, taken), taken), :] for core in (0, 1)], 0
        )

    q_pos, q_begin = of_both_cores(q_pos_ref), of_both_cores(q_begin_ref)
    queries = [
        jnp.concatenate(
            [
                ref[span, h * HEAD : (h + 1) * HEAD]
                for h in range(g * group, (g + 1) * group)
                for ref in (q_ref, far_ref)
            ],
            0,
        )
        for g in range(kv_heads)
    ]

    def absorb(state, blocks, sources):
        bias = []
        for source in sources:
            key_pos = key_pos_ref[pl.ds(source, 1), :]
            bias.append(jnp.where((key_pos >= q_begin) & (key_pos <= q_pos), 0.0, MASKED))
        bias = jnp.concatenate(bias, 1)
        bias = jnp.concatenate([bias] * group, 0)
        out = []
        for g in range(kv_heads):
            top, total, acc = state[g]
            keys = jnp.concatenate([b[:, g * HEAD : (g + 1) * HEAD] for b in blocks], 0)
            values = jnp.concatenate(
                [b[:, key_width + g * HEAD : key_width + (g + 1) * HEAD] for b in blocks], 0
            )
            scores = lax.dot_general(
                queries[g], keys, (((1,), (1,)), ((), ())), preferred_element_type=f32
            )
            scores = scores * SCALE + bias
            new_top = jnp.maximum(top, jnp.max(scores, -1, keepdims=True))
            weights = jnp.exp2(scores - new_top)
            factor = jnp.exp2(top - new_top)
            total = total * factor + jnp.sum(weights, -1, keepdims=True)
            acc = acc * factor + jnp.dot(weights.astype(bf16), values, preferred_element_type=f32)
            out.append((new_top, total, acc))
        return tuple(out)

    state = (
        (
            jnp.full((group * both, 1), FLOOR, f32),
            jnp.zeros((group * both, 1), f32),
            jnp.zeros((group * both, HEAD), f32),
        ),
    ) * kv_heads
    if all(piece.count == 1 for piece in pieces):
        for i in range(0, len(pieces), 2):
            pair = pieces[i : i + 2]
            state = absorb(
                state, [p.arrays[0][...] for p in pair], [p.source_of(shard, 0) for p in pair]
            )
    else:
        for piece in pieces:

            def step(i, carried):
                at = pl.multiple_of(i * rows, rows)
                block = piece.arrays[0][pl.ds(at, rows), :]
                return absorb(carried, [block], [piece.source_of(shard, i)])

            state = lax.fori_loop(0, piece.count, step, state)

    mine_ref, stat_ref, packed_ref = refs
    heads = q_width // HEAD
    lane = lax.broadcasted_iota(jnp.int32, (taken, HEAD), 1)
    mine = jnp.zeros((taken, HEAD), f32)
    theirs = jnp.zeros((taken, HEAD), f32)
    for g in range(kv_heads):
        top, total, acc = state[g]
        for j in range(group):
            h = g * group + j
            cols = slice(h * HEAD, (h + 1) * HEAD)
            near = slice(j * both, j * both + taken)
            far = slice(j * both + taken, (j + 1) * both)
            mine_ref[:, cols] = acc[near]
            packed_ref[:, cols] = acc[far].astype(bf16)
            for value, at in ((top, h), (total, heads + h)):
                mine = jnp.where(lane == at, value[near], mine)
                theirs = jnp.where(lane % (2 * heads) == at, value[far], theirs)
    stat_ref[...] = mine
    high = theirs.astype(bf16).astype(f32)
    middle = (theirs - high).astype(bf16).astype(f32)
    low = theirs - high - middle
    third = lane // (2 * heads)
    parts = jnp.where(third == 0, high, jnp.where(third == 1, middle, low))
    packed_ref[:, q_width:] = parts.astype(bf16)


def stage_kernel(block_ref, len_ref, kv_ref, kv_out, key_pos_ref, q_pos_ref, q_begin_ref):
    kv_out[...] = kv_ref[...]
    shards, rows = key_pos_ref.shape
    half = rows // 2
    shard = lax.axis_index("seq")

    def picked(values, mask):
        return jnp.sum(jnp.where(mask, values, 0.0), -1, keepdims=True).astype(jnp.int32)

    def lanes(shape):
        return lax.broadcasted_iota(jnp.int32, shape, 1)

    blocks = block_ref[...].astype(f32)
    square = (shards, shards)
    first = picked(blocks, lanes(square) == lax.broadcasted_iota(jnp.int32, square, 0))
    index = lanes((shards, rows))
    key_pos_ref[...] = index + jnp.where(index < half, first, 2 * shards - 2 - first) * half

    held = []
    for s in (shard, shard ^ 1):
        first = picked(blocks, lanes(block_ref.shape) == s)
        held += [first, 2 * shards - 1 - first]
    q_pos = positions(held, half, 0, q_pos_ref.shape)
    q_pos_ref[...] = q_pos
    lengths = len_ref[...].astype(f32)
    begin = jnp.zeros_like(q_pos)
    for r in range(1, len_ref.shape[1]):
        start = picked(lengths, lanes(len_ref.shape) < r)
        begin = jnp.where(q_pos >= start, start, begin)
    q_begin_ref[...] = begin


def joined_rows(partials, first, half):
    q_width = partials[0].shape[1]
    heads = q_width // HEAD
    part = pl.ds(pl.multiple_of(first, half), half)
    held = []
    for mine_ref, stat_ref, packed_ref in zip(partials[::3], partials[1::3], partials[2::3]):
        span = slice(None) if mine_ref.shape[0] == half else part
        parts = packed_ref[span, q_width:].astype(f32)
        stats = parts
        for t in (1, 2):
            stats = stats + pltpu.roll(parts, HEAD - 2 * heads * t, 1)
        held += [(mine_ref, span, stat_ref[span, :]), (packed_ref, span, stats)]
    top = functools.reduce(jnp.maximum, [stats for _, _, stats in held])
    shares = [jnp.exp2(stats - top) for _, _, stats in held]
    total = sum(
        share * pltpu.roll(stats, HEAD - heads, 1) for share, (_, _, stats) in zip(shares, held)
    )
    shares = [share / total for share in shares]
    context = []
    for h in range(heads):
        cols = slice(h * HEAD, (h + 1) * HEAD)
        context.append(
            sum(
                ref[span, cols].astype(f32) * share[:, h : h + 1]
                for (ref, span, _), share in zip(held, shares)
            ).astype(bf16)
        )
    return jnp.concatenate(context, 1)


def leave_kernel(wo_ref, *refs):
    partials, sent_ref = refs[:-1], refs[-1]
    half = sent_ref.shape[0]
    context = joined_rows(partials, (1 - lax.axis_index("req")) * half, half)
    sent_ref[...] = jnp.dot(context, wo_ref[...], preferred_element_type=f32).astype(bf16)


def keep_kernel(wo_ref, tok_ref, mine_ref, *refs):
    others, partials, (out_ref, cache_ref) = refs[:2], refs[2:-2], refs[-2:]
    share = mine_ref.shape[0] // 2
    for i, other_ref in enumerate(others):
        part = slice(i * share, (i + 1) * share)
        cache_ref[part] = mine_ref[part] + other_ref[...]
    half = out_ref.shape[0]
    first = lax.axis_index("req") * half
    context = joined_rows(partials, first, half)
    residual = tok_ref[pl.ds(pl.multiple_of(first, half), half), :].astype(f32)
    out_ref[...] = jnp.dot(context, wo_ref[...], preferred_element_type=f32) + residual


def finish_kernel(kept_ref, received_ref, hidden_ref):
    hidden_ref[...] = (kept_ref[...] + received_ref[...].astype(f32)).astype(bf16)


def cache_kernel(pieces, block_ref, slot_ref, *refs):
    pieces, (mine_ref, *other_refs) = with_refs(pieces, refs)
    shard = lax.axis_index("seq")
    slots = mine_ref.shape[0]
    key_width = mine_ref.shape[3]
    rows = slots * PAGE // 2
    pages = rows // 2 // PAGE
    for target in (mine_ref, *other_refs):
        target[...] = jnp.zeros_like(target)
    share = slots // len(other_refs)

    def place(ref, at, source):
        for k, block in enumerate(blocks_of(block_ref, source)):
            for j in range(pages):
                slot = slot_ref[block * pages + j]
                holder = slot // slots
                local = slot - holder * slots
                offset = at + (k * pages + j) * PAGE
                if not isinstance(offset, int):
                    offset = pl.multiple_of(offset, PAGE)

                def write(target, at_slot):
                    target[at_slot, 0] = ref[pl.ds(offset, PAGE), :key_width]
                    target[at_slot, 1] = ref[pl.ds(offset, PAGE), key_width:]

                @pl.when(holder == shard)
                def _():
                    write(mine_ref, local)

                for i, target in enumerate(other_refs):

                    @pl.when((holder == shard ^ 1) & (local // share == i))
                    def _():
                        write(target, local - i * share)

    for piece in pieces:
        if piece.count == 1:
            place(piece.arrays[0], 0, piece.source_of(shard, 0))
        else:

            def step(i, carry):
                place(piece.arrays[0], i * rows, piece.source_of(shard, i))
                return carry

            lax.fori_loop(0, piece.count, step, 0)


def tied_all(pieces, other):
    arrays, other = lax.optimization_barrier((operands(pieces), other))
    return with_refs(pieces, arrays)[0], other


def tied(piece, other):
    (piece,), other = tied_all([piece], other)
    return piece, other


def swap(x, n, bit):
    return lax.ppermute(x, "seq", [(i, i ^ bit) for i in range(n)])


class Piece:
    def __init__(self, arrays, source_of, count=1):
        self.arrays, self.source_of, self.count = arrays, source_of, count

    def moved(self, arrays):
        return Piece(arrays, self.source_of, self.count)


def operands(pieces):
    return [x for piece in pieces for x in piece.arrays]


def with_refs(pieces, refs):
    out = []
    for piece in pieces:
        taken, refs = refs[: len(piece.arrays)], refs[len(piece.arrays) :]
        out.append(piece.moved(taken))
    return out, refs


def at_distance(bits):
    return lambda shard, i: shard ^ bits


def move(x, pairs):
    return lax.ppermute(x, "seq", pairs)


def on_device(
    n, parts, tokens, norm_gain, w_query, key_projection, value_projection, w_out, lengths, block_split, page_slot,
):
    rows, width = tokens.shape
    half = rows // 2
    q_width = w_query.shape[1]
    kv_width = key_projection.shape[1] + value_projection.shape[1]
    kv, normed, turned = pl.pallas_call(
        project_kernel,
        out_shape=(
            struct((rows, kv_width), bf16),
            struct((rows, width), bf16),
            struct((rows, 2 * HEAD), f32),
        ),
        in_specs=in_hbm(7),
        out_specs=tuple(in_hbm(3)),
        scratch_shapes=[
            pltpu.SMEM(block_split.shape, jnp.int32),
            pltpu.SMEM(lengths.shape, jnp.int32),
            pltpu.VMEM((2 * half + 8, HEAD), f32),
            pltpu.VMEM((rows, width), bf16),
            pltpu.VMEM((1, width), f32),
            pltpu.VMEM(key_projection.shape, bf16),
            pltpu.VMEM(value_projection.shape, bf16),
            pltpu.VMEM((rows, kv_width), bf16),
            pltpu.VMEM((rows, width), bf16),
            pltpu.VMEM((rows, 2 * HEAD), f32),
            pltpu.SemaphoreType.DMA((5,)),
            pltpu.SemaphoreType.DMA((WEIGHT_STEPS,)),
            pltpu.SemaphoreType.DMA((WEIGHT_STEPS,)),
            pltpu.SemaphoreType.DMA((3,)),
        ],
        compiler_params=kernel_params(62),
        cost_estimate=cost(0, 0),
        name="project",
    )(
        block_split, lengths, rotary_constants(half), tokens, norm_gain.reshape(1, width),
        key_projection, value_projection,
    )
    staged, *places = pl.pallas_call(
        stage_kernel,
        out_shape=(
            struct((rows, kv_width), bf16),
            struct((n, rows), jnp.int32),
            struct((2 * rows, HEAD), jnp.int32),
            struct((2 * rows, HEAD), jnp.int32),
        ),
        in_specs=in_vmem(3),
        out_specs=tuple(in_vmem(4)),
        compiler_params=kernel_params(24),
        cost_estimate=cost(10**9, 10**7),
        name="stage",
    )(block_split.reshape(1, n), lengths.reshape(1, -1), kv)

    def project_queries(normed):
        queries = pl.pallas_call(
            query_kernel,
            out_shape=struct((rows, q_width), bf16),
            in_specs=in_vmem(3),
            out_specs=in_vmem(1)[0],
            compiler_params=kernel_params(24),
            cost_estimate=cost(0, 0),
            name="query",
        )(normed, turned, w_query)
        return queries, swap(queries, n, 1)

    def attend(queries, far_queries, pieces, side=None):
        arrays = operands(pieces)
        taken = rows if side is None else half
        mine, stats, packed = pl.pallas_call(
            functools.partial(attend_kernel, pieces, side),
            out_shape=(
                struct((taken, q_width), f32),
                struct((taken, HEAD), f32),
                struct((taken, q_width + HEAD), bf16),
            ),
            in_specs=in_vmem(5 + len(arrays)),
            out_specs=tuple(in_vmem(3)),
            compiler_params=kernel_params(32),
            cost_estimate=cost(0, 0),
            name="attend",
        )(*places, queries, far_queries, *arrays)
        return [mine, stats, packed]

    def place_pages(pieces):
        arrays = operands(pieces)
        shape = (2 * rows // PAGE, 2, PAGE, kv_width // 2)
        return pl.pallas_call(
            functools.partial(cache_kernel, pieces),
            out_shape=(struct(shape, bf16),) + (struct((shape[0] // 2,) + shape[1:], bf16),) * 2,
            in_specs=in_smem(2) + in_vmem(len(arrays)),
            out_specs=tuple(in_vmem(1 + 2)),
            compiler_params=kernel_params(32),
            cost_estimate=cost(0, 0),
            name="cache",
        )(block_split, page_slot, *arrays)

    if n == 16:

        def swapped(piece, bits):
            source = lambda shard, i: piece.source_of(shard ^ bits, i)
            return Piece([swap(piece.arrays[0], n, bits)], source)

        own = Piece([kv], at_distance(0))
        second, first, beside = swapped(own, 8), swapped(own, 4), swapped(own, 2)
        first_across = swapped(first, 2)
        first, normed = tied(first, normed)
        queries, far_queries = project_queries(normed)
        second, (staged, queries) = tied(second, (staged, queries))
        own = own.moved([staged])
        third = swapped(second, 4)
        last = swapped(second, 6)
        (second, first_across, beside), _ = tied_all([second, first_across, beside], ())
        early = [own, beside, first, second, first_across, last]
        partials = attend(queries, far_queries, early)
        partials[2] = swap(partials[2], n, 1)
        queries, partials[1] = lax.optimization_barrier((queries, partials[1]))
        remaining = [third, swapped(second, 2)]
        placed = early + remaining
    else:
        same = [list(range(c, n, 2)) for c in range(2)]
        gathered = lax.all_gather(kv, "seq", axis=0, tiled=True, axis_index_groups=same)
        remaining = [Piece([gathered], lambda shard, i: 2 * i + shard % 2, n // 2)]
        partials, placed = [], remaining
        queries, far_queries = project_queries(normed)
    leaving = attend(queries, far_queries, remaining, 1)
    queries, leaving[1] = lax.optimization_barrier((queries, leaving[1]))
    leaving[2] = swap(leaving[2], n, 1)
    staying = attend(queries, far_queries, remaining, 0)
    leaving[0], staying[1] = lax.optimization_barrier((leaving[0], staying[1]))
    sent = pl.pallas_call(
        leave_kernel,
        out_shape=struct((half, width), bf16),
        in_specs=in_vmem(4 + len(partials)),
        out_specs=in_vmem(1)[0],
        compiler_params=kernel_params(24),
        cost_estimate=cost(0, 0),
        name="leave",
    )(w_out, *partials, *leaving)
    received = lax.ppermute(sent, "req", [(i, (i + 1) % parts) for i in range(parts)])
    staying[2] = swap(staying[2], n, 1)
    placed, (staying[2], sent) = tied_all(placed, (staying[2], sent))
    cache, *other = place_pages(placed)
    kept, cache = pl.pallas_call(
        keep_kernel,
        out_shape=(struct((half, width), f32), struct(cache.shape, bf16)),
        in_specs=in_vmem(6 + 2 + len(partials)),
        out_specs=tuple(in_vmem(2)),
        compiler_params=kernel_params(24),
        cost_estimate=cost(0, 0),
        name="keep",
    )(w_out, tokens, cache, *[swap(x, n, 1) for x in other], *partials, *staying)
    hidden = pl.pallas_call(
        finish_kernel,
        out_shape=struct((half, width), bf16),
        in_specs=in_vmem(2),
        out_specs=in_vmem(1)[0],
        compiler_params=kernel_params(24),
        cost_estimate=cost(0, 0),
        name="finish",
    )(kept, received)
    return hidden, cache


def solution(mesh):
    in_specs = (
        P("seq", None),
        P(),
        P(None, "req"),
        P(None, "req"),
        P(None, "req"),
        P("req", None),
        P(),
        P(),
        P(),
    )
    out_specs = (P(("seq", "req"), None), P("seq", None, None, "req"))
    body = functools.partial(on_device, mesh.shape["seq"], mesh.shape["req"])
    return jax.shard_map(body, mesh=mesh, in_specs=in_specs, out_specs=out_specs, check_vma=False)
```

```python
import functools
import math

import jax
import jax.numpy as jnp
import numpy as np
from jax import lax
from jax.experimental import pallas as pl
from jax.experimental.pallas import tpu as pltpu
from jax.sharding import PartitionSpec as P

HEAD = 128
PAGE = 32
THETA = 1000000.0
EPS = 1e-05
MASKED = -1e30
FLOOR = -1e29
WEIGHT_STEPS = 2
MIB = 1024 * 1024
SCALE = math.log2(math.e) / math.sqrt(HEAD)

f32 = jnp.float32
bf16 = jnp.bfloat16
struct = jax.ShapeDtypeStruct


def in_vmem(count):
    return [pl.BlockSpec(memory_space=pltpu.VMEM)] * count


def in_smem(count):
    return [pl.BlockSpec(memory_space=pltpu.SMEM)] * count


def in_hbm(count):
    return [pl.BlockSpec(memory_space=pltpu.HBM)] * count


def kernel_params(mib):
    return pltpu.CompilerParams(vmem_limit_bytes=mib * MIB)


def cost(flops, moved):
    return pl.CostEstimate(flops=flops, bytes_accessed=moved, transcendentals=0)


def rotary_constants(half):
    exponent = np.arange(HEAD // 2, dtype=np.float64) * (2.0 / HEAD)
    freq = np.tile(THETA**-exponent, 2)[None, :]
    angle = np.arange(half, dtype=np.float64)[:, None] * freq
    rows = [np.cos(angle), np.sin(angle), np.broadcast_to(freq, (8, HEAD))]
    return jnp.asarray(np.concatenate(rows).astype(np.float32))


def blocks_of(block_ref, shard):
    first = block_ref[shard]
    return first, 2 * block_ref.shape[0] - 1 - first


def positions(blocks, half, dim, shape):
    index = lax.broadcasted_iota(jnp.int32, shape, dim)
    offset = blocks[0] * half
    for i, block in enumerate(blocks[1:], 1):
        offset = jnp.where(index >= i * half, (block - i) * half, offset)
    return index + offset


def rotate(u, cosine, signed_sine):
    return u * cosine + pltpu.roll(u, HEAD // 2, 1) * signed_sine


def weight_copies(source, scratch, sems):
    depth = scratch.shape[0] // WEIGHT_STEPS
    return [
        pltpu.make_async_copy(
            source.at[pl.ds(step * depth, depth), :], scratch.at[pl.ds(step * depth, depth), :], sems.at[step]
        )
        for step in range(WEIGHT_STEPS)
    ]


def stepped_dot(left, copies, scratch):
    depth = scratch.shape[0] // WEIGHT_STEPS
    total = None
    for step, copy in enumerate(copies):
        copy.wait()
        rows = slice(step * depth, (step + 1) * depth)
        part = jnp.dot(left[:, rows], scratch[rows, :], preferred_element_type=f32)
        total = part if total is None else total + part
    return total


def rotary_tables(block_ref, len_ref, turn_ref, half):
    prompts = len_ref.shape[0]
    blocks = blocks_of(block_ref, lax.axis_index("seq"))
    starts = [jnp.int32(0)]
    for r in range(prompts - 1):
        starts.append(starts[-1] + len_ref[r])
    count = 2 * prompts
    index = lax.broadcasted_iota(jnp.int32, (count, HEAD), 0)
    base = jnp.zeros((count, HEAD), jnp.int32)
    for k, block in enumerate(blocks):
        for p, start in enumerate(starts):
            base = jnp.where(index == k * prompts + p, block * half - start, base)
    angle = base.astype(f32) * turn_ref[2 * half : 2 * half + 1, :]
    base_cos, base_sin = jnp.cos(angle), jnp.sin(angle)
    row_cos, row_sin = turn_ref[:half, :], turn_ref[half : 2 * half, :]
    row = lax.broadcasted_iota(jnp.int32, (half, HEAD), 0)
    lane = lax.broadcasted_iota(jnp.int32, (half, HEAD), 1)
    cosines, sines = [], []
    for k, block in enumerate(blocks):
        at = k * prompts
        cos, sin = base_cos[at : at + 1], base_sin[at : at + 1]
        for p in range(1, prompts):
            inside = row >= starts[p] - block * half
            cos = jnp.where(inside, base_cos[at + p : at + p + 1], cos)
            sin = jnp.where(inside, base_sin[at + p : at + p + 1], sin)
        cosines.append(row_cos * cos - row_sin * sin)
        sine = row_sin * cos + row_cos * sin
        sines.append(jnp.where(lane < HEAD // 2, -sine, sine))
    return jnp.concatenate(cosines, 0), jnp.concatenate(sines, 0)


def project_kernel(
    block_hbm, len_hbm, turn_hbm, tok_hbm, gain_hbm, wk_hbm, wv_hbm,
    kv_hbm, normed_hbm, turned_hbm,
    block_ref, len_ref, turn_ref, tok_ref, gain_ref, k_weights, v_weights, kv_ref, normed_ref, turned_ref,
    small_sems, k_sems, v_sems, out_sems,
):
    small = [
        pltpu.make_async_copy(source, target, small_sems.at[i])
        for i, (source, target) in enumerate(
            (
                (tok_hbm, tok_ref),
                (block_hbm, block_ref),
                (len_hbm, len_ref),
                (turn_hbm, turn_ref),
                (gain_hbm, gain_ref),
            )
        )
    ]
    k_copies = weight_copies(wk_hbm, k_weights, k_sems)
    v_copies = weight_copies(wv_hbm, v_weights, v_sems)
    for copy in small + k_copies + v_copies:
        copy.start()
    rows = tok_ref.shape[0]
    key_width = wk_hbm.shape[1]
    for copy in small:
        copy.wait()
    wide = tok_ref[...].astype(f32)
    scale = lax.rsqrt(jnp.mean(wide * wide, -1, keepdims=True) + EPS)
    normed = (wide * scale * gain_ref[...]).astype(bf16)
    normed_ref[...] = normed
    writes = [
        pltpu.make_async_copy(source, target, out_sems.at[i])
        for i, (source, target) in enumerate(
            ((normed_ref, normed_hbm), (turned_ref, turned_hbm), (kv_ref, kv_hbm))
        )
    ]
    writes[0].start()
    cosine, sine = rotary_tables(block_ref, len_ref, turn_ref, rows // 2)
    turned_ref[:, :HEAD] = cosine
    turned_ref[:, HEAD:] = sine
    writes[1].start()
    product = stepped_dot(normed, k_copies, k_weights)
    for h in range(key_width // HEAD):
        cols = slice(h * HEAD, (h + 1) * HEAD)
        kv_ref[:, cols] = rotate(product[:, cols], cosine, sine).astype(bf16)
    kv_ref[:, key_width:] = stepped_dot(normed, v_copies, v_weights).astype(bf16)
    writes[2].start()
    for copy in writes:
        copy.wait()


def query_kernel(normed_ref, turned_ref, wq_ref, q_ref):
    product = jnp.dot(normed_ref[...], wq_ref[...], preferred_element_type=f32)
    cosine, sine = turned_ref[:, :HEAD], turned_ref[:, HEAD:]
    for h in range(q_ref.shape[1] // HEAD):
        cols = slice(h * HEAD, (h + 1) * HEAD)
        q_ref[:, cols] = rotate(product[:, cols], cosine, sine).astype(bf16)


def attend_kernel(pieces, side, key_pos_ref, q_pos_ref, q_begin_ref, q_ref, far_ref, *refs):
    pieces, refs = with_refs(pieces, refs)
    shard = lax.axis_index("seq")
    rows, q_width = q_ref.shape
    key_width = pieces[0].arrays[0].shape[1] // 2
    kv_heads = key_width // HEAD
    group = q_width // key_width
    if side is None:
        taken, first = rows, 0
        span = slice(None)
    else:
        part = lax.axis_index("req")
        taken = rows // 2
        first = pl.multiple_of((1 - part if side else part) * taken, taken)
        span = pl.ds(first, taken)
    both = 2 * taken

    def of_both_cores(ref):
        return jnp.concatenate(
            [ref[pl.ds(pl.multiple_of(core * rows + first, taken), taken), :] for core in (0, 1)], 0
        )

    q_pos, q_begin = of_both_cores(q_pos_ref), of_both_cores(q_begin_ref)
    queries = [
        jnp.concatenate(
            [
                ref[span, h * HEAD : (h + 1) * HEAD]
                for h in range(g * group, (g + 1) * group)
                for ref in (q_ref, far_ref)
            ],
            0,
        )
        for g in range(kv_heads)
    ]

    def absorb(state, blocks, sources):
        bias = []
        for source in sources:
            key_pos = key_pos_ref[pl.ds(source, 1), :]
            bias.append(jnp.where((key_pos >= q_begin) & (key_pos <= q_pos), 0.0, MASKED))
        bias = jnp.concatenate(bias, 1)
        bias = jnp.concatenate([bias] * group, 0)
        out = []
        for g in range(kv_heads):
            top, total, acc = state[g]
            keys = jnp.concatenate([b[:, g * HEAD : (g + 1) * HEAD] for b in blocks], 0)
            values = jnp.concatenate(
                [b[:, key_width + g * HEAD : key_width + (g + 1) * HEAD] for b in blocks], 0
            )
            scores = lax.dot_general(
                queries[g], keys, (((1,), (1,)), ((), ())), preferred_element_type=f32
            )
            scores = scores * SCALE + bias
            new_top = jnp.maximum(top, jnp.max(scores, -1, keepdims=True))
            weights = jnp.exp2(scores - new_top)
            factor = jnp.exp2(top - new_top)
            total = total * factor + jnp.sum(weights, -1, keepdims=True)
            acc = acc * factor + jnp.dot(weights.astype(bf16), values, preferred_element_type=f32)
            out.append((new_top, total, acc))
        return tuple(out)

    state = (
        (
            jnp.full((group * both, 1), FLOOR, f32),
            jnp.zeros((group * both, 1), f32),
            jnp.zeros((group * both, HEAD), f32),
        ),
    ) * kv_heads
    if all(piece.count == 1 for piece in pieces):
        for i in range(0, len(pieces), 2):
            pair = pieces[i : i + 2]
            state = absorb(
                state, [p.arrays[0][...] for p in pair], [p.source_of(shard, 0) for p in pair]
            )
    else:
        for piece in pieces:

            def step(i, carried):
                at = pl.multiple_of(i * rows, rows)
                block = piece.arrays[0][pl.ds(at, rows), :]
                return absorb(carried, [block], [piece.source_of(shard, i)])

            state = lax.fori_loop(0, piece.count, step, state)

    mine_ref, stat_ref, packed_ref = refs
    heads = q_width // HEAD
    lane = lax.broadcasted_iota(jnp.int32, (taken, HEAD), 1)
    mine = jnp.zeros((taken, HEAD), f32)
    theirs = jnp.zeros((taken, HEAD), f32)
    for g in range(kv_heads):
        top, total, acc = state[g]
        for j in range(group):
            h = g * group + j
            cols = slice(h * HEAD, (h + 1) * HEAD)
            near = slice(j * both, j * both + taken)
            far = slice(j * both + taken, (j + 1) * both)
            mine_ref[:, cols] = acc[near]
            packed_ref[:, cols] = acc[far].astype(bf16)
            for value, at in ((top, h), (total, heads + h)):
                mine = jnp.where(lane == at, value[near], mine)
                theirs = jnp.where(lane % (2 * heads) == at, value[far], theirs)
    stat_ref[...] = mine
    high = theirs.astype(bf16).astype(f32)
    middle = (theirs - high).astype(bf16).astype(f32)
    low = theirs - high - middle
    third = lane // (2 * heads)
    parts = jnp.where(third == 0, high, jnp.where(third == 1, middle, low))
    packed_ref[:, q_width:] = parts.astype(bf16)


def stage_kernel(block_ref, len_ref, kv_ref, kv_out, key_pos_ref, q_pos_ref, q_begin_ref):
    kv_out[...] = kv_ref[...]
    shards, rows = key_pos_ref.shape
    half = rows // 2
    shard = lax.axis_index("seq")

    def picked(values, mask):
        return jnp.sum(jnp.where(mask, values, 0.0), -1, keepdims=True).astype(jnp.int32)

    def lanes(shape):
        return lax.broadcasted_iota(jnp.int32, shape, 1)

    blocks = block_ref[...].astype(f32)
    square = (shards, shards)
    first = picked(blocks, lanes(square) == lax.broadcasted_iota(jnp.int32, square, 0))
    index = lanes((shards, rows))
    key_pos_ref[...] = index + jnp.where(index < half, first, 2 * shards - 2 - first) * half

    held = []
    for s in (shard, shard ^ 1):
        first = picked(blocks, lanes(block_ref.shape) == s)
        held += [first, 2 * shards - 1 - first]
    q_pos = positions(held, half, 0, q_pos_ref.shape)
    q_pos_ref[...] = q_pos
    lengths = len_ref[...].astype(f32)
    begin = jnp.zeros_like(q_pos)
    for r in range(1, len_ref.shape[1]):
        start = picked(lengths, lanes(len_ref.shape) < r)
        begin = jnp.where(q_pos >= start, start, begin)
    q_begin_ref[...] = begin


def joined_rows(partials, first, half):
    q_width = partials[0].shape[1]
    heads = q_width // HEAD
    part = pl.ds(pl.multiple_of(first, half), half)
    held = []
    for mine_ref, stat_ref, packed_ref in zip(partials[::3], partials[1::3], partials[2::3]):
        span = slice(None) if mine_ref.shape[0] == half else part
        parts = packed_ref[span, q_width:].astype(f32)
        stats = parts
        for t in (1, 2):
            stats = stats + pltpu.roll(parts, HEAD - 2 * heads * t, 1)
        held += [(mine_ref, span, stat_ref[span, :]), (packed_ref, span, stats)]
    top = functools.reduce(jnp.maximum, [stats for _, _, stats in held])
    shares = [jnp.exp2(stats - top) for _, _, stats in held]
    total = sum(
        share * pltpu.roll(stats, HEAD - heads, 1) for share, (_, _, stats) in zip(shares, held)
    )
    shares = [share / total for share in shares]
    context = []
    for h in range(heads):
        cols = slice(h * HEAD, (h + 1) * HEAD)
        context.append(
            sum(
                ref[span, cols].astype(f32) * share[:, h : h + 1]
                for (ref, span, _), share in zip(held, shares)
            ).astype(bf16)
        )
    return jnp.concatenate(context, 1)


def leave_kernel(wo_ref, *refs):
    partials, sent_ref = refs[:-1], refs[-1]
    half = sent_ref.shape[0]
    context = joined_rows(partials, (1 - lax.axis_index("req")) * half, half)
    sent_ref[...] = jnp.dot(context, wo_ref[...], preferred_element_type=f32).astype(bf16)


def keep_kernel(wo_ref, tok_ref, mine_ref, *refs):
    others, partials, (out_ref, cache_ref) = refs[:2], refs[2:-2], refs[-2:]
    share = mine_ref.shape[0] // 2
    for i, other_ref in enumerate(others):
        part = slice(i * share, (i + 1) * share)
        cache_ref[part] = mine_ref[part] + other_ref[...]
    half = out_ref.shape[0]
    first = lax.axis_index("req") * half
    context = joined_rows(partials, first, half)
    residual = tok_ref[pl.ds(pl.multiple_of(first, half), half), :].astype(f32)
    out_ref[...] = jnp.dot(context, wo_ref[...], preferred_element_type=f32) + residual


def finish_kernel(kept_ref, received_ref, hidden_ref):
    hidden_ref[...] = (kept_ref[...] + received_ref[...].astype(f32)).astype(bf16)


def cache_kernel(pieces, block_ref, slot_ref, *refs):
    pieces, (mine_ref, *other_refs) = with_refs(pieces, refs)
    shard = lax.axis_index("seq")
    slots = mine_ref.shape[0]
    key_width = mine_ref.shape[3]
    rows = slots * PAGE // 2
    pages = rows // 2 // PAGE
    for target in (mine_ref, *other_refs):
        target[...] = jnp.zeros_like(target)
    share = slots // len(other_refs)

    def place(ref, at, source):
        for k, block in enumerate(blocks_of(block_ref, source)):
            for j in range(pages):
                slot = slot_ref[block * pages + j]
                holder = slot // slots
                local = slot - holder * slots
                offset = at + (k * pages + j) * PAGE
                if not isinstance(offset, int):
                    offset = pl.multiple_of(offset, PAGE)

                def write(target, at_slot):
                    target[at_slot, 0] = ref[pl.ds(offset, PAGE), :key_width]
                    target[at_slot, 1] = ref[pl.ds(offset, PAGE), key_width:]

                @pl.when(holder == shard)
                def _():
                    write(mine_ref, local)

                for i, target in enumerate(other_refs):

                    @pl.when((holder == shard ^ 1) & (local // share == i))
                    def _():
                        write(target, local - i * share)

    for piece in pieces:
        if piece.count == 1:
            place(piece.arrays[0], 0, piece.source_of(shard, 0))
        else:

            def step(i, carry):
                place(piece.arrays[0], i * rows, piece.source_of(shard, i))
                return carry

            lax.fori_loop(0, piece.count, step, 0)


def tied_all(pieces, other):
    arrays, other = lax.optimization_barrier((operands(pieces), other))
    return with_refs(pieces, arrays)[0], other


def tied(piece, other):
    (piece,), other = tied_all([piece], other)
    return piece, other


def swap(x, n, bit):
    return lax.ppermute(x, "seq", [(i, i ^ bit) for i in range(n)])


class Piece:
    def __init__(self, arrays, source_of, count=1):
        self.arrays, self.source_of, self.count = arrays, source_of, count

    def moved(self, arrays):
        return Piece(arrays, self.source_of, self.count)


def operands(pieces):
    return [x for piece in pieces for x in piece.arrays]


def with_refs(pieces, refs):
    out = []
    for piece in pieces:
        taken, refs = refs[: len(piece.arrays)], refs[len(piece.arrays) :]
        out.append(piece.moved(taken))
    return out, refs


def at_distance(bits):
    return lambda shard, i: shard ^ bits


def move(x, pairs):
    return lax.ppermute(x, "seq", pairs)


def on_device(
    n, parts, tokens, norm_gain, w_query, key_projection, value_projection, w_out, lengths, block_split, page_slot,
):
    rows, width = tokens.shape
    half = rows // 2
    q_width = w_query.shape[1]
    kv_width = key_projection.shape[1] + value_projection.shape[1]
    kv, normed, turned = pl.pallas_call(
        project_kernel,
        out_shape=(
            struct((rows, kv_width), bf16),
            struct((rows, width), bf16),
            struct((rows, 2 * HEAD), f32),
        ),
        in_specs=in_hbm(7),
        out_specs=tuple(in_hbm(3)),
        scratch_shapes=[
            pltpu.SMEM(block_split.shape, jnp.int32),
            pltpu.SMEM(lengths.shape, jnp.int32),
            pltpu.VMEM((2 * half + 8, HEAD), f32),
            pltpu.VMEM((rows, width), bf16),
            pltpu.VMEM((1, width), f32),
            pltpu.VMEM(key_projection.shape, bf16),
            pltpu.VMEM(value_projection.shape, bf16),
            pltpu.VMEM((rows, kv_width), bf16),
            pltpu.VMEM((rows, width), bf16),
            pltpu.VMEM((rows, 2 * HEAD), f32),
            pltpu.SemaphoreType.DMA((5,)),
            pltpu.SemaphoreType.DMA((WEIGHT_STEPS,)),
            pltpu.SemaphoreType.DMA((WEIGHT_STEPS,)),
            pltpu.SemaphoreType.DMA((3,)),
        ],
        compiler_params=kernel_params(62),
        cost_estimate=cost(0, 0),
        name="project",
    )(
        block_split, lengths, rotary_constants(half), tokens, norm_gain.reshape(1, width),
        key_projection, value_projection,
    )
    staged, *places = pl.pallas_call(
        stage_kernel,
        out_shape=(
            struct((rows, kv_width), bf16),
            struct((n, rows), jnp.int32),
            struct((2 * rows, HEAD), jnp.int32),
            struct((2 * rows, HEAD), jnp.int32),
        ),
        in_specs=in_vmem(3),
        out_specs=tuple(in_vmem(4)),
        compiler_params=kernel_params(24),
        cost_estimate=cost(10**9, 10**7),
        name="stage",
    )(block_split.reshape(1, n), lengths.reshape(1, -1), kv)

    def project_queries(normed):
        queries = pl.pallas_call(
            query_kernel,
            out_shape=struct((rows, q_width), bf16),
            in_specs=in_vmem(3),
            out_specs=in_vmem(1)[0],
            compiler_params=kernel_params(24),
            cost_estimate=cost(0, 0),
            name="query",
        )(normed, turned, w_query)
        return queries, swap(queries, n, 1)

    def attend(queries, far_queries, pieces, side=None):
        arrays = operands(pieces)
        taken = rows if side is None else half
        mine, stats, packed = pl.pallas_call(
            functools.partial(attend_kernel, pieces, side),
            out_shape=(
                struct((taken, q_width), f32),
                struct((taken, HEAD), f32),
                struct((taken, q_width + HEAD), bf16),
            ),
            in_specs=in_vmem(5 + len(arrays)),
            out_specs=tuple(in_vmem(3)),
            compiler_params=kernel_params(32),
            cost_estimate=cost(0, 0),
            name="attend",
        )(*places, queries, far_queries, *arrays)
        return [mine, stats, packed]

    def place_pages(pieces):
        arrays = operands(pieces)
        shape = (2 * rows // PAGE, 2, PAGE, kv_width // 2)
        return pl.pallas_call(
            functools.partial(cache_kernel, pieces),
            out_shape=(struct(shape, bf16),) + (struct((shape[0] // 2,) + shape[1:], bf16),) * 2,
            in_specs=in_smem(2) + in_vmem(len(arrays)),
            out_specs=tuple(in_vmem(1 + 2)),
            compiler_params=kernel_params(32),
            cost_estimate=cost(0, 0),
            name="cache",
        )(block_split, page_slot, *arrays)

    if n == 16:

        def swapped(piece, bits):
            source = lambda shard, i: piece.source_of(shard ^ bits, i)
            return Piece([swap(piece.arrays[0], n, bits)], source)

        own = Piece([kv], at_distance(0))
        second, first, beside = swapped(own, 8), swapped(own, 4), swapped(own, 2)
        first_across = swapped(first, 2)
        first, (normed, staged) = tied(first, (normed, staged))
        queries, far_queries = project_queries(normed)
        second, (staged, queries) = tied(second, (staged, queries))
        own = own.moved([staged])
        third = swapped(second, 4)
        last = swapped(second, 6)
        (second, first_across, beside), _ = tied_all([second, first_across, beside], ())
        early = [own, beside, first, second, first_across]
        partials = attend(queries, far_queries, early)
        partials[2] = swap(partials[2], n, 1)
        queries, partials[1] = lax.optimization_barrier((queries, partials[1]))
        remaining = [third, last, swapped(second, 2)]
        placed = early + remaining
    else:
        same = [list(range(c, n, 2)) for c in range(2)]
        gathered = lax.all_gather(kv, "seq", axis=0, tiled=True, axis_index_groups=same)
        remaining = [Piece([gathered], lambda shard, i: 2 * i + shard % 2, n // 2)]
        partials, placed = [], remaining
        queries, far_queries = project_queries(normed)
    leaving = attend(queries, far_queries, remaining, 1)
    queries, leaving[1] = lax.optimization_barrier((queries, leaving[1]))
    leaving[2] = swap(leaving[2], n, 1)
    staying = attend(queries, far_queries, remaining, 0)
    leaving[0], staying[1] = lax.optimization_barrier((leaving[0], staying[1]))
    sent = pl.pallas_call(
        leave_kernel,
        out_shape=struct((half, width), bf16),
        in_specs=in_vmem(4 + len(partials)),
        out_specs=in_vmem(1)[0],
        compiler_params=kernel_params(24),
        cost_estimate=cost(0, 0),
        name="leave",
    )(w_out, *partials, *leaving)
    received = lax.ppermute(sent, "req", [(i, (i + 1) % parts) for i in range(parts)])
    staying[2] = swap(staying[2], n, 1)
    placed, (staying[2], sent) = tied_all(placed, (staying[2], sent))
    cache, *other = place_pages(placed)
    kept, cache = pl.pallas_call(
        keep_kernel,
        out_shape=(struct((half, width), f32), struct(cache.shape, bf16)),
        in_specs=in_vmem(6 + 2 + len(partials)),
        out_specs=tuple(in_vmem(2)),
        compiler_params=kernel_params(24),
        cost_estimate=cost(0, 0),
        name="keep",
    )(w_out, tokens, cache, *[swap(x, n, 1) for x in other], *partials, *staying)
    hidden = pl.pallas_call(
        finish_kernel,
        out_shape=struct((half, width), bf16),
        in_specs=in_vmem(2),
        out_specs=in_vmem(1)[0],
        compiler_params=kernel_params(24),
        cost_estimate=cost(0, 0),
        name="finish",
    )(kept, received)
    return hidden, cache


def solution(mesh):
    in_specs = (
        P("seq", None),
        P(),
        P(None, "req"),
        P(None, "req"),
        P(None, "req"),
        P("req", None),
        P(),
        P(),
        P(),
    )
    out_specs = (P(("seq", "req"), None), P("seq", None, None, "req"))
    body = functools.partial(on_device, mesh.shape["seq"], mesh.shape["req"])
    return jax.shard_map(body, mesh=mesh, in_specs=in_specs, out_specs=out_specs, check_vma=False)
```

```python
import functools
import math

import jax
import jax.numpy as jnp
import numpy as np
from jax import lax
from jax.experimental import pallas as pl
from jax.experimental.pallas import tpu as pltpu
from jax.sharding import PartitionSpec as P

HEAD = 128
PAGE = 32
THETA = 1000000.0
EPS = 1e-05
MASKED = -1e30
FLOOR = -1e29
WEIGHT_STEPS = 2
MIB = 1024 * 1024
SCALE = math.log2(math.e) / math.sqrt(HEAD)

f32 = jnp.float32
bf16 = jnp.bfloat16
struct = jax.ShapeDtypeStruct


def in_vmem(count):
    return [pl.BlockSpec(memory_space=pltpu.VMEM)] * count


def in_smem(count):
    return [pl.BlockSpec(memory_space=pltpu.SMEM)] * count


def in_hbm(count):
    return [pl.BlockSpec(memory_space=pltpu.HBM)] * count


def kernel_params(mib):
    return pltpu.CompilerParams(vmem_limit_bytes=mib * MIB)


def cost(flops, moved):
    return pl.CostEstimate(flops=flops, bytes_accessed=moved, transcendentals=0)


def rotary_constants(half):
    exponent = np.arange(HEAD // 2, dtype=np.float64) * (2.0 / HEAD)
    freq = np.tile(THETA**-exponent, 2)[None, :]
    angle = np.arange(half, dtype=np.float64)[:, None] * freq
    rows = [np.cos(angle), np.sin(angle), np.broadcast_to(freq, (8, HEAD))]
    return jnp.asarray(np.concatenate(rows).astype(np.float32))


def blocks_of(block_ref, shard):
    first = block_ref[shard]
    return first, 2 * block_ref.shape[0] - 1 - first


def positions(blocks, half, dim, shape):
    index = lax.broadcasted_iota(jnp.int32, shape, dim)
    offset = blocks[0] * half
    for i, block in enumerate(blocks[1:], 1):
        offset = jnp.where(index >= i * half, (block - i) * half, offset)
    return index + offset


def rotate(u, cosine, signed_sine):
    return u * cosine + pltpu.roll(u, HEAD // 2, 1) * signed_sine


def weight_copies(source, scratch, sems):
    depth = scratch.shape[0] // WEIGHT_STEPS
    return [
        pltpu.make_async_copy(
            source.at[pl.ds(step * depth, depth), :], scratch.at[pl.ds(step * depth, depth), :], sems.at[step]
        )
        for step in range(WEIGHT_STEPS)
    ]


def stepped_dot(left, copies, scratch):
    depth = scratch.shape[0] // WEIGHT_STEPS
    total = None
    for step, copy in enumerate(copies):
        copy.wait()
        rows = slice(step * depth, (step + 1) * depth)
        part = jnp.dot(left[:, rows], scratch[rows, :], preferred_element_type=f32)
        total = part if total is None else total + part
    return total


def rotary_tables(block_ref, len_ref, turn_ref, half):
    prompts = len_ref.shape[0]
    blocks = blocks_of(block_ref, lax.axis_index("seq"))
    starts = [jnp.int32(0)]
    for r in range(prompts - 1):
        starts.append(starts[-1] + len_ref[r])
    count = 2 * prompts
    index = lax.broadcasted_iota(jnp.int32, (count, HEAD), 0)
    base = jnp.zeros((count, HEAD), jnp.int32)
    for k, block in enumerate(blocks):
        for p, start in enumerate(starts):
            base = jnp.where(index == k * prompts + p, block * half - start, base)
    angle = base.astype(f32) * turn_ref[2 * half : 2 * half + 1, :]
    base_cos, base_sin = jnp.cos(angle), jnp.sin(angle)
    row_cos, row_sin = turn_ref[:half, :], turn_ref[half : 2 * half, :]
    row = lax.broadcasted_iota(jnp.int32, (half, HEAD), 0)
    lane = lax.broadcasted_iota(jnp.int32, (half, HEAD), 1)
    cosines, sines = [], []
    for k, block in enumerate(blocks):
        at = k * prompts
        cos, sin = base_cos[at : at + 1], base_sin[at : at + 1]
        for p in range(1, prompts):
            inside = row >= starts[p] - block * half
            cos = jnp.where(inside, base_cos[at + p : at + p + 1], cos)
            sin = jnp.where(inside, base_sin[at + p : at + p + 1], sin)
        cosines.append(row_cos * cos - row_sin * sin)
        sine = row_sin * cos + row_cos * sin
        sines.append(jnp.where(lane < HEAD // 2, -sine, sine))
    return jnp.concatenate(cosines, 0), jnp.concatenate(sines, 0)


def project_kernel(
    block_hbm, len_hbm, turn_hbm, tok_hbm, gain_hbm, wk_hbm, wv_hbm,
    kv_hbm, normed_hbm, turned_hbm,
    block_ref, len_ref, turn_ref, tok_ref, gain_ref, k_weights, v_weights, kv_ref, normed_ref, turned_ref,
    small_sems, k_sems, v_sems, out_sems,
):
    small = [
        pltpu.make_async_copy(source, target, small_sems.at[i])
        for i, (source, target) in enumerate(
            (
                (tok_hbm, tok_ref),
                (block_hbm, block_ref),
                (len_hbm, len_ref),
                (turn_hbm, turn_ref),
                (gain_hbm, gain_ref),
            )
        )
    ]
    k_copies = weight_copies(wk_hbm, k_weights, k_sems)
    v_copies = weight_copies(wv_hbm, v_weights, v_sems)
    for copy in small + k_copies + v_copies:
        copy.start()
    rows = tok_ref.shape[0]
    key_width = wk_hbm.shape[1]
    for copy in small:
        copy.wait()
    wide = tok_ref[...].astype(f32)
    scale = lax.rsqrt(jnp.mean(wide * wide, -1, keepdims=True) + EPS)
    normed = (wide * scale * gain_ref[...]).astype(bf16)
    normed_ref[...] = normed
    writes = [
        pltpu.make_async_copy(source, target, out_sems.at[i])
        for i, (source, target) in enumerate(
            ((normed_ref, normed_hbm), (turned_ref, turned_hbm), (kv_ref, kv_hbm))
        )
    ]
    writes[0].start()
    cosine, sine = rotary_tables(block_ref, len_ref, turn_ref, rows // 2)
    turned_ref[:, :HEAD] = cosine
    turned_ref[:, HEAD:] = sine
    writes[1].start()
    product = stepped_dot(normed, k_copies, k_weights)
    for h in range(key_width // HEAD):
        cols = slice(h * HEAD, (h + 1) * HEAD)
        kv_ref[:, cols] = rotate(product[:, cols], cosine, sine).astype(bf16)
    kv_ref[:, key_width:] = stepped_dot(normed, v_copies, v_weights).astype(bf16)
    writes[2].start()
    for copy in writes:
        copy.wait()


def query_kernel(normed_ref, turned_ref, wq_ref, q_ref):
    product = jnp.dot(normed_ref[...], wq_ref[...], preferred_element_type=f32)
    cosine, sine = turned_ref[:, :HEAD], turned_ref[:, HEAD:]
    for h in range(q_ref.shape[1] // HEAD):
        cols = slice(h * HEAD, (h + 1) * HEAD)
        q_ref[:, cols] = rotate(product[:, cols], cosine, sine).astype(bf16)


def attend_kernel(pieces, side, key_pos_ref, q_pos_ref, q_begin_ref, q_ref, far_ref, *refs):
    pieces, refs = with_refs(pieces, refs)
    shard = lax.axis_index("seq")
    rows, q_width = q_ref.shape
    key_width = pieces[0].arrays[0].shape[1] // 2
    kv_heads = key_width // HEAD
    group = q_width // key_width
    if side is None:
        taken, first = rows, 0
        span = slice(None)
    else:
        part = lax.axis_index("req")
        taken = rows // 2
        first = pl.multiple_of((1 - part if side else part) * taken, taken)
        span = pl.ds(first, taken)
    both = 2 * taken

    def of_both_cores(ref):
        return jnp.concatenate(
            [ref[pl.ds(pl.multiple_of(core * rows + first, taken), taken), :] for core in (0, 1)], 0
        )

    q_pos, q_begin = of_both_cores(q_pos_ref), of_both_cores(q_begin_ref)
    queries = [
        jnp.concatenate(
            [
                ref[span, h * HEAD : (h + 1) * HEAD]
                for h in range(g * group, (g + 1) * group)
                for ref in (q_ref, far_ref)
            ],
            0,
        )
        for g in range(kv_heads)
    ]

    def absorb(state, blocks, sources):
        bias = []
        for source in sources:
            key_pos = key_pos_ref[pl.ds(source, 1), :]
            bias.append(jnp.where((key_pos >= q_begin) & (key_pos <= q_pos), 0.0, MASKED))
        bias = jnp.concatenate(bias, 1)
        bias = jnp.concatenate([bias] * group, 0)
        out = []
        for g in range(kv_heads):
            top, total, acc = state[g]
            keys = jnp.concatenate([b[:, g * HEAD : (g + 1) * HEAD] for b in blocks], 0)
            values = jnp.concatenate(
                [b[:, key_width + g * HEAD : key_width + (g + 1) * HEAD] for b in blocks], 0
            )
            scores = lax.dot_general(
                queries[g], keys, (((1,), (1,)), ((), ())), preferred_element_type=f32
            )
            scores = scores * SCALE + bias
            new_top = jnp.maximum(top, jnp.max(scores, -1, keepdims=True))
            weights = jnp.exp2(scores - new_top)
            factor = jnp.exp2(top - new_top)
            total = total * factor + jnp.sum(weights, -1, keepdims=True)
            acc = acc * factor + jnp.dot(weights.astype(bf16), values, preferred_element_type=f32)
            out.append((new_top, total, acc))
        return tuple(out)

    state = (
        (
            jnp.full((group * both, 1), FLOOR, f32),
            jnp.zeros((group * both, 1), f32),
            jnp.zeros((group * both, HEAD), f32),
        ),
    ) * kv_heads
    if all(piece.count == 1 for piece in pieces):
        for i in range(0, len(pieces), 2):
            pair = pieces[i : i + 2]
            state = absorb(
                state, [p.arrays[0][...] for p in pair], [p.source_of(shard, 0) for p in pair]
            )
    else:
        for piece in pieces:

            def step(i, carried):
                at = pl.multiple_of(i * rows, rows)
                block = piece.arrays[0][pl.ds(at, rows), :]
                return absorb(carried, [block], [piece.source_of(shard, i)])

            state = lax.fori_loop(0, piece.count, step, state)

    mine_ref, stat_ref, packed_ref = refs
    heads = q_width // HEAD
    lane = lax.broadcasted_iota(jnp.int32, (taken, HEAD), 1)
    mine = jnp.zeros((taken, HEAD), f32)
    theirs = jnp.zeros((taken, HEAD), f32)
    for g in range(kv_heads):
        top, total, acc = state[g]
        for j in range(group):
            h = g * group + j
            cols = slice(h * HEAD, (h + 1) * HEAD)
            near = slice(j * both, j * both + taken)
            far = slice(j * both + taken, (j + 1) * both)
            mine_ref[:, cols] = acc[near]
            packed_ref[:, cols] = acc[far].astype(bf16)
            for value, at in ((top, h), (total, heads + h)):
                mine = jnp.where(lane == at, value[near], mine)
                theirs = jnp.where(lane % (2 * heads) == at, value[far], theirs)
    stat_ref[...] = mine
    high = theirs.astype(bf16).astype(f32)
    middle = (theirs - high).astype(bf16).astype(f32)
    low = theirs - high - middle
    third = lane // (2 * heads)
    parts = jnp.where(third == 0, high, jnp.where(third == 1, middle, low))
    packed_ref[:, q_width:] = parts.astype(bf16)


def stage_kernel(block_ref, len_ref, kv_ref, kv_out, key_pos_ref, q_pos_ref, q_begin_ref):
    kv_out[...] = kv_ref[...]
    shards, rows = key_pos_ref.shape
    half = rows // 2
    shard = lax.axis_index("seq")

    def picked(values, mask):
        return jnp.sum(jnp.where(mask, values, 0.0), -1, keepdims=True).astype(jnp.int32)

    def lanes(shape):
        return lax.broadcasted_iota(jnp.int32, shape, 1)

    blocks = block_ref[...].astype(f32)
    square = (shards, shards)
    first = picked(blocks, lanes(square) == lax.broadcasted_iota(jnp.int32, square, 0))
    index = lanes((shards, rows))
    key_pos_ref[...] = index + jnp.where(index < half, first, 2 * shards - 2 - first) * half

    held = []
    for s in (shard, shard ^ 1):
        first = picked(blocks, lanes(block_ref.shape) == s)
        held += [first, 2 * shards - 1 - first]
    q_pos = positions(held, half, 0, q_pos_ref.shape)
    q_pos_ref[...] = q_pos
    lengths = len_ref[...].astype(f32)
    begin = jnp.zeros_like(q_pos)
    for r in range(1, len_ref.shape[1]):
        start = picked(lengths, lanes(len_ref.shape) < r)
        begin = jnp.where(q_pos >= start, start, begin)
    q_begin_ref[...] = begin


def joined_rows(partials, first, half):
    q_width = partials[0].shape[1]
    heads = q_width // HEAD
    part = pl.ds(pl.multiple_of(first, half), half)
    held = []
    for mine_ref, stat_ref, packed_ref in zip(partials[::3], partials[1::3], partials[2::3]):
        span = slice(None) if mine_ref.shape[0] == half else part
        parts = packed_ref[span, q_width:].astype(f32)
        stats = parts
        for t in (1, 2):
            stats = stats + pltpu.roll(parts, HEAD - 2 * heads * t, 1)
        held += [(mine_ref, span, stat_ref[span, :]), (packed_ref, span, stats)]
    top = functools.reduce(jnp.maximum, [stats for _, _, stats in held])
    shares = [jnp.exp2(stats - top) for _, _, stats in held]
    total = sum(
        share * pltpu.roll(stats, HEAD - heads, 1) for share, (_, _, stats) in zip(shares, held)
    )
    shares = [share / total for share in shares]
    context = []
    for h in range(heads):
        cols = slice(h * HEAD, (h + 1) * HEAD)
        context.append(
            sum(
                ref[span, cols].astype(f32) * share[:, h : h + 1]
                for (ref, span, _), share in zip(held, shares)
            ).astype(bf16)
        )
    return jnp.concatenate(context, 1)


def leave_kernel(wo_ref, *refs):
    partials, sent_ref = refs[:-1], refs[-1]
    half = sent_ref.shape[0]
    context = joined_rows(partials, (1 - lax.axis_index("req")) * half, half)
    sent_ref[...] = jnp.dot(context, wo_ref[...], preferred_element_type=f32).astype(bf16)


def keep_kernel(wo_ref, tok_ref, mine_ref, *refs):
    others, partials, (out_ref, cache_ref) = refs[:2], refs[2:-2], refs[-2:]
    share = mine_ref.shape[0] // 2
    for i, other_ref in enumerate(others):
        part = slice(i * share, (i + 1) * share)
        cache_ref[part] = mine_ref[part] + other_ref[...]
    half = out_ref.shape[0]
    first = lax.axis_index("req") * half
    context = joined_rows(partials, first, half)
    residual = tok_ref[pl.ds(pl.multiple_of(first, half), half), :].astype(f32)
    out_ref[...] = jnp.dot(context, wo_ref[...], preferred_element_type=f32) + residual


def finish_kernel(kept_ref, received_ref, hidden_ref):
    hidden_ref[...] = (kept_ref[...] + received_ref[...].astype(f32)).astype(bf16)


def cache_kernel(pieces, block_ref, slot_ref, *refs):
    pieces, (mine_ref, *other_refs) = with_refs(pieces, refs)
    shard = lax.axis_index("seq")
    slots = mine_ref.shape[0]
    key_width = mine_ref.shape[3]
    rows = slots * PAGE // 2
    pages = rows // 2 // PAGE
    for target in (mine_ref, *other_refs):
        target[...] = jnp.zeros_like(target)
    share = slots // len(other_refs)

    def place(ref, at, source):
        for k, block in enumerate(blocks_of(block_ref, source)):
            for j in range(pages):
                slot = slot_ref[block * pages + j]
                holder = slot // slots
                local = slot - holder * slots
                offset = at + (k * pages + j) * PAGE
                if not isinstance(offset, int):
                    offset = pl.multiple_of(offset, PAGE)

                def write(target, at_slot):
                    target[at_slot, 0] = ref[pl.ds(offset, PAGE), :key_width]
                    target[at_slot, 1] = ref[pl.ds(offset, PAGE), key_width:]

                @pl.when(holder == shard)
                def _():
                    write(mine_ref, local)

                for i, target in enumerate(other_refs):

                    @pl.when((holder == shard ^ 1) & (local // share == i))
                    def _():
                        write(target, local - i * share)

    for piece in pieces:
        if piece.count == 1:
            place(piece.arrays[0], 0, piece.source_of(shard, 0))
        else:

            def step(i, carry):
                place(piece.arrays[0], i * rows, piece.source_of(shard, i))
                return carry

            lax.fori_loop(0, piece.count, step, 0)


def tied_all(pieces, other):
    arrays, other = lax.optimization_barrier((operands(pieces), other))
    return with_refs(pieces, arrays)[0], other


def tied(piece, other):
    (piece,), other = tied_all([piece], other)
    return piece, other


def swap(x, n, bit):
    return lax.ppermute(x, "seq", [(i, i ^ bit) for i in range(n)])


class Piece:
    def __init__(self, arrays, source_of, count=1):
        self.arrays, self.source_of, self.count = arrays, source_of, count

    def moved(self, arrays):
        return Piece(arrays, self.source_of, self.count)


def operands(pieces):
    return [x for piece in pieces for x in piece.arrays]


def with_refs(pieces, refs):
    out = []
    for piece in pieces:
        taken, refs = refs[: len(piece.arrays)], refs[len(piece.arrays) :]
        out.append(piece.moved(taken))
    return out, refs


def at_distance(bits):
    return lambda shard, i: shard ^ bits


def move(x, pairs):
    return lax.ppermute(x, "seq", pairs)


def on_device(
    n, parts, tokens, norm_gain, w_query, key_projection, value_projection, w_out, lengths, block_split, page_slot,
):
    rows, width = tokens.shape
    half = rows // 2
    q_width = w_query.shape[1]
    kv_width = key_projection.shape[1] + value_projection.shape[1]
    kv, normed, turned = pl.pallas_call(
        project_kernel,
        out_shape=(
            struct((rows, kv_width), bf16),
            struct((rows, width), bf16),
            struct((rows, 2 * HEAD), f32),
        ),
        in_specs=in_hbm(7),
        out_specs=tuple(in_hbm(3)),
        scratch_shapes=[
            pltpu.SMEM(block_split.shape, jnp.int32),
            pltpu.SMEM(lengths.shape, jnp.int32),
            pltpu.VMEM((2 * half + 8, HEAD), f32),
            pltpu.VMEM((rows, width), bf16),
            pltpu.VMEM((1, width), f32),
            pltpu.VMEM(key_projection.shape, bf16),
            pltpu.VMEM(value_projection.shape, bf16),
            pltpu.VMEM((rows, kv_width), bf16),
            pltpu.VMEM((rows, width), bf16),
            pltpu.VMEM((rows, 2 * HEAD), f32),
            pltpu.SemaphoreType.DMA((5,)),
            pltpu.SemaphoreType.DMA((WEIGHT_STEPS,)),
            pltpu.SemaphoreType.DMA((WEIGHT_STEPS,)),
            pltpu.SemaphoreType.DMA((3,)),
        ],
        compiler_params=kernel_params(62),
        cost_estimate=cost(0, 0),
        name="project",
    )(
        block_split, lengths, rotary_constants(half), tokens, norm_gain.reshape(1, width),
        key_projection, value_projection,
    )
    staged, *places = pl.pallas_call(
        stage_kernel,
        out_shape=(
            struct((rows, kv_width), bf16),
            struct((n, rows), jnp.int32),
            struct((2 * rows, HEAD), jnp.int32),
            struct((2 * rows, HEAD), jnp.int32),
        ),
        in_specs=in_vmem(3),
        out_specs=tuple(in_vmem(4)),
        compiler_params=kernel_params(24),
        cost_estimate=cost(10**9, 10**7),
        name="stage",
    )(block_split.reshape(1, n), lengths.reshape(1, -1), kv)

    def project_queries(normed):
        queries = pl.pallas_call(
            query_kernel,
            out_shape=struct((rows, q_width), bf16),
            in_specs=in_vmem(3),
            out_specs=in_vmem(1)[0],
            compiler_params=kernel_params(24),
            cost_estimate=cost(0, 0),
            name="query",
        )(normed, turned, w_query)
        return queries, swap(queries, n, 1)

    def attend(queries, far_queries, pieces, side=None):
        arrays = operands(pieces)
        taken = rows if side is None else half
        mine, stats, packed = pl.pallas_call(
            functools.partial(attend_kernel, pieces, side),
            out_shape=(
                struct((taken, q_width), f32),
                struct((taken, HEAD), f32),
                struct((taken, q_width + HEAD), bf16),
            ),
            in_specs=in_vmem(5 + len(arrays)),
            out_specs=tuple(in_vmem(3)),
            compiler_params=kernel_params(32),
            cost_estimate=cost(0, 0),
            name="attend",
        )(*places, queries, far_queries, *arrays)
        return [mine, stats, packed]

    def place_pages(pieces):
        arrays = operands(pieces)
        shape = (2 * rows // PAGE, 2, PAGE, kv_width // 2)
        return pl.pallas_call(
            functools.partial(cache_kernel, pieces),
            out_shape=(struct(shape, bf16),) + (struct((shape[0] // 2,) + shape[1:], bf16),) * 2,
            in_specs=in_smem(2) + in_vmem(len(arrays)),
            out_specs=tuple(in_vmem(1 + 2)),
            compiler_params=kernel_params(32),
            cost_estimate=cost(0, 0),
            name="cache",
        )(block_split, page_slot, *arrays)

    if n == 16:

        def swapped(piece, bits):
            source = lambda shard, i: piece.source_of(shard ^ bits, i)
            return Piece([swap(piece.arrays[0], n, bits)], source)

        own = Piece([kv], at_distance(0))
        second, first, beside = swapped(own, 8), swapped(own, 4), swapped(own, 2)
        first, (normed, staged) = tied(first, (normed, staged))
        first_across = swapped(first, 2)
        queries, far_queries = project_queries(normed)
        second, (staged, queries) = tied(second, (staged, queries))
        own = own.moved([staged])
        third = swapped(second, 4)
        last = swapped(second, 6)
        (second, first_across, beside), _ = tied_all([second, first_across, beside], ())
        early = [own, beside, first, second, first_across]
        partials = attend(queries, far_queries, early)
        partials[2] = swap(partials[2], n, 1)
        queries, partials[1] = lax.optimization_barrier((queries, partials[1]))
        remaining = [third, last, swapped(second, 2)]
        placed = early + remaining
    else:
        same = [list(range(c, n, 2)) for c in range(2)]
        gathered = lax.all_gather(kv, "seq", axis=0, tiled=True, axis_index_groups=same)
        remaining = [Piece([gathered], lambda shard, i: 2 * i + shard % 2, n // 2)]
        partials, placed = [], remaining
        queries, far_queries = project_queries(normed)
    leaving = attend(queries, far_queries, remaining, 1)
    queries, leaving[1] = lax.optimization_barrier((queries, leaving[1]))
    leaving[2] = swap(leaving[2], n, 1)
    staying = attend(queries, far_queries, remaining, 0)
    leaving[0], staying[1] = lax.optimization_barrier((leaving[0], staying[1]))
    sent = pl.pallas_call(
        leave_kernel,
        out_shape=struct((half, width), bf16),
        in_specs=in_vmem(4 + len(partials)),
        out_specs=in_vmem(1)[0],
        compiler_params=kernel_params(24),
        cost_estimate=cost(0, 0),
        name="leave",
    )(w_out, *partials, *leaving)
    received = lax.ppermute(sent, "req", [(i, (i + 1) % parts) for i in range(parts)])
    staying[2] = swap(staying[2], n, 1)
    placed, (staying[2], sent) = tied_all(placed, (staying[2], sent))
    cache, *other = place_pages(placed)
    kept, cache = pl.pallas_call(
        keep_kernel,
        out_shape=(struct((half, width), f32), struct(cache.shape, bf16)),
        in_specs=in_vmem(6 + 2 + len(partials)),
        out_specs=tuple(in_vmem(2)),
        compiler_params=kernel_params(24),
        cost_estimate=cost(0, 0),
        name="keep",
    )(w_out, tokens, cache, *[swap(x, n, 1) for x in other], *partials, *staying)
    hidden = pl.pallas_call(
        finish_kernel,
        out_shape=struct((half, width), bf16),
        in_specs=in_vmem(2),
        out_specs=in_vmem(1)[0],
        compiler_params=kernel_params(24),
        cost_estimate=cost(0, 0),
        name="finish",
    )(kept, received)
    return hidden, cache


def solution(mesh):
    in_specs = (
        P("seq", None),
        P(),
        P(None, "req"),
        P(None, "req"),
        P(None, "req"),
        P("req", None),
        P(),
        P(),
        P(),
    )
    out_specs = (P(("seq", "req"), None), P("seq", None, None, "req"))
    body = functools.partial(on_device, mesh.shape["seq"], mesh.shape["req"])
    return jax.shard_map(body, mesh=mesh, in_specs=in_specs, out_specs=out_specs, check_vma=False)
```

```python
import functools
import math

import jax
import jax.numpy as jnp
import numpy as np
from jax import lax
from jax.experimental import pallas as pl
from jax.experimental.pallas import tpu as pltpu
from jax.sharding import PartitionSpec as P

HEAD = 128
PAGE = 32
THETA = 1000000.0
EPS = 1e-05
MASKED = -1e30
FLOOR = -1e29
WEIGHT_STEPS = 2
MIB = 1024 * 1024
SCALE = math.log2(math.e) / math.sqrt(HEAD)

f32 = jnp.float32
bf16 = jnp.bfloat16
struct = jax.ShapeDtypeStruct


def in_vmem(count):
    return [pl.BlockSpec(memory_space=pltpu.VMEM)] * count


def in_smem(count):
    return [pl.BlockSpec(memory_space=pltpu.SMEM)] * count


def in_hbm(count):
    return [pl.BlockSpec(memory_space=pltpu.HBM)] * count


def kernel_params(mib):
    return pltpu.CompilerParams(vmem_limit_bytes=mib * MIB)


def cost(flops, moved):
    return pl.CostEstimate(flops=flops, bytes_accessed=moved, transcendentals=0)


def rotary_constants(half):
    exponent = np.arange(HEAD // 2, dtype=np.float64) * (2.0 / HEAD)
    freq = np.tile(THETA**-exponent, 2)[None, :]
    angle = np.arange(half, dtype=np.float64)[:, None] * freq
    rows = [np.cos(angle), np.sin(angle), np.broadcast_to(freq, (8, HEAD))]
    return jnp.asarray(np.concatenate(rows).astype(np.float32))


def blocks_of(block_ref, shard):
    first = block_ref[shard]
    return first, 2 * block_ref.shape[0] - 1 - first


def positions(blocks, half, dim, shape):
    index = lax.broadcasted_iota(jnp.int32, shape, dim)
    offset = blocks[0] * half
    for i, block in enumerate(blocks[1:], 1):
        offset = jnp.where(index >= i * half, (block - i) * half, offset)
    return index + offset


def rotate(u, cosine, signed_sine):
    return u * cosine + pltpu.roll(u, HEAD // 2, 1) * signed_sine


def weight_copies(source, scratch, sems):
    depth = scratch.shape[0] // WEIGHT_STEPS
    return [
        pltpu.make_async_copy(
            source.at[pl.ds(step * depth, depth), :], scratch.at[pl.ds(step * depth, depth), :], sems.at[step]
        )
        for step in range(WEIGHT_STEPS)
    ]


def stepped_dot(left, copies, scratch):
    depth = scratch.shape[0] // WEIGHT_STEPS
    total = None
    for step, copy in enumerate(copies):
        copy.wait()
        rows = slice(step * depth, (step + 1) * depth)
        part = jnp.dot(left[:, rows], scratch[rows, :], preferred_element_type=f32)
        total = part if total is None else total + part
    return total


def rotary_tables(block_ref, len_ref, turn_ref, half):
    prompts = len_ref.shape[0]
    blocks = blocks_of(block_ref, lax.axis_index("seq"))
    starts = [jnp.int32(0)]
    for r in range(prompts - 1):
        starts.append(starts[-1] + len_ref[r])
    count = 2 * prompts
    index = lax.broadcasted_iota(jnp.int32, (count, HEAD), 0)
    base = jnp.zeros((count, HEAD), jnp.int32)
    for k, block in enumerate(blocks):
        for p, start in enumerate(starts):
            base = jnp.where(index == k * prompts + p, block * half - start, base)
    angle = base.astype(f32) * turn_ref[2 * half : 2 * half + 1, :]
    base_cos, base_sin = jnp.cos(angle), jnp.sin(angle)
    row_cos, row_sin = turn_ref[:half, :], turn_ref[half : 2 * half, :]
    row = lax.broadcasted_iota(jnp.int32, (half, HEAD), 0)
    lane = lax.broadcasted_iota(jnp.int32, (half, HEAD), 1)
    cosines, sines = [], []
    for k, block in enumerate(blocks):
        at = k * prompts
        cos, sin = base_cos[at : at + 1], base_sin[at : at + 1]
        for p in range(1, prompts):
            inside = row >= starts[p] - block * half
            cos = jnp.where(inside, base_cos[at + p : at + p + 1], cos)
            sin = jnp.where(inside, base_sin[at + p : at + p + 1], sin)
        cosines.append(row_cos * cos - row_sin * sin)
        sine = row_sin * cos + row_cos * sin
        sines.append(jnp.where(lane < HEAD // 2, -sine, sine))
    return jnp.concatenate(cosines, 0), jnp.concatenate(sines, 0)


def project_kernel(
    block_hbm, len_hbm, turn_hbm, tok_hbm, gain_hbm, wk_hbm, wv_hbm,
    kv_hbm, normed_hbm, turned_hbm,
    block_ref, len_ref, turn_ref, tok_ref, gain_ref, k_weights, v_weights, kv_ref, normed_ref, turned_ref,
    small_sems, k_sems, v_sems, out_sems,
):
    small = [
        pltpu.make_async_copy(source, target, small_sems.at[i])
        for i, (source, target) in enumerate(
            (
                (tok_hbm, tok_ref),
                (block_hbm, block_ref),
                (len_hbm, len_ref),
                (turn_hbm, turn_ref),
                (gain_hbm, gain_ref),
            )
        )
    ]
    k_copies = weight_copies(wk_hbm, k_weights, k_sems)
    v_copies = weight_copies(wv_hbm, v_weights, v_sems)
    for copy in small + k_copies + v_copies:
        copy.start()
    rows = tok_ref.shape[0]
    key_width = wk_hbm.shape[1]
    for copy in small:
        copy.wait()
    wide = tok_ref[...].astype(f32)
    scale = lax.rsqrt(jnp.mean(wide * wide, -1, keepdims=True) + EPS)
    normed = (wide * scale * gain_ref[...]).astype(bf16)
    normed_ref[...] = normed
    writes = [
        pltpu.make_async_copy(source, target, out_sems.at[i])
        for i, (source, target) in enumerate(
            ((normed_ref, normed_hbm), (turned_ref, turned_hbm), (kv_ref, kv_hbm))
        )
    ]
    writes[0].start()
    cosine, sine = rotary_tables(block_ref, len_ref, turn_ref, rows // 2)
    turned_ref[:, :HEAD] = cosine
    turned_ref[:, HEAD:] = sine
    writes[1].start()
    product = stepped_dot(normed, k_copies, k_weights)
    for h in range(key_width // HEAD):
        cols = slice(h * HEAD, (h + 1) * HEAD)
        kv_ref[:, cols] = rotate(product[:, cols], cosine, sine).astype(bf16)
    kv_ref[:, key_width:] = stepped_dot(normed, v_copies, v_weights).astype(bf16)
    writes[2].start()
    for copy in writes:
        copy.wait()


def query_kernel(normed_ref, turned_ref, wq_ref, q_ref):
    product = jnp.dot(normed_ref[...], wq_ref[...], preferred_element_type=f32)
    cosine, sine = turned_ref[:, :HEAD], turned_ref[:, HEAD:]
    for h in range(q_ref.shape[1] // HEAD):
        cols = slice(h * HEAD, (h + 1) * HEAD)
        q_ref[:, cols] = rotate(product[:, cols], cosine, sine).astype(bf16)


def attend_kernel(pieces, side, key_pos_ref, q_pos_ref, q_begin_ref, q_ref, far_ref, *refs):
    pieces, refs = with_refs(pieces, refs)
    shard = lax.axis_index("seq")
    rows, q_width = q_ref.shape
    key_width = pieces[0].arrays[0].shape[1] // 2
    kv_heads = key_width // HEAD
    group = q_width // key_width
    if side is None:
        taken, first = rows, 0
        span = slice(None)
    else:
        part = lax.axis_index("req")
        taken = rows // 2
        first = pl.multiple_of((1 - part if side else part) * taken, taken)
        span = pl.ds(first, taken)
    both = 2 * taken

    def of_both_cores(ref):
        return jnp.concatenate(
            [ref[pl.ds(pl.multiple_of(core * rows + first, taken), taken), :] for core in (0, 1)], 0
        )

    q_pos, q_begin = of_both_cores(q_pos_ref), of_both_cores(q_begin_ref)
    queries = [
        jnp.concatenate(
            [
                ref[span, h * HEAD : (h + 1) * HEAD]
                for h in range(g * group, (g + 1) * group)
                for ref in (q_ref, far_ref)
            ],
            0,
        )
        for g in range(kv_heads)
    ]

    def absorb(state, blocks, sources):
        bias = []
        for source in sources:
            key_pos = key_pos_ref[pl.ds(source, 1), :]
            bias.append(jnp.where((key_pos >= q_begin) & (key_pos <= q_pos), 0.0, MASKED))
        bias = jnp.concatenate(bias, 1)
        bias = jnp.concatenate([bias] * group, 0)
        out = []
        for g in range(kv_heads):
            top, total, acc = state[g]
            keys = jnp.concatenate([b[:, g * HEAD : (g + 1) * HEAD] for b in blocks], 0)
            values = jnp.concatenate(
                [b[:, key_width + g * HEAD : key_width + (g + 1) * HEAD] for b in blocks], 0
            )
            scores = lax.dot_general(
                queries[g], keys, (((1,), (1,)), ((), ())), preferred_element_type=f32
            )
            scores = scores * SCALE + bias
            new_top = jnp.maximum(top, jnp.max(scores, -1, keepdims=True))
            weights = jnp.exp2(scores - new_top)
            factor = jnp.exp2(top - new_top)
            total = total * factor + jnp.sum(weights, -1, keepdims=True)
            acc = acc * factor + jnp.dot(weights.astype(bf16), values, preferred_element_type=f32)
            out.append((new_top, total, acc))
        return tuple(out)

    state = (
        (
            jnp.full((group * both, 1), FLOOR, f32),
            jnp.zeros((group * both, 1), f32),
            jnp.zeros((group * both, HEAD), f32),
        ),
    ) * kv_heads
    if all(piece.count == 1 for piece in pieces):
        for i in range(0, len(pieces), 2):
            pair = pieces[i : i + 2]
            state = absorb(
                state, [p.arrays[0][...] for p in pair], [p.source_of(shard, 0) for p in pair]
            )
    else:
        for piece in pieces:

            def step(i, carried):
                at = pl.multiple_of(i * rows, rows)
                block = piece.arrays[0][pl.ds(at, rows), :]
                return absorb(carried, [block], [piece.source_of(shard, i)])

            state = lax.fori_loop(0, piece.count, step, state)

    mine_ref, stat_ref, packed_ref = refs
    heads = q_width // HEAD
    lane = lax.broadcasted_iota(jnp.int32, (taken, HEAD), 1)
    mine = jnp.zeros((taken, HEAD), f32)
    theirs = jnp.zeros((taken, HEAD), f32)
    for g in range(kv_heads):
        top, total, acc = state[g]
        for j in range(group):
            h = g * group + j
            cols = slice(h * HEAD, (h + 1) * HEAD)
            near = slice(j * both, j * both + taken)
            far = slice(j * both + taken, (j + 1) * both)
            mine_ref[:, cols] = acc[near]
            packed_ref[:, cols] = acc[far].astype(bf16)
            for value, at in ((top, h), (total, heads + h)):
                mine = jnp.where(lane == at, value[near], mine)
                theirs = jnp.where(lane % (2 * heads) == at, value[far], theirs)
    stat_ref[...] = mine
    high = theirs.astype(bf16).astype(f32)
    middle = (theirs - high).astype(bf16).astype(f32)
    low = theirs - high - middle
    third = lane // (2 * heads)
    parts = jnp.where(third == 0, high, jnp.where(third == 1, middle, low))
    packed_ref[:, q_width:] = parts.astype(bf16)


def stage_kernel(block_ref, len_ref, kv_ref, kv_out, key_pos_ref, q_pos_ref, q_begin_ref):
    kv_out[...] = kv_ref[...]
    shards, rows = key_pos_ref.shape
    half = rows // 2
    shard = lax.axis_index("seq")

    def picked(values, mask):
        return jnp.sum(jnp.where(mask, values, 0.0), -1, keepdims=True).astype(jnp.int32)

    def lanes(shape):
        return lax.broadcasted_iota(jnp.int32, shape, 1)

    blocks = block_ref[...].astype(f32)
    square = (shards, shards)
    first = picked(blocks, lanes(square) == lax.broadcasted_iota(jnp.int32, square, 0))
    index = lanes((shards, rows))
    key_pos_ref[...] = index + jnp.where(index < half, first, 2 * shards - 2 - first) * half

    held = []
    for s in (shard, shard ^ 1):
        first = picked(blocks, lanes(block_ref.shape) == s)
        held += [first, 2 * shards - 1 - first]
    q_pos = positions(held, half, 0, q_pos_ref.shape)
    q_pos_ref[...] = q_pos
    lengths = len_ref[...].astype(f32)
    begin = jnp.zeros_like(q_pos)
    for r in range(1, len_ref.shape[1]):
        start = picked(lengths, lanes(len_ref.shape) < r)
        begin = jnp.where(q_pos >= start, start, begin)
    q_begin_ref[...] = begin


def joined_rows(partials, first, half):
    q_width = partials[0].shape[1]
    heads = q_width // HEAD
    part = pl.ds(pl.multiple_of(first, half), half)
    held = []
    for mine_ref, stat_ref, packed_ref in zip(partials[::3], partials[1::3], partials[2::3]):
        span = slice(None) if mine_ref.shape[0] == half else part
        parts = packed_ref[span, q_width:].astype(f32)
        stats = parts
        for t in (1, 2):
            stats = stats + pltpu.roll(parts, HEAD - 2 * heads * t, 1)
        held += [(mine_ref, span, stat_ref[span, :]), (packed_ref, span, stats)]
    top = functools.reduce(jnp.maximum, [stats for _, _, stats in held])
    shares = [jnp.exp2(stats - top) for _, _, stats in held]
    total = sum(
        share * pltpu.roll(stats, HEAD - heads, 1) for share, (_, _, stats) in zip(shares, held)
    )
    shares = [share / total for share in shares]
    context = []
    for h in range(heads):
        cols = slice(h * HEAD, (h + 1) * HEAD)
        context.append(
            sum(
                ref[span, cols].astype(f32) * share[:, h : h + 1]
                for (ref, span, _), share in zip(held, shares)
            ).astype(bf16)
        )
    return jnp.concatenate(context, 1)


def leave_kernel(wo_ref, *refs):
    partials, sent_ref = refs[:-1], refs[-1]
    half = sent_ref.shape[0]
    context = joined_rows(partials, (1 - lax.axis_index("req")) * half, half)
    sent_ref[...] = jnp.dot(context, wo_ref[...], preferred_element_type=f32).astype(bf16)


def keep_kernel(wo_ref, tok_ref, mine_ref, *refs):
    others, partials, (out_ref, cache_ref) = refs[:2], refs[2:-2], refs[-2:]
    share = mine_ref.shape[0] // 2
    for i, other_ref in enumerate(others):
        part = slice(i * share, (i + 1) * share)
        cache_ref[part] = mine_ref[part] + other_ref[...]
    half = out_ref.shape[0]
    first = lax.axis_index("req") * half
    context = joined_rows(partials, first, half)
    residual = tok_ref[pl.ds(pl.multiple_of(first, half), half), :].astype(f32)
    out_ref[...] = jnp.dot(context, wo_ref[...], preferred_element_type=f32) + residual


def finish_kernel(kept_ref, received_ref, hidden_ref):
    hidden_ref[...] = (kept_ref[...] + received_ref[...].astype(f32)).astype(bf16)


def cache_kernel(pieces, block_ref, slot_ref, *refs):
    pieces, (mine_ref, *other_refs) = with_refs(pieces, refs)
    shard = lax.axis_index("seq")
    slots = mine_ref.shape[0]
    key_width = mine_ref.shape[3]
    rows = slots * PAGE // 2
    pages = rows // 2 // PAGE
    for target in (mine_ref, *other_refs):
        target[...] = jnp.zeros_like(target)
    share = slots // len(other_refs)

    def place(ref, at, source):
        for k, block in enumerate(blocks_of(block_ref, source)):
            for j in range(pages):
                slot = slot_ref[block * pages + j]
                holder = slot // slots
                local = slot - holder * slots
                offset = at + (k * pages + j) * PAGE
                if not isinstance(offset, int):
                    offset = pl.multiple_of(offset, PAGE)

                def write(target, at_slot):
                    target[at_slot, 0] = ref[pl.ds(offset, PAGE), :key_width]
                    target[at_slot, 1] = ref[pl.ds(offset, PAGE), key_width:]

                @pl.when(holder == shard)
                def _():
                    write(mine_ref, local)

                for i, target in enumerate(other_refs):

                    @pl.when((holder == shard ^ 1) & (local // share == i))
                    def _():
                        write(target, local - i * share)

    for piece in pieces:
        if piece.count == 1:
            place(piece.arrays[0], 0, piece.source_of(shard, 0))
        else:

            def step(i, carry):
                place(piece.arrays[0], i * rows, piece.source_of(shard, i))
                return carry

            lax.fori_loop(0, piece.count, step, 0)


def tied_all(pieces, other):
    arrays, other = lax.optimization_barrier((operands(pieces), other))
    return with_refs(pieces, arrays)[0], other


def tied(piece, other):
    (piece,), other = tied_all([piece], other)
    return piece, other


def swap(x, n, bit):
    return lax.ppermute(x, "seq", [(i, i ^ bit) for i in range(n)])


class Piece:
    def __init__(self, arrays, source_of, count=1):
        self.arrays, self.source_of, self.count = arrays, source_of, count

    def moved(self, arrays):
        return Piece(arrays, self.source_of, self.count)


def operands(pieces):
    return [x for piece in pieces for x in piece.arrays]


def with_refs(pieces, refs):
    out = []
    for piece in pieces:
        taken, refs = refs[: len(piece.arrays)], refs[len(piece.arrays) :]
        out.append(piece.moved(taken))
    return out, refs


def at_distance(bits):
    return lambda shard, i: shard ^ bits


def move(x, pairs):
    return lax.ppermute(x, "seq", pairs)


def on_device(
    n, parts, tokens, norm_gain, w_query, key_projection, value_projection, w_out, lengths, block_split, page_slot,
):
    rows, width = tokens.shape
    half = rows // 2
    q_width = w_query.shape[1]
    kv_width = key_projection.shape[1] + value_projection.shape[1]
    kv, normed, turned = pl.pallas_call(
        project_kernel,
        out_shape=(
            struct((rows, kv_width), bf16),
            struct((rows, width), bf16),
            struct((rows, 2 * HEAD), f32),
        ),
        in_specs=in_hbm(7),
        out_specs=tuple(in_hbm(3)),
        scratch_shapes=[
            pltpu.SMEM(block_split.shape, jnp.int32),
            pltpu.SMEM(lengths.shape, jnp.int32),
            pltpu.VMEM((2 * half + 8, HEAD), f32),
            pltpu.VMEM((rows, width), bf16),
            pltpu.VMEM((1, width), f32),
            pltpu.VMEM(key_projection.shape, bf16),
            pltpu.VMEM(value_projection.shape, bf16),
            pltpu.VMEM((rows, kv_width), bf16),
            pltpu.VMEM((rows, width), bf16),
            pltpu.VMEM((rows, 2 * HEAD), f32),
            pltpu.SemaphoreType.DMA((5,)),
            pltpu.SemaphoreType.DMA((WEIGHT_STEPS,)),
            pltpu.SemaphoreType.DMA((WEIGHT_STEPS,)),
            pltpu.SemaphoreType.DMA((3,)),
        ],
        compiler_params=kernel_params(62),
        cost_estimate=cost(0, 0),
        name="project",
    )(
        block_split, lengths, rotary_constants(half), tokens, norm_gain.reshape(1, width),
        key_projection, value_projection,
    )
    staged, *places = pl.pallas_call(
        stage_kernel,
        out_shape=(
            struct((rows, kv_width), bf16),
            struct((n, rows), jnp.int32),
            struct((2 * rows, HEAD), jnp.int32),
            struct((2 * rows, HEAD), jnp.int32),
        ),
        in_specs=in_vmem(3),
        out_specs=tuple(in_vmem(4)),
        compiler_params=kernel_params(24),
        cost_estimate=cost(10**9, 10**7),
        name="stage",
    )(block_split.reshape(1, n), lengths.reshape(1, -1), kv)

    def project_queries(normed):
        queries = pl.pallas_call(
            query_kernel,
            out_shape=struct((rows, q_width), bf16),
            in_specs=in_vmem(3),
            out_specs=in_vmem(1)[0],
            compiler_params=kernel_params(24),
            cost_estimate=cost(0, 0),
            name="query",
        )(normed, turned, w_query)
        return queries, swap(queries, n, 1)

    def attend(queries, far_queries, pieces, side=None):
        arrays = operands(pieces)
        taken = rows if side is None else half
        mine, stats, packed = pl.pallas_call(
            functools.partial(attend_kernel, pieces, side),
            out_shape=(
                struct((taken, q_width), f32),
                struct((taken, HEAD), f32),
                struct((taken, q_width + HEAD), bf16),
            ),
            in_specs=in_vmem(5 + len(arrays)),
            out_specs=tuple(in_vmem(3)),
            compiler_params=kernel_params(32),
            cost_estimate=cost(0, 0),
            name="attend",
        )(*places, queries, far_queries, *arrays)
        return [mine, stats, packed]

    def place_pages(pieces):
        arrays = operands(pieces)
        shape = (2 * rows // PAGE, 2, PAGE, kv_width // 2)
        return pl.pallas_call(
            functools.partial(cache_kernel, pieces),
            out_shape=(struct(shape, bf16),) + (struct((shape[0] // 2,) + shape[1:], bf16),) * 2,
            in_specs=in_smem(2) + in_vmem(len(arrays)),
            out_specs=tuple(in_vmem(1 + 2)),
            compiler_params=kernel_params(32),
            cost_estimate=cost(0, 0),
            name="cache",
        )(block_split, page_slot, *arrays)

    if n == 16:

        def swapped(piece, bits):
            source = lambda shard, i: piece.source_of(shard ^ bits, i)
            return Piece([swap(piece.arrays[0], n, bits)], source)

        own = Piece([kv], at_distance(0))
        second, first, beside = swapped(own, 8), swapped(own, 4), swapped(own, 2)
        first, (normed, staged) = tied(first, (normed, staged))
        first_across = swapped(first, 2)
        queries, far_queries = project_queries(normed)
        second, (staged, queries) = tied(second, (staged, queries))
        own = own.moved([staged])
        last = swapped(second, 6)
        (second, first_across, beside), _ = tied_all([second, first_across, beside], ())
        third = swapped(second, 4)
        early = [own, beside, first, second, first_across]
        partials = attend(queries, far_queries, early)
        partials[2] = swap(partials[2], n, 1)
        queries, partials[1] = lax.optimization_barrier((queries, partials[1]))
        remaining = [third, last, swapped(second, 2)]
        placed = early + remaining
    else:
        same = [list(range(c, n, 2)) for c in range(2)]
        gathered = lax.all_gather(kv, "seq", axis=0, tiled=True, axis_index_groups=same)
        remaining = [Piece([gathered], lambda shard, i: 2 * i + shard % 2, n // 2)]
        partials, placed = [], remaining
        queries, far_queries = project_queries(normed)
    leaving = attend(queries, far_queries, remaining, 1)
    queries, leaving[1] = lax.optimization_barrier((queries, leaving[1]))
    leaving[2] = swap(leaving[2], n, 1)
    staying = attend(queries, far_queries, remaining, 0)
    leaving[0], staying[1] = lax.optimization_barrier((leaving[0], staying[1]))
    sent = pl.pallas_call(
        leave_kernel,
        out_shape=struct((half, width), bf16),
        in_specs=in_vmem(4 + len(partials)),
        out_specs=in_vmem(1)[0],
        compiler_params=kernel_params(24),
        cost_estimate=cost(0, 0),
        name="leave",
    )(w_out, *partials, *leaving)
    received = lax.ppermute(sent, "req", [(i, (i + 1) % parts) for i in range(parts)])
    staying[2] = swap(staying[2], n, 1)
    placed, (staying[2], sent) = tied_all(placed, (staying[2], sent))
    cache, *other = place_pages(placed)
    kept, cache = pl.pallas_call(
        keep_kernel,
        out_shape=(struct((half, width), f32), struct(cache.shape, bf16)),
        in_specs=in_vmem(6 + 2 + len(partials)),
        out_specs=tuple(in_vmem(2)),
        compiler_params=kernel_params(24),
        cost_estimate=cost(0, 0),
        name="keep",
    )(w_out, tokens, cache, *[swap(x, n, 1) for x in other], *partials, *staying)
    hidden = pl.pallas_call(
        finish_kernel,
        out_shape=struct((half, width), bf16),
        in_specs=in_vmem(2),
        out_specs=in_vmem(1)[0],
        compiler_params=kernel_params(24),
        cost_estimate=cost(0, 0),
        name="finish",
    )(kept, received)
    return hidden, cache


def solution(mesh):
    in_specs = (
        P("seq", None),
        P(),
        P(None, "req"),
        P(None, "req"),
        P(None, "req"),
        P("req", None),
        P(),
        P(),
        P(),
    )
    out_specs = (P(("seq", "req"), None), P("seq", None, None, "req"))
    body = functools.partial(on_device, mesh.shape["seq"], mesh.shape["req"])
    return jax.shard_map(body, mesh=mesh, in_specs=in_specs, out_specs=out_specs, check_vma=False)
```

```python
import functools
import math

import jax
import jax.numpy as jnp
import numpy as np
from jax import lax
from jax.experimental import pallas as pl
from jax.experimental.pallas import tpu as pltpu
from jax.sharding import PartitionSpec as P

HEAD = 128
PAGE = 32
THETA = 1000000.0
EPS = 1e-05
MASKED = -1e30
FLOOR = -1e29
WEIGHT_STEPS = 2
MIB = 1024 * 1024
SCALE = math.log2(math.e) / math.sqrt(HEAD)

f32 = jnp.float32
bf16 = jnp.bfloat16
struct = jax.ShapeDtypeStruct


def in_vmem(count):
    return [pl.BlockSpec(memory_space=pltpu.VMEM)] * count


def in_smem(count):
    return [pl.BlockSpec(memory_space=pltpu.SMEM)] * count


def in_hbm(count):
    return [pl.BlockSpec(memory_space=pltpu.HBM)] * count


def kernel_params(mib):
    return pltpu.CompilerParams(vmem_limit_bytes=mib * MIB)


def cost(flops, moved):
    return pl.CostEstimate(flops=flops, bytes_accessed=moved, transcendentals=0)


def rotary_constants(half):
    exponent = np.arange(HEAD // 2, dtype=np.float64) * (2.0 / HEAD)
    freq = np.tile(THETA**-exponent, 2)[None, :]
    angle = np.arange(half, dtype=np.float64)[:, None] * freq
    rows = [np.cos(angle), np.sin(angle), np.broadcast_to(freq, (8, HEAD))]
    return jnp.asarray(np.concatenate(rows).astype(np.float32))


def blocks_of(block_ref, shard):
    first = block_ref[shard]
    return first, 2 * block_ref.shape[0] - 1 - first


def positions(blocks, half, dim, shape):
    index = lax.broadcasted_iota(jnp.int32, shape, dim)
    offset = blocks[0] * half
    for i, block in enumerate(blocks[1:], 1):
        offset = jnp.where(index >= i * half, (block - i) * half, offset)
    return index + offset


def rotate(u, cosine, signed_sine):
    return u * cosine + pltpu.roll(u, HEAD // 2, 1) * signed_sine


def weight_copies(source, scratch, sems):
    depth = scratch.shape[0] // WEIGHT_STEPS
    return [
        pltpu.make_async_copy(
            source.at[pl.ds(step * depth, depth), :], scratch.at[pl.ds(step * depth, depth), :], sems.at[step]
        )
        for step in range(WEIGHT_STEPS)
    ]


def stepped_dot(left, copies, scratch):
    depth = scratch.shape[0] // WEIGHT_STEPS
    total = None
    for step, copy in enumerate(copies):
        copy.wait()
        rows = slice(step * depth, (step + 1) * depth)
        part = jnp.dot(left[:, rows], scratch[rows, :], preferred_element_type=f32)
        total = part if total is None else total + part
    return total


def rotary_tables(block_ref, len_ref, turn_ref, half):
    prompts = len_ref.shape[0]
    blocks = blocks_of(block_ref, lax.axis_index("seq"))
    starts = [jnp.int32(0)]
    for r in range(prompts - 1):
        starts.append(starts[-1] + len_ref[r])
    count = 2 * prompts
    index = lax.broadcasted_iota(jnp.int32, (count, HEAD), 0)
    base = jnp.zeros((count, HEAD), jnp.int32)
    for k, block in enumerate(blocks):
        for p, start in enumerate(starts):
            base = jnp.where(index == k * prompts + p, block * half - start, base)
    angle = base.astype(f32) * turn_ref[2 * half : 2 * half + 1, :]
    base_cos, base_sin = jnp.cos(angle), jnp.sin(angle)
    row_cos, row_sin = turn_ref[:half, :], turn_ref[half : 2 * half, :]
    row = lax.broadcasted_iota(jnp.int32, (half, HEAD), 0)
    lane = lax.broadcasted_iota(jnp.int32, (half, HEAD), 1)
    cosines, sines = [], []
    for k, block in enumerate(blocks):
        at = k * prompts
        cos, sin = base_cos[at : at + 1], base_sin[at : at + 1]
        for p in range(1, prompts):
            inside = row >= starts[p] - block * half
            cos = jnp.where(inside, base_cos[at + p : at + p + 1], cos)
            sin = jnp.where(inside, base_sin[at + p : at + p + 1], sin)
        cosines.append(row_cos * cos - row_sin * sin)
        sine = row_sin * cos + row_cos * sin
        sines.append(jnp.where(lane < HEAD // 2, -sine, sine))
    return jnp.concatenate(cosines, 0), jnp.concatenate(sines, 0)


def project_kernel(
    block_hbm, len_hbm, turn_hbm, tok_hbm, gain_hbm, wk_hbm, wv_hbm,
    kv_hbm, normed_hbm, turned_hbm,
    block_ref, len_ref, turn_ref, tok_ref, gain_ref, k_weights, v_weights, kv_ref, normed_ref, turned_ref,
    small_sems, k_sems, v_sems, out_sems,
):
    small = [
        pltpu.make_async_copy(source, target, small_sems.at[i])
        for i, (source, target) in enumerate(
            (
                (tok_hbm, tok_ref),
                (block_hbm, block_ref),
                (len_hbm, len_ref),
                (turn_hbm, turn_ref),
                (gain_hbm, gain_ref),
            )
        )
    ]
    k_copies = weight_copies(wk_hbm, k_weights, k_sems)
    v_copies = weight_copies(wv_hbm, v_weights, v_sems)
    for copy in small + k_copies + v_copies:
        copy.start()
    rows = tok_ref.shape[0]
    key_width = wk_hbm.shape[1]
    for copy in small:
        copy.wait()
    wide = tok_ref[...].astype(f32)
    scale = lax.rsqrt(jnp.mean(wide * wide, -1, keepdims=True) + EPS)
    normed = (wide * scale * gain_ref[...]).astype(bf16)
    normed_ref[...] = normed
    writes = [
        pltpu.make_async_copy(source, target, out_sems.at[i])
        for i, (source, target) in enumerate(
            ((normed_ref, normed_hbm), (turned_ref, turned_hbm), (kv_ref, kv_hbm))
        )
    ]
    writes[0].start()
    cosine, sine = rotary_tables(block_ref, len_ref, turn_ref, rows // 2)
    turned_ref[:, :HEAD] = cosine
    turned_ref[:, HEAD:] = sine
    writes[1].start()
    product = stepped_dot(normed, k_copies, k_weights)
    for h in range(key_width // HEAD):
        cols = slice(h * HEAD, (h + 1) * HEAD)
        kv_ref[:, cols] = rotate(product[:, cols], cosine, sine).astype(bf16)
    kv_ref[:, key_width:] = stepped_dot(normed, v_copies, v_weights).astype(bf16)
    writes[2].start()
    for copy in writes:
        copy.wait()


def query_kernel(normed_ref, turned_ref, wq_ref, q_ref):
    product = jnp.dot(normed_ref[...], wq_ref[...], preferred_element_type=f32)
    cosine, sine = turned_ref[:, :HEAD], turned_ref[:, HEAD:]
    for h in range(q_ref.shape[1] // HEAD):
        cols = slice(h * HEAD, (h + 1) * HEAD)
        q_ref[:, cols] = rotate(product[:, cols], cosine, sine).astype(bf16)


def attend_kernel(pieces, side, key_pos_ref, q_pos_ref, q_begin_ref, q_ref, far_ref, *refs):
    pieces, refs = with_refs(pieces, refs)
    shard = lax.axis_index("seq")
    rows, q_width = q_ref.shape
    key_width = pieces[0].arrays[0].shape[1] // 2
    kv_heads = key_width // HEAD
    group = q_width // key_width
    if side is None:
        taken, first = rows, 0
        span = slice(None)
    else:
        part = lax.axis_index("req")
        taken = rows // 2
        first = pl.multiple_of((1 - part if side else part) * taken, taken)
        span = pl.ds(first, taken)
    both = 2 * taken

    def of_both_cores(ref):
        return jnp.concatenate(
            [ref[pl.ds(pl.multiple_of(core * rows + first, taken), taken), :] for core in (0, 1)], 0
        )

    q_pos, q_begin = of_both_cores(q_pos_ref), of_both_cores(q_begin_ref)
    queries = [
        jnp.concatenate(
            [
                ref[span, h * HEAD : (h + 1) * HEAD]
                for h in range(g * group, (g + 1) * group)
                for ref in (q_ref, far_ref)
            ],
            0,
        )
        for g in range(kv_heads)
    ]

    def absorb(state, blocks, sources):
        bias = []
        for source in sources:
            key_pos = key_pos_ref[pl.ds(source, 1), :]
            bias.append(jnp.where((key_pos >= q_begin) & (key_pos <= q_pos), 0.0, MASKED))
        bias = jnp.concatenate(bias, 1)
        bias = jnp.concatenate([bias] * group, 0)
        out = []
        for g in range(kv_heads):
            top, total, acc = state[g]
            keys = jnp.concatenate([b[:, g * HEAD : (g + 1) * HEAD] for b in blocks], 0)
            values = jnp.concatenate(
                [b[:, key_width + g * HEAD : key_width + (g + 1) * HEAD] for b in blocks], 0
            )
            scores = lax.dot_general(
                queries[g], keys, (((1,), (1,)), ((), ())), preferred_element_type=f32
            )
            scores = scores * SCALE + bias
            new_top = jnp.maximum(top, jnp.max(scores, -1, keepdims=True))
            weights = jnp.exp2(scores - new_top)
            factor = jnp.exp2(top - new_top)
            total = total * factor + jnp.sum(weights, -1, keepdims=True)
            acc = acc * factor + jnp.dot(weights.astype(bf16), values, preferred_element_type=f32)
            out.append((new_top, total, acc))
        return tuple(out)

    state = (
        (
            jnp.full((group * both, 1), FLOOR, f32),
            jnp.zeros((group * both, 1), f32),
            jnp.zeros((group * both, HEAD), f32),
        ),
    ) * kv_heads
    if all(piece.count == 1 for piece in pieces):
        for i in range(0, len(pieces), 2):
            pair = pieces[i : i + 2]
            state = absorb(
                state, [p.arrays[0][...] for p in pair], [p.source_of(shard, 0) for p in pair]
            )
    else:
        for piece in pieces:

            def step(i, carried):
                at = pl.multiple_of(i * rows, rows)
                block = piece.arrays[0][pl.ds(at, rows), :]
                return absorb(carried, [block], [piece.source_of(shard, i)])

            state = lax.fori_loop(0, piece.count, step, state)

    mine_ref, stat_ref, packed_ref = refs
    heads = q_width // HEAD
    lane = lax.broadcasted_iota(jnp.int32, (taken, HEAD), 1)
    mine = jnp.zeros((taken, HEAD), f32)
    theirs = jnp.zeros((taken, HEAD), f32)
    for g in range(kv_heads):
        top, total, acc = state[g]
        for j in range(group):
            h = g * group + j
            cols = slice(h * HEAD, (h + 1) * HEAD)
            near = slice(j * both, j * both + taken)
            far = slice(j * both + taken, (j + 1) * both)
            mine_ref[:, cols] = acc[near]
            packed_ref[:, cols] = acc[far].astype(bf16)
            for value, at in ((top, h), (total, heads + h)):
                mine = jnp.where(lane == at, value[near], mine)
                theirs = jnp.where(lane % (2 * heads) == at, value[far], theirs)
    stat_ref[...] = mine
    high = theirs.astype(bf16).astype(f32)
    middle = (theirs - high).astype(bf16).astype(f32)
    low = theirs - high - middle
    third = lane // (2 * heads)
    parts = jnp.where(third == 0, high, jnp.where(third == 1, middle, low))
    packed_ref[:, q_width:] = parts.astype(bf16)


def stage_kernel(block_ref, len_ref, kv_ref, kv_out, key_pos_ref, q_pos_ref, q_begin_ref):
    kv_out[...] = kv_ref[...]
    shards, rows = key_pos_ref.shape
    half = rows // 2
    shard = lax.axis_index("seq")

    def picked(values, mask):
        return jnp.sum(jnp.where(mask, values, 0.0), -1, keepdims=True).astype(jnp.int32)

    def lanes(shape):
        return lax.broadcasted_iota(jnp.int32, shape, 1)

    blocks = block_ref[...].astype(f32)
    square = (shards, shards)
    first = picked(blocks, lanes(square) == lax.broadcasted_iota(jnp.int32, square, 0))
    index = lanes((shards, rows))
    key_pos_ref[...] = index + jnp.where(index < half, first, 2 * shards - 2 - first) * half

    held = []
    for s in (shard, shard ^ 1):
        first = picked(blocks, lanes(block_ref.shape) == s)
        held += [first, 2 * shards - 1 - first]
    q_pos = positions(held, half, 0, q_pos_ref.shape)
    q_pos_ref[...] = q_pos
    lengths = len_ref[...].astype(f32)
    begin = jnp.zeros_like(q_pos)
    for r in range(1, len_ref.shape[1]):
        start = picked(lengths, lanes(len_ref.shape) < r)
        begin = jnp.where(q_pos >= start, start, begin)
    q_begin_ref[...] = begin


def joined_rows(partials, first, half):
    q_width = partials[0].shape[1]
    heads = q_width // HEAD
    part = pl.ds(pl.multiple_of(first, half), half)
    held = []
    for mine_ref, stat_ref, packed_ref in zip(partials[::3], partials[1::3], partials[2::3]):
        span = slice(None) if mine_ref.shape[0] == half else part
        parts = packed_ref[span, q_width:].astype(f32)
        stats = parts
        for t in (1, 2):
            stats = stats + pltpu.roll(parts, HEAD - 2 * heads * t, 1)
        held += [(mine_ref, span, stat_ref[span, :]), (packed_ref, span, stats)]
    top = functools.reduce(jnp.maximum, [stats for _, _, stats in held])
    shares = [jnp.exp2(stats - top) for _, _, stats in held]
    total = sum(
        share * pltpu.roll(stats, HEAD - heads, 1) for share, (_, _, stats) in zip(shares, held)
    )
    shares = [share / total for share in shares]
    context = []
    for h in range(heads):
        cols = slice(h * HEAD, (h + 1) * HEAD)
        context.append(
            sum(
                ref[span, cols].astype(f32) * share[:, h : h + 1]
                for (ref, span, _), share in zip(held, shares)
            ).astype(bf16)
        )
    return jnp.concatenate(context, 1)


def leave_kernel(wo_ref, *refs):
    partials, sent_ref = refs[:-1], refs[-1]
    half = sent_ref.shape[0]
    context = joined_rows(partials, (1 - lax.axis_index("req")) * half, half)
    sent_ref[...] = jnp.dot(context, wo_ref[...], preferred_element_type=f32).astype(bf16)


def keep_kernel(wo_ref, tok_ref, mine_ref, *refs):
    others, partials, (out_ref, cache_ref) = refs[:2], refs[2:-2], refs[-2:]
    share = mine_ref.shape[0] // 2
    for i, other_ref in enumerate(others):
        part = slice(i * share, (i + 1) * share)
        cache_ref[part] = mine_ref[part] + other_ref[...]
    half = out_ref.shape[0]
    first = lax.axis_index("req") * half
    context = joined_rows(partials, first, half)
    residual = tok_ref[pl.ds(pl.multiple_of(first, half), half), :].astype(f32)
    out_ref[...] = jnp.dot(context, wo_ref[...], preferred_element_type=f32) + residual


def finish_kernel(kept_ref, received_ref, hidden_ref):
    hidden_ref[...] = (kept_ref[...] + received_ref[...].astype(f32)).astype(bf16)


def cache_kernel(pieces, block_ref, slot_ref, *refs):
    pieces, (mine_ref, *other_refs) = with_refs(pieces, refs)
    shard = lax.axis_index("seq")
    slots = mine_ref.shape[0]
    key_width = mine_ref.shape[3]
    rows = slots * PAGE // 2
    pages = rows // 2 // PAGE
    for target in (mine_ref, *other_refs):
        target[...] = jnp.zeros_like(target)
    share = slots // len(other_refs)

    def place(ref, at, source):
        for k, block in enumerate(blocks_of(block_ref, source)):
            for j in range(pages):
                slot = slot_ref[block * pages + j]
                holder = slot // slots
                local = slot - holder * slots
                offset = at + (k * pages + j) * PAGE
                if not isinstance(offset, int):
                    offset = pl.multiple_of(offset, PAGE)

                def write(target, at_slot):
                    target[at_slot, 0] = ref[pl.ds(offset, PAGE), :key_width]
                    target[at_slot, 1] = ref[pl.ds(offset, PAGE), key_width:]

                @pl.when(holder == shard)
                def _():
                    write(mine_ref, local)

                for i, target in enumerate(other_refs):

                    @pl.when((holder == shard ^ 1) & (local // share == i))
                    def _():
                        write(target, local - i * share)

    for piece in pieces:
        if piece.count == 1:
            place(piece.arrays[0], 0, piece.source_of(shard, 0))
        else:

            def step(i, carry):
                place(piece.arrays[0], i * rows, piece.source_of(shard, i))
                return carry

            lax.fori_loop(0, piece.count, step, 0)


def tied_all(pieces, other):
    arrays, other = lax.optimization_barrier((operands(pieces), other))
    return with_refs(pieces, arrays)[0], other


def tied(piece, other):
    (piece,), other = tied_all([piece], other)
    return piece, other


def swap(x, n, bit):
    return lax.ppermute(x, "seq", [(i, i ^ bit) for i in range(n)])


class Piece:
    def __init__(self, arrays, source_of, count=1):
        self.arrays, self.source_of, self.count = arrays, source_of, count

    def moved(self, arrays):
        return Piece(arrays, self.source_of, self.count)


def operands(pieces):
    return [x for piece in pieces for x in piece.arrays]


def with_refs(pieces, refs):
    out = []
    for piece in pieces:
        taken, refs = refs[: len(piece.arrays)], refs[len(piece.arrays) :]
        out.append(piece.moved(taken))
    return out, refs


def at_distance(bits):
    return lambda shard, i: shard ^ bits


def move(x, pairs):
    return lax.ppermute(x, "seq", pairs)


def on_device(
    n, parts, tokens, norm_gain, w_query, key_projection, value_projection, w_out, lengths, block_split, page_slot,
):
    rows, width = tokens.shape
    half = rows // 2
    q_width = w_query.shape[1]
    kv_width = key_projection.shape[1] + value_projection.shape[1]
    kv, normed, turned = pl.pallas_call(
        project_kernel,
        out_shape=(
            struct((rows, kv_width), bf16),
            struct((rows, width), bf16),
            struct((rows, 2 * HEAD), f32),
        ),
        in_specs=in_hbm(7),
        out_specs=tuple(in_hbm(3)),
        scratch_shapes=[
            pltpu.SMEM(block_split.shape, jnp.int32),
            pltpu.SMEM(lengths.shape, jnp.int32),
            pltpu.VMEM((2 * half + 8, HEAD), f32),
            pltpu.VMEM((rows, width), bf16),
            pltpu.VMEM((1, width), f32),
            pltpu.VMEM(key_projection.shape, bf16),
            pltpu.VMEM(value_projection.shape, bf16),
            pltpu.VMEM((rows, kv_width), bf16),
            pltpu.VMEM((rows, width), bf16),
            pltpu.VMEM((rows, 2 * HEAD), f32),
            pltpu.SemaphoreType.DMA((5,)),
            pltpu.SemaphoreType.DMA((WEIGHT_STEPS,)),
            pltpu.SemaphoreType.DMA((WEIGHT_STEPS,)),
            pltpu.SemaphoreType.DMA((3,)),
        ],
        compiler_params=kernel_params(62),
        cost_estimate=cost(0, 0),
        name="project",
    )(
        block_split, lengths, rotary_constants(half), tokens, norm_gain.reshape(1, width),
        key_projection, value_projection,
    )
    staged, *places = pl.pallas_call(
        stage_kernel,
        out_shape=(
            struct((rows, kv_width), bf16),
            struct((n, rows), jnp.int32),
            struct((2 * rows, HEAD), jnp.int32),
            struct((2 * rows, HEAD), jnp.int32),
        ),
        in_specs=in_vmem(3),
        out_specs=tuple(in_vmem(4)),
        compiler_params=kernel_params(24),
        cost_estimate=cost(10**9, 10**7),
        name="stage",
    )(block_split.reshape(1, n), lengths.reshape(1, -1), kv)

    def project_queries(normed):
        queries = pl.pallas_call(
            query_kernel,
            out_shape=struct((rows, q_width), bf16),
            in_specs=in_vmem(3),
            out_specs=in_vmem(1)[0],
            compiler_params=kernel_params(24),
            cost_estimate=cost(0, 0),
            name="query",
        )(normed, turned, w_query)
        return queries, swap(queries, n, 1)

    def attend(queries, far_queries, pieces, side=None):
        arrays = operands(pieces)
        taken = rows if side is None else half
        mine, stats, packed = pl.pallas_call(
            functools.partial(attend_kernel, pieces, side),
            out_shape=(
                struct((taken, q_width), f32),
                struct((taken, HEAD), f32),
                struct((taken, q_width + HEAD), bf16),
            ),
            in_specs=in_vmem(5 + len(arrays)),
            out_specs=tuple(in_vmem(3)),
            compiler_params=kernel_params(32),
            cost_estimate=cost(0, 0),
            name="attend",
        )(*places, queries, far_queries, *arrays)
        return [mine, stats, packed]

    def place_pages(pieces):
        arrays = operands(pieces)
        shape = (2 * rows // PAGE, 2, PAGE, kv_width // 2)
        return pl.pallas_call(
            functools.partial(cache_kernel, pieces),
            out_shape=(struct(shape, bf16),) + (struct((shape[0] // 2,) + shape[1:], bf16),) * 2,
            in_specs=in_smem(2) + in_vmem(len(arrays)),
            out_specs=tuple(in_vmem(1 + 2)),
            compiler_params=kernel_params(32),
            cost_estimate=cost(0, 0),
            name="cache",
        )(block_split, page_slot, *arrays)

    if n == 16:

        def swapped(piece, bits):
            source = lambda shard, i: piece.source_of(shard ^ bits, i)
            return Piece([swap(piece.arrays[0], n, bits)], source)

        own = Piece([kv], at_distance(0))
        second, first, beside = swapped(own, 8), swapped(own, 4), swapped(own, 2)
        first, (normed, staged) = tied(first, (normed, staged))
        first_across = swapped(first, 2)
        queries, far_queries = project_queries(normed)
        second, (staged, queries) = tied(second, (staged, queries))
        own = own.moved([staged])
        (second, first_across, beside), _ = tied_all([second, first_across, beside], ())
        third = swapped(second, 4)
        last = swapped(second, 6)
        early = [own, beside, first, second, first_across]
        partials = attend(queries, far_queries, early)
        partials[2] = swap(partials[2], n, 1)
        queries, partials[1] = lax.optimization_barrier((queries, partials[1]))
        remaining = [third, swapped(second, 2), last]
        placed = early + remaining
    else:
        same = [list(range(c, n, 2)) for c in range(2)]
        gathered = lax.all_gather(kv, "seq", axis=0, tiled=True, axis_index_groups=same)
        remaining = [Piece([gathered], lambda shard, i: 2 * i + shard % 2, n // 2)]
        partials, placed = [], remaining
        queries, far_queries = project_queries(normed)
    leaving = attend(queries, far_queries, remaining, 1)
    queries, leaving[1] = lax.optimization_barrier((queries, leaving[1]))
    leaving[2] = swap(leaving[2], n, 1)
    staying = attend(queries, far_queries, remaining, 0)
    leaving[0], staying[1] = lax.optimization_barrier((leaving[0], staying[1]))
    sent = pl.pallas_call(
        leave_kernel,
        out_shape=struct((half, width), bf16),
        in_specs=in_vmem(4 + len(partials)),
        out_specs=in_vmem(1)[0],
        compiler_params=kernel_params(24),
        cost_estimate=cost(0, 0),
        name="leave",
    )(w_out, *partials, *leaving)
    received = lax.ppermute(sent, "req", [(i, (i + 1) % parts) for i in range(parts)])
    staying[2] = swap(staying[2], n, 1)
    placed, (staying[2], sent) = tied_all(placed, (staying[2], sent))
    cache, *other = place_pages(placed)
    kept, cache = pl.pallas_call(
        keep_kernel,
        out_shape=(struct((half, width), f32), struct(cache.shape, bf16)),
        in_specs=in_vmem(6 + 2 + len(partials)),
        out_specs=tuple(in_vmem(2)),
        compiler_params=kernel_params(24),
        cost_estimate=cost(0, 0),
        name="keep",
    )(w_out, tokens, cache, *[swap(x, n, 1) for x in other], *partials, *staying)
    hidden = pl.pallas_call(
        finish_kernel,
        out_shape=struct((half, width), bf16),
        in_specs=in_vmem(2),
        out_specs=in_vmem(1)[0],
        compiler_params=kernel_params(24),
        cost_estimate=cost(0, 0),
        name="finish",
    )(kept, received)
    return hidden, cache


def solution(mesh):
    in_specs = (
        P("seq", None),
        P(),
        P(None, "req"),
        P(None, "req"),
        P(None, "req"),
        P("req", None),
        P(),
        P(),
        P(),
    )
    out_specs = (P(("seq", "req"), None), P("seq", None, None, "req"))
    body = functools.partial(on_device, mesh.shape["seq"], mesh.shape["req"])
    return jax.shard_map(body, mesh=mesh, in_specs=in_specs, out_specs=out_specs, check_vma=False)
```
